32 devices in a mesh: tile: 16 (over z, y, core), freq: 2 (over x).
Axes of the slice: x: 2, y: 2, z: 4, core: 2. Of those that a mesh axis runs over, the one named last changes fastest.
Arguments:
- visibilities: float32 [2, 2048, 2, 128], P('freq', 'tile'), may hold values from -6 to 6
- uv_cell: int32 [2, 2048, 2, 128], P('freq', 'tile'), may hold values from 0 to 120
- sub_pixel: int32 [2, 2048, 2, 128], P('freq', 'tile'), may hold values from 0 to 7
- w_plane: int32 [2, 2048], P('freq', 'tile'), may hold values from 0 to 15
- block_tile: int32 [2, 2048], P('freq', 'tile'), may hold values from 0 to 31, as said below
- model_grid: bfloat16 [2, 32, 128, 256], P('freq', 'tile'), may hold values from -3 to 3
- kernel_table: bfloat16 [16, 8, 8], replicated, may hold values from 0.049804688 to 1
- coupling: float32 [2, 2], replicated, may hold values from -4 to 4
Outputs:
- residuals: float32 [2, 2048, 2, 128], P('freq', 'tile')
- coupled_grid: float32 [2, 32, 128, 256], P('freq', 'tile')
The draws below stay inside these ranges and needn't reach their ends.
Inputs may be any that keep to these rules, and one draw needn't show every extreme that they name: `block_tile`: among the 128 blocks of one plane on one device (aligned blocks), at most 24 have tiles of one owner, the owner of tile k being k // 2; in every plane some owner gets exactly 24 blocks from every device.
All inputs are finite; a program needn't handle non-finite values.
Results may differ from the reference program's by a relative error of at most 0.0034.
Values may be sent and summed in bfloat16 or wider, within the bound.
No kernel may reach another device: no remote copies, remote signals or barrier semaphores. Data moves between devices by JAX's collectives and lax.ppermute only.
A program may use at most 64 MiB of HBM per device.

```python
import math
import jax
import jax.numpy as jnp
from jax import lax

TS = 128
KS = 8
OS = 8
W_PLANES = 16
ROWS = 128
TILES_DEV = 2
BLK_DEV = 128
FREQ = 2
TILES = 32
BLOCKS = 2048
CAP = 24


def draw_block_tile(key, part):
    owners = BLOCKS // BLK_DEV
    position_holders = owners * CAP
    hottest = jax.random.randint(jax.random.fold_in(key, 11), (FREQ,), 0, owners)
    device_base = jax.random.fold_in(key, 23)

    def one_device(index):
        plane = index // owners
        device_key = jax.random.fold_in(device_base, index)
        noise_key, tile_key, order_key = jax.random.split(device_key, 3)
        slot_owner = jnp.arange(position_holders, dtype=jnp.int32) // CAP
        ahead = (slot_owner - hottest[plane]) % owners
        separation_gap = jnp.minimum(ahead, owners - ahead)
        reward_extra = jnp.where(separation_gap == 0, 8, jnp.maximum(0, 3 - separation_gap))
        random_jitter = jax.random.randint(noise_key, (position_holders,), 0, 4096)
        rating_value = (reward_extra * 4096 + random_jitter) * position_holders + jnp.arange(position_holders, dtype=jnp.int32)
        chosen = lax.top_k(rating_value, BLK_DEV)[1]
        owner = chosen // CAP
        local = jax.random.randint(tile_key, (BLK_DEV,), 0, TILES_DEV)
        order = jax.random.permutation(order_key, BLK_DEV)
        return (owner * TILES_DEV + local)[order].astype(jnp.int32)
    tiles = jax.vmap(one_device)(jnp.arange(FREQ * owners, dtype=jnp.int32))
    return tiles.reshape(FREQ, BLOCKS)


def plant(drawn, own_key, smallest, top_value):
    spot = [jax.random.randint(jax.random.fold_in(own_key, axis), (), 0, length) for axis, length in enumerate(drawn.shape)]
    longest = drawn.shape.index(max(drawn.shape))
    beside = spot[:longest] + [(spot[longest] + 1) % drawn.shape[longest]] + spot[longest + 1:]
    return drawn.at[tuple(spot)].set(smallest).at[tuple(beside)].set(top_value)


def block_levels(key, dims, cuts, low, largest):
    level = 1.0
    for position, blocks in cuts:
        heights = jax.random.uniform(jax.random.fold_in(jax.random.fold_in(key, 6), position), (blocks,), jnp.float32, low / len(cuts), largest / len(cuts))
        level = level * jnp.repeat(jnp.exp(heights), dims[position] // blocks).reshape((-1,) + (1,) * (len(dims) - 1 - position))
    return level


def normal_values(key, dims, spread, reach, cuts=(), kind=jnp.bfloat16):
    loudness = block_levels(key, dims, cuts, -0.22, 0.18) if cuts else 1.0
    result = jax.random.normal(key, dims, jnp.float32) * spread * loudness
    return jnp.minimum(jnp.maximum(result, -reach), reach).astype(kind)


def setup_inputs(seed: int = 0) -> dict:
    seeds = jax.random.split(jax.random.key(seed), 9)
    return {
        "visibilities": normal_values(seeds[0], (FREQ, BLOCKS, 2, ROWS), 1.0, 6.0, ((0, 2), (1, 16)), jnp.float32),
        "uv_cell": plant(jax.random.randint(seeds[1], (FREQ, BLOCKS, 2, ROWS), 0, TS - KS + 1), jax.random.fold_in(seeds[1], 1), 0, TS - KS).astype(jnp.int32),
        "sub_pixel": plant(jax.random.randint(seeds[2], (FREQ, BLOCKS, 2, ROWS), 0, OS), jax.random.fold_in(seeds[2], 1), 0, OS - 1).astype(jnp.int32),
        "w_plane": plant(jax.random.randint(seeds[3], (FREQ, BLOCKS), 0, W_PLANES), jax.random.fold_in(seeds[3], 1), 0, W_PLANES - 1).astype(jnp.int32),
        "block_tile": draw_block_tile(jax.random.fold_in(seeds[8], 71), 0),
        "model_grid": normal_values(seeds[5], (FREQ, TILES, TS, 2 * TS), 0.5, 3.0, ((0, 2), (1, 16))),
        "kernel_table": jnp.clip(jnp.exp(jax.random.uniform(seeds[6], (W_PLANES, OS, KS), jnp.float32, math.log(0.049804688), math.log(1.0))), 0.049804688, 1.0).astype(jnp.bfloat16),
        "coupling": normal_values(seeds[7], (FREQ, FREQ), FREQ ** -0.5, 4.0, (), jnp.float32),
    }


def plane_work(samples, cells, offsets, planes, tiles, model, kernel_table):
    cluster_count = 256
    count = samples.shape[0] // cluster_count
    spans = jnp.arange(KS, dtype=jnp.int32)

    def advance(grid_sum, pieces):
        sample_part, cell_part, offset_part, plane_part, tile_part = pieces
        row_taps = kernel_table[plane_part[:, None], offset_part[:, 0, :]].astype(jnp.float32)
        column_taps = kernel_table[plane_part[:, None], offset_part[:, 1, :]].astype(jnp.float32)
        cell_rows = cell_part[:, 0, :, None, None] + spans[None, None, :, None]
        cell_columns = cell_part[:, 1, :, None, None] + spans[None, None, None, :]
        tile_index = tile_part[:, None, None, None]
        real_patch = model[tile_index, cell_rows, cell_columns].astype(jnp.float32)
        imag_patch = model[tile_index, cell_rows, cell_columns + TS].astype(jnp.float32)
        outer = row_taps[:, :, :, None] * column_taps[:, :, None, :]
        model_real = jnp.sum(real_patch * outer, axis=(2, 3))
        model_imag = jnp.sum(imag_patch * outer, axis=(2, 3))
        residual = sample_part - jnp.stack([model_real, model_imag], axis=1)
        weighted = (residual[:, :, :, None] * column_taps[:, None, :, :]).astype(jnp.bfloat16)
        weighted = lax.optimization_barrier(weighted).astype(jnp.float32)
        add_real = row_taps[:, :, :, None] * weighted[:, 0, :, None, :]
        imaginary_addend = row_taps[:, :, :, None] * weighted[:, 1, :, None, :]
        grid_sum = grid_sum.at[tile_index, cell_rows, cell_columns].add(add_real)
        grid_sum = grid_sum.at[tile_index, cell_rows, cell_columns + TS].add(imaginary_addend)
        return grid_sum, residual

    def split(values):
        return values.reshape((count, cluster_count) + values.shape[1:])

    start_grid = jnp.zeros((TILES, TS, 2 * TS), jnp.float32)
    grid_sum, residual = lax.scan(advance, start_grid, (split(samples), split(cells), split(offsets), split(planes), split(tiles)))
    return grid_sum, residual.reshape(samples.shape)


def reference(visibilities, uv_cell, sub_pixel, w_plane, block_tile, model_grid, kernel_table, coupling):
    def one_plane(pieces):
        return plane_work(pieces[0], pieces[1], pieces[2], pieces[3], pieces[4], pieces[5], kernel_table)

    grids, residuals = lax.map(one_plane, (visibilities, uv_cell, sub_pixel, w_plane, block_tile, model_grid))
    rounded = grids.astype(jnp.bfloat16).astype(jnp.float32)
    coupled_grid = jnp.einsum("fg,gtij->ftij", coupling, rounded, precision=lax.Precision.HIGHEST)
    return residuals, coupled_grid
```

```python
import jax
import jax.numpy as jnp
from jax import lax
from jax.experimental import pallas as pl
from jax.experimental.pallas import tpu as pltpu
from jax.sharding import PartitionSpec as P

UNROLL = 4


def spread_parts(start, offset, table_row):
    lane_row = lax.broadcasted_iota(jnp.int32, (16, 128), 0)
    delta = lane_row - jnp.broadcast_to(start, (16, 128))
    index = (delta & 15) + jnp.broadcast_to(offset * 16, (16, 128))
    table = jnp.broadcast_to(table_row, (8, 128))
    taps = jnp.concatenate(
        [
            jnp.take_along_axis(table, index[:8], axis=1, mode="promise_in_bounds"),
            jnp.take_along_axis(table, index[8:], axis=1, mode="promise_in_bounds"),
        ],
        axis=0,
    )
    group = (15 - delta) >> 4
    return taps, group


def grid_kernel(
    plane_ref, tile_ref, vis_ref, cell_ref, sub_ref, table_ref, model_ref, residual_ref, grid_ref
):
    blocks = vis_ref.shape[0] // 2
    side = model_ref.shape[2]
    groups = side // 16
    grid_ref[...] = jnp.zeros_like(grid_ref)

    def one_block(b):
        tile = tile_ref[b]
        table_row = table_ref[pl.ds(plane_ref[b], 1), :]
        row_taps, row_group = spread_parts(
            cell_ref[pl.ds(2 * b, 1), :], sub_ref[pl.ds(2 * b, 1), :], table_row
        )
        column_taps, column_group = spread_parts(
            cell_ref[pl.ds(2 * b + 1, 1), :], sub_ref[pl.ds(2 * b + 1, 1), :], table_row
        )
        zero = jnp.zeros((16, 128), jnp.bfloat16)
        row_taps = row_taps.astype(jnp.bfloat16)
        row_group = row_group.astype(jnp.float32).astype(jnp.bfloat16)
        row_matrix = jnp.concatenate(
            [jnp.where(row_group == k, row_taps, zero) for k in range(groups)], axis=0
        )
        partial = jnp.dot(model_ref[tile], row_matrix, preferred_element_type=jnp.float32)
        samples = []
        for part in range(2):
            picked = jnp.zeros((16, 128), jnp.float32)
            for k in range(groups):
                low = part * side + 16 * k
                picked = jnp.where(column_group == k, partial[low : low + 16], picked)
            model = jnp.sum(picked * column_taps, axis=0, keepdims=True)
            residual = vis_ref[pl.ds(2 * b + part, 1), :] - model
            residual_ref[pl.ds(2 * b + part, 1), :] = residual
            samples.append((residual * column_taps).astype(jnp.bfloat16))
        column_group = column_group.astype(jnp.float32).astype(jnp.bfloat16)
        weighted = jnp.concatenate(
            [
                jnp.where(column_group == k, samples[part], zero)
                for part in range(2)
                for k in range(groups)
            ],
            axis=0,
        )
        grid_ref[tile] += lax.dot_general(
            row_matrix,
            weighted,
            (((1,), (1,)), ((), ())),
            preferred_element_type=jnp.float32,
        )

    def step(turn, carry):
        for which in range(UNROLL):
            one_block(turn * UNROLL + which)
        return carry

    lax.fori_loop(0, blocks // UNROLL, step, 0)


def grid_blocks(planes, tiles, samples, cells, offsets, table, model):
    blocks = samples.shape[0]
    rows = samples.shape[2]
    count, wide, side = model.shape
    vmem = pl.BlockSpec(memory_space=pltpu.VMEM)
    smem = pl.BlockSpec(memory_space=pltpu.SMEM)
    residual, grid = pl.pallas_call(
        grid_kernel,
        out_shape=(
            jax.ShapeDtypeStruct((2 * blocks, rows), jnp.float32),
            jax.ShapeDtypeStruct((count, side, wide), jnp.float32),
        ),
        in_specs=[smem, smem, vmem, vmem, vmem, vmem, vmem],
        out_specs=(vmem, vmem),
        compiler_params=pltpu.CompilerParams(vmem_limit_bytes=48 * 1024 * 1024),
        name="grid_blocks",
    )(
        planes,
        tiles,
        samples.reshape(2 * blocks, rows),
        cells.reshape(2 * blocks, rows),
        offsets.reshape(2 * blocks, rows),
        table,
        model,
    )
    return residual.reshape(blocks, 2, rows), grid


def body(visibilities, uv_cell, sub_pixel, w_plane, block_tile, model_grid, kernel_table, coupling):
    kernel_planes, oversample, support = kernel_table.shape
    table = jnp.pad(kernel_table.astype(jnp.float32), ((0, 0), (0, 0), (0, 16 - support))).reshape(
        kernel_planes, 16 * oversample
    )
    model = lax.all_gather(jnp.swapaxes(model_grid[0], 1, 2), "tile", axis=0, tiled=True)
    residual, grid = grid_blocks(
        w_plane[0], block_tile[0], visibilities[0], uv_cell[0], sub_pixel[0], table, model
    )
    grid_sum = lax.psum_scatter(grid, "tile", scatter_dimension=0, tiled=True)
    grid_rounded = grid_sum.astype(jnp.bfloat16)[None]
    own_row = lax.dynamic_index_in_dim(coupling, lax.axis_index("freq"), 0, keepdims=False)
    coupled_grid = jnp.sum(
        own_row[:, None, None, None]
        * lax.all_gather(grid_rounded, "freq", axis=0, tiled=True).astype(jnp.float32),
        axis=0,
    )[None]
    return (residual[None], coupled_grid)


def solution(mesh):
    return jax.shard_map(
        body,
        mesh=mesh,
        in_specs=(
            P("freq", "tile", None, None),
            P("freq", "tile", None, None),
            P("freq", "tile", None, None),
            P("freq", "tile"),
            P("freq", "tile"),
            P("freq", "tile", None, None),
            P(),
            P(),
        ),
        out_specs=(P("freq", "tile", None, None), P("freq", "tile", None, None)),
        check_vma=False,
    )
```

```python
import jax
import jax.numpy as jnp
from jax import lax
from jax.experimental import pallas as pl
from jax.experimental.pallas import tpu as pltpu
from jax.sharding import PartitionSpec as P

UNROLL = 4
VMEM = pl.BlockSpec(memory_space=pltpu.VMEM)
SMEM = pl.BlockSpec(memory_space=pltpu.SMEM)
PARAMS = pltpu.CompilerParams(vmem_limit_bytes=32 * 1024 * 1024)


def pack_kernel(owners, capacity, tiles_here, planes, plane_ref, tile_ref, vis_ref, cell_ref, sub_ref,
                sent_ref, slot_ref, count_ref):
    blocks = tile_ref.shape[0]
    pairs = owners // 2
    part = lax.broadcasted_iota(jnp.int32, (4, 128), 0)
    lane = lax.broadcasted_iota(jnp.int32, (4, 128), 1)
    sent_ref[...] = jnp.zeros_like(sent_ref)
    for d in range(owners):
        sent_ref[d * (capacity + 1) + capacity] = jnp.where(part == 0, float(planes), 0.0)
    for h in range(pairs):
        count_ref[h] = 0

    def step(b, carry):
        tile = tile_ref[b]
        owner = lax.div(tile, tiles_here)
        high = (owner >= pairs).astype(jnp.int32)
        pair = owner - high * pairs
        rank = count_ref[pair]
        count_ref[pair] = rank + 1
        place = rank >> 1
        target = pair + (rank & 1) * pairs
        local = tile - owner * tiles_here + high * tiles_here
        slot_ref[b] = target * capacity + place
        position = (cell_ref[b] * 8 + sub_ref[b]).astype(jnp.float32)
        sent_ref[target * (capacity + 1) + place] = jnp.concatenate([vis_ref[b], position], axis=0)
        about = target * (capacity + 1) + capacity
        value = jnp.where(part == 0, plane_ref[b], jnp.where(part == 1, local, place + 1))
        sent_ref[about] = jnp.where(
            (lane == place) | (part == 2), value.astype(jnp.float32), sent_ref[about]
        )
        return carry

    lax.fori_loop(0, blocks, step, 0)


def spread_parts(position, table_row):
    position = jnp.broadcast_to(position, (16, 128))
    delta = lax.broadcasted_iota(jnp.int32, (16, 128), 0) - (position >> 3)
    index = (delta & 15) + ((position & 7) << 4)
    table = jnp.broadcast_to(table_row, (8, 128))
    taps = jnp.concatenate(
        [
            jnp.take_along_axis(table, index[:8], axis=1, mode="promise_in_bounds"),
            jnp.take_along_axis(table, index[8:], axis=1, mode="promise_in_bounds"),
        ],
        axis=0,
    )
    return taps, (15 - delta) >> 4


def grid_kernel(owners, capacity, member_ref, got_ref, table_ref, model_ref, residual_ref, own_ref,
                other_ref, turned_ref, grid_ref, about_ref, list_ref, sem):
    tiles, side, wide = model_ref.shape
    groups = side // 16
    zero_row = table_ref.shape[0] - 8
    copies = [
        pltpu.make_async_copy(
            got_ref.at[s * (capacity + 1) + capacity], about_ref.at[s], sem.at[s]
        )
        for s in range(owners)
    ]
    for copy in copies:
        copy.start()
    for t in range(tiles):
        turned_ref[t] = model_ref[t].T
    grid_ref[...] = jnp.zeros_like(grid_ref)
    for copy in copies:
        copy.wait()

    total = jnp.int32(0)
    for s in range(owners):
        total = total + about_ref[s, 2, 0].astype(jnp.int32)
    spare = (UNROLL - total % UNROLL) % UNROLL
    for u in range(UNROLL):
        list_ref[u] = zero_row * 65536

    def enlist(s, filled):
        for k in range(capacity):
            entry = (about_ref[s, 0, k] * 65536.0 + about_ref[s, 1, k] * 4096.0).astype(jnp.int32)
            list_ref[filled + k] = entry + s * capacity + k
        return filled + about_ref[s, 2, 0].astype(jnp.int32)

    lax.fori_loop(0, owners, enlist, spare)

    def one_block(which):
        entry = list_ref[which]
        slot = entry & 4095
        tile = (entry >> 12) & 15
        data = got_ref[slot + lax.div(slot, capacity)]
        position = data[2:4].astype(jnp.int32)
        table_row = table_ref[pl.ds(entry >> 16, 1), :]
        row_taps, row_group = spread_parts(position[0:1], table_row)
        column_taps, column_group = spread_parts(position[1:2], table_row)
        zero = jnp.zeros((16, 128), jnp.bfloat16)
        row_taps = row_taps.astype(jnp.bfloat16)
        row_group = row_group.astype(jnp.float32).astype(jnp.bfloat16)
        row_matrix = jnp.concatenate(
            [jnp.where(row_group == k, row_taps, zero) for k in range(groups)], axis=0
        )
        partial = jnp.dot(turned_ref[tile], row_matrix, preferred_element_type=jnp.float32)
        residuals, samples = [], []
        for part in range(2):
            picked = jnp.zeros((16, 128), jnp.float32)
            for k in range(groups):
                low = part * side + 16 * k
                picked = jnp.where(column_group == k, partial[low : low + 16], picked)
            model = jnp.sum(picked * column_taps, axis=0, keepdims=True)
            residual = data[part : part + 1] - model
            residuals.append(residual)
            samples.append((residual * column_taps).astype(jnp.bfloat16))
        residual_ref[slot] = jnp.concatenate(residuals, axis=0).astype(jnp.bfloat16)
        column_group = column_group.astype(jnp.float32).astype(jnp.bfloat16)
        weighted = jnp.concatenate(
            [
                jnp.where(column_group == k, samples[part], zero)
                for part in range(2)
                for k in range(groups)
            ],
            axis=0,
        )
        grid_ref[tile] += lax.dot_general(
            row_matrix,
            weighted,
            (((1,), (1,)), ((), ())),
            preferred_element_type=jnp.float32,
        )

    def step(turn, carry):
        for which in range(UNROLL):
            one_block(turn * UNROLL + which)
        return carry

    lax.fori_loop(0, (total + spare) // UNROLL, step, 0)
    half = tiles // 2
    member = member_ref[0]
    for t in range(half):
        own_ref[t] = grid_ref[member * half + t]
        other_ref[t] = grid_ref[(1 - member) * half + t].astype(jnp.bfloat16)


def body(visibilities, uv_cell, sub_pixel, w_plane, block_tile, model_grid, kernel_table, coupling):
    owners = lax.axis_size("tile")
    pairs = owners // 2
    _, blocks, _, rows = visibilities.shape
    capacity = 3 * blocks // owners
    _, tiles_here, side, wide = model_grid.shape
    planes, oversample, support = kernel_table.shape
    slots = owners * capacity
    me = lax.axis_index("tile")
    member = me // pairs
    swap = [(t, (t + pairs) % owners) for t in range(owners)]

    sent, slot = pl.pallas_call(
        lambda *refs: pack_kernel(owners, capacity, tiles_here, planes, *refs),
        out_shape=(
            jax.ShapeDtypeStruct((slots + owners, 4, rows), jnp.float32),
            jax.ShapeDtypeStruct((blocks,), jnp.int32),
        ),
        in_specs=[SMEM, SMEM, VMEM, VMEM, VMEM],
        out_specs=(VMEM, SMEM),
        scratch_shapes=[pltpu.SMEM((pairs,), jnp.int32)],
        compiler_params=PARAMS,
        name="pack_blocks",
    )(w_plane[0], block_tile[0], visibilities[0], uv_cell[0], sub_pixel[0])
    got = lax.all_to_all(sent, "tile", split_axis=0, concat_axis=0, tiled=True)

    model_own = model_grid[0]
    model_other = lax.ppermute(model_own, "tile", swap)
    model = jnp.where(
        member == 0,
        jnp.concatenate([model_own, model_other]),
        jnp.concatenate([model_other, model_own]),
    )
    table = jnp.pad(
        kernel_table.astype(jnp.float32), ((0, 8), (0, 0), (0, 16 - support))
    ).reshape(planes + 8, 16 * oversample)
    residual, own, other = pl.pallas_call(
        lambda *refs: grid_kernel(owners, capacity, *refs),
        out_shape=(
            jax.ShapeDtypeStruct((slots, 2, rows), jnp.bfloat16),
            jax.ShapeDtypeStruct((tiles_here, side, wide), jnp.float32),
            jax.ShapeDtypeStruct((tiles_here, side, wide), jnp.bfloat16),
        ),
        in_specs=[SMEM, VMEM, VMEM, VMEM],
        out_specs=(VMEM, VMEM, VMEM),
        scratch_shapes=[
            pltpu.VMEM((2 * tiles_here, wide, side), jnp.bfloat16),
            pltpu.VMEM((2 * tiles_here, side, wide), jnp.float32),
            pltpu.SMEM((owners, 4, rows), jnp.float32),
            pltpu.SMEM((slots + capacity + UNROLL,), jnp.int32),
            pltpu.SemaphoreType.DMA((owners,)),
        ],
        compiler_params=PARAMS,
        name="grid_blocks",
    )(member[None], got, table, model)

    returned = lax.all_to_all(residual, "tile", split_axis=0, concat_axis=0, tiled=True)
    residuals = jnp.take(returned, slot, axis=0, mode="clip").astype(jnp.float32)[None]
    grid_sum = own + lax.ppermute(other, "tile", swap).astype(jnp.float32)
    grid_rounded = grid_sum.astype(jnp.bfloat16)[None]
    own_row = lax.dynamic_index_in_dim(coupling, lax.axis_index("freq"), 0, keepdims=False)
    coupled_grid = jnp.sum(
        own_row[:, None, None, None]
        * lax.all_gather(grid_rounded, "freq", axis=0, tiled=True).astype(jnp.float32),
        axis=0,
    )[None]
    return (residuals, coupled_grid)


def solution(mesh):
    return jax.shard_map(
        body,
        mesh=mesh,
        in_specs=(
            P("freq", "tile", None, None),
            P("freq", "tile", None, None),
            P("freq", "tile", None, None),
            P("freq", "tile"),
            P("freq", "tile"),
            P("freq", "tile", None, None),
            P(),
            P(),
        ),
        out_specs=(P("freq", "tile", None, None), P("freq", "tile", None, None)),
        check_vma=False,
    )
```

```python
import jax
import jax.numpy as jnp
from jax import lax
from jax.experimental import pallas as pl
from jax.experimental.pallas import tpu as pltpu
from jax.sharding import PartitionSpec as P

UNROLL = 4
VMEM = pl.BlockSpec(memory_space=pltpu.VMEM)
SMEM = pl.BlockSpec(memory_space=pltpu.SMEM)
ANY = pl.BlockSpec(memory_space=pl.ANY)
PARAMS = pltpu.CompilerParams(vmem_limit_bytes=32 * 1024 * 1024)
TILE_CODE = 4096
PLANE_CODE = 65536


def pack_kernel(pairs, capacity, tiles_here, planes, plane_ref, tile_ref, vis_hbm, cell_hbm, sub_hbm,
                sent_ref, slot_ref, vis_ref, cell_ref, sub_ref, about_ref, count_ref, load_sem, about_sem):
    blocks = tile_ref.shape[0]
    loads = [
        pltpu.make_async_copy(source, target, load_sem.at[i])
        for i, (source, target) in enumerate(
            [(vis_hbm, vis_ref), (cell_hbm, cell_ref), (sub_hbm, sub_ref)]
        )
    ]
    for copy in loads:
        copy.start()
    part = lax.broadcasted_iota(jnp.int32, (4, 128), 0)
    empty = jnp.where(part == 0, float(planes * PLANE_CODE), 0.0)
    abouts = [d * (capacity + 1) + capacity for d in range(pairs)]
    for d in range(pairs):
        sent_ref[d * (capacity + 1)] = jnp.zeros((4, 128), jnp.float32)
        sent_ref[abouts[d]] = empty
        count_ref[d] = 0
    fills = [
        pltpu.make_async_copy(sent_ref.at[abouts[d]], about_ref.at[d], about_sem.at[d])
        for d in range(pairs)
    ]
    for copy in fills:
        copy.start()
    for copy in fills + loads:
        copy.wait()

    def one_block(b):
        tile = tile_ref[b]
        owner = lax.div(tile, tiles_here)
        high = (owner >= pairs).astype(jnp.int32)
        pair = owner - high * pairs
        local = tile - (owner - high) * tiles_here
        place = count_ref[pair]
        count_ref[pair] = place + 1
        slot_ref[b] = pair * capacity + place
        code = (plane_ref[b] * PLANE_CODE + local * TILE_CODE).astype(jnp.float32)
        about_ref[pair, 0, place] = code
        position = (cell_ref[b] * 8 + sub_ref[b]).astype(jnp.float32)
        sent_ref[pair * (capacity + 1) + place] = jnp.concatenate([vis_ref[b], position], axis=0)

    def step(turn, carry):
        for which in range(8):
            one_block(turn * 8 + which)
        return carry

    lax.fori_loop(0, blocks // 8, step, 0)
    for d in range(pairs):
        about_ref[d, 1, 0] = count_ref[d].astype(jnp.float32)
    returns = [
        pltpu.make_async_copy(about_ref.at[d], sent_ref.at[abouts[d]], about_sem.at[d])
        for d in range(pairs)
    ]
    for copy in returns:
        copy.start()
    for copy in returns:
        copy.wait()


def spread_parts(position, table_row):
    position = jnp.broadcast_to(position, (16, 128))
    delta = lax.broadcasted_iota(jnp.int32, (16, 128), 0) - (position >> 3)
    index = (delta & 15) + ((position & 7) << 4)
    table = jnp.broadcast_to(table_row, (8, 128))
    taps = jnp.concatenate(
        [
            jnp.take_along_axis(table, index[:8], axis=1, mode="promise_in_bounds"),
            jnp.take_along_axis(table, index[8:], axis=1, mode="promise_in_bounds"),
        ],
        axis=0,
    )
    return taps, (15 - delta) >> 4


def grid_kernel(pairs, capacity, member_ref, got_ref, table_ref, model_ref, residual_ref, own_ref,
                other_ref, turned_ref, grid_ref, row_ref, partial_ref, code_ref, about_ref, list_ref, sem):
    tiles, side, wide = model_ref.shape
    groups = side // 16
    zero_row = table_ref.shape[0] - 8
    lane = lax.broadcasted_iota(jnp.int32, (1, 128), 1)
    for s in range(pairs):
        about = got_ref[s * (capacity + 1) + capacity].astype(jnp.int32)
        code_ref[s, 0:1, :] = about[0:1] + (lane + s * capacity)
        code_ref[s, 1:2, :] = about[1:2]
    fill = pltpu.make_async_copy(code_ref, about_ref, sem)
    fill.start()
    for t in range(tiles):
        turned_ref[t] = model_ref[t].T
    grid_ref[...] = jnp.zeros_like(grid_ref)
    fill.wait()

    total = jnp.int32(0)
    for s in range(pairs):
        total = total + about_ref[s, 1, 0]
    spare = jnp.where(total == 0, UNROLL, lax.rem(UNROLL - lax.rem(total, UNROLL), UNROLL))
    for u in range(UNROLL):
        list_ref[u] = zero_row * PLANE_CODE

    def enlist(s, filled):
        for k in range(capacity):
            list_ref[filled + k] = about_ref[s, 0, k]
        return filled + about_ref[s, 1, 0]

    lax.fori_loop(0, pairs, enlist, spare)
    chunks = lax.div(total + spare, UNROLL)
    zero = jnp.zeros((16, 128), jnp.bfloat16)

    def read(which):
        entry = list_ref[which]
        slot = entry & (TILE_CODE - 1)
        tile = lax.div(entry, TILE_CODE) & 15
        table_row = table_ref[pl.ds(lax.div(entry, PLANE_CODE), 1), :]
        return slot, tile, table_row, got_ref[slot + lax.div(slot, capacity)]

    def front(which, u):
        _, tile, table_row, data = read(which)
        taps, group = spread_parts(data[2:3].astype(jnp.int32), table_row)
        taps = taps.astype(jnp.bfloat16)
        group = group.astype(jnp.float32).astype(jnp.bfloat16)
        row_matrix = jnp.concatenate(
            [jnp.where(group == k, taps, zero) for k in range(groups)], axis=0
        )
        row_ref[u] = row_matrix
        partial_ref[u] = jnp.dot(turned_ref[tile], row_matrix, preferred_element_type=jnp.float32)

    def back(which, u):
        slot, tile, table_row, data = read(which)
        taps, group = spread_parts(data[3:4].astype(jnp.int32), table_row)
        residuals, samples = [], []
        for part in range(2):
            picked = jnp.zeros((16, 128), jnp.float32)
            for k in range(groups):
                low = part * side + 16 * k
                picked = jnp.where(group == k, partial_ref[u, low : low + 16], picked)
            model = jnp.sum(picked * taps, axis=0, keepdims=True)
            residual = data[part : part + 1] - model
            residuals.append(residual)
            samples.append((residual * taps).astype(jnp.bfloat16))
        residual_ref[slot] = jnp.concatenate(residuals, axis=0).astype(jnp.bfloat16)
        group = group.astype(jnp.float32).astype(jnp.bfloat16)
        weighted = jnp.concatenate(
            [
                jnp.where(group == k, samples[part], zero)
                for part in range(2)
                for k in range(groups)
            ],
            axis=0,
        )
        grid_ref[tile] += lax.dot_general(
            row_ref[u],
            weighted,
            (((1,), (1,)), ((), ())),
            preferred_element_type=jnp.float32,
        )

    def step(turn, carry):
        for u in range(UNROLL):
            back((turn - 1) * UNROLL + u, u)
        for u in range(UNROLL):
            front(turn * UNROLL + u, u)
        return carry

    for u in range(UNROLL):
        front(u, u)
    lax.fori_loop(1, chunks, step, 0)
    for u in range(UNROLL):
        back((chunks - 1) * UNROLL + u, u)
    half = tiles // 2
    member = member_ref[0]
    for t in range(half):
        own_ref[t] = grid_ref[member * half + t]
        other_ref[t] = grid_ref[(1 - member) * half + t].astype(jnp.bfloat16)


def body(visibilities, uv_cell, sub_pixel, w_plane, block_tile, model_grid, kernel_table, coupling):
    owners = lax.axis_size("tile")
    pairs = owners // 2
    _, blocks, _, rows = visibilities.shape
    capacity = 2 * (3 * blocks // owners)
    _, tiles_here, side, wide = model_grid.shape
    planes, oversample, support = kernel_table.shape
    slots = pairs * capacity
    member = lax.axis_index("tile") // pairs
    swap = [(t, (t + pairs) % owners) for t in range(owners)]
    halves = [list(range(pairs)), list(range(pairs, owners))]

    model_own = model_grid[0]
    model_other = lax.ppermute(model_own, "tile", swap)
    sent, slot = pl.pallas_call(
        lambda *refs: pack_kernel(pairs, capacity, tiles_here, planes, *refs),
        out_shape=(
            jax.ShapeDtypeStruct((slots + pairs, 4, rows), jnp.float32),
            jax.ShapeDtypeStruct((blocks,), jnp.int32),
        ),
        in_specs=[SMEM, SMEM, ANY, ANY, ANY],
        out_specs=(VMEM, SMEM),
        scratch_shapes=[
            pltpu.VMEM((blocks, 2, rows), jnp.float32),
            pltpu.VMEM((blocks, 2, rows), jnp.int32),
            pltpu.VMEM((blocks, 2, rows), jnp.int32),
            pltpu.SMEM((pairs, 4, rows), jnp.float32),
            pltpu.SMEM((pairs,), jnp.int32),
            pltpu.SemaphoreType.DMA((3,)),
            pltpu.SemaphoreType.DMA((pairs,)),
        ],
        compiler_params=PARAMS,
        name="pack_blocks",
    )(w_plane[0], block_tile[0], visibilities[0], uv_cell[0], sub_pixel[0])
    sent, model_other = lax.optimization_barrier((sent, model_other))
    got = lax.all_to_all(
        sent, "tile", split_axis=0, concat_axis=0, tiled=True, axis_index_groups=halves
    )
    model = jnp.where(
        member == 0,
        jnp.concatenate([model_own, model_other]),
        jnp.concatenate([model_other, model_own]),
    )
    table = jnp.pad(
        kernel_table.astype(jnp.float32), ((0, 8), (0, 0), (0, 16 - support))
    ).reshape(planes + 8, 16 * oversample)
    residual, own, other = pl.pallas_call(
        lambda *refs: grid_kernel(pairs, capacity, *refs),
        out_shape=(
            jax.ShapeDtypeStruct((slots, 2, rows), jnp.bfloat16),
            jax.ShapeDtypeStruct((tiles_here, side, wide), jnp.float32),
            jax.ShapeDtypeStruct((tiles_here, side, wide), jnp.bfloat16),
        ),
        in_specs=[SMEM, VMEM, VMEM, VMEM],
        out_specs=(VMEM, VMEM, VMEM),
        scratch_shapes=[
            pltpu.VMEM((2 * tiles_here, wide, side), jnp.bfloat16),
            pltpu.VMEM((2 * tiles_here, side, wide), jnp.float32),
            pltpu.VMEM((UNROLL, side, rows), jnp.bfloat16),
            pltpu.VMEM((UNROLL, wide, rows), jnp.float32),
            pltpu.VMEM((pairs, 2, rows), jnp.int32),
            pltpu.SMEM((pairs, 2, rows), jnp.int32),
            pltpu.SMEM((slots + capacity + 2 * UNROLL,), jnp.int32),
            pltpu.SemaphoreType.DMA,
        ],
        compiler_params=PARAMS,
        name="grid_blocks",
    )(member[None], got, table, model)

    returned = lax.all_to_all(
        residual, "tile", split_axis=0, concat_axis=0, tiled=True, axis_index_groups=halves
    )
    residuals = jnp.take(returned, slot, axis=0, mode="clip").astype(jnp.float32)[None]
    grid_sum = own + lax.ppermute(other, "tile", swap).astype(jnp.float32)
    grid_rounded = grid_sum.astype(jnp.bfloat16)[None]
    own_row = lax.dynamic_index_in_dim(coupling, lax.axis_index("freq"), 0, keepdims=False)
    coupled_grid = jnp.sum(
        own_row[:, None, None, None]
        * lax.all_gather(grid_rounded, "freq", axis=0, tiled=True).astype(jnp.float32),
        axis=0,
    )[None]
    return (residuals, coupled_grid)


def solution(mesh):
    return jax.shard_map(
        body,
        mesh=mesh,
        in_specs=(
            P("freq", "tile", None, None),
            P("freq", "tile", None, None),
            P("freq", "tile", None, None),
            P("freq", "tile"),
            P("freq", "tile"),
            P("freq", "tile", None, None),
            P(),
            P(),
        ),
        out_specs=(P("freq", "tile", None, None), P("freq", "tile", None, None)),
        check_vma=False,
    )
```

```python
import jax
import jax.numpy as jnp
from jax import lax
from jax.experimental import pallas as pl
from jax.experimental.pallas import tpu as pltpu
from jax.sharding import PartitionSpec as P

UNROLL = 4
VMEM = pl.BlockSpec(memory_space=pltpu.VMEM)
SMEM = pl.BlockSpec(memory_space=pltpu.SMEM)
HBM = pl.BlockSpec(memory_space=pltpu.HBM)
PARAMS = pltpu.CompilerParams(vmem_limit_bytes=32 * 1024 * 1024)
WHOLE_PARAMS = pltpu.CompilerParams(vmem_limit_bytes=62 * 1024 * 1024)
TILE_SHIFT = 12
PLANE_SHIFT = 16


def scalar_div(value, count):
    shift = count.bit_length() - 1
    return value >> shift if count == 1 << shift else lax.div(value, count)


def pack_kernel(pairs, capacity, tiles_here, planes, plane_ref, tile_ref, vis_hbm, cell_hbm, sub_hbm,
                sent_ref, slot_ref, vis_ref, cell_ref, sub_ref, about_ref, count_ref, load_sem, about_sem):
    blocks = tile_ref.shape[0]
    loads = [
        pltpu.make_async_copy(source, target, load_sem.at[i])
        for i, (source, target) in enumerate(
            [(vis_hbm, vis_ref), (cell_hbm, cell_ref), (sub_hbm, sub_ref)]
        )
    ]
    for copy in loads:
        copy.start()
    part = lax.broadcasted_iota(jnp.int32, (4, 128), 0)
    empty = jnp.where(part == 0, float(planes << PLANE_SHIFT), 0.0)
    abouts = [d * (capacity + 1) + capacity for d in range(pairs)]
    for d in range(pairs):
        sent_ref[d * (capacity + 1)] = jnp.zeros((4, 128), jnp.float32)
        sent_ref[abouts[d]] = empty
        count_ref[d] = 0
    fills = [
        pltpu.make_async_copy(sent_ref.at[abouts[d]], about_ref.at[d], about_sem.at[d])
        for d in range(pairs)
    ]
    for copy in fills:
        copy.start()
    for copy in fills + loads:
        copy.wait()

    def assign(b):
        tile = tile_ref[b]
        owner = scalar_div(tile, tiles_here)
        high = (owner >= pairs).astype(jnp.int32)
        pair = owner - high * pairs
        local = tile - (owner - high) * tiles_here
        place = count_ref[pair]
        count_ref[pair] = place + 1
        slot_ref[b] = pair * (capacity + 1) + place
        code = (plane_ref[b] << PLANE_SHIFT) + (local << TILE_SHIFT)
        about_ref[pair, 0, place] = code.astype(jnp.float32)

    def move(b):
        position = (cell_ref[b] * 8 + sub_ref[b]).astype(jnp.float32)
        sent_ref[slot_ref[b]] = jnp.concatenate([vis_ref[b], position], axis=0)

    def step(turn, carry):
        for which in range(8):
            assign(turn * 8 + which)
        for which in range(8):
            move(turn * 8 + which)
        return carry

    lax.fori_loop(0, blocks // 8, step, 0)
    for d in range(pairs):
        about_ref[d, 1, 0] = count_ref[d].astype(jnp.float32)
    returns = [
        pltpu.make_async_copy(about_ref.at[d], sent_ref.at[abouts[d]], about_sem.at[d])
        for d in range(pairs)
    ]
    for copy in returns:
        copy.start()
    for copy in returns:
        copy.wait()


def spread_parts(position, table_row):
    position = jnp.broadcast_to(position, (16, 128))
    delta = lax.broadcasted_iota(jnp.int32, (16, 128), 0) - (position >> 3)
    index = (delta & 15) + ((position & 7) << 4)
    table = jnp.broadcast_to(table_row, (8, 128))
    taps = jnp.concatenate(
        [
            jnp.take_along_axis(table, index[:8], axis=1, mode="promise_in_bounds"),
            jnp.take_along_axis(table, index[8:], axis=1, mode="promise_in_bounds"),
        ],
        axis=0,
    )
    return taps, (15 - delta) >> 4


def grid_kernel(pairs, capacity, member_ref, got_ref, table_ref, model_ref, residual_ref, own_ref,
                other_ref, turned_ref, grid_ref, row_ref, partial_ref, code_ref, about_ref, list_ref, sem):
    tiles, side, wide = model_ref.shape
    groups = side // 16
    zero_row = table_ref.shape[0] - 8
    lane = lax.broadcasted_iota(jnp.int32, (1, 128), 1)
    for s in range(pairs):
        about = got_ref[s * (capacity + 1) + capacity].astype(jnp.int32)
        code_ref[s, 0:1, :] = about[0:1] + (lane + s * (capacity + 1))
        code_ref[s, 1:2, :] = about[1:2]
    fill = pltpu.make_async_copy(code_ref, about_ref, sem)
    fill.start()
    for t in range(tiles):
        turned_ref[t] = model_ref[t].T
    grid_ref[...] = jnp.zeros_like(grid_ref)
    fill.wait()

    total = jnp.int32(0)
    for s in range(pairs):
        total = total + about_ref[s, 1, 0]
    spare = jnp.where(total == 0, UNROLL, -total & (UNROLL - 1))
    for u in range(UNROLL):
        list_ref[u] = zero_row << PLANE_SHIFT

    def enlist(s, filled):
        for k in range(capacity):
            list_ref[filled + k] = about_ref[s, 0, k]
        return filled + about_ref[s, 1, 0]

    lax.fori_loop(0, pairs, enlist, spare)
    chunks = scalar_div(total + spare, UNROLL)
    zero = jnp.zeros((16, 128), jnp.bfloat16)

    def read(which):
        entry = list_ref[which]
        slot = entry & ((1 << TILE_SHIFT) - 1)
        tile = (entry >> TILE_SHIFT) & 15
        return slot, tile, table_ref[pl.ds(entry >> PLANE_SHIFT, 1), :], got_ref[slot]

    def front(which, u):
        _, tile, table_row, data = read(which)
        taps, group = spread_parts(data[2:3].astype(jnp.int32), table_row)
        taps = taps.astype(jnp.bfloat16)
        group = group.astype(jnp.float32).astype(jnp.bfloat16)
        row_matrix = jnp.concatenate(
            [jnp.where(group == k, taps, zero) for k in range(groups)], axis=0
        )
        row_ref[u] = row_matrix
        partial_ref[u] = jnp.dot(turned_ref[tile], row_matrix, preferred_element_type=jnp.float32)

    def back(which, u):
        slot, tile, table_row, data = read(which)
        taps, group = spread_parts(data[3:4].astype(jnp.int32), table_row)
        residuals, samples = [], []
        for part in range(2):
            picked = jnp.zeros((16, 128), jnp.float32)
            for k in range(groups):
                low = part * side + 16 * k
                picked = jnp.where(group == k, partial_ref[u, low : low + 16], picked)
            model = jnp.sum(picked * taps, axis=0, keepdims=True)
            residual = data[part : part + 1] - model
            residuals.append(residual)
            samples.append((residual * taps).astype(jnp.bfloat16))
        residual_ref[slot] = jnp.concatenate(residuals, axis=0).astype(jnp.bfloat16)
        group = group.astype(jnp.float32).astype(jnp.bfloat16)
        weighted = jnp.concatenate(
            [
                jnp.where(group == k, samples[part], zero)
                for part in range(2)
                for k in range(groups)
            ],
            axis=0,
        )
        grid_ref[tile] += lax.dot_general(
            row_ref[u],
            weighted,
            (((1,), (1,)), ((), ())),
            preferred_element_type=jnp.float32,
        )

    def step(turn, carry):
        for u in range(UNROLL):
            back((turn - 1) * UNROLL + u, u)
        for u in range(UNROLL):
            front(turn * UNROLL + u, u)
        return carry

    for u in range(UNROLL):
        front(u, u)
    lax.fori_loop(1, chunks, step, 0)
    for u in range(UNROLL):
        back((chunks - 1) * UNROLL + u, u)
    half = tiles // 2
    member = member_ref[0]
    for t in range(half):
        own_ref[t] = grid_ref[member * half + t]
        other_ref[t] = grid_ref[(1 - member) * half + t].astype(jnp.bfloat16)


def body(visibilities, uv_cell, sub_pixel, w_plane, block_tile, model_grid, kernel_table, coupling):
    owners = lax.axis_size("tile")
    pairs = owners // 2
    _, blocks, _, rows = visibilities.shape
    capacity = 2 * (3 * blocks // owners)
    _, tiles_here, side, wide = model_grid.shape
    planes, oversample, support = kernel_table.shape
    slots = pairs * (capacity + 1)
    member = lax.axis_index("tile") // pairs
    swap = [(t, (t + pairs) % owners) for t in range(owners)]
    halves = [list(range(pairs)), list(range(pairs, owners))]

    model_own = model_grid[0]
    model_other = lax.ppermute(model_own, "tile", swap)
    sent, slot = pl.pallas_call(
        lambda *refs: pack_kernel(pairs, capacity, tiles_here, planes, *refs),
        out_shape=(
            jax.ShapeDtypeStruct((slots, 4, rows), jnp.float32),
            jax.ShapeDtypeStruct((blocks,), jnp.int32),
        ),
        in_specs=[SMEM, SMEM, HBM, HBM, HBM],
        out_specs=(VMEM, SMEM),
        scratch_shapes=[
            pltpu.VMEM((blocks, 2, rows), jnp.float32),
            pltpu.VMEM((blocks, 2, rows), jnp.int32),
            pltpu.VMEM((blocks, 2, rows), jnp.int32),
            pltpu.SMEM((pairs, 4, rows), jnp.float32),
            pltpu.SMEM((pairs,), jnp.int32),
            pltpu.SemaphoreType.DMA((3,)),
            pltpu.SemaphoreType.DMA((pairs,)),
        ],
        compiler_params=WHOLE_PARAMS,
        name="pack_blocks",
    )(w_plane[0], block_tile[0], visibilities[0], uv_cell[0], sub_pixel[0])
    sent, model_other = lax.optimization_barrier((sent, model_other))
    got = lax.all_to_all(
        sent, "tile", split_axis=0, concat_axis=0, tiled=True, axis_index_groups=halves
    )
    model = jnp.where(
        member == 0,
        jnp.concatenate([model_own, model_other]),
        jnp.concatenate([model_other, model_own]),
    )
    table = jnp.pad(
        kernel_table.astype(jnp.float32), ((0, 8), (0, 0), (0, 16 - support))
    ).reshape(planes + 8, 16 * oversample)
    residual, own, other = pl.pallas_call(
        lambda *refs: grid_kernel(pairs, capacity, *refs),
        out_shape=(
            jax.ShapeDtypeStruct((slots, 2, rows), jnp.bfloat16),
            jax.ShapeDtypeStruct((tiles_here, side, wide), jnp.float32),
            jax.ShapeDtypeStruct((tiles_here, side, wide), jnp.bfloat16),
        ),
        in_specs=[SMEM, VMEM, VMEM, VMEM],
        out_specs=(VMEM, VMEM, VMEM),
        scratch_shapes=[
            pltpu.VMEM((2 * tiles_here, wide, side), jnp.bfloat16),
            pltpu.VMEM((2 * tiles_here, side, wide), jnp.float32),
            pltpu.VMEM((UNROLL, side, rows), jnp.bfloat16),
            pltpu.VMEM((UNROLL, wide, rows), jnp.float32),
            pltpu.VMEM((pairs, 2, rows), jnp.int32),
            pltpu.SMEM((pairs, 2, rows), jnp.int32),
            pltpu.SMEM((slots + capacity + 2 * UNROLL,), jnp.int32),
            pltpu.SemaphoreType.DMA,
        ],
        compiler_params=PARAMS,
        name="grid_blocks",
    )(member[None], got, table, model)

    returned = lax.all_to_all(
        residual, "tile", split_axis=0, concat_axis=0, tiled=True, axis_index_groups=halves
    )
    residuals = jnp.take(returned, slot, axis=0, mode="clip").astype(jnp.float32)[None]
    grid_sum = own + lax.ppermute(other, "tile", swap).astype(jnp.float32)
    grid_rounded = grid_sum.astype(jnp.bfloat16)[None]
    own_row = lax.dynamic_index_in_dim(coupling, lax.axis_index("freq"), 0, keepdims=False)
    coupled_grid = jnp.sum(
        own_row[:, None, None, None]
        * lax.all_gather(grid_rounded, "freq", axis=0, tiled=True).astype(jnp.float32),
        axis=0,
    )[None]
    return (residuals, coupled_grid)


def solution(mesh):
    return jax.shard_map(
        body,
        mesh=mesh,
        in_specs=(
            P("freq", "tile", None, None),
            P("freq", "tile", None, None),
            P("freq", "tile", None, None),
            P("freq", "tile"),
            P("freq", "tile"),
            P("freq", "tile", None, None),
            P(),
            P(),
        ),
        out_specs=(P("freq", "tile", None, None), P("freq", "tile", None, None)),
        check_vma=False,
    )
```

```python
import jax
import jax.numpy as jnp
from jax import lax
from jax.experimental import pallas as pl
from jax.experimental.pallas import tpu as pltpu
from jax.sharding import PartitionSpec as P

UNROLL = 4
VMEM = pl.BlockSpec(memory_space=pltpu.VMEM)
SMEM = pl.BlockSpec(memory_space=pltpu.SMEM)
HBM = pl.BlockSpec(memory_space=pltpu.HBM)
PARAMS = pltpu.CompilerParams(vmem_limit_bytes=32 * 1024 * 1024)
WHOLE_PARAMS = pltpu.CompilerParams(vmem_limit_bytes=62 * 1024 * 1024)
TILE_SHIFT = 12
PLANE_SHIFT = 16


def scalar_div(value, count):
    shift = count.bit_length() - 1
    return value >> shift if count == 1 << shift else lax.div(value, count)


def first_slot(local, rank, capacity):
    half = capacity // 2
    return (local >> 1) * half + jnp.where((local & 1) == 0, rank, half - 1 - rank)


def pack_kernel(pairs, capacity, tiles_here, planes, plane_ref, tile_ref, vis_hbm, cell_hbm, sub_hbm,
                sent_ref, slot_ref, vis_ref, cell_ref, sub_ref, about_ref, count_ref, load_sem, about_sem):
    blocks = tile_ref.shape[0]
    loads = [
        pltpu.make_async_copy(source, target, load_sem.at[i])
        for i, (source, target) in enumerate(
            [(vis_hbm, vis_ref), (cell_hbm, cell_ref), (sub_hbm, sub_ref)]
        )
    ]
    for copy in loads:
        copy.start()
    part = lax.broadcasted_iota(jnp.int32, (4, 128), 0)
    empty = jnp.where(part == 0, float(planes << PLANE_SHIFT), 0.0)
    abouts = [d * (capacity + 1) + capacity for d in range(pairs)]
    for d in range(pairs):
        sent_ref[abouts[d]] = empty
        for t in range(2 * tiles_here):
            count_ref[d * 2 * tiles_here + t] = 0
    fills = [
        pltpu.make_async_copy(sent_ref.at[abouts[d]], about_ref.at[d], about_sem.at[d])
        for d in range(pairs)
    ]
    for copy in fills:
        copy.start()
    for copy in fills + loads:
        copy.wait()

    def assign(b):
        tile = tile_ref[b]
        owner = scalar_div(tile, tiles_here)
        high = (owner >= pairs).astype(jnp.int32)
        pair = owner - high * pairs
        local = tile - (owner - high) * tiles_here
        key = pair * (2 * tiles_here) + local
        rank = count_ref[key]
        count_ref[key] = rank + 1
        place = first_slot(local, rank, capacity)
        slot_ref[b] = pair * (capacity + 1) + place
        code = (plane_ref[b] << PLANE_SHIFT) + (local << TILE_SHIFT)
        about_ref[pair, 0, place] = code.astype(jnp.float32)

    def move(b):
        position = (cell_ref[b] * 8 + sub_ref[b]).astype(jnp.float32)
        sent_ref[slot_ref[b]] = jnp.concatenate([vis_ref[b], position], axis=0)

    def step(turn, carry):
        for which in range(8):
            assign(turn * 8 + which)
        for which in range(8):
            move(turn * 8 + which)
        return carry

    lax.fori_loop(0, blocks // 8, step, 0)
    for d in range(pairs):
        for t in range(2 * tiles_here):
            about_ref[d, 1, t] = count_ref[d * 2 * tiles_here + t].astype(jnp.float32)
    returns = [
        pltpu.make_async_copy(about_ref.at[d], sent_ref.at[abouts[d]], about_sem.at[d])
        for d in range(pairs)
    ]
    for copy in returns:
        copy.start()
    for copy in returns:
        copy.wait()


def spread_parts(position, table_row):
    position = jnp.broadcast_to(position, (16, 128))
    delta = lax.broadcasted_iota(jnp.int32, (16, 128), 0) - (position >> 3)
    index = (delta & 15) + ((position & 7) << 4)
    table = jnp.broadcast_to(table_row, (8, 128))
    taps = jnp.concatenate(
        [
            jnp.take_along_axis(table, index[:8], axis=1, mode="promise_in_bounds"),
            jnp.take_along_axis(table, index[8:], axis=1, mode="promise_in_bounds"),
        ],
        axis=0,
    )
    return taps, (15 - delta) >> 4


def grid_kernel(pairs, capacity, member_ref, got_ref, table_ref, model_ref, residual_ref, own_ref,
                other_ref, turned_ref, grid_ref, row_ref, kept_ref, partial_ref, weighted_ref, code_ref, about_ref, list_ref, sem):
    tiles, side, wide = model_ref.shape
    groups = side // 16
    zero_row = table_ref.shape[0] - 8
    lane = lax.broadcasted_iota(jnp.int32, (1, 128), 1)
    for s in range(pairs):
        about = got_ref[s * (capacity + 1) + capacity].astype(jnp.int32)
        code_ref[s, 0:1, :] = about[0:1] + (lane + s * (capacity + 1))
        code_ref[s, 1:2, :] = about[1:2]
    fill = pltpu.make_async_copy(code_ref, about_ref, sem)
    fill.start()
    for t in range(tiles):
        turned_ref[t] = model_ref[t].T
    grid_ref[...] = jnp.zeros_like(grid_ref)
    fill.wait()

    start = jnp.int32(0)
    for t in range(tiles):
        count = jnp.int32(0)
        for s in range(pairs):
            count = count + about_ref[s, 1, t]
        spare = -count & (UNROLL - 1)
        for u in range(UNROLL):
            list_ref[start + u] = (zero_row << PLANE_SHIFT) + (t << TILE_SHIFT) + capacity

        def enlist(s, filled, t=t):
            for k in range(capacity // 2):
                place = k if t % 2 == 0 else capacity // 2 - 1 - k
                list_ref[filled + k] = about_ref[s, 0, t // 2 * (capacity // 2) + place]
            return filled + about_ref[s, 1, t]

        lax.fori_loop(0, pairs, enlist, start + spare)
        start = start + count + spare
    for u in range(UNROLL):
        list_ref[start + u] = (zero_row << PLANE_SHIFT) + capacity
    chunks = jnp.maximum(start >> UNROLL.bit_length() - 1, 1)
    zero = jnp.zeros((16, 128), jnp.bfloat16)

    def read(which):
        entry = list_ref[which]
        slot = entry & ((1 << TILE_SHIFT) - 1)
        return slot, table_ref[pl.ds(entry >> PLANE_SHIFT, 1), :], got_ref[slot]

    def chunk_tile(turn):
        return (list_ref[turn * UNROLL] >> TILE_SHIFT) & 15

    def front(turn):
        for u in range(UNROLL):
            _, table_row, data = read(turn * UNROLL + u)
            taps, group = spread_parts(data[2:3].astype(jnp.int32), table_row)
            taps = taps.astype(jnp.bfloat16)
            group = group.astype(jnp.float32).astype(jnp.bfloat16)
            for k in range(groups):
                row_ref[16 * k : 16 * k + 16, 128 * u : 128 * u + 128] = jnp.where(
                    group == k, taps, zero
                )
        partial_ref[...] = jnp.dot(
            turned_ref[chunk_tile(turn)], row_ref[...], preferred_element_type=jnp.float32
        )

    def back(turn):
        kept_ref[...] = row_ref[...]
        for u in range(UNROLL):
            slot, table_row, data = read(turn * UNROLL + u)
            columns = slice(128 * u, 128 * u + 128)
            taps, group = spread_parts(data[3:4].astype(jnp.int32), table_row)
            residuals, samples = [], []
            for part in range(2):
                picked = jnp.zeros((16, 128), jnp.float32)
                for k in range(groups):
                    low = part * side + 16 * k
                    picked = jnp.where(group == k, partial_ref[low : low + 16, columns], picked)
                model = jnp.sum(picked * taps, axis=0, keepdims=True)
                residual = data[part : part + 1] - model
                residuals.append(residual)
                samples.append((residual * taps).astype(jnp.bfloat16))
            residual_ref[slot] = jnp.concatenate(residuals, axis=0).astype(jnp.bfloat16)
            group = group.astype(jnp.float32).astype(jnp.bfloat16)
            for part in range(2):
                for k in range(groups):
                    low = part * side + 16 * k
                    weighted_ref[low : low + 16, columns] = jnp.where(
                        group == k, samples[part], zero
                    )
        grid_ref[chunk_tile(turn)] += lax.dot_general(
            kept_ref[...],
            weighted_ref[...],
            (((1,), (1,)), ((), ())),
            preferred_element_type=jnp.float32,
        )

    def step(turn, carry):
        back(turn - 1)
        front(turn)
        return carry

    front(0)
    lax.fori_loop(1, chunks, step, 0)
    back(chunks - 1)
    half = tiles // 2
    member = member_ref[0]
    for t in range(half):
        own_ref[t] = grid_ref[member * half + t]
        other_ref[t] = grid_ref[(1 - member) * half + t].astype(jnp.bfloat16)


def body(visibilities, uv_cell, sub_pixel, w_plane, block_tile, model_grid, kernel_table, coupling):
    owners = lax.axis_size("tile")
    pairs = owners // 2
    _, blocks, _, rows = visibilities.shape
    capacity = 2 * (3 * blocks // owners)
    _, tiles_here, side, wide = model_grid.shape
    planes, oversample, support = kernel_table.shape
    slots = pairs * (capacity + 1)
    member = lax.axis_index("tile") // pairs
    swap = [(t, (t + pairs) % owners) for t in range(owners)]
    halves = [list(range(pairs)), list(range(pairs, owners))]

    model_own = model_grid[0]
    model_other = lax.ppermute(model_own, "tile", swap)
    sent, slot = pl.pallas_call(
        lambda *refs: pack_kernel(pairs, capacity, tiles_here, planes, *refs),
        out_shape=(
            jax.ShapeDtypeStruct((slots, 4, rows), jnp.float32),
            jax.ShapeDtypeStruct((blocks,), jnp.int32),
        ),
        in_specs=[SMEM, SMEM, HBM, HBM, HBM],
        out_specs=(VMEM, SMEM),
        scratch_shapes=[
            pltpu.VMEM((blocks, 2, rows), jnp.float32),
            pltpu.VMEM((blocks, 2, rows), jnp.int32),
            pltpu.VMEM((blocks, 2, rows), jnp.int32),
            pltpu.SMEM((pairs, 4, rows), jnp.float32),
            pltpu.SMEM((pairs * 2 * tiles_here,), jnp.int32),
            pltpu.SemaphoreType.DMA((3,)),
            pltpu.SemaphoreType.DMA((pairs,)),
        ],
        compiler_params=WHOLE_PARAMS,
        name="pack_blocks",
    )(w_plane[0], block_tile[0], visibilities[0], uv_cell[0], sub_pixel[0])
    sent, model_other = lax.optimization_barrier((sent, model_other))
    got = lax.all_to_all(
        sent, "tile", split_axis=0, concat_axis=0, tiled=True, axis_index_groups=halves
    )
    model = jnp.where(
        member == 0,
        jnp.concatenate([model_own, model_other]),
        jnp.concatenate([model_other, model_own]),
    )
    table = jnp.pad(
        kernel_table.astype(jnp.float32), ((0, 8), (0, 0), (0, 16 - support))
    ).reshape(planes + 8, 16 * oversample)
    residual, own, other = pl.pallas_call(
        lambda *refs: grid_kernel(pairs, capacity, *refs),
        out_shape=(
            jax.ShapeDtypeStruct((slots, 2, rows), jnp.bfloat16),
            jax.ShapeDtypeStruct((tiles_here, side, wide), jnp.float32),
            jax.ShapeDtypeStruct((tiles_here, side, wide), jnp.bfloat16),
        ),
        in_specs=[SMEM, VMEM, VMEM, VMEM],
        out_specs=(VMEM, VMEM, VMEM),
        scratch_shapes=[
            pltpu.VMEM((2 * tiles_here, wide, side), jnp.bfloat16),
            pltpu.VMEM((2 * tiles_here, side, wide), jnp.float32),
            pltpu.VMEM((side, UNROLL * rows), jnp.bfloat16),
            pltpu.VMEM((side, UNROLL * rows), jnp.bfloat16),
            pltpu.VMEM((wide, UNROLL * rows), jnp.float32),
            pltpu.VMEM((wide, UNROLL * rows), jnp.bfloat16),
            pltpu.VMEM((pairs, 2, rows), jnp.int32),
            pltpu.SMEM((pairs, 2, rows), jnp.int32),
            pltpu.SMEM((slots + capacity + 2 * tiles_here * UNROLL + UNROLL,), jnp.int32),
            pltpu.SemaphoreType.DMA,
        ],
        compiler_params=PARAMS,
        name="grid_blocks",
    )(member[None], got, table, model)

    returned = lax.all_to_all(
        residual, "tile", split_axis=0, concat_axis=0, tiled=True, axis_index_groups=halves
    )
    residuals = jnp.take(returned, slot, axis=0, mode="clip").astype(jnp.float32)[None]
    grid_sum = own + lax.ppermute(other, "tile", swap).astype(jnp.float32)
    grid_rounded = grid_sum.astype(jnp.bfloat16)[None]
    own_row = lax.dynamic_index_in_dim(coupling, lax.axis_index("freq"), 0, keepdims=False)
    coupled_grid = jnp.sum(
        own_row[:, None, None, None]
        * lax.all_gather(grid_rounded, "freq", axis=0, tiled=True).astype(jnp.float32),
        axis=0,
    )[None]
    return (residuals, coupled_grid)


def solution(mesh):
    return jax.shard_map(
        body,
        mesh=mesh,
        in_specs=(
            P("freq", "tile", None, None),
            P("freq", "tile", None, None),
            P("freq", "tile", None, None),
            P("freq", "tile"),
            P("freq", "tile"),
            P("freq", "tile", None, None),
            P(),
            P(),
        ),
        out_specs=(P("freq", "tile", None, None), P("freq", "tile", None, None)),
        check_vma=False,
    )
```

```python
import jax
import jax.numpy as jnp
from jax import lax
from jax.experimental import pallas as pl
from jax.experimental.pallas import tpu as pltpu
from jax.sharding import PartitionSpec as P

UNROLL = 4
VMEM = pl.BlockSpec(memory_space=pltpu.VMEM)
SMEM = pl.BlockSpec(memory_space=pltpu.SMEM)
HBM = pl.BlockSpec(memory_space=pltpu.HBM)
PARAMS = pltpu.CompilerParams(vmem_limit_bytes=32 * 1024 * 1024)
WHOLE_PARAMS = pltpu.CompilerParams(vmem_limit_bytes=62 * 1024 * 1024)
TILE_SHIFT = 12
PLANE_SHIFT = 16


def scalar_div(value, count):
    shift = count.bit_length() - 1
    return value >> shift if count == 1 << shift else lax.div(value, count)


def first_slot(local, rank, capacity):
    half = capacity // 2
    return (local >> 1) * half + jnp.where((local & 1) == 0, rank, half - 1 - rank)


def pack_kernel(pairs, capacity, tiles_here, planes, plane_ref, tile_ref, vis_hbm, cell_hbm, sub_hbm,
                sent_ref, slot_ref, vis_ref, cell_ref, sub_ref, about_ref, count_ref, load_sem, about_sem):
    blocks = tile_ref.shape[0]
    loads = [
        pltpu.make_async_copy(source, target, load_sem.at[i])
        for i, (source, target) in enumerate(
            [(vis_hbm, vis_ref), (cell_hbm, cell_ref), (sub_hbm, sub_ref)]
        )
    ]
    for copy in loads:
        copy.start()
    part = lax.broadcasted_iota(jnp.int32, (4, 128), 0)
    empty = jnp.where(part == 0, float(planes << PLANE_SHIFT), 0.0)
    abouts = [d * (capacity + 1) + capacity for d in range(pairs)]
    for d in range(pairs):
        sent_ref[abouts[d]] = empty
        for t in range(2 * tiles_here):
            count_ref[d * 2 * tiles_here + t] = 0
    fills = [
        pltpu.make_async_copy(sent_ref.at[abouts[d]], about_ref.at[d], about_sem.at[d])
        for d in range(pairs)
    ]
    for copy in fills:
        copy.start()
    for copy in fills + loads:
        copy.wait()

    def assign(b):
        tile = tile_ref[b]
        owner = scalar_div(tile, tiles_here)
        high = (owner >= pairs).astype(jnp.int32)
        pair = owner - high * pairs
        local = tile - (owner - high) * tiles_here
        key = pair * (2 * tiles_here) + local
        rank = count_ref[key]
        count_ref[key] = rank + 1
        place = first_slot(local, rank, capacity)
        slot_ref[b] = pair * (capacity + 1) + place
        code = (plane_ref[b] << PLANE_SHIFT) + (local << TILE_SHIFT)
        about_ref[pair, 0, place] = code.astype(jnp.float32)

    def move(b):
        position = (cell_ref[b] * 8 + sub_ref[b]).astype(jnp.float32)
        sent_ref[slot_ref[b]] = jnp.concatenate([vis_ref[b], position], axis=0)

    def step(turn, carry):
        for which in range(8):
            assign(turn * 8 + which)
        for which in range(8):
            move(turn * 8 + which)
        return carry

    lax.fori_loop(0, blocks // 8, step, 0)
    for d in range(pairs):
        for t in range(2 * tiles_here):
            about_ref[d, 1, t] = count_ref[d * 2 * tiles_here + t].astype(jnp.float32)
    returns = [
        pltpu.make_async_copy(about_ref.at[d], sent_ref.at[abouts[d]], about_sem.at[d])
        for d in range(pairs)
    ]
    for copy in returns:
        copy.start()
    for copy in returns:
        copy.wait()


def spread_parts(position, table_row):
    position = jnp.broadcast_to(position, (16, 128))
    delta = lax.broadcasted_iota(jnp.int32, (16, 128), 0) - (position >> 3)
    index = (delta & 15) + ((position & 7) << 4)
    table = jnp.broadcast_to(table_row, (8, 128))
    taps = jnp.concatenate(
        [
            jnp.take_along_axis(table, index[:8], axis=1, mode="promise_in_bounds"),
            jnp.take_along_axis(table, index[8:], axis=1, mode="promise_in_bounds"),
        ],
        axis=0,
    )
    return taps, (15 - delta) >> 4


def grid_kernel(pairs, capacity, member_ref, got_ref, table_ref, model_ref, residual_ref, own_ref,
                other_ref, turned_ref, grid_ref, row_ref, kept_ref, partial_ref, weighted_ref, code_ref, about_ref, list_ref, sem):
    tiles, side, wide = model_ref.shape
    groups = side // 16
    zero_row = table_ref.shape[0] - 8
    lane = lax.broadcasted_iota(jnp.int32, (1, 128), 1)
    for s in range(pairs):
        about = got_ref[s * (capacity + 1) + capacity].astype(jnp.int32)
        code_ref[s, 0:1, :] = about[0:1] + (lane + s * (capacity + 1))
        code_ref[s, 1:2, :] = about[1:2]
    fill = pltpu.make_async_copy(code_ref, about_ref, sem)
    fill.start()
    for t in range(tiles):
        turned_ref[t] = model_ref[t].T
    grid_ref[...] = jnp.zeros_like(grid_ref)
    fill.wait()

    start = jnp.int32(0)
    for t in range(tiles):
        count = jnp.int32(0)
        for s in range(pairs):
            count = count + about_ref[s, 1, t]
        spare = -count & (UNROLL - 1)
        for u in range(UNROLL):
            list_ref[start + u] = (zero_row << PLANE_SHIFT) + (t << TILE_SHIFT) + capacity

        def enlist(s, filled, t=t):
            for k in range(capacity // 2):
                place = k if t % 2 == 0 else capacity // 2 - 1 - k
                list_ref[filled + k] = about_ref[s, 0, t // 2 * (capacity // 2) + place]
            return filled + about_ref[s, 1, t]

        lax.fori_loop(0, pairs, enlist, start + spare)
        start = start + count + spare
    for u in range(UNROLL):
        list_ref[start + u] = (zero_row << PLANE_SHIFT) + capacity
    chunks = jnp.maximum(start >> UNROLL.bit_length() - 1, 1)
    zero = jnp.zeros((16, 128), jnp.bfloat16)

    def read(which):
        entry = list_ref[which]
        slot = entry & ((1 << TILE_SHIFT) - 1)
        return slot, table_ref[pl.ds(entry >> PLANE_SHIFT, 1), :], got_ref[slot]

    def chunk_tile(turn):
        return (list_ref[turn * UNROLL] >> TILE_SHIFT) & 15

    def front(turn):
        for u in range(UNROLL):
            _, table_row, data = read(turn * UNROLL + u)
            taps, group = spread_parts(data[2:3].astype(jnp.int32), table_row)
            taps = taps.astype(jnp.bfloat16)
            group = group.astype(jnp.float32).astype(jnp.bfloat16)
            for k in range(groups):
                row_ref[16 * k : 16 * k + 16, 128 * u : 128 * u + 128] = jnp.where(
                    group == k, taps, zero
                )
        partial_ref[...] = jnp.dot(
            turned_ref[chunk_tile(turn)], row_ref[...], preferred_element_type=jnp.float32
        )

    def back(turn):
        kept_ref[...] = row_ref[...]
        for u in range(UNROLL):
            slot, table_row, data = read(turn * UNROLL + u)
            columns = slice(128 * u, 128 * u + 128)
            taps, group = spread_parts(data[3:4].astype(jnp.int32), table_row)
            residuals, samples = [], []
            for part in range(2):
                picked = jnp.zeros((16, 128), jnp.float32)
                for k in range(groups):
                    low = part * side + 16 * k
                    picked = jnp.where(group == k, partial_ref[low : low + 16, columns], picked)
                model = jnp.sum(picked * taps, axis=0, keepdims=True)
                residual = data[part : part + 1] - model
                residuals.append(residual)
                samples.append((residual * taps).astype(jnp.bfloat16))
            residual_ref[slot] = jnp.concatenate(residuals, axis=0).astype(jnp.bfloat16)
            group = group.astype(jnp.float32).astype(jnp.bfloat16)
            for part in range(2):
                for k in range(groups):
                    low = part * side + 16 * k
                    weighted_ref[low : low + 16, columns] = jnp.where(
                        group == k, samples[part], zero
                    )
        grid_ref[chunk_tile(turn)] += lax.dot_general(
            weighted_ref[...],
            kept_ref[...],
            (((1,), (1,)), ((), ())),
            preferred_element_type=jnp.float32,
        )

    def step(turn, carry):
        back(turn - 1)
        front(turn)
        return carry

    front(0)
    lax.fori_loop(1, chunks, step, 0)
    back(chunks - 1)
    half = tiles // 2
    member = member_ref[0]
    for t in range(half):
        own_ref[t] = grid_ref[member * half + t].T
        other_ref[t] = grid_ref[(1 - member) * half + t].T.astype(jnp.bfloat16)


def body(visibilities, uv_cell, sub_pixel, w_plane, block_tile, model_grid, kernel_table, coupling):
    owners = lax.axis_size("tile")
    pairs = owners // 2
    _, blocks, _, rows = visibilities.shape
    capacity = 2 * (3 * blocks // owners)
    _, tiles_here, side, wide = model_grid.shape
    planes, oversample, support = kernel_table.shape
    slots = pairs * (capacity + 1)
    member = lax.axis_index("tile") // pairs
    swap = [(t, (t + pairs) % owners) for t in range(owners)]
    halves = [list(range(pairs)), list(range(pairs, owners))]

    model_own = model_grid[0]
    model_other = lax.ppermute(model_own, "tile", swap)
    sent, slot = pl.pallas_call(
        lambda *refs: pack_kernel(pairs, capacity, tiles_here, planes, *refs),
        out_shape=(
            jax.ShapeDtypeStruct((slots, 4, rows), jnp.float32),
            jax.ShapeDtypeStruct((blocks,), jnp.int32),
        ),
        in_specs=[SMEM, SMEM, HBM, HBM, HBM],
        out_specs=(VMEM, SMEM),
        scratch_shapes=[
            pltpu.VMEM((blocks, 2, rows), jnp.float32),
            pltpu.VMEM((blocks, 2, rows), jnp.int32),
            pltpu.VMEM((blocks, 2, rows), jnp.int32),
            pltpu.SMEM((pairs, 4, rows), jnp.float32),
            pltpu.SMEM((pairs * 2 * tiles_here,), jnp.int32),
            pltpu.SemaphoreType.DMA((3,)),
            pltpu.SemaphoreType.DMA((pairs,)),
        ],
        compiler_params=WHOLE_PARAMS,
        name="pack_blocks",
    )(w_plane[0], block_tile[0], visibilities[0], uv_cell[0], sub_pixel[0])
    sent, model_other = lax.optimization_barrier((sent, model_other))
    got = lax.all_to_all(
        sent, "tile", split_axis=0, concat_axis=0, tiled=True, axis_index_groups=halves
    )
    model = jnp.where(
        member == 0,
        jnp.concatenate([model_own, model_other]),
        jnp.concatenate([model_other, model_own]),
    )
    table = jnp.pad(
        kernel_table.astype(jnp.float32), ((0, 8), (0, 0), (0, 16 - support))
    ).reshape(planes + 8, 16 * oversample)
    residual, own, other = pl.pallas_call(
        lambda *refs: grid_kernel(pairs, capacity, *refs),
        out_shape=(
            jax.ShapeDtypeStruct((slots, 2, rows), jnp.bfloat16),
            jax.ShapeDtypeStruct((tiles_here, side, wide), jnp.float32),
            jax.ShapeDtypeStruct((tiles_here, side, wide), jnp.bfloat16),
        ),
        in_specs=[SMEM, VMEM, VMEM, VMEM],
        out_specs=(VMEM, VMEM, VMEM),
        scratch_shapes=[
            pltpu.VMEM((2 * tiles_here, wide, side), jnp.bfloat16),
            pltpu.VMEM((2 * tiles_here, wide, side), jnp.float32),
            pltpu.VMEM((side, UNROLL * rows), jnp.bfloat16),
            pltpu.VMEM((side, UNROLL * rows), jnp.bfloat16),
            pltpu.VMEM((wide, UNROLL * rows), jnp.float32),
            pltpu.VMEM((wide, UNROLL * rows), jnp.bfloat16),
            pltpu.VMEM((pairs, 2, rows), jnp.int32),
            pltpu.SMEM((pairs, 2, rows), jnp.int32),
            pltpu.SMEM((slots + capacity + 2 * tiles_here * UNROLL + UNROLL,), jnp.int32),
            pltpu.SemaphoreType.DMA,
        ],
        compiler_params=PARAMS,
        name="grid_blocks",
    )(member[None], got, table, model)

    returned = lax.all_to_all(
        residual, "tile", split_axis=0, concat_axis=0, tiled=True, axis_index_groups=halves
    )
    residuals = jnp.take(returned, slot, axis=0, mode="clip").astype(jnp.float32)[None]
    grid_sum = own + lax.ppermute(other, "tile", swap).astype(jnp.float32)
    grid_rounded = grid_sum.astype(jnp.bfloat16)[None]
    own_row = lax.dynamic_index_in_dim(coupling, lax.axis_index("freq"), 0, keepdims=False)
    coupled_grid = jnp.sum(
        own_row[:, None, None, None]
        * lax.all_gather(grid_rounded, "freq", axis=0, tiled=True).astype(jnp.float32),
        axis=0,
    )[None]
    return (residuals, coupled_grid)


def solution(mesh):
    return jax.shard_map(
        body,
        mesh=mesh,
        in_specs=(
            P("freq", "tile", None, None),
            P("freq", "tile", None, None),
            P("freq", "tile", None, None),
            P("freq", "tile"),
            P("freq", "tile"),
            P("freq", "tile", None, None),
            P(),
            P(),
        ),
        out_specs=(P("freq", "tile", None, None), P("freq", "tile", None, None)),
        check_vma=False,
    )
```

```python
import jax
import jax.numpy as jnp
from jax import lax
from jax.experimental import pallas as pl
from jax.experimental.pallas import tpu as pltpu
from jax.sharding import PartitionSpec as P

UNROLL = 4
VMEM = pl.BlockSpec(memory_space=pltpu.VMEM)
SMEM = pl.BlockSpec(memory_space=pltpu.SMEM)
HBM = pl.BlockSpec(memory_space=pltpu.HBM)
PARAMS = pltpu.CompilerParams(vmem_limit_bytes=32 * 1024 * 1024)
WHOLE_PARAMS = pltpu.CompilerParams(vmem_limit_bytes=62 * 1024 * 1024)
TILE_SHIFT = 12
PLANE_SHIFT = 16


def scalar_div(value, count):
    shift = count.bit_length() - 1
    return value >> shift if count == 1 << shift else lax.div(value, count)


def first_slot(local, rank, capacity):
    half = capacity // 2
    return (local >> 1) * half + jnp.where((local & 1) == 0, rank, half - 1 - rank)


def pack_kernel(pairs, capacity, tiles_here, planes, plane_ref, tile_ref, vis_hbm, cell_hbm, sub_hbm,
                sent_ref, slot_ref, vis_ref, cell_ref, sub_ref, about_ref, count_ref, load_sem, about_sem):
    blocks = tile_ref.shape[0]
    loads = [
        pltpu.make_async_copy(source, target, load_sem.at[i])
        for i, (source, target) in enumerate(
            [(vis_hbm, vis_ref), (cell_hbm, cell_ref), (sub_hbm, sub_ref)]
        )
    ]
    for copy in loads:
        copy.start()
    part = lax.broadcasted_iota(jnp.int32, (4, 128), 0)
    empty = jnp.where(part == 0, float(planes << PLANE_SHIFT), 0.0)
    abouts = [d * (capacity + 1) + capacity for d in range(pairs)]
    for d in range(pairs):
        sent_ref[abouts[d]] = empty
        for t in range(2 * tiles_here):
            count_ref[d * 2 * tiles_here + t] = 0
    fills = [
        pltpu.make_async_copy(sent_ref.at[abouts[d]], about_ref.at[d], about_sem.at[d])
        for d in range(pairs)
    ]
    for copy in fills:
        copy.start()
    for copy in fills + loads:
        copy.wait()

    def assign(b):
        tile = tile_ref[b]
        owner = scalar_div(tile, tiles_here)
        high = (owner >= pairs).astype(jnp.int32)
        pair = owner - high * pairs
        local = tile - (owner - high) * tiles_here
        key = pair * (2 * tiles_here) + local
        rank = count_ref[key]
        count_ref[key] = rank + 1
        place = first_slot(local, rank, capacity)
        slot_ref[b] = pair * (capacity + 1) + place
        code = (plane_ref[b] << PLANE_SHIFT) + (local << TILE_SHIFT)
        about_ref[pair, 0, place] = code.astype(jnp.float32)

    def move(b):
        position = (cell_ref[b] * 8 + sub_ref[b]).astype(jnp.float32)
        sent_ref[slot_ref[b]] = jnp.concatenate([vis_ref[b], position], axis=0)

    def step(turn, carry):
        for which in range(8):
            assign(turn * 8 + which)
        for which in range(8):
            move(turn * 8 + which)
        return carry

    lax.fori_loop(0, blocks // 8, step, 0)
    for d in range(pairs):
        for t in range(2 * tiles_here):
            about_ref[d, 1, t] = count_ref[d * 2 * tiles_here + t].astype(jnp.float32)
    returns = [
        pltpu.make_async_copy(about_ref.at[d], sent_ref.at[abouts[d]], about_sem.at[d])
        for d in range(pairs)
    ]
    for copy in returns:
        copy.start()
    for copy in returns:
        copy.wait()


def spread_parts(position, table_row):
    position = jnp.broadcast_to(position, (16, 128))
    delta = lax.broadcasted_iota(jnp.int32, (16, 128), 0) - (position >> 3)
    index = (delta & 15) + ((position & 7) << 4)
    table = jnp.broadcast_to(table_row, (8, 128))
    taps = jnp.concatenate(
        [
            jnp.take_along_axis(table, index[:8], axis=1, mode="promise_in_bounds"),
            jnp.take_along_axis(table, index[8:], axis=1, mode="promise_in_bounds"),
        ],
        axis=0,
    )
    return taps, (15 - delta) >> 4


def grid_kernel(pairs, capacity, member_ref, got_ref, table_ref, model_ref, residual_ref, own_ref,
                other_ref, turned_ref, grid_ref, row_a, row_b, partial_a, partial_b, weighted_ref, code_ref, about_ref, list_ref, sem):
    tiles, side, wide = model_ref.shape
    groups = side // 16
    zero_row = table_ref.shape[0] - 8
    lane = lax.broadcasted_iota(jnp.int32, (1, 128), 1)
    for s in range(pairs):
        about = got_ref[s * (capacity + 1) + capacity].astype(jnp.int32)
        code_ref[s, 0:1, :] = about[0:1] + (lane + s * (capacity + 1))
        code_ref[s, 1:2, :] = about[1:2]
    fill = pltpu.make_async_copy(code_ref, about_ref, sem)
    fill.start()
    for t in range(tiles):
        turned_ref[t] = model_ref[t].T
    grid_ref[...] = jnp.zeros_like(grid_ref)
    fill.wait()

    start = jnp.int32(0)
    for t in range(tiles):
        count = jnp.int32(0)
        for s in range(pairs):
            count = count + about_ref[s, 1, t]
        spare = -count & (UNROLL - 1)
        for u in range(UNROLL):
            list_ref[start + u] = (zero_row << PLANE_SHIFT) + (t << TILE_SHIFT) + capacity

        def enlist(s, filled, t=t):
            for k in range(capacity // 2):
                place = k if t % 2 == 0 else capacity // 2 - 1 - k
                list_ref[filled + k] = about_ref[s, 0, t // 2 * (capacity // 2) + place]
            return filled + about_ref[s, 1, t]

        lax.fori_loop(0, pairs, enlist, start + spare)
        start = start + count + spare
    for u in range(2 * UNROLL):
        list_ref[start + u] = (zero_row << PLANE_SHIFT) + capacity
    chunks = start >> UNROLL.bit_length() - 1
    zero = jnp.zeros((16, 128), jnp.bfloat16)

    def read(which):
        entry = list_ref[which]
        slot = entry & ((1 << TILE_SHIFT) - 1)
        return slot, table_ref[pl.ds(entry >> PLANE_SHIFT, 1), :], got_ref[slot]

    def chunk_tile(turn):
        return (list_ref[turn * UNROLL] >> TILE_SHIFT) & 15

    def front(turn, row_ref, partial_ref):
        for u in range(UNROLL):
            _, table_row, data = read(turn * UNROLL + u)
            taps, group = spread_parts(data[2:3].astype(jnp.int32), table_row)
            taps = taps.astype(jnp.bfloat16)
            group = group.astype(jnp.float32).astype(jnp.bfloat16)
            for k in range(groups):
                row_ref[16 * k : 16 * k + 16, 128 * u : 128 * u + 128] = jnp.where(
                    group == k, taps, zero
                )
        partial_ref[...] = jnp.dot(
            turned_ref[chunk_tile(turn)], row_ref[...], preferred_element_type=jnp.float32
        )

    def back(turn, row_ref, partial_ref):
        for u in range(UNROLL):
            slot, table_row, data = read(turn * UNROLL + u)
            columns = slice(128 * u, 128 * u + 128)
            taps, group = spread_parts(data[3:4].astype(jnp.int32), table_row)
            residuals, samples = [], []
            for part in range(2):
                picked = jnp.zeros((16, 128), jnp.float32)
                for k in range(groups):
                    low = part * side + 16 * k
                    picked = jnp.where(group == k, partial_ref[low : low + 16, columns], picked)
                model = jnp.sum(picked * taps, axis=0, keepdims=True)
                residual = data[part : part + 1] - model
                residuals.append(residual)
                samples.append((residual * taps).astype(jnp.bfloat16))
            residual_ref[slot] = jnp.concatenate(residuals, axis=0).astype(jnp.bfloat16)
            group = group.astype(jnp.float32).astype(jnp.bfloat16)
            for part in range(2):
                for k in range(groups):
                    low = part * side + 16 * k
                    weighted_ref[low : low + 16, columns] = jnp.where(
                        group == k, samples[part], zero
                    )
        grid_ref[chunk_tile(turn)] += lax.dot_general(
            row_ref[...],
            weighted_ref[...],
            (((1,), (1,)), ((), ())),
            preferred_element_type=jnp.float32,
        )

    def step(turn, carry):
        front(2 * turn + 1, row_b, partial_b)
        back(2 * turn, row_a, partial_a)
        front(2 * turn + 2, row_a, partial_a)
        back(2 * turn + 1, row_b, partial_b)
        return carry

    front(0, row_a, partial_a)
    lax.fori_loop(0, (chunks + 1) >> 1, step, 0)
    half = tiles // 2
    member = member_ref[0]
    for t in range(half):
        own_ref[t] = grid_ref[member * half + t]
        other_ref[t] = grid_ref[(1 - member) * half + t].astype(jnp.bfloat16)


def body(visibilities, uv_cell, sub_pixel, w_plane, block_tile, model_grid, kernel_table, coupling):
    owners = lax.axis_size("tile")
    pairs = owners // 2
    _, blocks, _, rows = visibilities.shape
    capacity = 2 * (3 * blocks // owners)
    _, tiles_here, side, wide = model_grid.shape
    planes, oversample, support = kernel_table.shape
    slots = pairs * (capacity + 1)
    member = lax.axis_index("tile") // pairs
    swap = [(t, (t + pairs) % owners) for t in range(owners)]
    halves = [list(range(pairs)), list(range(pairs, owners))]

    model_own = model_grid[0]
    model_other = lax.ppermute(model_own, "tile", swap)
    sent, slot = pl.pallas_call(
        lambda *refs: pack_kernel(pairs, capacity, tiles_here, planes, *refs),
        out_shape=(
            jax.ShapeDtypeStruct((slots, 4, rows), jnp.float32),
            jax.ShapeDtypeStruct((blocks,), jnp.int32),
        ),
        in_specs=[SMEM, SMEM, HBM, HBM, HBM],
        out_specs=(VMEM, SMEM),
        scratch_shapes=[
            pltpu.VMEM((blocks, 2, rows), jnp.float32),
            pltpu.VMEM((blocks, 2, rows), jnp.int32),
            pltpu.VMEM((blocks, 2, rows), jnp.int32),
            pltpu.SMEM((pairs, 4, rows), jnp.float32),
            pltpu.SMEM((pairs * 2 * tiles_here,), jnp.int32),
            pltpu.SemaphoreType.DMA((3,)),
            pltpu.SemaphoreType.DMA((pairs,)),
        ],
        compiler_params=WHOLE_PARAMS,
        name="pack_blocks",
    )(w_plane[0], block_tile[0], visibilities[0], uv_cell[0], sub_pixel[0])
    sent, model_other = lax.optimization_barrier((sent, model_other))
    got = lax.all_to_all(
        sent, "tile", split_axis=0, concat_axis=0, tiled=True, axis_index_groups=halves
    )
    model = jnp.where(
        member == 0,
        jnp.concatenate([model_own, model_other]),
        jnp.concatenate([model_other, model_own]),
    )
    table = jnp.pad(
        kernel_table.astype(jnp.float32), ((0, 8), (0, 0), (0, 16 - support))
    ).reshape(planes + 8, 16 * oversample)
    residual, own, other = pl.pallas_call(
        lambda *refs: grid_kernel(pairs, capacity, *refs),
        out_shape=(
            jax.ShapeDtypeStruct((slots, 2, rows), jnp.bfloat16),
            jax.ShapeDtypeStruct((tiles_here, side, wide), jnp.float32),
            jax.ShapeDtypeStruct((tiles_here, side, wide), jnp.bfloat16),
        ),
        in_specs=[SMEM, VMEM, VMEM, VMEM],
        out_specs=(VMEM, VMEM, VMEM),
        scratch_shapes=[
            pltpu.VMEM((2 * tiles_here, wide, side), jnp.bfloat16),
            pltpu.VMEM((2 * tiles_here, side, wide), jnp.float32),
            pltpu.VMEM((side, UNROLL * rows), jnp.bfloat16),
            pltpu.VMEM((side, UNROLL * rows), jnp.bfloat16),
            pltpu.VMEM((wide, UNROLL * rows), jnp.float32),
            pltpu.VMEM((wide, UNROLL * rows), jnp.float32),
            pltpu.VMEM((wide, UNROLL * rows), jnp.bfloat16),
            pltpu.VMEM((pairs, 2, rows), jnp.int32),
            pltpu.SMEM((pairs, 2, rows), jnp.int32),
            pltpu.SMEM((slots + capacity + 2 * tiles_here * UNROLL + UNROLL,), jnp.int32),
            pltpu.SemaphoreType.DMA,
        ],
        compiler_params=PARAMS,
        name="grid_blocks",
    )(member[None], got, table, model)

    returned = lax.all_to_all(
        residual, "tile", split_axis=0, concat_axis=0, tiled=True, axis_index_groups=halves
    )
    residuals = jnp.take(returned, slot, axis=0, mode="clip").astype(jnp.float32)[None]
    grid_sum = own + lax.ppermute(other, "tile", swap).astype(jnp.float32)
    grid_rounded = grid_sum.astype(jnp.bfloat16)[None]
    own_row = lax.dynamic_index_in_dim(coupling, lax.axis_index("freq"), 0, keepdims=False)
    coupled_grid = jnp.sum(
        own_row[:, None, None, None]
        * lax.all_gather(grid_rounded, "freq", axis=0, tiled=True).astype(jnp.float32),
        axis=0,
    )[None]
    return (residuals, coupled_grid)


def solution(mesh):
    return jax.shard_map(
        body,
        mesh=mesh,
        in_specs=(
            P("freq", "tile", None, None),
            P("freq", "tile", None, None),
            P("freq", "tile", None, None),
            P("freq", "tile"),
            P("freq", "tile"),
            P("freq", "tile", None, None),
            P(),
            P(),
        ),
        out_specs=(P("freq", "tile", None, None), P("freq", "tile", None, None)),
        check_vma=False,
    )
```

```python
import jax
import jax.numpy as jnp
from jax import lax
from jax.experimental import pallas as pl
from jax.experimental.pallas import tpu as pltpu
from jax.sharding import PartitionSpec as P

UNROLL = 4
VMEM = pl.BlockSpec(memory_space=pltpu.VMEM)
SMEM = pl.BlockSpec(memory_space=pltpu.SMEM)
HBM = pl.BlockSpec(memory_space=pltpu.HBM)
PARAMS = pltpu.CompilerParams(vmem_limit_bytes=32 * 1024 * 1024)
WHOLE_PARAMS = pltpu.CompilerParams(vmem_limit_bytes=62 * 1024 * 1024)
TILE_SHIFT = 12
PLANE_SHIFT = 16


def scalar_div(value, count):
    shift = count.bit_length() - 1
    return value >> shift if count == 1 << shift else lax.div(value, count)


def first_slot(local, rank, capacity):
    half = capacity // 2
    return (local >> 1) * half + jnp.where((local & 1) == 0, rank, half - 1 - rank)


def pack_kernel(pairs, capacity, tiles_here, planes, plane_hbm, tile_hbm, vis_hbm, cell_hbm, sub_hbm,
                sent_ref, slot_ref, plane_ref, tile_ref, vis_ref, cell_ref, sub_ref, about_ref, count_ref,
                load_sem, about_sem):
    blocks = tile_ref.shape[0]
    loads = [
        pltpu.make_async_copy(source, target, load_sem.at[i])
        for i, (source, target) in enumerate(
            [
                (tile_hbm, tile_ref),
                (plane_hbm, plane_ref),
                (vis_hbm, vis_ref),
                (cell_hbm, cell_ref),
                (sub_hbm, sub_ref),
            ]
        )
    ]
    for copy in loads:
        copy.start()
    part = lax.broadcasted_iota(jnp.int32, (4, 128), 0)
    empty = jnp.where(part == 0, float(planes << PLANE_SHIFT), 0.0)
    abouts = [d * (capacity + 1) + capacity for d in range(pairs)]
    for d in range(pairs):
        sent_ref[abouts[d]] = empty
        for t in range(2 * tiles_here):
            count_ref[d * 2 * tiles_here + t] = 0
    fills = [
        pltpu.make_async_copy(sent_ref.at[abouts[d]], about_ref.at[d], about_sem.at[d])
        for d in range(pairs)
    ]
    for copy in fills:
        copy.start()
    for copy in fills + loads[:2]:
        copy.wait()

    def assign(b):
        tile = tile_ref[b]
        owner = scalar_div(tile, tiles_here)
        high = (owner >= pairs).astype(jnp.int32)
        pair = owner - high * pairs
        local = tile - (owner - high) * tiles_here
        key = pair * (2 * tiles_here) + local
        rank = count_ref[key]
        count_ref[key] = rank + 1
        place = first_slot(local, rank, capacity)
        slot_ref[b] = pair * (capacity + 1) + place
        code = (plane_ref[b] << PLANE_SHIFT) + (local << TILE_SHIFT)
        about_ref[pair, 0, place] = code.astype(jnp.float32)

    def move(b):
        position = (cell_ref[b] * 8 + sub_ref[b]).astype(jnp.float32)
        sent_ref[slot_ref[b]] = jnp.concatenate([vis_ref[b], position], axis=0)

    def each(work):
        def step(turn, carry):
            for which in range(8):
                work(turn * 8 + which)
            return carry

        lax.fori_loop(0, blocks // 8, step, 0)

    each(assign)
    for d in range(pairs):
        for t in range(2 * tiles_here):
            about_ref[d, 1, t] = count_ref[d * 2 * tiles_here + t].astype(jnp.float32)
    returns = [
        pltpu.make_async_copy(about_ref.at[d], sent_ref.at[abouts[d]], about_sem.at[d])
        for d in range(pairs)
    ]
    for copy in returns:
        copy.start()
    for copy in loads[2:]:
        copy.wait()
    each(move)
    for copy in returns:
        copy.wait()


def unpack_kernel(slot_ref, returned_ref, residual_ref):
    def step(turn, carry):
        for which in range(8):
            b = turn * 8 + which
            residual_ref[b] = returned_ref[slot_ref[b]].astype(jnp.float32)
        return carry

    lax.fori_loop(0, residual_ref.shape[0] // 8, step, 0)


def spread_parts(start, offset, table):
    sublane = lax.broadcasted_iota(jnp.int32, (8, 128), 0)
    taps, group = [], []
    for low in (0, 8):
        delta = sublane + low - start
        taps.append(
            jnp.take_along_axis(table, (delta & 15) + offset, axis=1, mode="promise_in_bounds")
        )
        group.append((15 - delta) >> 4)
    return jnp.concatenate(taps, axis=0), jnp.concatenate(group, axis=0)


def grid_kernel(pairs, capacity, member_ref, got_ref, table_ref, model_ref, residual_ref, own_ref,
                other_ref, turned_ref, grid_ref, row_a, row_b, partial_a, partial_b, weighted_a, weighted_b, code_ref, about_ref, list_ref, sem):
    tiles, side, wide = model_ref.shape
    groups = side // 16
    zero_row = table_ref.shape[0] - 8
    lane = lax.broadcasted_iota(jnp.int32, (1, 128), 1)
    for s in range(pairs):
        about = got_ref[s * (capacity + 1) + capacity].astype(jnp.int32)
        code_ref[s, 0:1, :] = about[0:1] + (lane + s * (capacity + 1))
        code_ref[s, 1:2, :] = about[1:2]
    fill = pltpu.make_async_copy(code_ref, about_ref, sem)
    fill.start()
    for t in range(tiles):
        turned_ref[t] = model_ref[t].T
    grid_ref[...] = jnp.zeros_like(grid_ref)
    fill.wait()

    start = jnp.int32(0)
    for t in range(tiles):
        count = jnp.int32(0)
        for s in range(pairs):
            count = count + about_ref[s, 1, t]
        spare = -count & (UNROLL - 1)
        for u in range(UNROLL):
            list_ref[start + u] = (zero_row << PLANE_SHIFT) + (t << TILE_SHIFT) + capacity

        def enlist(s, filled, t=t):
            first = t // 2 * (capacity // 2)
            found = about_ref[s, 1, t]

            def some(turn, carry):
                for which in range(8):
                    k = turn * 8 + which
                    place = k if t % 2 == 0 else capacity // 2 - 1 - k
                    list_ref[filled + k] = about_ref[s, 0, jnp.maximum(first + place, 0)]
                return carry

            lax.fori_loop(0, (found + 7) >> 3, some, 0)
            return filled + found

        lax.fori_loop(0, pairs, enlist, start + spare)
        start = start + count + spare
    for u in range(2 * UNROLL):
        list_ref[start + u] = (zero_row << PLANE_SHIFT) + capacity
    chunks = start >> UNROLL.bit_length() - 1
    zero = jnp.zeros((16, 128), jnp.bfloat16)

    def read(which):
        entry = list_ref[which]
        slot = entry & ((1 << TILE_SHIFT) - 1)
        data = got_ref[slot]
        position = data.astype(jnp.int32)
        start, offset = position >> 3, (position & 7) << 4
        table = jnp.broadcast_to(table_ref[pl.ds(entry >> PLANE_SHIFT, 1), :], (8, 128))

        def parts(row):
            return spread_parts(
                jnp.broadcast_to(start[row : row + 1], (8, 128)),
                jnp.broadcast_to(offset[row : row + 1], (8, 128)),
                table,
            )

        return slot, data, parts

    def chunk_tile(turn):
        return (list_ref[turn * UNROLL] >> TILE_SHIFT) & 15

    def front(turn, row_ref, partial_ref):
        for u in range(UNROLL):
            _, _, parts = read(turn * UNROLL + u)
            taps, group = parts(2)
            taps = taps.astype(jnp.bfloat16)
            group = group.astype(jnp.float32).astype(jnp.bfloat16)
            for k in range(groups):
                row_ref[16 * k : 16 * k + 16, 128 * u : 128 * u + 128] = jnp.where(
                    group == k, taps, zero
                )
        partial_ref[...] = jnp.dot(
            turned_ref[chunk_tile(turn)], row_ref[...], preferred_element_type=jnp.float32
        )

    def back(turn, row_ref, partial_ref, weighted_ref):
        for u in range(UNROLL):
            slot, data, parts = read(turn * UNROLL + u)
            columns = slice(128 * u, 128 * u + 128)
            taps, group = parts(3)
            residuals, samples = [], []
            for part in range(2):
                picked = jnp.zeros((16, 128), jnp.float32)
                for k in range(groups):
                    low = part * side + 16 * k
                    picked = jnp.where(group == k, partial_ref[low : low + 16, columns], picked)
                model = jnp.sum(picked * taps, axis=0, keepdims=True)
                residual = data[part : part + 1] - model
                residuals.append(residual)
                samples.append((residual * taps).astype(jnp.bfloat16))
            residual_ref[slot] = jnp.concatenate(residuals, axis=0).astype(jnp.bfloat16)
            group = group.astype(jnp.float32).astype(jnp.bfloat16)
            for part in range(2):
                for k in range(groups):
                    low = part * side + 16 * k
                    weighted_ref[low : low + 16, columns] = jnp.where(
                        group == k, samples[part], zero
                    )
        grid_ref[chunk_tile(turn)] += lax.dot_general(
            row_ref[...],
            weighted_ref[...],
            (((1,), (1,)), ((), ())),
            preferred_element_type=jnp.float32,
        )

    def step(turn, carry):
        front(2 * turn + 1, row_b, partial_b)
        back(2 * turn, row_a, partial_a, weighted_a)
        front(2 * turn + 2, row_a, partial_a)
        back(2 * turn + 1, row_b, partial_b, weighted_b)
        return carry

    front(0, row_a, partial_a)
    lax.fori_loop(0, (chunks + 1) >> 1, step, 0)
    half = tiles // 2
    member = member_ref[0]
    for t in range(half):
        own_ref[t] = grid_ref[member * half + t]
        other_ref[t] = grid_ref[(1 - member) * half + t].astype(jnp.bfloat16)


def body(visibilities, uv_cell, sub_pixel, w_plane, block_tile, model_grid, kernel_table, coupling):
    owners = lax.axis_size("tile")
    pairs = owners // 2
    _, blocks, _, rows = visibilities.shape
    capacity = 2 * (3 * blocks // owners)
    _, tiles_here, side, wide = model_grid.shape
    planes, oversample, support = kernel_table.shape
    slots = pairs * (capacity + 1)
    member = lax.axis_index("tile") // pairs
    swap = [(t, (t + pairs) % owners) for t in range(owners)]
    halves = [list(range(pairs)), list(range(pairs, owners))]

    model_own = model_grid[0]
    model_other = lax.ppermute(model_own, "tile", swap)
    sent, slot = pl.pallas_call(
        lambda *refs: pack_kernel(pairs, capacity, tiles_here, planes, *refs),
        out_shape=(
            jax.ShapeDtypeStruct((slots, 4, rows), jnp.float32),
            jax.ShapeDtypeStruct((blocks,), jnp.int32),
        ),
        in_specs=[HBM] * 5,
        out_specs=(VMEM, SMEM),
        scratch_shapes=[
            pltpu.SMEM((blocks,), jnp.int32),
            pltpu.SMEM((blocks,), jnp.int32),
            pltpu.VMEM((blocks, 2, rows), jnp.float32),
            pltpu.VMEM((blocks, 2, rows), jnp.int32),
            pltpu.VMEM((blocks, 2, rows), jnp.int32),
            pltpu.SMEM((pairs, 4, rows), jnp.float32),
            pltpu.SMEM((pairs * 2 * tiles_here,), jnp.int32),
            pltpu.SemaphoreType.DMA((5,)),
            pltpu.SemaphoreType.DMA((pairs,)),
        ],
        compiler_params=WHOLE_PARAMS,
        name="pack_blocks",
    )(w_plane[0], block_tile[0], visibilities[0], uv_cell[0], sub_pixel[0])
    got = lax.all_to_all(
        sent, "tile", split_axis=0, concat_axis=0, tiled=True, axis_index_groups=halves
    )
    model = jnp.where(
        member == 0,
        jnp.concatenate([model_own, model_other]),
        jnp.concatenate([model_other, model_own]),
    )
    table = jnp.pad(
        kernel_table.astype(jnp.float32), ((0, 8), (0, 0), (0, 16 - support))
    ).reshape(planes + 8, 16 * oversample)
    residual, own, other = pl.pallas_call(
        lambda *refs: grid_kernel(pairs, capacity, *refs),
        out_shape=(
            jax.ShapeDtypeStruct((slots, 2, rows), jnp.bfloat16),
            jax.ShapeDtypeStruct((tiles_here, side, wide), jnp.float32),
            jax.ShapeDtypeStruct((tiles_here, side, wide), jnp.bfloat16),
        ),
        in_specs=[SMEM, VMEM, VMEM, VMEM],
        out_specs=(VMEM, VMEM, VMEM),
        scratch_shapes=[
            pltpu.VMEM((2 * tiles_here, wide, side), jnp.bfloat16),
            pltpu.VMEM((2 * tiles_here, side, wide), jnp.float32),
            pltpu.VMEM((side, UNROLL * rows), jnp.bfloat16),
            pltpu.VMEM((side, UNROLL * rows), jnp.bfloat16),
            pltpu.VMEM((wide, UNROLL * rows), jnp.float32),
            pltpu.VMEM((wide, UNROLL * rows), jnp.float32),
            pltpu.VMEM((wide, UNROLL * rows), jnp.bfloat16),
            pltpu.VMEM((wide, UNROLL * rows), jnp.bfloat16),
            pltpu.VMEM((pairs, 2, rows), jnp.int32),
            pltpu.SMEM((pairs, 2, rows), jnp.int32),
            pltpu.SMEM((slots + capacity + 2 * tiles_here * UNROLL + UNROLL,), jnp.int32),
            pltpu.SemaphoreType.DMA,
        ],
        compiler_params=PARAMS,
        name="grid_blocks",
    )(member[None], got, table, model)

    returned = lax.all_to_all(
        residual, "tile", split_axis=0, concat_axis=0, tiled=True, axis_index_groups=halves
    )
    grid_sum = own + lax.ppermute(other, "tile", swap).astype(jnp.float32)
    grid_rounded = grid_sum.astype(jnp.bfloat16)
    freqs = lax.axis_size("freq")
    plane = lax.axis_index("freq")
    own_row = lax.dynamic_index_in_dim(coupling, plane, 0, keepdims=False)
    if freqs == 2:
        grid_next = lax.ppermute(grid_rounded, "freq", [(0, 1), (1, 0)])
        coupled_grid = own_row[plane] * grid_rounded.astype(jnp.float32) + own_row[
            1 - plane
        ] * grid_next.astype(jnp.float32)
    else:
        gathered = lax.all_gather(grid_rounded[None], "freq", axis=0, tiled=True)
        coupled_grid = jnp.sum(own_row[:, None, None, None] * gathered.astype(jnp.float32), axis=0)
    residuals = pl.pallas_call(
        unpack_kernel,
        out_shape=jax.ShapeDtypeStruct((blocks, 2, rows), jnp.float32),
        in_specs=[SMEM, VMEM],
        out_specs=VMEM,
        compiler_params=PARAMS,
        cost_estimate=pl.CostEstimate(flops=0, bytes_accessed=4000000, transcendentals=0),
        name="unpack_residuals",
    )(slot, returned)
    return (residuals[None], coupled_grid[None])


def solution(mesh):
    return jax.shard_map(
        body,
        mesh=mesh,
        in_specs=(
            P("freq", "tile", None, None),
            P("freq", "tile", None, None),
            P("freq", "tile", None, None),
            P("freq", "tile"),
            P("freq", "tile"),
            P("freq", "tile", None, None),
            P(),
            P(),
        ),
        out_specs=(P("freq", "tile", None, None), P("freq", "tile", None, None)),
        check_vma=False,
    )
```

```python
import jax
import jax.numpy as jnp
from jax import lax
from jax.experimental import pallas as pl
from jax.experimental.pallas import tpu as pltpu
from jax.sharding import PartitionSpec as P

UNROLL = 8
VMEM = pl.BlockSpec(memory_space=pltpu.VMEM)
SMEM = pl.BlockSpec(memory_space=pltpu.SMEM)
HBM = pl.BlockSpec(memory_space=pltpu.HBM)
PARAMS = pltpu.CompilerParams(vmem_limit_bytes=32 * 1024 * 1024)
WHOLE_PARAMS = pltpu.CompilerParams(vmem_limit_bytes=62 * 1024 * 1024)
TILE_SHIFT = 12
PLANE_SHIFT = 16


def scalar_div(value, count):
    shift = count.bit_length() - 1
    return value >> shift if count == 1 << shift else lax.div(value, count)


def first_slot(local, rank, capacity):
    half = capacity // 2
    return (local >> 1) * half + jnp.where((local & 1) == 0, rank, half - 1 - rank)


def pack_kernel(pairs, capacity, tiles_here, planes, plane_hbm, tile_hbm, vis_hbm, cell_hbm, sub_hbm,
                sent_ref, slot_ref, plane_ref, tile_ref, vis_ref, cell_ref, sub_ref, about_ref, count_ref,
                load_sem, about_sem):
    blocks = tile_ref.shape[0]
    loads = [
        pltpu.make_async_copy(source, target, load_sem.at[i])
        for i, (source, target) in enumerate(
            [
                (tile_hbm, tile_ref),
                (plane_hbm, plane_ref),
                (vis_hbm, vis_ref),
                (cell_hbm, cell_ref),
                (sub_hbm, sub_ref),
            ]
        )
    ]
    for copy in loads:
        copy.start()
    part = lax.broadcasted_iota(jnp.int32, (4, 128), 0)
    empty = jnp.where(part == 0, float(planes << PLANE_SHIFT), 0.0)
    abouts = [d * (capacity + 1) + capacity for d in range(pairs)]
    for d in range(pairs):
        sent_ref[abouts[d]] = empty
        for t in range(2 * tiles_here):
            count_ref[d * 2 * tiles_here + t] = 0
    fills = [
        pltpu.make_async_copy(sent_ref.at[abouts[d]], about_ref.at[d], about_sem.at[d])
        for d in range(pairs)
    ]
    for copy in fills:
        copy.start()
    for copy in fills + loads[:2]:
        copy.wait()

    def assign(b):
        tile = tile_ref[b]
        owner = scalar_div(tile, tiles_here)
        high = (owner >= pairs).astype(jnp.int32)
        pair = owner - high * pairs
        local = tile - (owner - high) * tiles_here
        key = pair * (2 * tiles_here) + local
        rank = count_ref[key]
        count_ref[key] = rank + 1
        place = first_slot(local, rank, capacity)
        slot_ref[b] = pair * (capacity + 1) + place
        code = (plane_ref[b] << PLANE_SHIFT) + (local << TILE_SHIFT)
        about_ref[pair, 0, place] = code.astype(jnp.float32)

    def move(b):
        position = (cell_ref[b] * 8 + sub_ref[b]).astype(jnp.float32)
        sent_ref[slot_ref[b]] = jnp.concatenate([vis_ref[b], position], axis=0)

    def each(work):
        def step(turn, carry):
            for which in range(8):
                work(turn * 8 + which)
            return carry

        lax.fori_loop(0, blocks // 8, step, 0)

    each(assign)
    for d in range(pairs):
        for t in range(2 * tiles_here):
            about_ref[d, 1, t] = count_ref[d * 2 * tiles_here + t].astype(jnp.float32)
    returns = [
        pltpu.make_async_copy(about_ref.at[d], sent_ref.at[abouts[d]], about_sem.at[d])
        for d in range(pairs)
    ]
    for copy in returns:
        copy.start()
    for copy in loads[2:]:
        copy.wait()
    each(move)
    for copy in returns:
        copy.wait()


def finish_kernel(plane_ref, coupling_ref, slot_ref, returned_ref, *refs):
    *grid_refs, residual_ref, coupled_ref = refs
    plane = plane_ref[0]
    if len(grid_refs) == 2:
        grids = [(plane, grid_refs[0]), (1 - plane, grid_refs[1])]
    else:
        grids = [(g, grid_refs[0].at[g]) for g in range(grid_refs[0].shape[0])]
    coupled_ref[...] = sum(
        coupling_ref[plane, g] * grid_ref[...].astype(jnp.float32) for g, grid_ref in grids
    )

    def step(turn, carry):
        for which in range(8):
            b = turn * 8 + which
            residual_ref[b] = returned_ref[slot_ref[b]].astype(jnp.float32)
        return carry

    lax.fori_loop(0, residual_ref.shape[0] // 8, step, 0)


def spread_parts(start, offset, table):
    sublane = lax.broadcasted_iota(jnp.int32, (8, 128), 0)
    taps, group = [], []
    for low in (0, 8):
        delta = sublane + low - start
        taps.append(
            jnp.take_along_axis(table, (delta & 15) + offset, axis=1, mode="promise_in_bounds")
        )
        group.append((15 - delta) >> 4)
    return jnp.concatenate(taps, axis=0), jnp.concatenate(group, axis=0)


def grid_kernel(pairs, capacity, member_ref, got_ref, table_ref, model_ref, residual_ref, own_ref,
                other_ref, turned_ref, grid_ref, row_a, row_b, partial_a, partial_b, weighted_a, weighted_b, code_ref, about_ref, list_ref, sem):
    tiles, side, wide = model_ref.shape
    groups = side // 16
    zero_row = table_ref.shape[0] - 8
    lane = lax.broadcasted_iota(jnp.int32, (1, 128), 1)
    for s in range(pairs):
        about = got_ref[s * (capacity + 1) + capacity].astype(jnp.int32)
        code_ref[s, 0:1, :] = about[0:1] + (lane + s * (capacity + 1))
        code_ref[s, 1:2, :] = about[1:2]
    fill = pltpu.make_async_copy(code_ref, about_ref, sem)
    fill.start()
    for t in range(tiles):
        turned_ref[t] = model_ref[t].T
    grid_ref[...] = jnp.zeros_like(grid_ref)
    fill.wait()

    start = jnp.int32(0)
    for t in range(tiles):
        count = jnp.int32(0)
        for s in range(pairs):
            count = count + about_ref[s, 1, t]
        spare = -count & (UNROLL - 1)
        for u in range(UNROLL):
            list_ref[start + u] = (zero_row << PLANE_SHIFT) + (t << TILE_SHIFT) + capacity

        def enlist(s, filled, t=t):
            first = t // 2 * (capacity // 2)
            found = about_ref[s, 1, t]

            def some(turn, carry):
                for which in range(8):
                    k = turn * 8 + which
                    place = k if t % 2 == 0 else capacity // 2 - 1 - k
                    list_ref[filled + k] = about_ref[s, 0, jnp.maximum(first + place, 0)]
                return carry

            lax.fori_loop(0, (found + 7) >> 3, some, 0)
            return filled + found

        lax.fori_loop(0, pairs, enlist, start + spare)
        start = start + count + spare
    for u in range(2 * UNROLL):
        list_ref[start + u] = (zero_row << PLANE_SHIFT) + capacity
    chunks = start >> UNROLL.bit_length() - 1
    zero = jnp.zeros((16, 128), jnp.bfloat16)

    def read(which):
        entry = list_ref[which]
        slot = entry & ((1 << TILE_SHIFT) - 1)
        data = got_ref[slot]
        position = data.astype(jnp.int32)
        start, offset = position >> 3, (position & 7) << 4
        table = jnp.broadcast_to(table_ref[pl.ds(entry >> PLANE_SHIFT, 1), :], (8, 128))

        def parts(row):
            return spread_parts(
                jnp.broadcast_to(start[row : row + 1], (8, 128)),
                jnp.broadcast_to(offset[row : row + 1], (8, 128)),
                table,
            )

        return slot, data, parts

    def chunk_tile(turn):
        return (list_ref[turn * UNROLL] >> TILE_SHIFT) & 15

    def front(turn, row_ref, partial_ref):
        for u in range(UNROLL):
            _, _, parts = read(turn * UNROLL + u)
            taps, group = parts(2)
            taps = taps.astype(jnp.bfloat16)
            group = group.astype(jnp.float32).astype(jnp.bfloat16)
            for k in range(groups):
                row_ref[16 * k : 16 * k + 16, 128 * u : 128 * u + 128] = jnp.where(
                    group == k, taps, zero
                )
        partial_ref[...] = jnp.dot(
            turned_ref[chunk_tile(turn)], row_ref[...], preferred_element_type=jnp.float32
        )

    def back(turn, row_ref, partial_ref, weighted_ref):
        for u in range(UNROLL):
            slot, data, parts = read(turn * UNROLL + u)
            columns = slice(128 * u, 128 * u + 128)
            taps, group = parts(3)
            residuals, samples = [], []
            for part in range(2):
                picked = jnp.zeros((16, 128), jnp.float32)
                for k in range(groups):
                    low = part * side + 16 * k
                    picked = jnp.where(group == k, partial_ref[low : low + 16, columns], picked)
                model = jnp.sum(picked * taps, axis=0, keepdims=True)
                residual = data[part : part + 1] - model
                residuals.append(residual)
                samples.append((residual * taps).astype(jnp.bfloat16))
            residual_ref[slot] = jnp.concatenate(residuals, axis=0).astype(jnp.bfloat16)
            group = group.astype(jnp.float32).astype(jnp.bfloat16)
            for part in range(2):
                for k in range(groups):
                    low = part * side + 16 * k
                    weighted_ref[low : low + 16, columns] = jnp.where(
                        group == k, samples[part], zero
                    )
        grid_ref[chunk_tile(turn)] += lax.dot_general(
            row_ref[...],
            weighted_ref[...],
            (((1,), (1,)), ((), ())),
            preferred_element_type=jnp.float32,
        )

    def step(turn, carry):
        front(2 * turn + 1, row_b, partial_b)
        back(2 * turn, row_a, partial_a, weighted_a)
        front(2 * turn + 2, row_a, partial_a)
        back(2 * turn + 1, row_b, partial_b, weighted_b)
        return carry

    front(0, row_a, partial_a)
    lax.fori_loop(0, (chunks + 1) >> 1, step, 0)
    half = tiles // 2
    member = member_ref[0]
    for t in range(half):
        own_ref[t] = grid_ref[member * half + t]
        other_ref[t] = grid_ref[(1 - member) * half + t].astype(jnp.bfloat16)


def body(visibilities, uv_cell, sub_pixel, w_plane, block_tile, model_grid, kernel_table, coupling):
    owners = lax.axis_size("tile")
    pairs = owners // 2
    _, blocks, _, rows = visibilities.shape
    capacity = 2 * (3 * blocks // owners)
    _, tiles_here, side, wide = model_grid.shape
    planes, oversample, support = kernel_table.shape
    slots = pairs * (capacity + 1)
    member = lax.axis_index("tile") // pairs
    swap = [(t, (t + pairs) % owners) for t in range(owners)]
    halves = [list(range(pairs)), list(range(pairs, owners))]

    model_own = model_grid[0]
    model_other = lax.ppermute(model_own, "tile", swap)
    sent, slot = pl.pallas_call(
        lambda *refs: pack_kernel(pairs, capacity, tiles_here, planes, *refs),
        out_shape=(
            jax.ShapeDtypeStruct((slots, 4, rows), jnp.float32),
            jax.ShapeDtypeStruct((blocks,), jnp.int32),
        ),
        in_specs=[HBM] * 5,
        out_specs=(VMEM, SMEM),
        scratch_shapes=[
            pltpu.SMEM((blocks,), jnp.int32),
            pltpu.SMEM((blocks,), jnp.int32),
            pltpu.VMEM((blocks, 2, rows), jnp.float32),
            pltpu.VMEM((blocks, 2, rows), jnp.int32),
            pltpu.VMEM((blocks, 2, rows), jnp.int32),
            pltpu.SMEM((pairs, 4, rows), jnp.float32),
            pltpu.SMEM((pairs * 2 * tiles_here,), jnp.int32),
            pltpu.SemaphoreType.DMA((5,)),
            pltpu.SemaphoreType.DMA((pairs,)),
        ],
        compiler_params=WHOLE_PARAMS,
        name="pack_blocks",
    )(w_plane[0], block_tile[0], visibilities[0], uv_cell[0], sub_pixel[0])
    got = lax.all_to_all(
        sent, "tile", split_axis=0, concat_axis=0, tiled=True, axis_index_groups=halves
    )
    model = jnp.where(
        member == 0,
        jnp.concatenate([model_own, model_other]),
        jnp.concatenate([model_other, model_own]),
    )
    table = jnp.pad(
        kernel_table.astype(jnp.float32), ((0, 8), (0, 0), (0, 16 - support))
    ).reshape(planes + 8, 16 * oversample)
    residual, own, other = pl.pallas_call(
        lambda *refs: grid_kernel(pairs, capacity, *refs),
        out_shape=(
            jax.ShapeDtypeStruct((slots, 2, rows), jnp.bfloat16),
            jax.ShapeDtypeStruct((tiles_here, side, wide), jnp.float32),
            jax.ShapeDtypeStruct((tiles_here, side, wide), jnp.bfloat16),
        ),
        in_specs=[SMEM, VMEM, VMEM, VMEM],
        out_specs=(VMEM, VMEM, VMEM),
        scratch_shapes=[
            pltpu.VMEM((2 * tiles_here, wide, side), jnp.bfloat16),
            pltpu.VMEM((2 * tiles_here, side, wide), jnp.float32),
            pltpu.VMEM((side, UNROLL * rows), jnp.bfloat16),
            pltpu.VMEM((side, UNROLL * rows), jnp.bfloat16),
            pltpu.VMEM((wide, UNROLL * rows), jnp.float32),
            pltpu.VMEM((wide, UNROLL * rows), jnp.float32),
            pltpu.VMEM((wide, UNROLL * rows), jnp.bfloat16),
            pltpu.VMEM((wide, UNROLL * rows), jnp.bfloat16),
            pltpu.VMEM((pairs, 2, rows), jnp.int32),
            pltpu.SMEM((pairs, 2, rows), jnp.int32),
            pltpu.SMEM((slots + capacity + 2 * tiles_here * UNROLL + UNROLL,), jnp.int32),
            pltpu.SemaphoreType.DMA,
        ],
        compiler_params=PARAMS,
        name="grid_blocks",
    )(member[None], got, table, model)

    returned = lax.all_to_all(
        residual, "tile", split_axis=0, concat_axis=0, tiled=True, axis_index_groups=halves
    )
    got_other, returned = lax.optimization_barrier((lax.ppermute(other, "tile", swap), returned))
    grid_rounded = (own + got_other.astype(jnp.float32)).astype(jnp.bfloat16)
    if lax.axis_size("freq") == 2:
        grids = [grid_rounded, lax.ppermute(grid_rounded, "freq", [(0, 1), (1, 0)])]
    else:
        grids = [lax.all_gather(grid_rounded, "freq", axis=0)]
    residuals, coupled_grid = pl.pallas_call(
        finish_kernel,
        out_shape=(
            jax.ShapeDtypeStruct((blocks, 2, rows), jnp.float32),
            jax.ShapeDtypeStruct((tiles_here, side, wide), jnp.float32),
        ),
        in_specs=[SMEM, SMEM, SMEM, VMEM] + [VMEM] * len(grids),
        out_specs=(VMEM, VMEM),
        compiler_params=PARAMS,
        name="finish",
    )(lax.axis_index("freq")[None], coupling, slot, returned, *grids)
    return (residuals[None], coupled_grid[None])


def solution(mesh):
    return jax.shard_map(
        body,
        mesh=mesh,
        in_specs=(
            P("freq", "tile", None, None),
            P("freq", "tile", None, None),
            P("freq", "tile", None, None),
            P("freq", "tile"),
            P("freq", "tile"),
            P("freq", "tile", None, None),
            P(),
            P(),
        ),
        out_specs=(P("freq", "tile", None, None), P("freq", "tile", None, None)),
        check_vma=False,
    )
```

```python
import jax
import jax.numpy as jnp
from jax import lax
from jax.experimental import pallas as pl
from jax.experimental.pallas import tpu as pltpu
from jax.sharding import PartitionSpec as P

UNROLL = 8
VMEM = pl.BlockSpec(memory_space=pltpu.VMEM)
SMEM = pl.BlockSpec(memory_space=pltpu.SMEM)
HBM = pl.BlockSpec(memory_space=pltpu.HBM)
PARAMS = pltpu.CompilerParams(vmem_limit_bytes=32 * 1024 * 1024)
WHOLE_PARAMS = pltpu.CompilerParams(vmem_limit_bytes=62 * 1024 * 1024)
TILE_SHIFT = 12
PLANE_SHIFT = 16


def scalar_div(value, count):
    shift = count.bit_length() - 1
    return value >> shift if count == 1 << shift else lax.div(value, count)


def first_slot(local, rank, capacity):
    half = capacity // 2
    return (local >> 1) * half + jnp.where((local & 1) == 0, rank, half - 1 - rank)


def pack_kernel(pairs, capacity, tiles_here, planes, plane_hbm, tile_hbm, vis_hbm, cell_hbm, sub_hbm,
                sent_ref, slot_ref, plane_ref, tile_ref, vis_ref, cell_ref, sub_ref, about_ref, count_ref,
                load_sem, about_sem):
    blocks = tile_ref.shape[0]
    loads = [
        pltpu.make_async_copy(source, target, load_sem.at[i])
        for i, (source, target) in enumerate(
            [
                (tile_hbm, tile_ref),
                (plane_hbm, plane_ref),
                (vis_hbm, vis_ref),
                (cell_hbm, cell_ref),
                (sub_hbm, sub_ref),
            ]
        )
    ]
    for copy in loads:
        copy.start()
    part = lax.broadcasted_iota(jnp.int32, (4, 128), 0)
    empty = jnp.where(part == 0, float(planes << PLANE_SHIFT), 0.0)
    abouts = [d * (capacity + 1) + capacity for d in range(pairs)]
    for d in range(pairs):
        sent_ref[abouts[d]] = empty
        for t in range(2 * tiles_here):
            count_ref[d * 2 * tiles_here + t] = 0
    fills = [
        pltpu.make_async_copy(sent_ref.at[abouts[d]], about_ref.at[d], about_sem.at[d])
        for d in range(pairs)
    ]
    for copy in fills:
        copy.start()
    for copy in fills + loads[:2]:
        copy.wait()

    def assign(b):
        tile = tile_ref[b]
        owner = scalar_div(tile, tiles_here)
        high = (owner >= pairs).astype(jnp.int32)
        pair = owner - high * pairs
        local = tile - (owner - high) * tiles_here
        key = pair * (2 * tiles_here) + local
        rank = count_ref[key]
        count_ref[key] = rank + 1
        place = first_slot(local, rank, capacity)
        slot_ref[b] = pair * (capacity + 1) + place
        code = (plane_ref[b] << PLANE_SHIFT) + (local << TILE_SHIFT)
        about_ref[pair, 0, place] = code.astype(jnp.float32)

    def move(b):
        position = (cell_ref[b] * 8 + sub_ref[b]).astype(jnp.float32)
        sent_ref[slot_ref[b]] = jnp.concatenate([vis_ref[b], position], axis=0)

    def each(work):
        def step(turn, carry):
            for which in range(8):
                work(turn * 8 + which)
            return carry

        lax.fori_loop(0, blocks // 8, step, 0)

    each(assign)
    for d in range(pairs):
        for t in range(2 * tiles_here):
            about_ref[d, 1, t] = count_ref[d * 2 * tiles_here + t].astype(jnp.float32)
    returns = [
        pltpu.make_async_copy(about_ref.at[d], sent_ref.at[abouts[d]], about_sem.at[d])
        for d in range(pairs)
    ]
    for copy in returns:
        copy.start()
    for copy in loads[2:]:
        copy.wait()
    each(move)
    for copy in returns:
        copy.wait()


def finish_kernel(plane_ref, coupling_ref, slot_ref, returned_ref, grid_ref, residual_ref, coupled_ref):
    coupled_ref[...] = sum(
        coupling_ref[plane_ref[0], g] * grid_ref[g].astype(jnp.float32)
        for g in range(grid_ref.shape[0])
    )

    def step(turn, carry):
        for which in range(8):
            b = turn * 8 + which
            residual_ref[b] = returned_ref[slot_ref[b]].astype(jnp.float32)
        return carry

    lax.fori_loop(0, residual_ref.shape[0] // 8, step, 0)


def spread_parts(start, offset, table):
    sublane = lax.broadcasted_iota(jnp.int32, (8, 128), 0)
    taps, group = [], []
    for low in (0, 8):
        delta = sublane + low - start
        taps.append(
            jnp.take_along_axis(table, (delta & 15) + offset, axis=1, mode="promise_in_bounds")
        )
        group.append((15 - delta) >> 4)
    return jnp.concatenate(taps, axis=0), jnp.concatenate(group, axis=0)


def grid_kernel(pairs, capacity, member_ref, got_ref, table_ref, model_ref, residual_ref, own_ref,
                other_ref, turned_ref, grid_ref, row_a, row_b, partial_a, partial_b, weighted_a, weighted_b, code_ref, about_ref, list_ref, sem):
    tiles, side, wide = model_ref.shape
    groups = side // 16
    zero_row = table_ref.shape[0] - 8
    lane = lax.broadcasted_iota(jnp.int32, (1, 128), 1)
    for s in range(pairs):
        about = got_ref[s * (capacity + 1) + capacity].astype(jnp.int32)
        code_ref[s, 0:1, :] = about[0:1] + (lane + s * (capacity + 1))
        code_ref[s, 1:2, :] = about[1:2]
    fill = pltpu.make_async_copy(code_ref, about_ref, sem)
    fill.start()
    for t in range(tiles):
        turned_ref[t] = model_ref[t].T
    grid_ref[...] = jnp.zeros_like(grid_ref)
    fill.wait()

    start = jnp.int32(0)
    for t in range(tiles):
        count = jnp.int32(0)
        for s in range(pairs):
            count = count + about_ref[s, 1, t]
        spare = -count & (UNROLL - 1)
        for u in range(UNROLL):
            list_ref[start + u] = (zero_row << PLANE_SHIFT) + (t << TILE_SHIFT) + capacity

        def enlist(s, filled, t=t):
            first = t // 2 * (capacity // 2)
            found = about_ref[s, 1, t]

            def some(turn, carry):
                for which in range(8):
                    k = turn * 8 + which
                    place = k if t % 2 == 0 else capacity // 2 - 1 - k
                    list_ref[filled + k] = about_ref[s, 0, jnp.maximum(first + place, 0)]
                return carry

            lax.fori_loop(0, (found + 7) >> 3, some, 0)
            return filled + found

        lax.fori_loop(0, pairs, enlist, start + spare)
        start = start + count + spare
    for u in range(2 * UNROLL):
        list_ref[start + u] = (zero_row << PLANE_SHIFT) + capacity
    chunks = start >> UNROLL.bit_length() - 1

    def read(which):
        entry = list_ref[which]
        slot = entry & ((1 << TILE_SHIFT) - 1)
        data = got_ref[slot]
        position = data.astype(jnp.int32)
        start, offset = position >> 3, (position & 7) << 4
        table = jnp.broadcast_to(table_ref[pl.ds(entry >> PLANE_SHIFT, 1), :], (8, 128))

        def parts(row):
            return spread_parts(
                jnp.broadcast_to(start[row : row + 1], (8, 128)),
                jnp.broadcast_to(offset[row : row + 1], (8, 128)),
                table,
            )

        return slot, data, parts

    def chunk_tile(turn):
        return (list_ref[turn * UNROLL] >> TILE_SHIFT) & 15

    def front(turn, row_ref, partial_ref):
        for u in range(UNROLL):
            _, _, parts = read(turn * UNROLL + u)
            taps, group = parts(2)
            for k in range(groups):
                row_ref[16 * k : 16 * k + 16, 128 * u : 128 * u + 128] = jnp.where(
                    group == k, taps, 0.0
                ).astype(jnp.bfloat16)
        partial_ref[...] = jnp.dot(
            turned_ref[chunk_tile(turn)], row_ref[...], preferred_element_type=jnp.float32
        )

    def back(turn, row_ref, partial_ref, weighted_ref):
        for u in range(UNROLL):
            slot, data, parts = read(turn * UNROLL + u)
            columns = slice(128 * u, 128 * u + 128)
            taps, group = parts(3)
            residuals, samples = [], []
            for part in range(2):
                picked = jnp.zeros((16, 128), jnp.float32)
                for k in range(groups):
                    low = part * side + 16 * k
                    picked = jnp.where(group == k, partial_ref[low : low + 16, columns], picked)
                model = jnp.sum(picked * taps, axis=0, keepdims=True)
                residual = data[part : part + 1] - model
                residuals.append(residual)
                samples.append(residual * taps)
            residual_ref[slot] = jnp.concatenate(residuals, axis=0).astype(jnp.bfloat16)
            for part in range(2):
                for k in range(groups):
                    low = part * side + 16 * k
                    weighted_ref[low : low + 16, columns] = jnp.where(
                        group == k, samples[part], 0.0
                    ).astype(jnp.bfloat16)
        grid_ref[chunk_tile(turn)] += lax.dot_general(
            row_ref[...],
            weighted_ref[...],
            (((1,), (1,)), ((), ())),
            preferred_element_type=jnp.float32,
        )

    def step(turn, carry):
        front(2 * turn + 1, row_b, partial_b)
        back(2 * turn, row_a, partial_a, weighted_a)
        front(2 * turn + 2, row_a, partial_a)
        back(2 * turn + 1, row_b, partial_b, weighted_b)
        return carry

    front(0, row_a, partial_a)
    lax.fori_loop(0, (chunks + 1) >> 1, step, 0)
    half = tiles // 2
    member = member_ref[0]
    for t in range(half):
        own_ref[t] = grid_ref[member * half + t]
        other_ref[t] = grid_ref[(1 - member) * half + t].astype(jnp.bfloat16)


def body(visibilities, uv_cell, sub_pixel, w_plane, block_tile, model_grid, kernel_table, coupling):
    owners = lax.axis_size("tile")
    pairs = owners // 2
    _, blocks, _, rows = visibilities.shape
    capacity = 2 * (3 * blocks // owners)
    _, tiles_here, side, wide = model_grid.shape
    planes, oversample, support = kernel_table.shape
    slots = pairs * (capacity + 1)
    member = lax.axis_index("tile") // pairs
    swap = [(t, (t + pairs) % owners) for t in range(owners)]
    halves = [list(range(pairs)), list(range(pairs, owners))]

    model_own = model_grid[0]
    model_other = lax.ppermute(model_own, "tile", swap)
    sent, slot = pl.pallas_call(
        lambda *refs: pack_kernel(pairs, capacity, tiles_here, planes, *refs),
        out_shape=(
            jax.ShapeDtypeStruct((slots, 4, rows), jnp.float32),
            jax.ShapeDtypeStruct((blocks,), jnp.int32),
        ),
        in_specs=[HBM] * 5,
        out_specs=(VMEM, SMEM),
        scratch_shapes=[
            pltpu.SMEM((blocks,), jnp.int32),
            pltpu.SMEM((blocks,), jnp.int32),
            pltpu.VMEM((blocks, 2, rows), jnp.float32),
            pltpu.VMEM((blocks, 2, rows), jnp.int32),
            pltpu.VMEM((blocks, 2, rows), jnp.int32),
            pltpu.SMEM((pairs, 4, rows), jnp.float32),
            pltpu.SMEM((pairs * 2 * tiles_here,), jnp.int32),
            pltpu.SemaphoreType.DMA((5,)),
            pltpu.SemaphoreType.DMA((pairs,)),
        ],
        compiler_params=WHOLE_PARAMS,
        name="pack_blocks",
    )(w_plane[0], block_tile[0], visibilities[0], uv_cell[0], sub_pixel[0])
    got = lax.all_to_all(
        sent, "tile", split_axis=0, concat_axis=0, tiled=True, axis_index_groups=halves
    )
    model = jnp.where(
        member == 0,
        jnp.concatenate([model_own, model_other]),
        jnp.concatenate([model_other, model_own]),
    )
    table = jnp.pad(
        kernel_table.astype(jnp.float32), ((0, 8), (0, 0), (0, 16 - support))
    ).reshape(planes + 8, 16 * oversample)
    residual, own, other = pl.pallas_call(
        lambda *refs: grid_kernel(pairs, capacity, *refs),
        out_shape=(
            jax.ShapeDtypeStruct((slots, 2, rows), jnp.bfloat16),
            jax.ShapeDtypeStruct((tiles_here, side, wide), jnp.float32),
            jax.ShapeDtypeStruct((tiles_here, side, wide), jnp.bfloat16),
        ),
        in_specs=[SMEM, VMEM, VMEM, VMEM],
        out_specs=(VMEM, VMEM, VMEM),
        scratch_shapes=[
            pltpu.VMEM((2 * tiles_here, wide, side), jnp.bfloat16),
            pltpu.VMEM((2 * tiles_here, side, wide), jnp.float32),
            pltpu.VMEM((side, UNROLL * rows), jnp.bfloat16),
            pltpu.VMEM((side, UNROLL * rows), jnp.bfloat16),
            pltpu.VMEM((wide, UNROLL * rows), jnp.float32),
            pltpu.VMEM((wide, UNROLL * rows), jnp.float32),
            pltpu.VMEM((wide, UNROLL * rows), jnp.bfloat16),
            pltpu.VMEM((wide, UNROLL * rows), jnp.bfloat16),
            pltpu.VMEM((pairs, 2, rows), jnp.int32),
            pltpu.SMEM((pairs, 2, rows), jnp.int32),
            pltpu.SMEM((slots + capacity + 2 * tiles_here * UNROLL + UNROLL,), jnp.int32),
            pltpu.SemaphoreType.DMA,
        ],
        compiler_params=PARAMS,
        name="grid_blocks",
    )(member[None], got, table, model)

    returned = lax.all_to_all(
        residual, "tile", split_axis=0, concat_axis=0, tiled=True, axis_index_groups=halves
    )
    grid_sum = own + lax.ppermute(other, "tile", swap).astype(jnp.float32)
    grids = lax.all_gather(grid_sum.astype(jnp.bfloat16)[None], "freq", axis=0, tiled=True)
    residuals, coupled_grid = pl.pallas_call(
        finish_kernel,
        out_shape=(
            jax.ShapeDtypeStruct((blocks, 2, rows), jnp.float32),
            jax.ShapeDtypeStruct((tiles_here, side, wide), jnp.float32),
        ),
        in_specs=[SMEM, SMEM, SMEM, VMEM, VMEM],
        out_specs=(VMEM, VMEM),
        compiler_params=PARAMS,
        name="finish",
    )(lax.axis_index("freq")[None], coupling, slot, returned, grids)
    return (residuals[None], coupled_grid[None])


def solution(mesh):
    return jax.shard_map(
        body,
        mesh=mesh,
        in_specs=(
            P("freq", "tile", None, None),
            P("freq", "tile", None, None),
            P("freq", "tile", None, None),
            P("freq", "tile"),
            P("freq", "tile"),
            P("freq", "tile", None, None),
            P(),
            P(),
        ),
        out_specs=(P("freq", "tile", None, None), P("freq", "tile", None, None)),
        check_vma=False,
    )
```

```python
import jax
import jax.numpy as jnp
from jax import lax
from jax.experimental import pallas as pl
from jax.experimental.pallas import tpu as pltpu
from jax.sharding import PartitionSpec as P

UNROLL = 2
CHUNKS = 8
AHEAD = 2
VMEM = pl.BlockSpec(memory_space=pltpu.VMEM)
SMEM = pl.BlockSpec(memory_space=pltpu.SMEM)
HBM = pl.BlockSpec(memory_space=pltpu.HBM)
PARAMS = pltpu.CompilerParams(vmem_limit_bytes=32 * 1024 * 1024)
WHOLE_PARAMS = pltpu.CompilerParams(vmem_limit_bytes=62 * 1024 * 1024)
TILE_SHIFT = 12
PLANE_SHIFT = 16


def scalar_div(value, count):
    shift = count.bit_length() - 1
    return value >> shift if count == 1 << shift else lax.div(value, count)


def first_slot(local, rank, capacity):
    half = capacity // 2
    return (local >> 1) * half + jnp.where((local & 1) == 0, rank, half - 1 - rank)


def pack_kernel(pairs, capacity, tiles_here, planes, plane_hbm, tile_hbm, vis_hbm, cell_hbm, sub_hbm,
                sent_ref, slot_ref, plane_ref, tile_ref, vis_ref, cell_ref, sub_ref, about_ref, count_ref,
                load_sem, about_sem):
    blocks = tile_ref.shape[0]
    loads = [
        pltpu.make_async_copy(source, target, load_sem.at[i])
        for i, (source, target) in enumerate(
            [
                (tile_hbm, tile_ref),
                (plane_hbm, plane_ref),
                (vis_hbm, vis_ref),
                (cell_hbm, cell_ref),
                (sub_hbm, sub_ref),
            ]
        )
    ]
    for copy in loads:
        copy.start()
    part = lax.broadcasted_iota(jnp.int32, (4, 128), 0)
    empty = jnp.where(part == 0, float(planes << PLANE_SHIFT), 0.0)
    abouts = [d * (capacity + 1) + capacity for d in range(pairs)]
    for d in range(pairs):
        sent_ref[abouts[d]] = empty
        for t in range(2 * tiles_here):
            count_ref[d * 2 * tiles_here + t] = 0
    fills = [
        pltpu.make_async_copy(sent_ref.at[abouts[d]], about_ref.at[d], about_sem.at[d])
        for d in range(pairs)
    ]
    for copy in fills:
        copy.start()
    for copy in fills + loads[:2]:
        copy.wait()

    def assign(b):
        tile = tile_ref[b]
        owner = scalar_div(tile, tiles_here)
        high = (owner >= pairs).astype(jnp.int32)
        pair = owner - high * pairs
        local = tile - (owner - high) * tiles_here
        key = pair * (2 * tiles_here) + local
        rank = count_ref[key]
        count_ref[key] = rank + 1
        place = first_slot(local, rank, capacity)
        slot_ref[b] = pair * (capacity + 1) + place
        code = (plane_ref[b] << PLANE_SHIFT) + (local << TILE_SHIFT)
        about_ref[pair, 0, place] = code.astype(jnp.float32)

    def move(b):
        position = (cell_ref[b] * 8 + sub_ref[b]).astype(jnp.float32)
        sent_ref[slot_ref[b]] = jnp.concatenate([vis_ref[b], position], axis=0)

    def each(work):
        def step(turn, carry):
            for which in range(8):
                work(turn * 8 + which)
            return carry

        lax.fori_loop(0, blocks // 8, step, 0)

    each(assign)
    for d in range(pairs):
        for t in range(2 * tiles_here):
            about_ref[d, 1, t] = count_ref[d * 2 * tiles_here + t].astype(jnp.float32)
    returns = [
        pltpu.make_async_copy(about_ref.at[d], sent_ref.at[abouts[d]], about_sem.at[d])
        for d in range(pairs)
    ]
    for copy in returns:
        copy.start()
    for copy in loads[2:]:
        copy.wait()
    each(move)
    for copy in returns:
        copy.wait()


def finish_kernel(plane_ref, coupling_ref, slot_ref, returned_ref, grid_ref, residual_ref, coupled_ref):
    coupled_ref[...] = sum(
        coupling_ref[plane_ref[0], g] * grid_ref[g].astype(jnp.float32)
        for g in range(grid_ref.shape[0])
    )

    def step(turn, carry):
        for which in range(8):
            b = turn * 8 + which
            residual_ref[b] = returned_ref[slot_ref[b]].astype(jnp.float32)
        return carry

    lax.fori_loop(0, residual_ref.shape[0] // 8, step, 0)


def spread_parts(start, offset, table):
    sublane = lax.broadcasted_iota(jnp.int32, (8, 128), 0)
    taps, group = [], []
    for low in (0, 8):
        delta = sublane + low - start
        taps.append(
            jnp.take_along_axis(table, (delta & 15) + offset, axis=1, mode="promise_in_bounds")
        )
        group.append((15 - delta) >> 4)
    return jnp.concatenate(taps, axis=0), jnp.concatenate(group, axis=0)


def grid_kernel(pairs, capacity, member_ref, got_ref, table_ref, model_ref, residual_ref, own_ref,
                other_ref, turned_ref, grid_ref, code_ref, about_ref, list_ref, sem, *buffers):
    row_refs, partial_refs, weighted_refs = buffers[:4], buffers[4:8], buffers[8:]
    tiles, side, wide = model_ref.shape
    groups = side // 16
    zero_row = table_ref.shape[0] - 8
    lane = lax.broadcasted_iota(jnp.int32, (1, 128), 1)
    for s in range(pairs):
        about = got_ref[s * (capacity + 1) + capacity].astype(jnp.int32)
        code_ref[s, 0:1, :] = about[0:1] + (lane + s * (capacity + 1))
        code_ref[s, 1:2, :] = about[1:2]
    fill = pltpu.make_async_copy(code_ref, about_ref, sem)
    fill.start()
    for t in range(tiles):
        turned_ref[t] = model_ref[t].T
    grid_ref[...] = jnp.zeros_like(grid_ref)
    fill.wait()

    start = jnp.int32(0)
    for t in range(tiles):
        count = jnp.int32(0)
        for s in range(pairs):
            count = count + about_ref[s, 1, t]
        spare = -count & (UNROLL - 1)
        for u in range(UNROLL):
            list_ref[start + u] = (zero_row << PLANE_SHIFT) + (t << TILE_SHIFT) + capacity

        def enlist(s, filled, t=t):
            first = t // 2 * (capacity // 2)
            found = about_ref[s, 1, t]

            def some(turn, carry):
                for which in range(8):
                    k = turn * 8 + which
                    place = k if t % 2 == 0 else capacity // 2 - 1 - k
                    list_ref[filled + k] = about_ref[s, 0, jnp.maximum(first + place, 0)]
                return carry

            lax.fori_loop(0, (found + 7) >> 3, some, 0)
            return filled + found

        lax.fori_loop(0, pairs, enlist, start + spare)
        start = start + count + spare
    for u in range((CHUNKS + AHEAD) * UNROLL):
        list_ref[start + u] = (zero_row << PLANE_SHIFT) + capacity
    chunks = start >> UNROLL.bit_length() - 1
    zero = jnp.zeros((16, 128), jnp.bfloat16)

    def read(which):
        entry = list_ref[which]
        slot = entry & ((1 << TILE_SHIFT) - 1)
        data = got_ref[slot]
        position = data.astype(jnp.int32)
        start, offset = position >> 3, (position & 7) << 4
        table = jnp.broadcast_to(table_ref[pl.ds(entry >> PLANE_SHIFT, 1), :], (8, 128))

        def parts(row):
            return spread_parts(
                jnp.broadcast_to(start[row : row + 1], (8, 128)),
                jnp.broadcast_to(offset[row : row + 1], (8, 128)),
                table,
            )

        return slot, data, parts

    def chunk_tile(turn):
        return (list_ref[turn * UNROLL] >> TILE_SHIFT) & 15

    def front(turn, which):
        row_ref, partial_ref = row_refs[which % len(row_refs)], partial_refs[which % len(partial_refs)]
        for u in range(UNROLL):
            _, _, parts = read(turn * UNROLL + u)
            taps, group = parts(2)
            taps = taps.astype(jnp.bfloat16)
            group = group.astype(jnp.float32).astype(jnp.bfloat16)
            for k in range(groups):
                row_ref[16 * k : 16 * k + 16, 128 * u : 128 * u + 128] = jnp.where(
                    group == k, taps, zero
                )
        partial_ref[...] = jnp.dot(
            turned_ref[chunk_tile(turn)], row_ref[...], preferred_element_type=jnp.float32
        )

    def back(turn, which):
        row_ref, partial_ref = row_refs[which % len(row_refs)], partial_refs[which % len(partial_refs)]
        weighted_ref = weighted_refs[which % len(weighted_refs)]
        for u in range(UNROLL):
            slot, data, parts = read(turn * UNROLL + u)
            columns = slice(128 * u, 128 * u + 128)
            taps, group = parts(3)
            residuals, samples = [], []
            for part in range(2):
                picked = jnp.zeros((16, 128), jnp.float32)
                for k in range(groups):
                    low = part * side + 16 * k
                    picked = jnp.where(group == k, partial_ref[low : low + 16, columns], picked)
                model = jnp.sum(picked * taps, axis=0, keepdims=True)
                residual = data[part : part + 1] - model
                residuals.append(residual)
                samples.append((residual * taps).astype(jnp.bfloat16))
            residual_ref[slot] = jnp.concatenate(residuals, axis=0).astype(jnp.bfloat16)
            group = group.astype(jnp.float32).astype(jnp.bfloat16)
            for part in range(2):
                for k in range(groups):
                    low = part * side + 16 * k
                    weighted_ref[low : low + 16, columns] = jnp.where(
                        group == k, samples[part], zero
                    )
        grid_ref[chunk_tile(turn)] += lax.dot_general(
            row_ref[...],
            weighted_ref[...],
            (((1,), (1,)), ((), ())),
            preferred_element_type=jnp.float32,
        )

    def step(turn, carry):
        for which in range(CHUNKS):
            front(turn * CHUNKS + which + AHEAD, which + AHEAD)
            back(turn * CHUNKS + which, which)
        return carry

    for which in range(AHEAD):
        front(which, which)
    lax.fori_loop(0, scalar_div(chunks + CHUNKS - 1, CHUNKS), step, 0)
    half = tiles // 2
    member = member_ref[0]
    for t in range(half):
        own_ref[t] = grid_ref[member * half + t]
        other_ref[t] = grid_ref[(1 - member) * half + t].astype(jnp.bfloat16)


def body(visibilities, uv_cell, sub_pixel, w_plane, block_tile, model_grid, kernel_table, coupling):
    owners = lax.axis_size("tile")
    pairs = owners // 2
    _, blocks, _, rows = visibilities.shape
    capacity = 2 * (3 * blocks // owners)
    _, tiles_here, side, wide = model_grid.shape
    planes, oversample, support = kernel_table.shape
    slots = pairs * (capacity + 1)
    member = lax.axis_index("tile") // pairs
    swap = [(t, (t + pairs) % owners) for t in range(owners)]
    halves = [list(range(pairs)), list(range(pairs, owners))]

    model_own = model_grid[0]
    model_other = lax.ppermute(model_own, "tile", swap)
    sent, slot = pl.pallas_call(
        lambda *refs: pack_kernel(pairs, capacity, tiles_here, planes, *refs),
        out_shape=(
            jax.ShapeDtypeStruct((slots, 4, rows), jnp.float32),
            jax.ShapeDtypeStruct((blocks,), jnp.int32),
        ),
        in_specs=[HBM] * 5,
        out_specs=(VMEM, SMEM),
        scratch_shapes=[
            pltpu.SMEM((blocks,), jnp.int32),
            pltpu.SMEM((blocks,), jnp.int32),
            pltpu.VMEM((blocks, 2, rows), jnp.float32),
            pltpu.VMEM((blocks, 2, rows), jnp.int32),
            pltpu.VMEM((blocks, 2, rows), jnp.int32),
            pltpu.SMEM((pairs, 4, rows), jnp.float32),
            pltpu.SMEM((pairs * 2 * tiles_here,), jnp.int32),
            pltpu.SemaphoreType.DMA((5,)),
            pltpu.SemaphoreType.DMA((pairs,)),
        ],
        compiler_params=WHOLE_PARAMS,
        name="pack_blocks",
    )(w_plane[0], block_tile[0], visibilities[0], uv_cell[0], sub_pixel[0])
    got = lax.all_to_all(
        sent, "tile", split_axis=0, concat_axis=0, tiled=True, axis_index_groups=halves
    )
    slot, got = lax.optimization_barrier((slot + lax.div(lax.axis_index("tile"), owners), got))
    model = jnp.where(
        member == 0,
        jnp.concatenate([model_own, model_other]),
        jnp.concatenate([model_other, model_own]),
    )
    table = jnp.pad(
        kernel_table.astype(jnp.float32), ((0, 8), (0, 0), (0, 16 - support))
    ).reshape(planes + 8, 16 * oversample)
    residual, own, other = pl.pallas_call(
        lambda *refs: grid_kernel(pairs, capacity, *refs),
        out_shape=(
            jax.ShapeDtypeStruct((slots, 2, rows), jnp.bfloat16),
            jax.ShapeDtypeStruct((tiles_here, side, wide), jnp.float32),
            jax.ShapeDtypeStruct((tiles_here, side, wide), jnp.bfloat16),
        ),
        in_specs=[SMEM, VMEM, VMEM, VMEM],
        out_specs=(VMEM, VMEM, VMEM),
        scratch_shapes=[
            pltpu.VMEM((2 * tiles_here, wide, side), jnp.bfloat16),
            pltpu.VMEM((2 * tiles_here, side, wide), jnp.float32),
            pltpu.VMEM((pairs, 2, rows), jnp.int32),
            pltpu.SMEM((pairs, 2, rows), jnp.int32),
            pltpu.SMEM(
                (slots + capacity + (2 * tiles_here + CHUNKS + AHEAD) * UNROLL,), jnp.int32
            ),
            pltpu.SemaphoreType.DMA,
            *[pltpu.VMEM((side, UNROLL * rows), jnp.bfloat16)] * 4,
            *[pltpu.VMEM((wide, UNROLL * rows), jnp.float32)] * 4,
            *[pltpu.VMEM((wide, UNROLL * rows), jnp.bfloat16)] * 2,
        ],
        compiler_params=PARAMS,
        name="grid_blocks",
    )(member[None], got, table, model)

    returned = lax.all_to_all(
        residual, "tile", split_axis=0, concat_axis=0, tiled=True, axis_index_groups=halves
    )
    grid_sum = own + lax.ppermute(other, "tile", swap).astype(jnp.float32)
    grids = lax.all_gather(grid_sum.astype(jnp.bfloat16)[None], "freq", axis=0, tiled=True)
    residuals, coupled_grid = pl.pallas_call(
        finish_kernel,
        out_shape=(
            jax.ShapeDtypeStruct((blocks, 2, rows), jnp.float32),
            jax.ShapeDtypeStruct((tiles_here, side, wide), jnp.float32),
        ),
        in_specs=[SMEM, SMEM, SMEM, VMEM, VMEM],
        out_specs=(VMEM, VMEM),
        compiler_params=PARAMS,
        name="finish",
    )(lax.axis_index("freq")[None], coupling, slot, returned, grids)
    return (residuals[None], coupled_grid[None])


def solution(mesh):
    return jax.shard_map(
        body,
        mesh=mesh,
        in_specs=(
            P("freq", "tile", None, None),
            P("freq", "tile", None, None),
            P("freq", "tile", None, None),
            P("freq", "tile"),
            P("freq", "tile"),
            P("freq", "tile", None, None),
            P(),
            P(),
        ),
        out_specs=(P("freq", "tile", None, None), P("freq", "tile", None, None)),
        check_vma=False,
    )
```

```python
import jax
import jax.numpy as jnp
from jax import lax
from jax.experimental import pallas as pl
from jax.experimental.pallas import tpu as pltpu
from jax.sharding import PartitionSpec as P

UNROLL = 2
CHUNKS = 8
AHEAD = 2
VMEM = pl.BlockSpec(memory_space=pltpu.VMEM)
SMEM = pl.BlockSpec(memory_space=pltpu.SMEM)
HBM = pl.BlockSpec(memory_space=pltpu.HBM)
PARAMS = pltpu.CompilerParams(vmem_limit_bytes=32 * 1024 * 1024)
WHOLE_PARAMS = pltpu.CompilerParams(vmem_limit_bytes=62 * 1024 * 1024)
TILE_SHIFT = 12
PLANE_SHIFT = 16
SOURCE_SHIFT = 21


def scalar_div(value, count):
    shift = count.bit_length() - 1
    return value >> shift if count == 1 << shift else lax.div(value, count)


def pack_kernel(pairs, capacity, tiles_here, plane_hbm, tile_hbm, vis_hbm, cell_hbm, sub_hbm,
                first_hbm, last_hbm, slot_ref, plane_ref, tile_ref, vis_ref, cell_ref, sub_ref, sent_ref,
                about_ref, turned_ref, count_ref, load_sem, about_sem, sent_sem):
    blocks = tile_ref.shape[0]
    half = capacity // 2
    stride = 2 * half + 1
    loads = [
        pltpu.make_async_copy(source, target, load_sem.at[i])
        for i, (source, target) in enumerate(
            [
                (tile_hbm, tile_ref),
                (plane_hbm, plane_ref),
                (vis_hbm, vis_ref),
                (cell_hbm, cell_ref),
                (sub_hbm, sub_ref),
            ]
        )
    ]
    for copy in loads:
        copy.start()
    for d in range(pairs):
        for t in range(2 * tiles_here):
            count_ref[d * 2 * tiles_here + t] = 0
        for k in range(2 * half):
            about_ref[2 * d, 0, k] = 0.0
            about_ref[2 * d + 1, 0, k] = 0.0
    for copy in loads[:2]:
        copy.wait()

    def assign(b):
        tile = tile_ref[b]
        owner = scalar_div(tile, tiles_here)
        high = (owner >= pairs).astype(jnp.int32)
        pair = owner - high * pairs
        local = tile - (owner - high) * tiles_here
        key = pair * (2 * tiles_here) + local
        rank = count_ref[key]
        count_ref[key] = rank + 1
        place = jnp.where((local & 1) == 0, rank, capacity - 1 - rank)
        last = (place >= half).astype(jnp.int32)
        lane = place - last * half + (local >> 1) * half
        target = 2 * pair + last
        slot_ref[b] = target * stride + lane
        about_ref[target, 0, lane] = (plane_ref[b] << PLANE_SHIFT).astype(jnp.float32)

    def move(b):
        position = (cell_ref[b] * 8 + sub_ref[b]).astype(jnp.float32)
        sent_ref[slot_ref[b]] = jnp.concatenate([vis_ref[b], position], axis=0)

    def each(work):
        def step(turn, carry):
            for which in range(8):
                work(turn * 8 + which)
            return carry

        lax.fori_loop(0, blocks // 8, step, 0)

    each(assign)
    for d in range(pairs):
        for t in range(2 * tiles_here):
            count = count_ref[d * 2 * tiles_here + t]
            near, far = jnp.minimum(count, half), jnp.maximum(count - half, 0)
            about_ref[2 * d, 1, t] = (near if t % 2 == 0 else far).astype(jnp.float32)
            about_ref[2 * d + 1, 1, t] = (far if t % 2 == 0 else near).astype(jnp.float32)
    turn_about = pltpu.make_async_copy(about_ref, turned_ref, about_sem)
    turn_about.start()
    for copy in loads[2:]:
        copy.wait()
    each(move)
    turn_about.wait()
    part = lax.broadcasted_iota(jnp.int32, (4, 128), 0)
    lane = lax.broadcasted_iota(jnp.int32, (4, 128), 1)
    filled = ((part == 0) & (lane < 2 * half)) | ((part == 1) & (lane < 2 * tiles_here))
    for d in range(2 * pairs):
        sent_ref[d * stride + 2 * half] = jnp.where(filled, turned_ref[d], 0.0)
    stores = [
        pltpu.make_async_copy(
            sent_ref.at[pl.ds((2 * d + last) * stride, stride)],
            target.at[pl.ds(d * stride, stride)],
            sent_sem.at[2 * d + last],
        )
        for last, target in enumerate([first_hbm, last_hbm])
        for d in range(pairs)
    ]
    for copy in stores:
        copy.start()
    for copy in stores:
        copy.wait()


def finish_kernel(row_ref, slot_ref, returned_ref, grid_ref, residual_ref, coupled_ref):
    coupled_ref[...] = sum(
        row_ref[g] * grid_ref[g].astype(jnp.float32) for g in range(grid_ref.shape[0])
    )

    def step(turn, carry):
        for which in range(8):
            b = turn * 8 + which
            residual_ref[b] = returned_ref[slot_ref[b]].astype(jnp.float32)
        return carry

    lax.fori_loop(0, residual_ref.shape[0] // 8, step, 0)


def spread_parts(start, offset, table):
    sublane = lax.broadcasted_iota(jnp.int32, (8, 128), 0)
    taps, group = [], []
    for low in (0, 8):
        delta = sublane + low - start
        taps.append(
            jnp.take_along_axis(table, (delta & 15) + offset, axis=1, mode="promise_in_bounds")
        )
        group.append((15 - delta) >> 4)
    return jnp.concatenate(taps, axis=0), jnp.concatenate(group, axis=0)


def grid_kernel(pairs, half, first, *refs):
    if first:
        got_ref, table_ref, model_ref, residual_ref, turned_ref, grid_ref, *scratch = refs
    else:
        (member_ref, got_ref, table_ref, turned_ref, before_ref, earlier_ref, residual_ref, own_ref,
         other_ref, grid_ref, *scratch) = refs
    code_ref, about_ref, list_ref, sem, *buffers = scratch
    row_refs, partial_refs, weighted_refs = buffers[:4], buffers[4:8], buffers[8:]
    tiles, wide, side = turned_ref.shape
    groups = side // 16
    stride = 2 * half + 1
    zero_row = table_ref.shape[0] - 8
    lane = lax.broadcasted_iota(jnp.int32, (1, 128), 1)
    for s in range(pairs):
        about = got_ref[s * stride + 2 * half].astype(jnp.int32)
        code_ref[s, 0:1, :] = about[0:1] + (lane + (s * stride + (s << SOURCE_SHIFT)))
        code_ref[s, 1:2, :] = about[1:2]
    fill = pltpu.make_async_copy(code_ref, about_ref, sem)
    fill.start()
    if first:
        for t in range(tiles):
            turned_ref[t] = model_ref[t].T
        grid_ref[...] = jnp.zeros_like(grid_ref)
    else:
        grid_ref[...] = before_ref[...]
        for s in range(pairs):
            residual_ref[pl.ds(2 * s * stride, stride)] = earlier_ref[pl.ds(s * stride, stride)]
    fill.wait()

    start = jnp.int32(0)
    for t in range(tiles):
        count = jnp.int32(0)
        for s in range(pairs):
            count = count + about_ref[s, 1, t]
        spare = -count & (UNROLL - 1)
        for u in range(UNROLL):
            list_ref[start + u] = (zero_row << PLANE_SHIFT) + (t << TILE_SHIFT) + 2 * half

        def enlist(s, filled, t=t):
            base = t // 2 * half
            found = about_ref[s, 1, t]

            def some(turn, carry):
                for which in range(8):
                    k = turn * 8 + which
                    place = k if t % 2 == 0 else half - 1 - k
                    code = about_ref[s, 0, jnp.maximum(base + place, 0)]
                    list_ref[filled + k] = code + (t << TILE_SHIFT)
                return carry

            lax.fori_loop(0, (found + 7) >> 3, some, 0)
            return filled + found

        lax.fori_loop(0, pairs, enlist, start + spare)
        start = start + count + spare
    for u in range((CHUNKS + AHEAD) * UNROLL):
        list_ref[start + u] = (zero_row << PLANE_SHIFT) + 2 * half
    chunks = start >> UNROLL.bit_length() - 1
    zero = jnp.zeros((16, 128), jnp.bfloat16)

    def read(which):
        entry = list_ref[which]
        slot = entry & ((1 << TILE_SHIFT) - 1)
        data = got_ref[slot]
        position = data.astype(jnp.int32)
        start, offset = position >> 3, (position & 7) << 4
        plane = (entry >> PLANE_SHIFT) & ((1 << (SOURCE_SHIFT - PLANE_SHIFT)) - 1)
        table = jnp.broadcast_to(table_ref[pl.ds(plane, 1), :], (8, 128))

        def parts(row):
            return spread_parts(
                jnp.broadcast_to(start[row : row + 1], (8, 128)),
                jnp.broadcast_to(offset[row : row + 1], (8, 128)),
                table,
            )

        place = slot if first else slot + ((entry >> SOURCE_SHIFT) + 1) * stride
        return place, data, parts

    def chunk_tile(turn):
        return (list_ref[turn * UNROLL] >> TILE_SHIFT) & 15

    def front(turn, which):
        row_ref, partial_ref = row_refs[which % len(row_refs)], partial_refs[which % len(partial_refs)]
        for u in range(UNROLL):
            _, _, parts = read(turn * UNROLL + u)
            taps, group = parts(2)
            taps = taps.astype(jnp.bfloat16)
            group = group.astype(jnp.float32).astype(jnp.bfloat16)
            for k in range(groups):
                row_ref[16 * k : 16 * k + 16, 128 * u : 128 * u + 128] = jnp.where(
                    group == k, taps, zero
                )
        partial_ref[...] = jnp.dot(
            turned_ref[chunk_tile(turn)], row_ref[...], preferred_element_type=jnp.float32
        )

    def back(turn, which):
        row_ref, partial_ref = row_refs[which % len(row_refs)], partial_refs[which % len(partial_refs)]
        weighted_ref = weighted_refs[which % len(weighted_refs)]
        for u in range(UNROLL):
            place, data, parts = read(turn * UNROLL + u)
            columns = slice(128 * u, 128 * u + 128)
            taps, group = parts(3)
            residuals, samples = [], []
            for part in range(2):
                picked = jnp.zeros((16, 128), jnp.float32)
                for k in range(groups):
                    low = part * side + 16 * k
                    picked = jnp.where(group == k, partial_ref[low : low + 16, columns], picked)
                model = jnp.sum(picked * taps, axis=0, keepdims=True)
                residual = data[part : part + 1] - model
                residuals.append(residual)
                samples.append((residual * taps).astype(jnp.bfloat16))
            residual_ref[place] = jnp.concatenate(residuals, axis=0).astype(jnp.bfloat16)
            group = group.astype(jnp.float32).astype(jnp.bfloat16)
            for part in range(2):
                for k in range(groups):
                    low = part * side + 16 * k
                    weighted_ref[low : low + 16, columns] = jnp.where(
                        group == k, samples[part], zero
                    )
        grid_ref[chunk_tile(turn)] += lax.dot_general(
            row_ref[...],
            weighted_ref[...],
            (((1,), (1,)), ((), ())),
            preferred_element_type=jnp.float32,
        )

    def step(turn, carry):
        for which in range(CHUNKS):
            front(turn * CHUNKS + which + AHEAD, which + AHEAD)
            back(turn * CHUNKS + which, which)
        return carry

    for which in range(AHEAD):
        front(which, which)
    lax.fori_loop(0, scalar_div(chunks + CHUNKS - 1, CHUNKS), step, 0)
    if not first:
        here = tiles // 2
        member = member_ref[0]
        for t in range(here):
            own_ref[t] = grid_ref[member * here + t]
            other_ref[t] = grid_ref[(1 - member) * here + t].astype(jnp.bfloat16)


def body(visibilities, uv_cell, sub_pixel, w_plane, block_tile, model_grid, kernel_table, coupling):
    owners = lax.axis_size("tile")
    pairs = owners // 2
    _, blocks, _, rows = visibilities.shape
    capacity = 3 * blocks // owners
    half = capacity // 2
    _, tiles_here, side, wide = model_grid.shape
    planes, oversample, support = kernel_table.shape
    slots = pairs * (2 * half + 1)
    tiles = 2 * tiles_here
    member = lax.axis_index("tile") // pairs
    swap = [(t, (t + pairs) % owners) for t in range(owners)]
    halves = [list(range(pairs)), list(range(pairs, owners))]

    def exchange(values):
        return lax.all_to_all(
            values, "tile", split_axis=0, concat_axis=0, tiled=True, axis_index_groups=halves
        )

    model_own = model_grid[0]
    model_other = lax.ppermute(model_own, "tile", swap)
    sent_first, sent_last, slot = pl.pallas_call(
        lambda *refs: pack_kernel(pairs, capacity, tiles_here, *refs),
        out_shape=(
            jax.ShapeDtypeStruct((slots, 4, rows), jnp.float32),
            jax.ShapeDtypeStruct((slots, 4, rows), jnp.float32),
            jax.ShapeDtypeStruct((blocks,), jnp.int32),
        ),
        in_specs=[HBM] * 5,
        out_specs=(HBM, HBM, SMEM),
        scratch_shapes=[
            pltpu.SMEM((blocks,), jnp.int32),
            pltpu.SMEM((blocks,), jnp.int32),
            pltpu.VMEM((blocks, 2, rows), jnp.float32),
            pltpu.VMEM((blocks, 2, rows), jnp.int32),
            pltpu.VMEM((blocks, 2, rows), jnp.int32),
            pltpu.VMEM((2 * slots, 4, rows), jnp.float32),
            pltpu.SMEM((2 * pairs, 4, rows), jnp.float32),
            pltpu.VMEM((2 * pairs, 4, rows), jnp.float32),
            pltpu.SMEM((pairs * tiles,), jnp.int32),
            pltpu.SemaphoreType.DMA((5,)),
            pltpu.SemaphoreType.DMA,
            pltpu.SemaphoreType.DMA((2 * pairs,)),
        ],
        compiler_params=WHOLE_PARAMS,
        name="pack_blocks",
    )(w_plane[0], block_tile[0], visibilities[0], uv_cell[0], sub_pixel[0])
    got_first = exchange(sent_first)
    got_last = exchange(sent_last)
    own_row = lax.dynamic_index_in_dim(coupling, lax.axis_index("freq"), 0, keepdims=False)
    slot, own_row, got_first = lax.optimization_barrier(
        (slot + lax.div(lax.axis_index("tile"), owners), own_row, got_first)
    )
    model = jnp.where(
        member == 0,
        jnp.concatenate([model_own, model_other]),
        jnp.concatenate([model_other, model_own]),
    )
    table = jnp.pad(
        kernel_table.astype(jnp.float32), ((0, 8), (0, 0), (0, 16 - support))
    ).reshape(planes + 8, 16 * oversample)

    def grid_blocks(first, out_shape, *operands):
        return pl.pallas_call(
            lambda *refs: grid_kernel(pairs, half, first, *refs),
            out_shape=out_shape,
            in_specs=[VMEM] * len(operands) if first else [SMEM] + [VMEM] * (len(operands) - 1),
            out_specs=tuple([VMEM] * len(out_shape)),
            scratch_shapes=([] if first else [pltpu.VMEM((tiles, side, wide), jnp.float32)])
            + [
                pltpu.VMEM((pairs, 2, rows), jnp.int32),
                pltpu.SMEM((pairs, 2, rows), jnp.int32),
                pltpu.SMEM((slots + capacity + (tiles + CHUNKS + AHEAD) * UNROLL,), jnp.int32),
                pltpu.SemaphoreType.DMA,
                *[pltpu.VMEM((side, UNROLL * rows), jnp.bfloat16)] * 4,
                *[pltpu.VMEM((wide, UNROLL * rows), jnp.float32)] * 4,
                *[pltpu.VMEM((wide, UNROLL * rows), jnp.bfloat16)] * 2,
            ],
            compiler_params=PARAMS,
            cost_estimate=pl.CostEstimate(
                flops=10**10, bytes_accessed=4 * 10**6, transcendentals=0
            ),
            name="grid_first" if first else "grid_last",
        )(*operands)

    residual, turned, grid = grid_blocks(
        True,
        (
            jax.ShapeDtypeStruct((slots, 2, rows), jnp.bfloat16),
            jax.ShapeDtypeStruct((tiles, wide, side), jnp.bfloat16),
            jax.ShapeDtypeStruct((tiles, side, wide), jnp.float32),
        ),
        got_first,
        table,
        model,
    )
    residual, own, other = grid_blocks(
        False,
        (
            jax.ShapeDtypeStruct((2 * slots, 2, rows), jnp.bfloat16),
            jax.ShapeDtypeStruct((tiles_here, side, wide), jnp.float32),
            jax.ShapeDtypeStruct((tiles_here, side, wide), jnp.bfloat16),
        ),
        member[None],
        got_last,
        table,
        turned,
        grid,
        residual,
    )

    returned = exchange(residual)
    grid_sum = own + lax.ppermute(other, "tile", swap).astype(jnp.float32)
    grids = lax.all_gather(grid_sum.astype(jnp.bfloat16)[None], "freq", axis=0, tiled=True)
    residuals, coupled_grid = pl.pallas_call(
        finish_kernel,
        out_shape=(
            jax.ShapeDtypeStruct((blocks, 2, rows), jnp.float32),
            jax.ShapeDtypeStruct((tiles_here, side, wide), jnp.float32),
        ),
        in_specs=[SMEM, SMEM, VMEM, VMEM],
        out_specs=(VMEM, VMEM),
        compiler_params=PARAMS,
        name="finish",
    )(own_row, slot, returned, grids)
    return (residuals[None], coupled_grid[None])


def solution(mesh):
    return jax.shard_map(
        body,
        mesh=mesh,
        in_specs=(
            P("freq", "tile", None, None),
            P("freq", "tile", None, None),
            P("freq", "tile", None, None),
            P("freq", "tile"),
            P("freq", "tile"),
            P("freq", "tile", None, None),
            P(),
            P(),
        ),
        out_specs=(P("freq", "tile", None, None), P("freq", "tile", None, None)),
        check_vma=False,
    )
```

```python
import jax
import jax.numpy as jnp
from jax import lax
from jax.experimental import pallas as pl
from jax.experimental.pallas import tpu as pltpu
from jax.sharding import PartitionSpec as P

UNROLL = 2
CHUNKS = 8
AHEAD = 2
VMEM = pl.BlockSpec(memory_space=pltpu.VMEM)
SMEM = pl.BlockSpec(memory_space=pltpu.SMEM)
HBM = pl.BlockSpec(memory_space=pltpu.HBM)
PARAMS = pltpu.CompilerParams(vmem_limit_bytes=32 * 1024 * 1024)
WHOLE_PARAMS = pltpu.CompilerParams(vmem_limit_bytes=62 * 1024 * 1024)
TILE_SHIFT = 12
PLANE_SHIFT = 16


def scalar_div(value, count):
    shift = count.bit_length() - 1
    return value >> shift if count == 1 << shift else lax.div(value, count)


def first_slot(local, rank, capacity):
    half = capacity // 2
    return (local >> 1) * half + jnp.where((local & 1) == 0, rank, half - 1 - rank)


def pack_kernel(pairs, capacity, tiles_here, planes, plane_hbm, tile_hbm, vis_hbm, cell_hbm, sub_hbm,
                sent_ref, slot_ref, plane_ref, tile_ref, vis_ref, cell_ref, sub_ref, about_ref, count_ref,
                load_sem, about_sem):
    blocks = tile_ref.shape[0]
    loads = [
        pltpu.make_async_copy(source, target, load_sem.at[i])
        for i, (source, target) in enumerate(
            [
                (tile_hbm, tile_ref),
                (plane_hbm, plane_ref),
                (vis_hbm, vis_ref),
                (cell_hbm, cell_ref),
                (sub_hbm, sub_ref),
            ]
        )
    ]
    for copy in loads:
        copy.start()
    part = lax.broadcasted_iota(jnp.int32, (4, 128), 0)
    empty = jnp.where(part == 0, float(planes << PLANE_SHIFT), 0.0)
    abouts = [d * (capacity + 1) + capacity for d in range(pairs)]
    for d in range(pairs):
        sent_ref[abouts[d]] = empty
        for t in range(2 * tiles_here):
            count_ref[d * 2 * tiles_here + t] = 0
    fills = [
        pltpu.make_async_copy(sent_ref.at[abouts[d]], about_ref.at[d], about_sem.at[d])
        for d in range(pairs)
    ]
    for copy in fills:
        copy.start()
    for copy in fills + loads[:2]:
        copy.wait()

    def assign(b):
        tile = tile_ref[b]
        owner = scalar_div(tile, tiles_here)
        high = (owner >= pairs).astype(jnp.int32)
        pair = owner - high * pairs
        local = tile - (owner - high) * tiles_here
        key = pair * (2 * tiles_here) + local
        rank = count_ref[key]
        count_ref[key] = rank + 1
        place = first_slot(local, rank, capacity)
        slot_ref[b] = pair * (capacity + 1) + place
        code = (plane_ref[b] << PLANE_SHIFT) + (local << TILE_SHIFT)
        about_ref[pair, 0, place] = code.astype(jnp.float32)

    def move(b):
        position = (cell_ref[b] * 8 + sub_ref[b]).astype(jnp.float32)
        sent_ref[slot_ref[b]] = jnp.concatenate([vis_ref[b], position], axis=0)

    def each(work):
        def step(turn, carry):
            for which in range(8):
                work(turn * 8 + which)
            return carry

        lax.fori_loop(0, blocks // 8, step, 0)

    each(assign)
    for d in range(pairs):
        for t in range(2 * tiles_here):
            about_ref[d, 1, t] = count_ref[d * 2 * tiles_here + t].astype(jnp.float32)
    returns = [
        pltpu.make_async_copy(about_ref.at[d], sent_ref.at[abouts[d]], about_sem.at[d])
        for d in range(pairs)
    ]
    for copy in returns:
        copy.start()
    for copy in loads[2:]:
        copy.wait()
    each(move)
    for copy in returns:
        copy.wait()


def finish_kernel(row_ref, slot_ref, returned_ref, grid_ref, residual_ref, coupled_ref):
    coupled_ref[...] = sum(
        row_ref[g] * grid_ref[g].astype(jnp.float32) for g in range(grid_ref.shape[0])
    )

    def step(turn, carry):
        for which in range(8):
            b = turn * 8 + which
            residual_ref[b] = returned_ref[slot_ref[b]].astype(jnp.float32)
        return carry

    lax.fori_loop(0, residual_ref.shape[0] // 8, step, 0)


def spread_parts(start, offset, table):
    sublane = lax.broadcasted_iota(jnp.int32, (8, 128), 0)
    taps, group = [], []
    for low in (0, 8):
        delta = sublane + low - start
        taps.append(
            jnp.take_along_axis(table, (delta & 15) + offset, axis=1, mode="promise_in_bounds")
        )
        group.append((15 - delta) >> 4)
    return jnp.concatenate(taps, axis=0), jnp.concatenate(group, axis=0)


def grid_kernel(pairs, capacity, member_ref, got_ref, table_ref, model_ref, residual_ref, own_ref,
                other_ref, turned_ref, grid_ref, code_ref, about_ref, list_ref, sem, *buffers):
    row_refs, partial_refs, weighted_refs = buffers[:4], buffers[4:8], buffers[8:]
    tiles, side, wide = model_ref.shape
    groups = side // 16
    zero_row = table_ref.shape[0] - 8
    lane = lax.broadcasted_iota(jnp.int32, (1, 128), 1)
    for s in range(pairs):
        about = got_ref[s * (capacity + 1) + capacity].astype(jnp.int32)
        code_ref[s, 0:1, :] = about[0:1] + (lane + s * (capacity + 1))
        code_ref[s, 1:2, :] = about[1:2]
    fill = pltpu.make_async_copy(code_ref, about_ref, sem)
    fill.start()
    for t in range(tiles):
        turned_ref[t] = model_ref[t].T
    grid_ref[...] = jnp.zeros_like(grid_ref)
    fill.wait()

    start = jnp.int32(0)
    for t in range(tiles):
        count = jnp.int32(0)
        for s in range(pairs):
            count = count + about_ref[s, 1, t]
        spare = -count & (UNROLL - 1)
        for u in range(UNROLL):
            list_ref[start + u] = (zero_row << PLANE_SHIFT) + (t << TILE_SHIFT) + capacity

        def enlist(s, filled, t=t):
            first = t // 2 * (capacity // 2)
            found = about_ref[s, 1, t]

            def some(turn, carry):
                for which in range(8):
                    k = turn * 8 + which
                    place = k if t % 2 == 0 else capacity // 2 - 1 - k
                    list_ref[filled + k] = about_ref[s, 0, jnp.maximum(first + place, 0)]
                return carry

            lax.fori_loop(0, (found + 7) >> 3, some, 0)
            return filled + found

        lax.fori_loop(0, pairs, enlist, start + spare)
        start = start + count + spare
    for u in range((CHUNKS + AHEAD) * UNROLL):
        list_ref[start + u] = (zero_row << PLANE_SHIFT) + capacity
    chunks = start >> UNROLL.bit_length() - 1
    zero = jnp.zeros((16, 128), jnp.bfloat16)

    def read(which):
        entry = list_ref[which]
        slot = entry & ((1 << TILE_SHIFT) - 1)
        data = got_ref[slot]
        position = data.astype(jnp.int32)
        start, offset = position >> 3, (position & 7) << 4
        table = jnp.broadcast_to(table_ref[pl.ds(entry >> PLANE_SHIFT, 1), :], (8, 128))

        def parts(row):
            return spread_parts(
                jnp.broadcast_to(start[row : row + 1], (8, 128)),
                jnp.broadcast_to(offset[row : row + 1], (8, 128)),
                table,
            )

        return slot, data, parts

    def chunk_tile(turn):
        return (list_ref[turn * UNROLL] >> TILE_SHIFT) & 15

    def front(turn, which):
        row_ref, partial_ref = row_refs[which % len(row_refs)], partial_refs[which % len(partial_refs)]
        for u in range(UNROLL):
            _, _, parts = read(turn * UNROLL + u)
            taps, group = parts(2)
            taps = taps.astype(jnp.bfloat16)
            group = group.astype(jnp.float32).astype(jnp.bfloat16)
            for k in range(groups):
                row_ref[16 * k : 16 * k + 16, 128 * u : 128 * u + 128] = jnp.where(
                    group == k, taps, zero
                )
        partial_ref[...] = jnp.dot(
            turned_ref[chunk_tile(turn)], row_ref[...], preferred_element_type=jnp.float32
        )

    def back(turn, which):
        row_ref, partial_ref = row_refs[which % len(row_refs)], partial_refs[which % len(partial_refs)]
        weighted_ref = weighted_refs[which % len(weighted_refs)]
        for u in range(UNROLL):
            slot, data, parts = read(turn * UNROLL + u)
            columns = slice(128 * u, 128 * u + 128)
            taps, group = parts(3)
            residuals, samples = [], []
            for part in range(2):
                picked = jnp.zeros((16, 128), jnp.float32)
                for k in range(groups):
                    low = part * side + 16 * k
                    picked = jnp.where(group == k, partial_ref[low : low + 16, columns], picked)
                model = jnp.sum(picked * taps, axis=0, keepdims=True)
                residual = data[part : part + 1] - model
                residuals.append(residual)
                samples.append((residual * taps).astype(jnp.bfloat16))
            residual_ref[slot] = jnp.concatenate(residuals, axis=0).astype(jnp.bfloat16)
            group = group.astype(jnp.float32).astype(jnp.bfloat16)
            for part in range(2):
                for k in range(groups):
                    low = part * side + 16 * k
                    weighted_ref[low : low + 16, columns] = jnp.where(
                        group == k, samples[part], zero
                    )
        grid_ref[chunk_tile(turn)] += lax.dot_general(
            row_ref[...],
            weighted_ref[...],
            (((1,), (1,)), ((), ())),
            preferred_element_type=jnp.float32,
        )

    def step(turn, carry):
        for which in range(CHUNKS):
            front(turn * CHUNKS + which + AHEAD, which + AHEAD)
            back(turn * CHUNKS + which, which)
        return carry

    for which in range(AHEAD):
        front(which, which)
    lax.fori_loop(0, scalar_div(chunks + CHUNKS - 1, CHUNKS), step, 0)
    half = tiles // 2
    member = member_ref[0]
    for t in range(half):
        own_ref[t] = grid_ref[member * half + t]
        other_ref[t] = grid_ref[(1 - member) * half + t].astype(jnp.bfloat16)


def body(visibilities, uv_cell, sub_pixel, w_plane, block_tile, model_grid, kernel_table, coupling):
    owners = lax.axis_size("tile")
    pairs = owners // 2
    _, blocks, _, rows = visibilities.shape
    capacity = 2 * (3 * blocks // owners)
    _, tiles_here, side, wide = model_grid.shape
    planes, oversample, support = kernel_table.shape
    slots = pairs * (capacity + 1)
    member = lax.axis_index("tile") // pairs
    swap = [(t, (t + pairs) % owners) for t in range(owners)]
    halves = [list(range(pairs)), list(range(pairs, owners))]

    model = lax.all_gather(
        model_grid[0],
        "tile",
        axis=0,
        tiled=True,
        axis_index_groups=[[t, t + pairs] for t in range(pairs)],
    )
    sent, slot = pl.pallas_call(
        lambda *refs: pack_kernel(pairs, capacity, tiles_here, planes, *refs),
        out_shape=(
            jax.ShapeDtypeStruct((slots, 4, rows), jnp.float32),
            jax.ShapeDtypeStruct((blocks,), jnp.int32),
        ),
        in_specs=[HBM] * 5,
        out_specs=(VMEM, SMEM),
        scratch_shapes=[
            pltpu.SMEM((blocks,), jnp.int32),
            pltpu.SMEM((blocks,), jnp.int32),
            pltpu.VMEM((blocks, 2, rows), jnp.float32),
            pltpu.VMEM((blocks, 2, rows), jnp.int32),
            pltpu.VMEM((blocks, 2, rows), jnp.int32),
            pltpu.SMEM((pairs, 4, rows), jnp.float32),
            pltpu.SMEM((pairs * 2 * tiles_here,), jnp.int32),
            pltpu.SemaphoreType.DMA((5,)),
            pltpu.SemaphoreType.DMA((pairs,)),
        ],
        compiler_params=WHOLE_PARAMS,
        name="pack_blocks",
    )(w_plane[0], block_tile[0], visibilities[0], uv_cell[0], sub_pixel[0])
    got = lax.all_to_all(
        sent, "tile", split_axis=0, concat_axis=0, tiled=True, axis_index_groups=halves
    )
    own_row = lax.dynamic_index_in_dim(coupling, lax.axis_index("freq"), 0, keepdims=False)
    slot, own_row, got = lax.optimization_barrier(
        (slot + lax.div(lax.axis_index("tile"), owners), own_row, got)
    )
    table = jnp.pad(
        kernel_table.astype(jnp.float32), ((0, 8), (0, 0), (0, 16 - support))
    ).reshape(planes + 8, 16 * oversample)
    residual, own, other = pl.pallas_call(
        lambda *refs: grid_kernel(pairs, capacity, *refs),
        out_shape=(
            jax.ShapeDtypeStruct((slots, 2, rows), jnp.bfloat16),
            jax.ShapeDtypeStruct((tiles_here, side, wide), jnp.float32),
            jax.ShapeDtypeStruct((tiles_here, side, wide), jnp.bfloat16),
        ),
        in_specs=[SMEM, VMEM, VMEM, VMEM],
        out_specs=(VMEM, VMEM, VMEM),
        scratch_shapes=[
            pltpu.VMEM((2 * tiles_here, wide, side), jnp.bfloat16),
            pltpu.VMEM((2 * tiles_here, side, wide), jnp.float32),
            pltpu.VMEM((pairs, 2, rows), jnp.int32),
            pltpu.SMEM((pairs, 2, rows), jnp.int32),
            pltpu.SMEM(
                (slots + capacity + (2 * tiles_here + CHUNKS + AHEAD) * UNROLL,), jnp.int32
            ),
            pltpu.SemaphoreType.DMA,
            *[pltpu.VMEM((side, UNROLL * rows), jnp.bfloat16)] * 4,
            *[pltpu.VMEM((wide, UNROLL * rows), jnp.float32)] * 4,
            *[pltpu.VMEM((wide, UNROLL * rows), jnp.bfloat16)] * 2,
        ],
        compiler_params=PARAMS,
        name="grid_blocks",
    )(member[None], got, table, model)

    returned = lax.all_to_all(
        residual, "tile", split_axis=0, concat_axis=0, tiled=True, axis_index_groups=halves
    )
    grid_sum = own + lax.ppermute(other, "tile", swap).astype(jnp.float32)
    grids = lax.all_gather(grid_sum.astype(jnp.bfloat16)[None], "freq", axis=0, tiled=True)
    residuals, coupled_grid = pl.pallas_call(
        finish_kernel,
        out_shape=(
            jax.ShapeDtypeStruct((blocks, 2, rows), jnp.float32),
            jax.ShapeDtypeStruct((tiles_here, side, wide), jnp.float32),
        ),
        in_specs=[SMEM, SMEM, VMEM, VMEM],
        out_specs=(VMEM, VMEM),
        compiler_params=PARAMS,
        name="finish",
    )(own_row, slot, returned, grids)
    return (residuals[None], coupled_grid[None])


def solution(mesh):
    return jax.shard_map(
        body,
        mesh=mesh,
        in_specs=(
            P("freq", "tile", None, None),
            P("freq", "tile", None, None),
            P("freq", "tile", None, None),
            P("freq", "tile"),
            P("freq", "tile"),
            P("freq", "tile", None, None),
            P(),
            P(),
        ),
        out_specs=(P("freq", "tile", None, None), P("freq", "tile", None, None)),
        check_vma=False,
    )
```

```python
import jax
import jax.numpy as jnp
from jax import lax
from jax.experimental import pallas as pl
from jax.experimental.pallas import tpu as pltpu
from jax.sharding import PartitionSpec as P

UNROLL = 2
CHUNKS = 8
AHEAD = 2
VMEM = pl.BlockSpec(memory_space=pltpu.VMEM)
SMEM = pl.BlockSpec(memory_space=pltpu.SMEM)
HBM = pl.BlockSpec(memory_space=pltpu.HBM)
PARAMS = pltpu.CompilerParams(vmem_limit_bytes=32 * 1024 * 1024)
WHOLE_PARAMS = pltpu.CompilerParams(vmem_limit_bytes=62 * 1024 * 1024)
TILE_SHIFT = 12
PLANE_SHIFT = 16
SOURCE_SHIFT = 21
FULL = 32767
SCALE = 2.0**20


def scalar_div(value, count):
    shift = count.bit_length() - 1
    return value >> shift if count == 1 << shift else lax.div(value, count)


def first_slot(local, rank, capacity):
    half = capacity // 2
    return (local >> 1) * half + jnp.where((local & 1) == 0, rank, half - 1 - rank)


def rows_per_source(capacity):
    return (3 * (capacity + 1) + 7) // 8 * 8


def two_halves(high, low):
    return (high << 16) | (low & 0xFFFF)


def pack_kernel(pairs, capacity, tiles_here, planes, plane_hbm, tile_hbm, vis_hbm, cell_hbm, sub_hbm,
                sent_ref, slot_ref, plane_ref, tile_ref, vis_ref, cell_ref, sub_ref, about_ref, turned_ref,
                count_ref, load_sem, about_sem):
    blocks = tile_ref.shape[0]
    stride = rows_per_source(capacity)
    loads = [
        pltpu.make_async_copy(source, target, load_sem.at[i])
        for i, (source, target) in enumerate(
            [
                (tile_hbm, tile_ref),
                (plane_hbm, plane_ref),
                (vis_hbm, vis_ref),
                (cell_hbm, cell_ref),
                (sub_hbm, sub_ref),
            ]
        )
    ]
    for copy in loads:
        copy.start()
    for d in range(pairs):
        for t in range(2 * tiles_here):
            count_ref[d * 2 * tiles_here + t] = 0
    for copy in loads[:2]:
        copy.wait()

    def assign(b):
        tile = tile_ref[b]
        owner = scalar_div(tile, tiles_here)
        high = (owner >= pairs).astype(jnp.int32)
        pair = owner - high * pairs
        local = tile - (owner - high) * tiles_here
        key = pair * (2 * tiles_here) + local
        rank = count_ref[key]
        count_ref[key] = rank + 1
        place = first_slot(local, rank, capacity)
        slot_ref[b] = pair * (capacity + 1) + place
        about_ref[pair, 0, place] = plane_ref[b] << PLANE_SHIFT

    def each(work):
        def step(turn, carry):
            for which in range(8):
                work(turn * 8 + which)
            return carry

        lax.fori_loop(0, blocks // 8, step, 0)

    each(assign)
    for d in range(pairs):
        for t in range(2 * tiles_here):
            about_ref[d, 1, t] = count_ref[d * 2 * tiles_here + t]
    turn_about = pltpu.make_async_copy(about_ref, turned_ref, about_sem)
    turn_about.start()
    for copy in loads[2:]:
        copy.wait()
    largest = jnp.max(jnp.max(jnp.abs(vis_ref[...]), axis=0), keepdims=True)
    largest = jnp.maximum(jnp.ceil(largest * SCALE), 1.0)
    inverse = (FULL * SCALE) / largest

    def move(b):
        slot = slot_ref[b]
        row = 3 * slot + scalar_div(slot, capacity + 1) * (stride - 3 * (capacity + 1))
        value = jnp.clip(jnp.round(vis_ref[b] * inverse), -FULL, FULL).astype(jnp.int32)
        for i, pair in enumerate([value, cell_ref[b], sub_ref[b]]):
            sent_ref[pl.ds(row + i, 1), :] = two_halves(pair[0:1], pair[1:2])

    each(move)
    turn_about.wait()
    lane = lax.broadcasted_iota(jnp.int32, (1, 128), 1)
    for d in range(pairs):
        row = d * stride + 3 * capacity
        sent_ref[row : row + 1, :] = turned_ref[d, 0:1, :]
        sent_ref[row + 1 : row + 2, :] = jnp.zeros((1, 128), jnp.int32)
        sent_ref[row + 2 : row + 3, :] = jnp.where(
            lane < 2 * tiles_here, turned_ref[d, 1:2, :], largest.astype(jnp.int32)
        )


def finish_kernel(row_ref, slot_ref, returned_ref, grid_ref, residual_ref, coupled_ref):
    coupled_ref[...] = sum(
        row_ref[g] * grid_ref[g].astype(jnp.float32) for g in range(grid_ref.shape[0])
    )

    def step(turn, carry):
        for which in range(8):
            b = turn * 8 + which
            residual_ref[b] = returned_ref[slot_ref[b]].astype(jnp.float32)
        return carry

    lax.fori_loop(0, residual_ref.shape[0] // 8, step, 0)


def spread_parts(start, offset, table):
    sublane = lax.broadcasted_iota(jnp.int32, (8, 128), 0)
    taps, group = [], []
    for low in (0, 8):
        delta = sublane + low - start
        taps.append(
            jnp.take_along_axis(table, (delta & 15) + offset, axis=1, mode="promise_in_bounds")
        )
        group.append((15 - delta) >> 4)
    return jnp.concatenate(taps, axis=0), jnp.concatenate(group, axis=0)


def grid_kernel(pairs, capacity, member_ref, got_ref, table_ref, model_ref, residual_ref, own_ref,
                other_ref, turned_ref, grid_ref, code_ref, about_ref, list_ref, sem, *buffers):
    row_refs, partial_refs, weighted_refs = buffers[:4], buffers[4:8], buffers[8:]
    tiles, side, wide = model_ref.shape
    groups = side // 16
    zero_row = table_ref.shape[0] - 8
    stride = rows_per_source(capacity)
    lane = lax.broadcasted_iota(jnp.int32, (1, 128), 1)
    for s in range(pairs):
        row = s * stride + 3 * capacity
        code_ref[s, 0:1, :] = got_ref[row : row + 1, :] + (
            lane + s * (capacity + 1) + (s << SOURCE_SHIFT)
        )
        code_ref[s, 1:2, :] = got_ref[row + 2 : row + 3, :]
    fill = pltpu.make_async_copy(code_ref, about_ref, sem)
    fill.start()
    for t in range(tiles):
        turned_ref[t] = model_ref[t].T
    grid_ref[...] = jnp.zeros_like(grid_ref)
    fill.wait()

    start = jnp.int32(0)
    for t in range(tiles):
        count = jnp.int32(0)
        for s in range(pairs):
            count = count + about_ref[s, 1, t]
        spare = -count & (UNROLL - 1)
        for u in range(UNROLL):
            list_ref[start + u] = (zero_row << PLANE_SHIFT) + (t << TILE_SHIFT) + capacity

        def enlist(s, filled, t=t):
            first = t // 2 * (capacity // 2)
            found = about_ref[s, 1, t]

            def some(turn, carry):
                for which in range(8):
                    k = turn * 8 + which
                    place = k if t % 2 == 0 else capacity // 2 - 1 - k
                    code = about_ref[s, 0, jnp.maximum(first + place, 0)]
                    list_ref[filled + k] = code + (t << TILE_SHIFT)
                return carry

            lax.fori_loop(0, (found + 7) >> 3, some, 0)
            return filled + found

        lax.fori_loop(0, pairs, enlist, start + spare)
        start = start + count + spare
    for u in range((CHUNKS + AHEAD) * UNROLL):
        list_ref[start + u] = (zero_row << PLANE_SHIFT) + capacity
    chunks = start >> UNROLL.bit_length() - 1
    zero = jnp.zeros((16, 128), jnp.bfloat16)

    def read(which):
        entry = list_ref[which]
        slot = entry & ((1 << TILE_SHIFT) - 1)
        plane = (entry >> PLANE_SHIFT) & ((1 << (SOURCE_SHIFT - PLANE_SHIFT)) - 1)
        source = entry >> SOURCE_SHIFT
        row = 3 * slot + source * (stride - 3 * (capacity + 1))
        table = jnp.broadcast_to(table_ref[pl.ds(plane, 1), :], (8, 128))

        def words(i):
            return got_ref[pl.ds(row + i, 1), :]

        def parts(shift):
            start = (words(1) >> shift) & 0xFFFF
            offset = ((words(2) >> shift) & 7) << 4
            return spread_parts(
                jnp.broadcast_to(start, (8, 128)), jnp.broadcast_to(offset, (8, 128)), table
            )

        def sample(part):
            step = about_ref[source, 1, tiles].astype(jnp.float32) * (1.0 / (FULL * SCALE))
            return ((words(0) << (16 * part)) >> 16).astype(jnp.float32) * step

        return slot, sample, parts

    def chunk_tile(turn):
        return (list_ref[turn * UNROLL] >> TILE_SHIFT) & 15

    def front(turn, which):
        row_ref, partial_ref = row_refs[which % len(row_refs)], partial_refs[which % len(partial_refs)]
        for u in range(UNROLL):
            _, _, parts = read(turn * UNROLL + u)
            taps, group = parts(16)
            taps = taps.astype(jnp.bfloat16)
            group = group.astype(jnp.float32).astype(jnp.bfloat16)
            for k in range(groups):
                row_ref[16 * k : 16 * k + 16, 128 * u : 128 * u + 128] = jnp.where(
                    group == k, taps, zero
                )
        partial_ref[...] = jnp.dot(
            turned_ref[chunk_tile(turn)], row_ref[...], preferred_element_type=jnp.float32
        )

    def back(turn, which):
        row_ref, partial_ref = row_refs[which % len(row_refs)], partial_refs[which % len(partial_refs)]
        weighted_ref = weighted_refs[which % len(weighted_refs)]
        for u in range(UNROLL):
            slot, sample, parts = read(turn * UNROLL + u)
            columns = slice(128 * u, 128 * u + 128)
            taps, group = parts(0)
            residuals, samples = [], []
            for part in range(2):
                picked = jnp.zeros((16, 128), jnp.float32)
                for k in range(groups):
                    low = part * side + 16 * k
                    picked = jnp.where(group == k, partial_ref[low : low + 16, columns], picked)
                model = jnp.sum(picked * taps, axis=0, keepdims=True)
                residual = sample(part) - model
                residuals.append(residual)
                samples.append((residual * taps).astype(jnp.bfloat16))
            residual_ref[slot] = jnp.concatenate(residuals, axis=0).astype(jnp.bfloat16)
            group = group.astype(jnp.float32).astype(jnp.bfloat16)
            for part in range(2):
                for k in range(groups):
                    low = part * side + 16 * k
                    weighted_ref[low : low + 16, columns] = jnp.where(
                        group == k, samples[part], zero
                    )
        grid_ref[chunk_tile(turn)] += lax.dot_general(
            row_ref[...],
            weighted_ref[...],
            (((1,), (1,)), ((), ())),
            preferred_element_type=jnp.float32,
        )

    def step(turn, carry):
        for which in range(CHUNKS):
            front(turn * CHUNKS + which + AHEAD, which + AHEAD)
            back(turn * CHUNKS + which, which)
        return carry

    for which in range(AHEAD):
        front(which, which)
    lax.fori_loop(0, scalar_div(chunks + CHUNKS - 1, CHUNKS), step, 0)
    half = tiles // 2
    member = member_ref[0]
    for t in range(half):
        own_ref[t] = grid_ref[member * half + t]
        other_ref[t] = grid_ref[(1 - member) * half + t].astype(jnp.bfloat16)


def body(visibilities, uv_cell, sub_pixel, w_plane, block_tile, model_grid, kernel_table, coupling):
    owners = lax.axis_size("tile")
    pairs = owners // 2
    _, blocks, _, rows = visibilities.shape
    capacity = 2 * (3 * blocks // owners)
    _, tiles_here, side, wide = model_grid.shape
    planes, oversample, support = kernel_table.shape
    slots = pairs * (capacity + 1)
    member = lax.axis_index("tile") // pairs
    swap = [(t, (t + pairs) % owners) for t in range(owners)]
    halves = [list(range(pairs)), list(range(pairs, owners))]

    model = lax.all_gather(
        model_grid[0],
        "tile",
        axis=0,
        tiled=True,
        axis_index_groups=[[t, t + pairs] for t in range(pairs)],
    )
    sent, slot = pl.pallas_call(
        lambda *refs: pack_kernel(pairs, capacity, tiles_here, planes, *refs),
        out_shape=(
            jax.ShapeDtypeStruct((pairs * rows_per_source(capacity), rows), jnp.int32),
            jax.ShapeDtypeStruct((blocks,), jnp.int32),
        ),
        in_specs=[HBM] * 5,
        out_specs=(VMEM, SMEM),
        scratch_shapes=[
            pltpu.SMEM((blocks,), jnp.int32),
            pltpu.SMEM((blocks,), jnp.int32),
            pltpu.VMEM((blocks, 2, rows), jnp.float32),
            pltpu.VMEM((blocks, 2, rows), jnp.int32),
            pltpu.VMEM((blocks, 2, rows), jnp.int32),
            pltpu.SMEM((pairs, 2, rows), jnp.int32),
            pltpu.VMEM((pairs, 2, rows), jnp.int32),
            pltpu.SMEM((pairs * 2 * tiles_here,), jnp.int32),
            pltpu.SemaphoreType.DMA((5,)),
            pltpu.SemaphoreType.DMA,
        ],
        compiler_params=WHOLE_PARAMS,
        name="pack_blocks",
    )(w_plane[0], block_tile[0], visibilities[0], uv_cell[0], sub_pixel[0])
    got = lax.all_to_all(
        sent, "tile", split_axis=0, concat_axis=0, tiled=True, axis_index_groups=halves
    )
    own_row = lax.dynamic_index_in_dim(coupling, lax.axis_index("freq"), 0, keepdims=False)
    slot, own_row, got = lax.optimization_barrier(
        (slot + lax.div(lax.axis_index("tile"), owners), own_row, got)
    )
    table = jnp.pad(
        kernel_table.astype(jnp.float32), ((0, 8), (0, 0), (0, 16 - support))
    ).reshape(planes + 8, 16 * oversample)
    residual, own, other = pl.pallas_call(
        lambda *refs: grid_kernel(pairs, capacity, *refs),
        out_shape=(
            jax.ShapeDtypeStruct((slots, 2, rows), jnp.bfloat16),
            jax.ShapeDtypeStruct((tiles_here, side, wide), jnp.float32),
            jax.ShapeDtypeStruct((tiles_here, side, wide), jnp.bfloat16),
        ),
        in_specs=[SMEM, VMEM, VMEM, VMEM],
        out_specs=(VMEM, VMEM, VMEM),
        scratch_shapes=[
            pltpu.VMEM((2 * tiles_here, wide, side), jnp.bfloat16),
            pltpu.VMEM((2 * tiles_here, side, wide), jnp.float32),
            pltpu.VMEM((pairs, 2, rows), jnp.int32),
            pltpu.SMEM((pairs, 2, rows), jnp.int32),
            pltpu.SMEM(
                (slots + capacity + (2 * tiles_here + CHUNKS + AHEAD) * UNROLL,), jnp.int32
            ),
            pltpu.SemaphoreType.DMA,
            *[pltpu.VMEM((side, UNROLL * rows), jnp.bfloat16)] * 4,
            *[pltpu.VMEM((wide, UNROLL * rows), jnp.float32)] * 4,
            *[pltpu.VMEM((wide, UNROLL * rows), jnp.bfloat16)] * 2,
        ],
        compiler_params=PARAMS,
        name="grid_blocks",
    )(member[None], got, table, model)

    returned = lax.all_to_all(
        residual, "tile", split_axis=0, concat_axis=0, tiled=True, axis_index_groups=halves
    )
    grid_sum = own + lax.ppermute(other, "tile", swap).astype(jnp.float32)
    grids = lax.all_gather(grid_sum.astype(jnp.bfloat16)[None], "freq", axis=0, tiled=True)
    residuals, coupled_grid = pl.pallas_call(
        finish_kernel,
        out_shape=(
            jax.ShapeDtypeStruct((blocks, 2, rows), jnp.float32),
            jax.ShapeDtypeStruct((tiles_here, side, wide), jnp.float32),
        ),
        in_specs=[SMEM, SMEM, VMEM, VMEM],
        out_specs=(VMEM, VMEM),
        compiler_params=PARAMS,
        name="finish",
    )(own_row, slot, returned, grids)
    return (residuals[None], coupled_grid[None])


def solution(mesh):
    return jax.shard_map(
        body,
        mesh=mesh,
        in_specs=(
            P("freq", "tile", None, None),
            P("freq", "tile", None, None),
            P("freq", "tile", None, None),
            P("freq", "tile"),
            P("freq", "tile"),
            P("freq", "tile", None, None),
            P(),
            P(),
        ),
        out_specs=(P("freq", "tile", None, None), P("freq", "tile", None, None)),
        check_vma=False,
    )
```

```python
import jax
import jax.numpy as jnp
from jax import lax
from jax.experimental import pallas as pl
from jax.experimental.pallas import tpu as pltpu
from jax.sharding import PartitionSpec as P

UNROLL = 2
CHUNKS = 8
AHEAD = 2
VMEM = pl.BlockSpec(memory_space=pltpu.VMEM)
SMEM = pl.BlockSpec(memory_space=pltpu.SMEM)
HBM = pl.BlockSpec(memory_space=pltpu.HBM)
PARAMS = pltpu.CompilerParams(vmem_limit_bytes=32 * 1024 * 1024)
WHOLE_PARAMS = pltpu.CompilerParams(vmem_limit_bytes=62 * 1024 * 1024)
TILE_SHIFT = 12
PLANE_SHIFT = 16
SOURCE_SHIFT = 21
FULL = 32767
SCALE = 2.0**20


def scalar_div(value, count):
    shift = count.bit_length() - 1
    return value >> shift if count == 1 << shift else lax.div(value, count)


def first_slot(local, rank, capacity):
    half = capacity // 2
    return (local >> 1) * half + jnp.where((local & 1) == 0, rank, half - 1 - rank)


def rows_per_source(capacity):
    return (3 * (capacity + 1) + 7) // 8 * 8


def two_halves(high, low):
    return (high << 16) | (low & 0xFFFF)


def pack_kernel(pairs, capacity, tiles_here, planes, plane_hbm, tile_hbm, vis_hbm, cell_hbm, sub_hbm,
                sent_ref, slot_ref, plane_ref, tile_ref, vis_ref, cell_ref, sub_ref, about_ref, turned_ref,
                count_ref, load_sem, about_sem):
    blocks = tile_ref.shape[0]
    stride = rows_per_source(capacity)
    loads = [
        pltpu.make_async_copy(source, target, load_sem.at[i])
        for i, (source, target) in enumerate(
            [
                (tile_hbm, tile_ref),
                (plane_hbm, plane_ref),
                (vis_hbm, vis_ref),
                (cell_hbm, cell_ref),
                (sub_hbm, sub_ref),
            ]
        )
    ]
    for copy in loads:
        copy.start()
    for d in range(pairs):
        for t in range(2 * tiles_here):
            count_ref[d * 2 * tiles_here + t] = 0
    for copy in loads[:2]:
        copy.wait()

    def assign(b):
        tile = tile_ref[b]
        owner = scalar_div(tile, tiles_here)
        high = (owner >= pairs).astype(jnp.int32)
        pair = owner - high * pairs
        local = tile - (owner - high) * tiles_here
        key = pair * (2 * tiles_here) + local
        rank = count_ref[key]
        count_ref[key] = rank + 1
        place = first_slot(local, rank, capacity)
        slot_ref[b] = pair * (capacity + 1) + place
        about_ref[pair, 0, place] = plane_ref[b] << PLANE_SHIFT

    def each(work):
        def step(turn, carry):
            for which in range(8):
                work(turn * 8 + which)
            return carry

        lax.fori_loop(0, blocks // 8, step, 0)

    each(assign)
    for d in range(pairs):
        for t in range(2 * tiles_here):
            about_ref[d, 1, t] = count_ref[d * 2 * tiles_here + t]
    turn_about = pltpu.make_async_copy(about_ref, turned_ref, about_sem)
    turn_about.start()
    for copy in loads[2:]:
        copy.wait()
    largest = jnp.max(jnp.max(jnp.abs(vis_ref[...]), axis=0), keepdims=True)
    largest = jnp.maximum(jnp.ceil(largest * SCALE), 1.0)
    inverse = (FULL * SCALE) / largest

    def move(b):
        slot = slot_ref[b]
        row = 3 * slot + scalar_div(slot, capacity + 1) * (stride - 3 * (capacity + 1))
        value = jnp.clip(jnp.round(vis_ref[b] * inverse), -FULL, FULL).astype(jnp.int32)
        for i, pair in enumerate([value, cell_ref[b], sub_ref[b]]):
            sent_ref[pl.ds(row + i, 1), :] = two_halves(pair[0:1], pair[1:2])

    each(move)
    turn_about.wait()
    lane = lax.broadcasted_iota(jnp.int32, (1, 128), 1)
    for d in range(pairs):
        row = d * stride + 3 * capacity
        sent_ref[row : row + 1, :] = turned_ref[d, 0:1, :]
        sent_ref[row + 1 : row + 2, :] = jnp.zeros((1, 128), jnp.int32)
        sent_ref[row + 2 : row + 3, :] = jnp.where(
            lane < 2 * tiles_here, turned_ref[d, 1:2, :], largest.astype(jnp.int32)
        )


def finish_kernel(row_ref, slot_ref, returned_ref, grid_ref, residual_ref, coupled_ref):
    coupled_ref[...] = sum(
        row_ref[g] * grid_ref[g].astype(jnp.float32) for g in range(grid_ref.shape[0])
    )

    def step(turn, carry):
        for which in range(8):
            b = turn * 8 + which
            residual_ref[b] = returned_ref[slot_ref[b]].astype(jnp.float32)
        return carry

    lax.fori_loop(0, residual_ref.shape[0] // 8, step, 0)


def spread_parts(start, offset, table):
    sublane = lax.broadcasted_iota(jnp.int32, (8, 128), 0)
    taps, group = [], []
    for low in (0, 8):
        delta = sublane + low - start
        taps.append(
            jnp.take_along_axis(table, (delta & 15) + offset, axis=1, mode="promise_in_bounds")
        )
        group.append((15 - delta) >> 4)
    return jnp.concatenate(taps, axis=0), jnp.concatenate(group, axis=0)


def grid_kernel(pairs, capacity, member_ref, got_ref, table_ref, model_ref, residual_ref, own_ref,
                other_ref, turned_ref, grid_ref, code_ref, about_ref, list_ref, sem, *buffers):
    row_refs, partial_refs, weighted_refs = buffers[:4], buffers[4:8], buffers[8:]
    tiles, side, wide = model_ref.shape
    groups = side // 16
    zero_row = table_ref.shape[0] - 8
    stride = rows_per_source(capacity)
    lane = lax.broadcasted_iota(jnp.int32, (1, 128), 1)
    for s in range(pairs):
        row = s * stride + 3 * capacity
        code_ref[s, 0:1, :] = got_ref[row : row + 1, :] + (
            lane + s * (capacity + 1) + (s << SOURCE_SHIFT)
        )
        code_ref[s, 1:2, :] = got_ref[row + 2 : row + 3, :]
    fill = pltpu.make_async_copy(code_ref, about_ref, sem)
    fill.start()
    for t in range(tiles):
        turned_ref[t] = model_ref[t].T
    grid_ref[...] = jnp.zeros_like(grid_ref)
    fill.wait()

    start = jnp.int32(0)
    for t in range(tiles):
        count = jnp.int32(0)
        for s in range(pairs):
            count = count + about_ref[s, 1, t]
        spare = -count & (UNROLL - 1)
        for u in range(UNROLL):
            list_ref[start + u] = (zero_row << PLANE_SHIFT) + (t << TILE_SHIFT) + capacity

        def enlist(s, filled, t=t):
            first = t // 2 * (capacity // 2)
            found = about_ref[s, 1, t]

            def some(turn, carry):
                for which in range(16):
                    k = turn * 16 + which
                    place = k if t % 2 == 0 else capacity // 2 - 1 - k
                    code = about_ref[s, 0, jnp.maximum(first + place, 0)]
                    list_ref[filled + k] = code + (t << TILE_SHIFT)
                return carry

            lax.fori_loop(0, (found + 15) >> 4, some, 0)
            return filled + found

        lax.fori_loop(0, pairs, enlist, start + spare)
        start = start + count + spare
    for u in range((CHUNKS + AHEAD) * UNROLL):
        list_ref[start + u] = (zero_row << PLANE_SHIFT) + capacity
    chunks = start >> UNROLL.bit_length() - 1
    zero = jnp.zeros((16, 128), jnp.bfloat16)

    def read(which):
        entry = list_ref[which]
        slot = entry & ((1 << TILE_SHIFT) - 1)
        plane = (entry >> PLANE_SHIFT) & ((1 << (SOURCE_SHIFT - PLANE_SHIFT)) - 1)
        source = entry >> SOURCE_SHIFT
        row = 3 * slot + source * (stride - 3 * (capacity + 1))
        table = jnp.broadcast_to(table_ref[pl.ds(plane, 1), :], (8, 128))

        def words(i):
            return got_ref[pl.ds(row + i, 1), :]

        def parts(shift):
            start = (words(1) >> shift) & 0xFFFF
            offset = ((words(2) >> shift) & 7) << 4
            return spread_parts(
                jnp.broadcast_to(start, (8, 128)), jnp.broadcast_to(offset, (8, 128)), table
            )

        def sample(part):
            step = about_ref[source, 1, tiles].astype(jnp.float32) * (1.0 / (FULL * SCALE))
            return ((words(0) << (16 * part)) >> 16).astype(jnp.float32) * step

        return slot, sample, parts

    def chunk_tile(turn):
        return (list_ref[turn * UNROLL] >> TILE_SHIFT) & 15

    def front(turn, which):
        row_ref, partial_ref = row_refs[which % len(row_refs)], partial_refs[which % len(partial_refs)]
        for u in range(UNROLL):
            _, _, parts = read(turn * UNROLL + u)
            taps, group = parts(16)
            taps = taps.astype(jnp.bfloat16)
            group = group.astype(jnp.float32).astype(jnp.bfloat16)
            for k in range(groups):
                row_ref[16 * k : 16 * k + 16, 128 * u : 128 * u + 128] = jnp.where(
                    group == k, taps, zero
                )
        partial_ref[...] = jnp.dot(
            turned_ref[chunk_tile(turn)], row_ref[...], preferred_element_type=jnp.float32
        )

    def back(turn, which):
        row_ref, partial_ref = row_refs[which % len(row_refs)], partial_refs[which % len(partial_refs)]
        weighted_ref = weighted_refs[which % len(weighted_refs)]
        for u in range(UNROLL):
            slot, sample, parts = read(turn * UNROLL + u)
            columns = slice(128 * u, 128 * u + 128)
            taps, group = parts(0)
            residuals, samples = [], []
            for part in range(2):
                picked = jnp.zeros((16, 128), jnp.float32)
                for k in range(groups):
                    low = part * side + 16 * k
                    picked = jnp.where(group == k, partial_ref[low : low + 16, columns], picked)
                model = jnp.sum(picked * taps, axis=0, keepdims=True)
                residual = sample(part) - model
                residuals.append(residual)
                samples.append((residual * taps).astype(jnp.bfloat16))
            residual_ref[slot] = jnp.concatenate(residuals, axis=0).astype(jnp.bfloat16)
            group = group.astype(jnp.float32).astype(jnp.bfloat16)
            for part in range(2):
                for k in range(groups):
                    low = part * side + 16 * k
                    weighted_ref[low : low + 16, columns] = jnp.where(
                        group == k, samples[part], zero
                    )
        grid_ref[chunk_tile(turn)] += lax.dot_general(
            weighted_ref[...],
            row_ref[...],
            (((1,), (1,)), ((), ())),
            preferred_element_type=jnp.float32,
        )

    def step(turn, carry):
        for which in range(CHUNKS):
            front(turn * CHUNKS + which + AHEAD, which + AHEAD)
            back(turn * CHUNKS + which, which)
        return carry

    for which in range(AHEAD):
        front(which, which)
    lax.fori_loop(0, scalar_div(chunks + CHUNKS - 1, CHUNKS), step, 0)
    half = tiles // 2
    member = member_ref[0]
    for t in range(half):
        own_ref[t] = grid_ref[member * half + t].T
        other_ref[t] = grid_ref[(1 - member) * half + t].T.astype(jnp.bfloat16)


def body(visibilities, uv_cell, sub_pixel, w_plane, block_tile, model_grid, kernel_table, coupling):
    owners = lax.axis_size("tile")
    pairs = owners // 2
    _, blocks, _, rows = visibilities.shape
    capacity = 2 * (3 * blocks // owners)
    _, tiles_here, side, wide = model_grid.shape
    planes, oversample, support = kernel_table.shape
    slots = pairs * (capacity + 1)
    member = lax.axis_index("tile") // pairs
    swap = [(t, (t + pairs) % owners) for t in range(owners)]
    halves = [list(range(pairs)), list(range(pairs, owners))]

    model = lax.all_gather(
        model_grid[0],
        "tile",
        axis=0,
        tiled=True,
        axis_index_groups=[[t, t + pairs] for t in range(pairs)],
    )
    sent, slot = pl.pallas_call(
        lambda *refs: pack_kernel(pairs, capacity, tiles_here, planes, *refs),
        out_shape=(
            jax.ShapeDtypeStruct((pairs * rows_per_source(capacity), rows), jnp.int32),
            jax.ShapeDtypeStruct((blocks,), jnp.int32),
        ),
        in_specs=[HBM] * 5,
        out_specs=(VMEM, SMEM),
        scratch_shapes=[
            pltpu.SMEM((blocks,), jnp.int32),
            pltpu.SMEM((blocks,), jnp.int32),
            pltpu.VMEM((blocks, 2, rows), jnp.float32),
            pltpu.VMEM((blocks, 2, rows), jnp.int32),
            pltpu.VMEM((blocks, 2, rows), jnp.int32),
            pltpu.SMEM((pairs, 2, rows), jnp.int32),
            pltpu.VMEM((pairs, 2, rows), jnp.int32),
            pltpu.SMEM((pairs * 2 * tiles_here,), jnp.int32),
            pltpu.SemaphoreType.DMA((5,)),
            pltpu.SemaphoreType.DMA,
        ],
        compiler_params=WHOLE_PARAMS,
        name="pack_blocks",
    )(w_plane[0], block_tile[0], visibilities[0], uv_cell[0], sub_pixel[0])
    got = lax.all_to_all(
        sent, "tile", split_axis=0, concat_axis=0, tiled=True, axis_index_groups=halves
    )
    own_row = lax.dynamic_index_in_dim(coupling, lax.axis_index("freq"), 0, keepdims=False)
    slot, own_row, got = lax.optimization_barrier(
        (slot + lax.div(lax.axis_index("tile"), owners), own_row, got)
    )
    table = jnp.pad(
        kernel_table.astype(jnp.float32), ((0, 8), (0, 0), (0, 16 - support))
    ).reshape(planes + 8, 16 * oversample)
    residual, own, other = pl.pallas_call(
        lambda *refs: grid_kernel(pairs, capacity, *refs),
        out_shape=(
            jax.ShapeDtypeStruct((slots, 2, rows), jnp.bfloat16),
            jax.ShapeDtypeStruct((tiles_here, side, wide), jnp.float32),
            jax.ShapeDtypeStruct((tiles_here, side, wide), jnp.bfloat16),
        ),
        in_specs=[SMEM, VMEM, VMEM, VMEM],
        out_specs=(VMEM, VMEM, VMEM),
        scratch_shapes=[
            pltpu.VMEM((2 * tiles_here, wide, side), jnp.bfloat16),
            pltpu.VMEM((2 * tiles_here, wide, side), jnp.float32),
            pltpu.VMEM((pairs, 2, rows), jnp.int32),
            pltpu.SMEM((pairs, 2, rows), jnp.int32),
            pltpu.SMEM(
                (slots + capacity + (2 * tiles_here + CHUNKS + AHEAD) * UNROLL,), jnp.int32
            ),
            pltpu.SemaphoreType.DMA,
            *[pltpu.VMEM((side, UNROLL * rows), jnp.bfloat16)] * 4,
            *[pltpu.VMEM((wide, UNROLL * rows), jnp.float32)] * 4,
            *[pltpu.VMEM((wide, UNROLL * rows), jnp.bfloat16)] * 2,
        ],
        compiler_params=PARAMS,
        name="grid_blocks",
    )(member[None], got, table, model)

    returned = lax.all_to_all(
        residual, "tile", split_axis=0, concat_axis=0, tiled=True, axis_index_groups=halves
    )
    grid_sum = own + lax.ppermute(other, "tile", swap).astype(jnp.float32)
    grids = lax.all_gather(grid_sum.astype(jnp.bfloat16)[None], "freq", axis=0, tiled=True)
    residuals, coupled_grid = pl.pallas_call(
        finish_kernel,
        out_shape=(
            jax.ShapeDtypeStruct((blocks, 2, rows), jnp.float32),
            jax.ShapeDtypeStruct((tiles_here, side, wide), jnp.float32),
        ),
        in_specs=[SMEM, SMEM, VMEM, VMEM],
        out_specs=(VMEM, VMEM),
        compiler_params=PARAMS,
        name="finish",
    )(own_row, slot, returned, grids)
    return (residuals[None], coupled_grid[None])


def solution(mesh):
    return jax.shard_map(
        body,
        mesh=mesh,
        in_specs=(
            P("freq", "tile", None, None),
            P("freq", "tile", None, None),
            P("freq", "tile", None, None),
            P("freq", "tile"),
            P("freq", "tile"),
            P("freq", "tile", None, None),
            P(),
            P(),
        ),
        out_specs=(P("freq", "tile", None, None), P("freq", "tile", None, None)),
        check_vma=False,
    )
```

```python
import jax
import jax.numpy as jnp
from jax import lax
from jax.experimental import pallas as pl
from jax.experimental.pallas import tpu as pltpu
from jax.sharding import PartitionSpec as P

UNROLL = 2
CHUNKS = 8
AHEAD = 2
VMEM = pl.BlockSpec(memory_space=pltpu.VMEM)
SMEM = pl.BlockSpec(memory_space=pltpu.SMEM)
HBM = pl.BlockSpec(memory_space=pltpu.HBM)
PARAMS = pltpu.CompilerParams(vmem_limit_bytes=32 * 1024 * 1024)
WHOLE_PARAMS = pltpu.CompilerParams(vmem_limit_bytes=62 * 1024 * 1024)
TILE_SHIFT = 12
PLANE_SHIFT = 16
SOURCE_SHIFT = 21
FULL = 32767
SCALE = 2.0**20


def scalar_div(value, count):
    shift = count.bit_length() - 1
    return value >> shift if count == 1 << shift else lax.div(value, count)


def first_slot(local, rank, capacity):
    half = capacity // 2
    return (local >> 1) * half + jnp.where((local & 1) == 0, rank, half - 1 - rank)


def rows_per_source(capacity):
    return (3 * (capacity + 1) + 7) // 8 * 8


def two_halves(high, low):
    return (high << 16) | (low & 0xFFFF)


def pack_kernel(pairs, capacity, tiles_here, planes, plane_hbm, tile_hbm, vis_hbm, cell_hbm, sub_hbm,
                sent_ref, slot_ref, plane_ref, tile_ref, vis_ref, cell_ref, sub_ref, about_ref, turned_ref,
                count_ref, load_sem, about_sem):
    blocks = tile_ref.shape[0]
    stride = rows_per_source(capacity)
    loads = [
        pltpu.make_async_copy(source, target, load_sem.at[i])
        for i, (source, target) in enumerate(
            [
                (tile_hbm, tile_ref),
                (plane_hbm, plane_ref),
                (vis_hbm, vis_ref),
                (cell_hbm, cell_ref),
                (sub_hbm, sub_ref),
            ]
        )
    ]
    for copy in loads:
        copy.start()
    for d in range(pairs):
        for t in range(2 * tiles_here):
            count_ref[d * 2 * tiles_here + t] = 0
    for copy in loads[:2]:
        copy.wait()

    def assign(b):
        tile = tile_ref[b]
        owner = scalar_div(tile, tiles_here)
        high = (owner >= pairs).astype(jnp.int32)
        pair = owner - high * pairs
        local = tile - (owner - high) * tiles_here
        key = pair * (2 * tiles_here) + local
        rank = count_ref[key]
        count_ref[key] = rank + 1
        place = first_slot(local, rank, capacity)
        slot_ref[b] = pair * (capacity + 1) + place
        about_ref[pair, 0, place] = plane_ref[b] << PLANE_SHIFT

    def each(work):
        def step(turn, carry):
            for which in range(8):
                work(turn * 8 + which)
            return carry

        lax.fori_loop(0, blocks // 8, step, 0)

    each(assign)
    for d in range(pairs):
        for t in range(2 * tiles_here):
            about_ref[d, 1, t] = count_ref[d * 2 * tiles_here + t]
    turn_about = pltpu.make_async_copy(about_ref, turned_ref, about_sem)
    turn_about.start()
    for copy in loads[2:]:
        copy.wait()
    largest = jnp.max(jnp.max(jnp.abs(vis_ref[...]), axis=0), keepdims=True)
    largest = jnp.maximum(jnp.ceil(largest * SCALE), 1.0)
    inverse = (FULL * SCALE) / largest

    def move(b):
        slot = slot_ref[b]
        row = 3 * slot + scalar_div(slot, capacity + 1) * (stride - 3 * (capacity + 1))
        value = jnp.clip(jnp.round(vis_ref[b] * inverse), -FULL, FULL).astype(jnp.int32)
        for i, pair in enumerate([value, cell_ref[b], sub_ref[b]]):
            sent_ref[pl.ds(row + i, 1), :] = two_halves(pair[0:1], pair[1:2])

    each(move)
    turn_about.wait()
    lane = lax.broadcasted_iota(jnp.int32, (1, 128), 1)
    for d in range(pairs):
        row = d * stride + 3 * capacity
        sent_ref[row : row + 1, :] = turned_ref[d, 0:1, :]
        sent_ref[row + 1 : row + 2, :] = jnp.zeros((1, 128), jnp.int32)
        sent_ref[row + 2 : row + 3, :] = jnp.where(
            lane < 2 * tiles_here, turned_ref[d, 1:2, :], largest.astype(jnp.int32)
        )


def finish_kernel(row_ref, slot_ref, returned_ref, grid_ref, residual_ref, coupled_ref):
    planes, tiles_here = grid_ref.shape[:2]
    for t in range(tiles_here):
        coupled_ref[t] = sum(
            row_ref[g] * grid_ref[g, t].astype(jnp.float32) for g in range(planes)
        ).T

    def step(turn, carry):
        for which in range(8):
            b = turn * 8 + which
            residual_ref[b] = returned_ref[slot_ref[b]].astype(jnp.float32)
        return carry

    lax.fori_loop(0, residual_ref.shape[0] // 8, step, 0)


def spread_parts(start, offset, table):
    sublane = lax.broadcasted_iota(jnp.int32, (8, 128), 0)
    taps, group = [], []
    for low in (0, 8):
        delta = sublane + low - start
        taps.append(
            jnp.take_along_axis(table, (delta & 15) + offset, axis=1, mode="promise_in_bounds")
        )
        group.append((15 - delta) >> 4)
    return jnp.concatenate(taps, axis=0), jnp.concatenate(group, axis=0)


def grid_kernel(pairs, capacity, member_ref, got_ref, table_ref, model_ref, residual_ref, own_ref,
                other_ref, turned_ref, grid_ref, code_ref, about_ref, list_ref, sem, *buffers):
    row_refs, picked_refs = buffers[:4], buffers[4:]
    tiles, side, wide = model_ref.shape
    groups = side // 16
    zero_row = table_ref.shape[0] - 8
    stride = rows_per_source(capacity)
    lane = lax.broadcasted_iota(jnp.int32, (1, 128), 1)
    for s in range(pairs):
        row = s * stride + 3 * capacity
        code_ref[s, 0:1, :] = got_ref[row : row + 1, :] + (
            lane + s * (capacity + 1) + (s << SOURCE_SHIFT)
        )
        code_ref[s, 1:2, :] = got_ref[row + 2 : row + 3, :]
    fill = pltpu.make_async_copy(code_ref, about_ref, sem)
    fill.start()
    for t in range(tiles):
        turned_ref[t] = model_ref[t].T
    grid_ref[...] = jnp.zeros_like(grid_ref)
    fill.wait()

    start = jnp.int32(0)
    for t in range(tiles):
        count = jnp.int32(0)
        for s in range(pairs):
            count = count + about_ref[s, 1, t]
        spare = -count & (UNROLL - 1)
        for u in range(UNROLL):
            list_ref[start + u] = (zero_row << PLANE_SHIFT) + (t << TILE_SHIFT) + capacity

        def enlist(s, filled, t=t):
            first = t // 2 * (capacity // 2)
            found = about_ref[s, 1, t]

            def some(turn, carry):
                for which in range(16):
                    k = turn * 16 + which
                    place = k if t % 2 == 0 else capacity // 2 - 1 - k
                    code = about_ref[s, 0, jnp.maximum(first + place, 0)]
                    list_ref[filled + k] = code + (t << TILE_SHIFT)
                return carry

            lax.fori_loop(0, (found + 15) >> 4, some, 0)
            return filled + found

        lax.fori_loop(0, pairs, enlist, start + spare)
        start = start + count + spare
    for u in range((CHUNKS + AHEAD) * UNROLL):
        list_ref[start + u] = (zero_row << PLANE_SHIFT) + capacity
    chunks = start >> UNROLL.bit_length() - 1
    zero = jnp.zeros((16, 128), jnp.bfloat16)

    def read(which):
        entry = list_ref[which]
        slot = entry & ((1 << TILE_SHIFT) - 1)
        plane = (entry >> PLANE_SHIFT) & ((1 << (SOURCE_SHIFT - PLANE_SHIFT)) - 1)
        source = entry >> SOURCE_SHIFT
        row = 3 * slot + source * (stride - 3 * (capacity + 1))
        table = jnp.broadcast_to(table_ref[pl.ds(plane, 1), :], (8, 128))

        def words(i):
            return got_ref[pl.ds(row + i, 1), :]

        def parts(shift):
            start = (words(1) >> shift) & 0xFFFF
            offset = ((words(2) >> shift) & 7) << 4
            return spread_parts(
                jnp.broadcast_to(start, (8, 128)), jnp.broadcast_to(offset, (8, 128)), table
            )

        def sample(part):
            step = about_ref[source, 1, tiles].astype(jnp.float32) * (1.0 / (FULL * SCALE))
            return ((words(0) << (16 * part)) >> 16).astype(jnp.float32) * step

        return slot, sample, parts

    def chunk_tile(turn):
        return (list_ref[turn * UNROLL] >> TILE_SHIFT) & 15

    def front(turn, which):
        row_ref, picked_ref = row_refs[which % len(row_refs)], picked_refs[which % len(picked_refs)]
        blocks = [read(turn * UNROLL + u) for u in range(UNROLL)]
        for u, (_, _, parts) in enumerate(blocks):
            taps, group = parts(16)
            taps = taps.astype(jnp.bfloat16)
            group = group.astype(jnp.float32).astype(jnp.bfloat16)
            for k in range(groups):
                row_ref[16 * k : 16 * k + 16, 128 * u : 128 * u + 128] = jnp.where(
                    group == k, taps, zero
                )
        partial = jnp.dot(
            turned_ref[chunk_tile(turn)], row_ref[...], preferred_element_type=jnp.float32
        )
        for u, (_, _, parts) in enumerate(blocks):
            columns = slice(128 * u, 128 * u + 128)
            taps, group = parts(0)
            for part in range(2):
                picked = jnp.zeros((16, 128), jnp.float32)
                for k in range(groups):
                    low = part * side + 16 * k
                    picked = jnp.where(group == k, partial[low : low + 16, columns], picked)
                picked_ref[part, :, columns] = picked * taps

    def back(turn, which):
        row_ref, picked_ref = row_refs[which % len(row_refs)], picked_refs[which % len(picked_refs)]
        weighted = []
        for u in range(UNROLL):
            slot, sample, parts = read(turn * UNROLL + u)
            columns = slice(128 * u, 128 * u + 128)
            taps, group = parts(0)
            group = group.astype(jnp.float32).astype(jnp.bfloat16)
            residuals, pieces = [], []
            for part in range(2):
                model = jnp.sum(picked_ref[part, :, columns], axis=0, keepdims=True)
                residual = sample(part) - model
                residuals.append(residual)
                value = (residual * taps).astype(jnp.bfloat16)
                pieces += [jnp.where(group == k, value, zero) for k in range(groups)]
            residual_ref[slot] = jnp.concatenate(residuals, axis=0).astype(jnp.bfloat16)
            weighted.append(jnp.concatenate(pieces, axis=0))
        grid_ref[chunk_tile(turn)] += lax.dot_general(
            jnp.concatenate(weighted, axis=1),
            row_ref[...],
            (((1,), (1,)), ((), ())),
            preferred_element_type=jnp.float32,
        )

    def step(turn, carry):
        for which in range(CHUNKS):
            front(turn * CHUNKS + which + AHEAD, which + AHEAD)
            back(turn * CHUNKS + which, which)
        return carry

    for which in range(AHEAD):
        front(which, which)
    lax.fori_loop(0, scalar_div(chunks + CHUNKS - 1, CHUNKS), step, 0)
    half = tiles // 2
    member = member_ref[0]
    for t in range(half):
        own_ref[t] = grid_ref[member * half + t]
        other_ref[t] = grid_ref[(1 - member) * half + t].astype(jnp.bfloat16)


def body(visibilities, uv_cell, sub_pixel, w_plane, block_tile, model_grid, kernel_table, coupling):
    owners = lax.axis_size("tile")
    pairs = owners // 2
    _, blocks, _, rows = visibilities.shape
    capacity = 2 * (3 * blocks // owners)
    _, tiles_here, side, wide = model_grid.shape
    planes, oversample, support = kernel_table.shape
    slots = pairs * (capacity + 1)
    member = lax.axis_index("tile") // pairs
    swap = [(t, (t + pairs) % owners) for t in range(owners)]
    halves = [list(range(pairs)), list(range(pairs, owners))]

    model = lax.all_gather(
        model_grid[0],
        "tile",
        axis=0,
        tiled=True,
        axis_index_groups=[[t, t + pairs] for t in range(pairs)],
    )
    sent, slot = pl.pallas_call(
        lambda *refs: pack_kernel(pairs, capacity, tiles_here, planes, *refs),
        out_shape=(
            jax.ShapeDtypeStruct((pairs * rows_per_source(capacity), rows), jnp.int32),
            jax.ShapeDtypeStruct((blocks,), jnp.int32),
        ),
        in_specs=[HBM] * 5,
        out_specs=(VMEM, SMEM),
        scratch_shapes=[
            pltpu.SMEM((blocks,), jnp.int32),
            pltpu.SMEM((blocks,), jnp.int32),
            pltpu.VMEM((blocks, 2, rows), jnp.float32),
            pltpu.VMEM((blocks, 2, rows), jnp.int32),
            pltpu.VMEM((blocks, 2, rows), jnp.int32),
            pltpu.SMEM((pairs, 2, rows), jnp.int32),
            pltpu.VMEM((pairs, 2, rows), jnp.int32),
            pltpu.SMEM((pairs * 2 * tiles_here,), jnp.int32),
            pltpu.SemaphoreType.DMA((5,)),
            pltpu.SemaphoreType.DMA,
        ],
        compiler_params=WHOLE_PARAMS,
        name="pack_blocks",
    )(w_plane[0], block_tile[0], visibilities[0], uv_cell[0], sub_pixel[0])
    got = lax.all_to_all(
        sent, "tile", split_axis=0, concat_axis=0, tiled=True, axis_index_groups=halves
    )
    own_row = lax.dynamic_index_in_dim(coupling, lax.axis_index("freq"), 0, keepdims=False)
    slot, own_row, got = lax.optimization_barrier(
        (slot + lax.div(lax.axis_index("tile"), owners), own_row, got)
    )
    table = jnp.pad(
        kernel_table.astype(jnp.float32), ((0, 8), (0, 0), (0, 16 - support))
    ).reshape(planes + 8, 16 * oversample)
    residual, own, other = pl.pallas_call(
        lambda *refs: grid_kernel(pairs, capacity, *refs),
        out_shape=(
            jax.ShapeDtypeStruct((slots, 2, rows), jnp.bfloat16),
            jax.ShapeDtypeStruct((tiles_here, wide, side), jnp.float32),
            jax.ShapeDtypeStruct((tiles_here, wide, side), jnp.bfloat16),
        ),
        in_specs=[SMEM, VMEM, VMEM, VMEM],
        out_specs=(VMEM, VMEM, VMEM),
        scratch_shapes=[
            pltpu.VMEM((2 * tiles_here, wide, side), jnp.bfloat16),
            pltpu.VMEM((2 * tiles_here, wide, side), jnp.float32),
            pltpu.VMEM((pairs, 2, rows), jnp.int32),
            pltpu.SMEM((pairs, 2, rows), jnp.int32),
            pltpu.SMEM(
                (slots + capacity + (2 * tiles_here + CHUNKS + AHEAD) * UNROLL,), jnp.int32
            ),
            pltpu.SemaphoreType.DMA,
            *[pltpu.VMEM((side, UNROLL * rows), jnp.bfloat16)] * 4,
            *[pltpu.VMEM((2, 16, UNROLL * rows), jnp.float32)] * 4,
        ],
        compiler_params=PARAMS,
        name="grid_blocks",
    )(member[None], got, table, model)

    returned = lax.all_to_all(
        residual, "tile", split_axis=0, concat_axis=0, tiled=True, axis_index_groups=halves
    )
    grid_sum = own + lax.ppermute(other, "tile", swap).astype(jnp.float32)
    grids = lax.all_gather(grid_sum.astype(jnp.bfloat16)[None], "freq", axis=0, tiled=True)
    residuals, coupled_grid = pl.pallas_call(
        finish_kernel,
        out_shape=(
            jax.ShapeDtypeStruct((blocks, 2, rows), jnp.float32),
            jax.ShapeDtypeStruct((tiles_here, side, wide), jnp.float32),
        ),
        in_specs=[SMEM, SMEM, VMEM, VMEM],
        out_specs=(VMEM, VMEM),
        compiler_params=PARAMS,
        name="finish",
    )(own_row, slot, returned, grids)
    return (residuals[None], coupled_grid[None])


def solution(mesh):
    return jax.shard_map(
        body,
        mesh=mesh,
        in_specs=(
            P("freq", "tile", None, None),
            P("freq", "tile", None, None),
            P("freq", "tile", None, None),
            P("freq", "tile"),
            P("freq", "tile"),
            P("freq", "tile", None, None),
            P(),
            P(),
        ),
        out_specs=(P("freq", "tile", None, None), P("freq", "tile", None, None)),
        check_vma=False,
    )
```

```python
import jax
import jax.numpy as jnp
from jax import lax
from jax.experimental import pallas as pl
from jax.experimental.pallas import tpu as pltpu
from jax.sharding import PartitionSpec as P

UNROLL = 2
CHUNKS = 15
AHEAD = 2
BUFFERS = 5
VMEM = pl.BlockSpec(memory_space=pltpu.VMEM)
SMEM = pl.BlockSpec(memory_space=pltpu.SMEM)
HBM = pl.BlockSpec(memory_space=pltpu.HBM)
PARAMS = pltpu.CompilerParams(vmem_limit_bytes=32 * 1024 * 1024)
WHOLE_PARAMS = pltpu.CompilerParams(vmem_limit_bytes=62 * 1024 * 1024)
TILE_SHIFT = 12
PLANE_SHIFT = 16
SOURCE_SHIFT = 21
FULL = 32767
SCALE = 2.0**20


def scalar_div(value, count):
    shift = count.bit_length() - 1
    return value >> shift if count == 1 << shift else lax.div(value, count)


def first_slot(local, rank, capacity):
    half = capacity // 2
    return (local >> 1) * half + jnp.where((local & 1) == 0, rank, half - 1 - rank)


def rows_per_source(capacity):
    return (3 * (capacity + 1) + 7) // 8 * 8


def two_halves(high, low):
    return (high << 16) | (low & 0xFFFF)


def pack_kernel(pairs, capacity, tiles_here, planes, plane_hbm, tile_hbm, vis_hbm, cell_hbm, sub_hbm,
                sent_ref, slot_ref, plane_ref, tile_ref, vis_ref, cell_ref, sub_ref, about_ref, turned_ref,
                count_ref, load_sem, about_sem):
    blocks = tile_ref.shape[0]
    stride = rows_per_source(capacity)
    loads = [
        pltpu.make_async_copy(source, target, load_sem.at[i])
        for i, (source, target) in enumerate(
            [
                (tile_hbm, tile_ref),
                (plane_hbm, plane_ref),
                (vis_hbm, vis_ref),
                (cell_hbm, cell_ref),
                (sub_hbm, sub_ref),
            ]
        )
    ]
    for copy in loads:
        copy.start()
    for d in range(pairs):
        for t in range(2 * tiles_here):
            count_ref[d * 2 * tiles_here + t] = 0
    for copy in loads[:2]:
        copy.wait()

    def assign(b):
        tile = tile_ref[b]
        owner = scalar_div(tile, tiles_here)
        high = (owner >= pairs).astype(jnp.int32)
        pair = owner - high * pairs
        local = tile - (owner - high) * tiles_here
        key = pair * (2 * tiles_here) + local
        rank = count_ref[key]
        count_ref[key] = rank + 1
        place = first_slot(local, rank, capacity)
        slot_ref[b] = pair * (capacity + 1) + place
        about_ref[pair, 0, place] = plane_ref[b] << PLANE_SHIFT

    def each(work):
        def step(turn, carry):
            for which in range(8):
                work(turn * 8 + which)
            return carry

        lax.fori_loop(0, blocks // 8, step, 0)

    each(assign)
    for d in range(pairs):
        for t in range(2 * tiles_here):
            about_ref[d, 1, t] = count_ref[d * 2 * tiles_here + t]
    turn_about = pltpu.make_async_copy(about_ref, turned_ref, about_sem)
    turn_about.start()
    for copy in loads[2:]:
        copy.wait()
    largest = jnp.max(jnp.max(jnp.abs(vis_ref[...]), axis=0), keepdims=True)
    largest = jnp.maximum(jnp.ceil(largest * SCALE), 1.0)
    inverse = (FULL * SCALE) / largest

    def move(b):
        slot = slot_ref[b]
        row = 3 * slot + scalar_div(slot, capacity + 1) * (stride - 3 * (capacity + 1))
        value = jnp.clip(jnp.round(vis_ref[b] * inverse), -FULL, FULL).astype(jnp.int32)
        for i, pair in enumerate([value, cell_ref[b], sub_ref[b]]):
            sent_ref[pl.ds(row + i, 1), :] = two_halves(pair[0:1], pair[1:2])

    each(move)
    turn_about.wait()
    lane = lax.broadcasted_iota(jnp.int32, (1, 128), 1)
    for d in range(pairs):
        row = d * stride + 3 * capacity
        sent_ref[row : row + 1, :] = turned_ref[d, 0:1, :]
        sent_ref[row + 1 : row + 2, :] = jnp.zeros((1, 128), jnp.int32)
        sent_ref[row + 2 : row + 3, :] = jnp.where(
            lane < 2 * tiles_here, turned_ref[d, 1:2, :], largest.astype(jnp.int32)
        )


def finish_kernel(row_ref, slot_ref, returned_ref, grid_ref, residual_ref, coupled_ref):
    planes, tiles_here = grid_ref.shape[:2]
    for t in range(tiles_here):
        coupled_ref[t] = sum(
            row_ref[g] * grid_ref[g, t].astype(jnp.float32) for g in range(planes)
        ).T

    def step(turn, carry):
        for which in range(8):
            b = turn * 8 + which
            residual_ref[b] = returned_ref[slot_ref[b]].astype(jnp.float32)
        return carry

    lax.fori_loop(0, residual_ref.shape[0] // 8, step, 0)


def spread_parts(start, offset, table):
    sublane = lax.broadcasted_iota(jnp.int32, (8, 128), 0)
    taps, group = [], []
    for low in (0, 8):
        delta = sublane + low - start
        taps.append(
            jnp.take_along_axis(table, (delta & 15) + offset, axis=1, mode="promise_in_bounds")
        )
        group.append((15 - delta) >> 4)
    return jnp.concatenate(taps, axis=0), jnp.concatenate(group, axis=0)


def grid_kernel(pairs, capacity, member_ref, got_ref, table_ref, model_ref, residual_ref, own_ref,
                other_ref, turned_ref, grid_ref, code_ref, about_ref, list_ref, sem, *buffers):
    row_refs, picked_refs = buffers[:BUFFERS], buffers[BUFFERS:]
    tiles, side, wide = model_ref.shape
    groups = side // 16
    zero_row = table_ref.shape[0] - 8
    stride = rows_per_source(capacity)
    lane = lax.broadcasted_iota(jnp.int32, (1, 128), 1)
    for s in range(pairs):
        row = s * stride + 3 * capacity
        code_ref[s, 0:1, :] = got_ref[row : row + 1, :] + (
            lane + s * (capacity + 1) + (s << SOURCE_SHIFT)
        )
        code_ref[s, 1:2, :] = got_ref[row + 2 : row + 3, :]
    fill = pltpu.make_async_copy(code_ref, about_ref, sem)
    fill.start()
    for t in range(tiles):
        turned_ref[t] = model_ref[t].T
    grid_ref[...] = jnp.zeros_like(grid_ref)
    fill.wait()

    start = jnp.int32(0)
    for t in range(tiles):
        count = jnp.int32(0)
        for s in range(pairs):
            count = count + about_ref[s, 1, t]
        spare = -count & (UNROLL - 1)
        for u in range(UNROLL):
            list_ref[start + u] = (zero_row << PLANE_SHIFT) + (t << TILE_SHIFT) + capacity

        def enlist(s, filled, t=t):
            first = t // 2 * (capacity // 2)
            found = about_ref[s, 1, t]

            def some(turn, carry):
                for which in range(16):
                    k = turn * 16 + which
                    place = k if t % 2 == 0 else capacity // 2 - 1 - k
                    code = about_ref[s, 0, jnp.maximum(first + place, 0)]
                    list_ref[filled + k] = code + (t << TILE_SHIFT)
                return carry

            lax.fori_loop(0, (found + 15) >> 4, some, 0)
            return filled + found

        lax.fori_loop(0, pairs, enlist, start + spare)
        start = start + count + spare
    for u in range((CHUNKS + AHEAD) * UNROLL):
        list_ref[start + u] = (zero_row << PLANE_SHIFT) + capacity
    chunks = start >> UNROLL.bit_length() - 1
    zero = jnp.zeros((16, 128), jnp.bfloat16)

    def read(which):
        entry = list_ref[which]
        slot = entry & ((1 << TILE_SHIFT) - 1)
        plane = (entry >> PLANE_SHIFT) & ((1 << (SOURCE_SHIFT - PLANE_SHIFT)) - 1)
        source = entry >> SOURCE_SHIFT
        row = 3 * slot + source * (stride - 3 * (capacity + 1))
        table = jnp.broadcast_to(table_ref[pl.ds(plane, 1), :], (8, 128))

        def words(i):
            return got_ref[pl.ds(row + i, 1), :]

        def parts(shift):
            start = (words(1) >> shift) & 0xFFFF
            offset = ((words(2) >> shift) & 7) << 4
            return spread_parts(
                jnp.broadcast_to(start, (8, 128)), jnp.broadcast_to(offset, (8, 128)), table
            )

        def sample(part):
            step = about_ref[source, 1, tiles].astype(jnp.float32) * (1.0 / (FULL * SCALE))
            return ((words(0) << (16 * part)) >> 16).astype(jnp.float32) * step

        return slot, sample, parts

    def chunk_tile(turn):
        return (list_ref[turn * UNROLL] >> TILE_SHIFT) & 15

    def front(turn, which):
        row_ref, picked_ref = row_refs[which % len(row_refs)], picked_refs[which % len(picked_refs)]
        blocks = [read(turn * UNROLL + u) for u in range(UNROLL)]
        for u, (_, _, parts) in enumerate(blocks):
            taps, group = parts(16)
            taps = taps.astype(jnp.bfloat16)
            group = group.astype(jnp.float32).astype(jnp.bfloat16)
            for k in range(groups):
                row_ref[16 * k : 16 * k + 16, 128 * u : 128 * u + 128] = jnp.where(
                    group == k, taps, zero
                )
        partial = jnp.dot(
            turned_ref[chunk_tile(turn)], row_ref[...], preferred_element_type=jnp.float32
        )
        for u, (_, _, parts) in enumerate(blocks):
            columns = slice(128 * u, 128 * u + 128)
            taps, group = parts(0)
            for part in range(2):
                picked = jnp.zeros((16, 128), jnp.float32)
                for k in range(groups):
                    low = part * side + 16 * k
                    picked = jnp.where(group == k, partial[low : low + 16, columns], picked)
                picked_ref[part, :, columns] = picked * taps

    def back(turn, which):
        row_ref, picked_ref = row_refs[which % len(row_refs)], picked_refs[which % len(picked_refs)]
        weighted = []
        for u in range(UNROLL):
            slot, sample, parts = read(turn * UNROLL + u)
            columns = slice(128 * u, 128 * u + 128)
            taps, group = parts(0)
            group = group.astype(jnp.float32).astype(jnp.bfloat16)
            residuals, pieces = [], []
            for part in range(2):
                model = jnp.sum(picked_ref[part, :, columns], axis=0, keepdims=True)
                residual = sample(part) - model
                residuals.append(residual)
                value = (residual * taps).astype(jnp.bfloat16)
                pieces += [jnp.where(group == k, value, zero) for k in range(groups)]
            residual_ref[slot] = jnp.concatenate(residuals, axis=0).astype(jnp.bfloat16)
            weighted.append(jnp.concatenate(pieces, axis=0))
        grid_ref[chunk_tile(turn)] += lax.dot_general(
            jnp.concatenate(weighted, axis=1),
            row_ref[...],
            (((1,), (1,)), ((), ())),
            preferred_element_type=jnp.float32,
        )

    def step(turn, carry):
        for which in range(CHUNKS):
            front(turn * CHUNKS + which + AHEAD, which + AHEAD)
            back(turn * CHUNKS + which, which)
        return carry

    for which in range(AHEAD):
        front(which, which)
    lax.fori_loop(0, scalar_div(chunks + CHUNKS - 1, CHUNKS), step, 0)
    half = tiles // 2
    member = member_ref[0]
    for t in range(half):
        own_ref[t] = grid_ref[member * half + t]
        other_ref[t] = grid_ref[(1 - member) * half + t].astype(jnp.bfloat16)


def body(visibilities, uv_cell, sub_pixel, w_plane, block_tile, model_grid, kernel_table, coupling):
    owners = lax.axis_size("tile")
    pairs = owners // 2
    _, blocks, _, rows = visibilities.shape
    capacity = 2 * (3 * blocks // owners)
    _, tiles_here, side, wide = model_grid.shape
    planes, oversample, support = kernel_table.shape
    slots = pairs * (capacity + 1)
    member = lax.axis_index("tile") // pairs
    swap = [(t, (t + pairs) % owners) for t in range(owners)]
    halves = [list(range(pairs)), list(range(pairs, owners))]

    model_own = model_grid[0]
    model_other = lax.ppermute(model_own, "tile", swap)
    sent, slot = pl.pallas_call(
        lambda *refs: pack_kernel(pairs, capacity, tiles_here, planes, *refs),
        out_shape=(
            jax.ShapeDtypeStruct((pairs * rows_per_source(capacity), rows), jnp.int32),
            jax.ShapeDtypeStruct((blocks,), jnp.int32),
        ),
        in_specs=[HBM] * 5,
        out_specs=(VMEM, SMEM),
        scratch_shapes=[
            pltpu.SMEM((blocks,), jnp.int32),
            pltpu.SMEM((blocks,), jnp.int32),
            pltpu.VMEM((blocks, 2, rows), jnp.float32),
            pltpu.VMEM((blocks, 2, rows), jnp.int32),
            pltpu.VMEM((blocks, 2, rows), jnp.int32),
            pltpu.SMEM((pairs, 2, rows), jnp.int32),
            pltpu.VMEM((pairs, 2, rows), jnp.int32),
            pltpu.SMEM((pairs * 2 * tiles_here,), jnp.int32),
            pltpu.SemaphoreType.DMA((5,)),
            pltpu.SemaphoreType.DMA,
        ],
        compiler_params=WHOLE_PARAMS,
        name="pack_blocks",
    )(w_plane[0], block_tile[0], visibilities[0], uv_cell[0], sub_pixel[0])
    sent, model_other = lax.optimization_barrier((sent, model_other))
    got = lax.all_to_all(
        sent, "tile", split_axis=0, concat_axis=0, tiled=True, axis_index_groups=halves
    )
    own_row = lax.dynamic_index_in_dim(coupling, lax.axis_index("freq"), 0, keepdims=False)
    slot, own_row, got = lax.optimization_barrier(
        (slot + lax.div(lax.axis_index("tile"), owners), own_row, got)
    )
    model = jnp.where(
        member == 0,
        jnp.concatenate([model_own, model_other]),
        jnp.concatenate([model_other, model_own]),
    )
    table = jnp.pad(
        kernel_table.astype(jnp.float32), ((0, 8), (0, 0), (0, 16 - support))
    ).reshape(planes + 8, 16 * oversample)
    residual, own, other = pl.pallas_call(
        lambda *refs: grid_kernel(pairs, capacity, *refs),
        out_shape=(
            jax.ShapeDtypeStruct((slots, 2, rows), jnp.bfloat16),
            jax.ShapeDtypeStruct((tiles_here, wide, side), jnp.float32),
            jax.ShapeDtypeStruct((tiles_here, wide, side), jnp.bfloat16),
        ),
        in_specs=[SMEM, VMEM, VMEM, VMEM],
        out_specs=(VMEM, VMEM, VMEM),
        scratch_shapes=[
            pltpu.VMEM((2 * tiles_here, wide, side), jnp.bfloat16),
            pltpu.VMEM((2 * tiles_here, wide, side), jnp.float32),
            pltpu.VMEM((pairs, 2, rows), jnp.int32),
            pltpu.SMEM((pairs, 2, rows), jnp.int32),
            pltpu.SMEM(
                (slots + capacity + (2 * tiles_here + CHUNKS + AHEAD) * UNROLL,), jnp.int32
            ),
            pltpu.SemaphoreType.DMA,
            *[pltpu.VMEM((side, UNROLL * rows), jnp.bfloat16)] * BUFFERS,
            *[pltpu.VMEM((2, 16, UNROLL * rows), jnp.float32)] * BUFFERS,
        ],
        compiler_params=PARAMS,
        name="grid_blocks",
    )(member[None], got, table, model)

    returned = lax.all_to_all(
        residual, "tile", split_axis=0, concat_axis=0, tiled=True, axis_index_groups=halves
    )
    grid_sum = own + lax.ppermute(other, "tile", swap).astype(jnp.float32)
    grids = lax.all_gather(grid_sum.astype(jnp.bfloat16)[None], "freq", axis=0, tiled=True)
    residuals, coupled_grid = pl.pallas_call(
        finish_kernel,
        out_shape=(
            jax.ShapeDtypeStruct((blocks, 2, rows), jnp.float32),
            jax.ShapeDtypeStruct((tiles_here, side, wide), jnp.float32),
        ),
        in_specs=[SMEM, SMEM, VMEM, VMEM],
        out_specs=(VMEM, VMEM),
        compiler_params=PARAMS,
        name="finish",
    )(own_row, slot, returned, grids)
    return (residuals[None], coupled_grid[None])


def solution(mesh):
    return jax.shard_map(
        body,
        mesh=mesh,
        in_specs=(
            P("freq", "tile", None, None),
            P("freq", "tile", None, None),
            P("freq", "tile", None, None),
            P("freq", "tile"),
            P("freq", "tile"),
            P("freq", "tile", None, None),
            P(),
            P(),
        ),
        out_specs=(P("freq", "tile", None, None), P("freq", "tile", None, None)),
        check_vma=False,
    )
```

```python
import jax
import jax.numpy as jnp
from jax import lax
from jax.experimental import pallas as pl
from jax.experimental.pallas import tpu as pltpu
from jax.sharding import PartitionSpec as P

UNROLL = 2
CHUNKS = 35
AHEAD = 2
BUFFERS = 5
VMEM = pl.BlockSpec(memory_space=pltpu.VMEM)
SMEM = pl.BlockSpec(memory_space=pltpu.SMEM)
HBM = pl.BlockSpec(memory_space=pltpu.HBM)
PARAMS = pltpu.CompilerParams(vmem_limit_bytes=32 * 1024 * 1024)
WHOLE_PARAMS = pltpu.CompilerParams(vmem_limit_bytes=62 * 1024 * 1024)
TILE_SHIFT = 12
PLANE_SHIFT = 16
SOURCE_SHIFT = 21
FULL = 32767
SCALE = 2.0**20


def scalar_div(value, count):
    shift = count.bit_length() - 1
    return value >> shift if count == 1 << shift else lax.div(value, count)


def first_slot(local, rank, capacity):
    half = capacity // 2
    return (local >> 1) * half + jnp.where((local & 1) == 0, rank, half - 1 - rank)


def rows_per_source(capacity):
    return (3 * (capacity + 1) + 7) // 8 * 8


def two_halves(high, low):
    return (high << 16) | (low & 0xFFFF)


def pack_kernel(pairs, capacity, tiles_here, planes, plane_hbm, tile_hbm, vis_hbm, cell_hbm, sub_hbm,
                sent_ref, slot_ref, plane_ref, tile_ref, vis_ref, cell_ref, sub_ref, about_ref, turned_ref,
                count_ref, load_sem, about_sem):
    blocks = tile_ref.shape[0]
    stride = rows_per_source(capacity)
    loads = [
        pltpu.make_async_copy(source, target, load_sem.at[i])
        for i, (source, target) in enumerate(
            [
                (tile_hbm, tile_ref),
                (plane_hbm, plane_ref),
                (vis_hbm, vis_ref),
                (cell_hbm, cell_ref),
                (sub_hbm, sub_ref),
            ]
        )
    ]
    for copy in loads:
        copy.start()
    for d in range(pairs):
        for t in range(2 * tiles_here):
            count_ref[d * 2 * tiles_here + t] = 0
    for copy in loads[:2]:
        copy.wait()

    def assign(b):
        tile = tile_ref[b]
        owner = scalar_div(tile, tiles_here)
        high = (owner >= pairs).astype(jnp.int32)
        pair = owner - high * pairs
        local = tile - (owner - high) * tiles_here
        key = pair * (2 * tiles_here) + local
        rank = count_ref[key]
        count_ref[key] = rank + 1
        place = first_slot(local, rank, capacity)
        slot_ref[b] = pair * (capacity + 1) + place
        about_ref[pair, 0, place] = plane_ref[b] << PLANE_SHIFT

    def each(work):
        def step(turn, carry):
            for which in range(8):
                work(turn * 8 + which)
            return carry

        lax.fori_loop(0, blocks // 8, step, 0)

    each(assign)
    for d in range(pairs):
        for t in range(2 * tiles_here):
            about_ref[d, 1, t] = count_ref[d * 2 * tiles_here + t]
    turn_about = pltpu.make_async_copy(about_ref, turned_ref, about_sem)
    turn_about.start()
    for copy in loads[2:]:
        copy.wait()
    largest = jnp.max(jnp.max(jnp.abs(vis_ref[...]), axis=0), keepdims=True)
    largest = jnp.maximum(jnp.ceil(largest * SCALE), 1.0)
    inverse = (FULL * SCALE) / largest

    def move(b):
        slot = slot_ref[b]
        row = 3 * slot + scalar_div(slot, capacity + 1) * (stride - 3 * (capacity + 1))
        value = jnp.clip(jnp.round(vis_ref[b] * inverse), -FULL, FULL).astype(jnp.int32)
        for i, pair in enumerate([value, cell_ref[b], sub_ref[b]]):
            sent_ref[pl.ds(row + i, 1), :] = two_halves(pair[0:1], pair[1:2])

    each(move)
    turn_about.wait()
    lane = lax.broadcasted_iota(jnp.int32, (1, 128), 1)
    for d in range(pairs):
        row = d * stride + 3 * capacity
        sent_ref[row : row + 1, :] = turned_ref[d, 0:1, :]
        sent_ref[row + 1 : row + 2, :] = jnp.zeros((1, 128), jnp.int32)
        sent_ref[row + 2 : row + 3, :] = jnp.where(
            lane < 2 * tiles_here, turned_ref[d, 1:2, :], largest.astype(jnp.int32)
        )


def finish_kernel(row_ref, slot_ref, returned_ref, grid_ref, residual_ref, coupled_ref):
    planes, tiles_here = grid_ref.shape[:2]
    for t in range(tiles_here):
        coupled_ref[t] = sum(
            row_ref[g] * grid_ref[g, t].astype(jnp.float32) for g in range(planes)
        ).T

    def step(turn, carry):
        for which in range(8):
            b = turn * 8 + which
            residual_ref[b] = returned_ref[slot_ref[b]].astype(jnp.float32)
        return carry

    lax.fori_loop(0, residual_ref.shape[0] // 8, step, 0)


def spread_parts(start, offset, table):
    sublane = lax.broadcasted_iota(jnp.int32, (8, 128), 0)
    taps, group = [], []
    for low in (0, 8):
        delta = sublane + low - start
        taps.append(
            jnp.take_along_axis(table, (delta & 15) + offset, axis=1, mode="promise_in_bounds")
        )
        group.append((15 - delta) >> 4)
    return jnp.concatenate(taps, axis=0), jnp.concatenate(group, axis=0)


def grid_kernel(pairs, capacity, member_ref, got_ref, table_ref, model_ref, residual_ref, own_ref,
                other_ref, turned_ref, grid_ref, code_ref, about_ref, list_ref, sem, *buffers):
    row_refs, picked_refs = buffers[:BUFFERS], buffers[BUFFERS:]
    tiles, side, wide = model_ref.shape
    groups = side // 16
    zero_row = table_ref.shape[0] - 8
    stride = rows_per_source(capacity)
    lane = lax.broadcasted_iota(jnp.int32, (1, 128), 1)
    for s in range(pairs):
        row = s * stride + 3 * capacity
        code_ref[s, 0:1, :] = got_ref[row : row + 1, :] + (
            lane + s * (capacity + 1) + (s << SOURCE_SHIFT)
        )
        code_ref[s, 1:2, :] = got_ref[row + 2 : row + 3, :]
    fill = pltpu.make_async_copy(code_ref, about_ref, sem)
    fill.start()
    for t in range(tiles):
        turned_ref[t] = model_ref[t].T
    grid_ref[...] = jnp.zeros_like(grid_ref)
    fill.wait()

    start = jnp.int32(0)
    for t in range(tiles):
        count = jnp.int32(0)
        for s in range(pairs):
            count = count + about_ref[s, 1, t]
        spare = -count & (UNROLL - 1)
        for u in range(UNROLL):
            list_ref[start + u] = (zero_row << PLANE_SHIFT) + (t << TILE_SHIFT) + capacity

        def enlist(s, filled, t=t):
            first = t // 2 * (capacity // 2)
            found = about_ref[s, 1, t]

            def some(turn, carry):
                for which in range(16):
                    k = turn * 16 + which
                    place = k if t % 2 == 0 else capacity // 2 - 1 - k
                    code = about_ref[s, 0, jnp.maximum(first + place, 0)]
                    list_ref[filled + k] = code + (t << TILE_SHIFT)
                return carry

            lax.fori_loop(0, (found + 15) >> 4, some, 0)
            return filled + found

        lax.fori_loop(0, pairs, enlist, start + spare)
        start = start + count + spare
    for u in range((CHUNKS + AHEAD) * UNROLL):
        list_ref[start + u] = (zero_row << PLANE_SHIFT) + capacity
    chunks = start >> UNROLL.bit_length() - 1
    zero = jnp.zeros((16, 128), jnp.bfloat16)

    def read(which):
        entry = list_ref[which]
        slot = entry & ((1 << TILE_SHIFT) - 1)
        plane = (entry >> PLANE_SHIFT) & ((1 << (SOURCE_SHIFT - PLANE_SHIFT)) - 1)
        source = entry >> SOURCE_SHIFT
        row = 3 * slot + source * (stride - 3 * (capacity + 1))
        table = jnp.broadcast_to(table_ref[pl.ds(plane, 1), :], (8, 128))

        def words(i):
            return got_ref[pl.ds(row + i, 1), :]

        def parts(shift):
            start = (words(1) >> shift) & 0xFFFF
            offset = ((words(2) >> shift) & 7) << 4
            return spread_parts(
                jnp.broadcast_to(start, (8, 128)), jnp.broadcast_to(offset, (8, 128)), table
            )

        def sample(part):
            step = about_ref[source, 1, tiles].astype(jnp.float32) * (1.0 / (FULL * SCALE))
            return ((words(0) << (16 * part)) >> 16).astype(jnp.float32) * step

        return slot, sample, parts

    def chunk_tile(turn):
        return (list_ref[turn * UNROLL] >> TILE_SHIFT) & 15

    def front(turn, which):
        row_ref, picked_ref = row_refs[which % len(row_refs)], picked_refs[which % len(picked_refs)]
        blocks = [read(turn * UNROLL + u) for u in range(UNROLL)]
        for u, (_, _, parts) in enumerate(blocks):
            taps, group = parts(16)
            taps = taps.astype(jnp.bfloat16)
            group = group.astype(jnp.float32).astype(jnp.bfloat16)
            for k in range(groups):
                row_ref[16 * k : 16 * k + 16, 128 * u : 128 * u + 128] = jnp.where(
                    group == k, taps, zero
                )
        partial = jnp.dot(
            turned_ref[chunk_tile(turn)], row_ref[...], preferred_element_type=jnp.float32
        )
        for u, (_, _, parts) in enumerate(blocks):
            columns = slice(128 * u, 128 * u + 128)
            taps, group = parts(0)
            for part in range(2):
                picked = jnp.zeros((16, 128), jnp.float32)
                for k in range(groups):
                    low = part * side + 16 * k
                    picked = jnp.where(group == k, partial[low : low + 16, columns], picked)
                picked_ref[part, :, columns] = picked * taps

    def back(turn, which):
        row_ref, picked_ref = row_refs[which % len(row_refs)], picked_refs[which % len(picked_refs)]
        weighted = []
        for u in range(UNROLL):
            slot, sample, parts = read(turn * UNROLL + u)
            columns = slice(128 * u, 128 * u + 128)
            taps, group = parts(0)
            group = group.astype(jnp.float32).astype(jnp.bfloat16)
            residuals, pieces = [], []
            for part in range(2):
                model = jnp.sum(picked_ref[part, :, columns], axis=0, keepdims=True)
                residual = sample(part) - model
                residuals.append(residual)
                value = (residual * taps).astype(jnp.bfloat16)
                pieces += [jnp.where(group == k, value, zero) for k in range(groups)]
            residual_ref[slot] = jnp.concatenate(residuals, axis=0).astype(jnp.bfloat16)
            weighted.append(jnp.concatenate(pieces, axis=0))
        grid_ref[chunk_tile(turn)] += lax.dot_general(
            jnp.concatenate(weighted, axis=1),
            row_ref[...],
            (((1,), (1,)), ((), ())),
            preferred_element_type=jnp.float32,
        )

    def step(turn, carry):
        for which in range(CHUNKS):
            front(turn * CHUNKS + which + AHEAD, which + AHEAD)
            back(turn * CHUNKS + which, which)
        return carry

    for which in range(AHEAD):
        front(which, which)
    lax.fori_loop(0, scalar_div(chunks + CHUNKS - 1, CHUNKS), step, 0)
    half = tiles // 2
    member = member_ref[0]
    for t in range(half):
        own_ref[t] = grid_ref[member * half + t]
        other_ref[t] = grid_ref[(1 - member) * half + t].astype(jnp.bfloat16)


def body(visibilities, uv_cell, sub_pixel, w_plane, block_tile, model_grid, kernel_table, coupling):
    owners = lax.axis_size("tile")
    pairs = owners // 2
    _, blocks, _, rows = visibilities.shape
    capacity = 2 * (3 * blocks // owners)
    _, tiles_here, side, wide = model_grid.shape
    planes, oversample, support = kernel_table.shape
    slots = pairs * (capacity + 1)
    member = lax.axis_index("tile") // pairs
    swap = [(t, (t + pairs) % owners) for t in range(owners)]
    halves = [list(range(pairs)), list(range(pairs, owners))]

    model = lax.all_gather(
        model_grid[0],
        "tile",
        axis=0,
        tiled=True,
        axis_index_groups=[[t, t + pairs] for t in range(pairs)],
    )
    sent, slot = pl.pallas_call(
        lambda *refs: pack_kernel(pairs, capacity, tiles_here, planes, *refs),
        out_shape=(
            jax.ShapeDtypeStruct((pairs * rows_per_source(capacity), rows), jnp.int32),
            jax.ShapeDtypeStruct((blocks,), jnp.int32),
        ),
        in_specs=[HBM] * 5,
        out_specs=(VMEM, SMEM),
        scratch_shapes=[
            pltpu.SMEM((blocks,), jnp.int32),
            pltpu.SMEM((blocks,), jnp.int32),
            pltpu.VMEM((blocks, 2, rows), jnp.float32),
            pltpu.VMEM((blocks, 2, rows), jnp.int32),
            pltpu.VMEM((blocks, 2, rows), jnp.int32),
            pltpu.SMEM((pairs, 2, rows), jnp.int32),
            pltpu.VMEM((pairs, 2, rows), jnp.int32),
            pltpu.SMEM((pairs * 2 * tiles_here,), jnp.int32),
            pltpu.SemaphoreType.DMA((5,)),
            pltpu.SemaphoreType.DMA,
        ],
        compiler_params=WHOLE_PARAMS,
        name="pack_blocks",
    )(w_plane[0], block_tile[0], visibilities[0], uv_cell[0], sub_pixel[0])
    got = lax.all_to_all(
        sent, "tile", split_axis=0, concat_axis=0, tiled=True, axis_index_groups=halves
    )
    own_row = lax.dynamic_index_in_dim(coupling, lax.axis_index("freq"), 0, keepdims=False)
    slot, own_row, got = lax.optimization_barrier(
        (slot + lax.div(lax.axis_index("tile"), owners), own_row, got)
    )
    table = jnp.pad(
        kernel_table.astype(jnp.float32), ((0, 8), (0, 0), (0, 16 - support))
    ).reshape(planes + 8, 16 * oversample)
    residual, own, other = pl.pallas_call(
        lambda *refs: grid_kernel(pairs, capacity, *refs),
        out_shape=(
            jax.ShapeDtypeStruct((slots, 2, rows), jnp.bfloat16),
            jax.ShapeDtypeStruct((tiles_here, wide, side), jnp.float32),
            jax.ShapeDtypeStruct((tiles_here, wide, side), jnp.bfloat16),
        ),
        in_specs=[SMEM, VMEM, VMEM, VMEM],
        out_specs=(VMEM, VMEM, VMEM),
        scratch_shapes=[
            pltpu.VMEM((2 * tiles_here, wide, side), jnp.bfloat16),
            pltpu.VMEM((2 * tiles_here, wide, side), jnp.float32),
            pltpu.VMEM((pairs, 2, rows), jnp.int32),
            pltpu.SMEM((pairs, 2, rows), jnp.int32),
            pltpu.SMEM(
                (slots + capacity + (2 * tiles_here + CHUNKS + AHEAD) * UNROLL,), jnp.int32
            ),
            pltpu.SemaphoreType.DMA,
            *[pltpu.VMEM((side, UNROLL * rows), jnp.bfloat16)] * BUFFERS,
            *[pltpu.VMEM((2, 16, UNROLL * rows), jnp.float32)] * BUFFERS,
        ],
        compiler_params=PARAMS,
        name="grid_blocks",
    )(member[None], got, table, model)

    returned = lax.all_to_all(
        residual, "tile", split_axis=0, concat_axis=0, tiled=True, axis_index_groups=halves
    )
    grid_sum = own + lax.ppermute(other, "tile", swap).astype(jnp.float32)
    grids = lax.all_gather(grid_sum.astype(jnp.bfloat16)[None], "freq", axis=0, tiled=True)
    residuals, coupled_grid = pl.pallas_call(
        finish_kernel,
        out_shape=(
            jax.ShapeDtypeStruct((blocks, 2, rows), jnp.float32),
            jax.ShapeDtypeStruct((tiles_here, side, wide), jnp.float32),
        ),
        in_specs=[SMEM, SMEM, VMEM, VMEM],
        out_specs=(VMEM, VMEM),
        compiler_params=PARAMS,
        name="finish",
    )(own_row, slot, returned, grids)
    return (residuals[None], coupled_grid[None])


def solution(mesh):
    return jax.shard_map(
        body,
        mesh=mesh,
        in_specs=(
            P("freq", "tile", None, None),
            P("freq", "tile", None, None),
            P("freq", "tile", None, None),
            P("freq", "tile"),
            P("freq", "tile"),
            P("freq", "tile", None, None),
            P(),
            P(),
        ),
        out_specs=(P("freq", "tile", None, None), P("freq", "tile", None, None)),
        check_vma=False,
    )
```

```python
import jax
import jax.numpy as jnp
from jax import lax
from jax.experimental import pallas as pl
from jax.experimental.pallas import tpu as pltpu
from jax.sharding import PartitionSpec as P

UNROLL = 2
CHUNKS = 35
AHEAD = 3
BUFFERS = 5
VMEM = pl.BlockSpec(memory_space=pltpu.VMEM)
SMEM = pl.BlockSpec(memory_space=pltpu.SMEM)
HBM = pl.BlockSpec(memory_space=pltpu.HBM)
PARAMS = pltpu.CompilerParams(vmem_limit_bytes=32 * 1024 * 1024)
WHOLE_PARAMS = pltpu.CompilerParams(vmem_limit_bytes=62 * 1024 * 1024)
TILE_SHIFT = 12
PLANE_SHIFT = 16
SOURCE_SHIFT = 21
FULL = 32767
SCALE = 2.0**20


def scalar_div(value, count):
    shift = count.bit_length() - 1
    return value >> shift if count == 1 << shift else lax.div(value, count)


def first_slot(local, rank, capacity):
    half = capacity // 2
    return (local >> 1) * half + jnp.where((local & 1) == 0, rank, half - 1 - rank)


def rows_per_source(capacity):
    return (3 * (capacity + 1) + 7) // 8 * 8


def two_halves(high, low):
    return (high << 16) | (low & 0xFFFF)


def pack_kernel(pairs, capacity, tiles_here, planes, plane_hbm, tile_hbm, vis_hbm, cell_hbm, sub_hbm,
                sent_ref, slot_ref, plane_ref, tile_ref, vis_ref, cell_ref, sub_ref, about_ref, turned_ref,
                count_ref, load_sem, about_sem):
    blocks = tile_ref.shape[0]
    stride = rows_per_source(capacity)
    loads = [
        pltpu.make_async_copy(source, target, load_sem.at[i])
        for i, (source, target) in enumerate(
            [
                (tile_hbm, tile_ref),
                (plane_hbm, plane_ref),
                (vis_hbm, vis_ref),
                (cell_hbm, cell_ref),
                (sub_hbm, sub_ref),
            ]
        )
    ]
    for copy in loads:
        copy.start()
    for d in range(pairs):
        for t in range(2 * tiles_here):
            count_ref[d * 2 * tiles_here + t] = 0
    for copy in loads[:2]:
        copy.wait()

    def assign(b):
        tile = tile_ref[b]
        owner = scalar_div(tile, tiles_here)
        high = (owner >= pairs).astype(jnp.int32)
        pair = owner - high * pairs
        local = tile - (owner - high) * tiles_here
        key = pair * (2 * tiles_here) + local
        rank = count_ref[key]
        count_ref[key] = rank + 1
        place = first_slot(local, rank, capacity)
        slot_ref[b] = pair * (capacity + 1) + place
        about_ref[pair, 0, place] = plane_ref[b] << PLANE_SHIFT

    def each(work):
        def step(turn, carry):
            for which in range(8):
                work(turn * 8 + which)
            return carry

        lax.fori_loop(0, blocks // 8, step, 0)

    each(assign)
    for d in range(pairs):
        for t in range(2 * tiles_here):
            about_ref[d, 1, t] = count_ref[d * 2 * tiles_here + t]
    turn_about = pltpu.make_async_copy(about_ref, turned_ref, about_sem)
    turn_about.start()
    for copy in loads[2:]:
        copy.wait()
    largest = jnp.max(jnp.max(jnp.abs(vis_ref[...]), axis=0), keepdims=True)
    largest = jnp.maximum(jnp.ceil(largest * SCALE), 1.0)
    inverse = (FULL * SCALE) / largest

    def move(b):
        slot = slot_ref[b]
        row = 3 * slot + scalar_div(slot, capacity + 1) * (stride - 3 * (capacity + 1))
        value = jnp.clip(jnp.round(vis_ref[b] * inverse), -FULL, FULL).astype(jnp.int32)
        for i, pair in enumerate([value, cell_ref[b], sub_ref[b]]):
            sent_ref[pl.ds(row + i, 1), :] = two_halves(pair[0:1], pair[1:2])

    each(move)
    turn_about.wait()
    lane = lax.broadcasted_iota(jnp.int32, (1, 128), 1)
    for d in range(pairs):
        row = d * stride + 3 * capacity
        sent_ref[row : row + 1, :] = turned_ref[d, 0:1, :]
        sent_ref[row + 1 : row + 2, :] = jnp.zeros((1, 128), jnp.int32)
        sent_ref[row + 2 : row + 3, :] = jnp.where(
            lane < 2 * tiles_here, turned_ref[d, 1:2, :], largest.astype(jnp.int32)
        )


def finish_kernel(row_ref, slot_ref, returned_ref, grid_ref, residual_ref, coupled_ref):
    planes, tiles_here = grid_ref.shape[:2]
    for t in range(tiles_here):
        coupled_ref[t] = sum(
            row_ref[g] * grid_ref[g, t].astype(jnp.float32) for g in range(planes)
        ).T

    def step(turn, carry):
        for which in range(8):
            b = turn * 8 + which
            residual_ref[b] = returned_ref[slot_ref[b]].astype(jnp.float32)
        return carry

    lax.fori_loop(0, residual_ref.shape[0] // 8, step, 0)


def spread_parts(start, offset, table):
    sublane = lax.broadcasted_iota(jnp.int32, (8, 128), 0)
    taps, group = [], []
    for low in (0, 8):
        delta = sublane + low - start
        taps.append(
            jnp.take_along_axis(table, (delta & 15) + offset, axis=1, mode="promise_in_bounds")
        )
        group.append((15 - delta) >> 4)
    return jnp.concatenate(taps, axis=0), jnp.concatenate(group, axis=0)


def grid_kernel(pairs, capacity, member_ref, got_ref, table_ref, model_ref, residual_ref, own_ref,
                other_ref, turned_ref, grid_ref, code_ref, about_ref, list_ref, sem, *buffers):
    row_refs, picked_refs, taps_refs, group_refs = (
        buffers[i * BUFFERS : (i + 1) * BUFFERS] for i in range(4)
    )
    tiles, side, wide = model_ref.shape
    groups = side // 16
    zero_row = table_ref.shape[0] - 8
    stride = rows_per_source(capacity)
    lane = lax.broadcasted_iota(jnp.int32, (1, 128), 1)
    for s in range(pairs):
        row = s * stride + 3 * capacity
        code_ref[s, 0:1, :] = got_ref[row : row + 1, :] + (
            lane + s * (capacity + 1) + (s << SOURCE_SHIFT)
        )
        code_ref[s, 1:2, :] = got_ref[row + 2 : row + 3, :]
    fill = pltpu.make_async_copy(code_ref, about_ref, sem)
    fill.start()
    for t in range(tiles):
        turned_ref[t] = model_ref[t].T
    grid_ref[...] = jnp.zeros_like(grid_ref)
    fill.wait()

    start = jnp.int32(0)
    for t in range(tiles):
        count = jnp.int32(0)
        for s in range(pairs):
            count = count + about_ref[s, 1, t]
        spare = -count & (UNROLL - 1)
        for u in range(UNROLL):
            list_ref[start + u] = (zero_row << PLANE_SHIFT) + (t << TILE_SHIFT) + capacity

        def enlist(s, filled, t=t):
            first = t // 2 * (capacity // 2)
            found = about_ref[s, 1, t]

            def some(turn, carry):
                for which in range(16):
                    k = turn * 16 + which
                    place = k if t % 2 == 0 else capacity // 2 - 1 - k
                    code = about_ref[s, 0, jnp.maximum(first + place, 0)]
                    list_ref[filled + k] = code + (t << TILE_SHIFT)
                return carry

            lax.fori_loop(0, (found + 15) >> 4, some, 0)
            return filled + found

        lax.fori_loop(0, pairs, enlist, start + spare)
        start = start + count + spare
    for u in range((CHUNKS + AHEAD) * UNROLL):
        list_ref[start + u] = (zero_row << PLANE_SHIFT) + capacity
    chunks = start >> UNROLL.bit_length() - 1
    zero = jnp.zeros((16, 128), jnp.bfloat16)

    def read(which):
        entry = list_ref[which]
        slot = entry & ((1 << TILE_SHIFT) - 1)
        plane = (entry >> PLANE_SHIFT) & ((1 << (SOURCE_SHIFT - PLANE_SHIFT)) - 1)
        source = entry >> SOURCE_SHIFT
        row = 3 * slot + source * (stride - 3 * (capacity + 1))
        table = jnp.broadcast_to(table_ref[pl.ds(plane, 1), :], (8, 128))

        def words(i):
            return got_ref[pl.ds(row + i, 1), :]

        def parts(shift):
            start = (words(1) >> shift) & 0xFFFF
            offset = ((words(2) >> shift) & 7) << 4
            return spread_parts(
                jnp.broadcast_to(start, (8, 128)), jnp.broadcast_to(offset, (8, 128)), table
            )

        def sample(part):
            step = about_ref[source, 1, tiles].astype(jnp.float32) * (1.0 / (FULL * SCALE))
            return ((words(0) << (16 * part)) >> 16).astype(jnp.float32) * step

        return slot, sample, parts

    def chunk_tile(turn):
        return (list_ref[turn * UNROLL] >> TILE_SHIFT) & 15

    def front(turn, which):
        row_ref, picked_ref = row_refs[which % BUFFERS], picked_refs[which % BUFFERS]
        taps_ref, group_ref = taps_refs[which % BUFFERS], group_refs[which % BUFFERS]
        blocks = [read(turn * UNROLL + u) for u in range(UNROLL)]
        for u, (_, _, parts) in enumerate(blocks):
            taps, group = parts(16)
            taps = taps.astype(jnp.bfloat16)
            group = group.astype(jnp.float32).astype(jnp.bfloat16)
            for k in range(groups):
                row_ref[16 * k : 16 * k + 16, 128 * u : 128 * u + 128] = jnp.where(
                    group == k, taps, zero
                )
        partial = jnp.dot(
            turned_ref[chunk_tile(turn)], row_ref[...], preferred_element_type=jnp.float32
        )
        for u, (_, _, parts) in enumerate(blocks):
            columns = slice(128 * u, 128 * u + 128)
            taps, group = parts(0)
            for part in range(2):
                picked = jnp.zeros((16, 128), jnp.float32)
                for k in range(groups):
                    low = part * side + 16 * k
                    picked = jnp.where(group == k, partial[low : low + 16, columns], picked)
                picked_ref[part, :, columns] = picked * taps
            taps_ref[:, columns] = taps
            group_ref[:, columns] = group.astype(jnp.float32).astype(jnp.bfloat16)

    def back(turn, which):
        row_ref, picked_ref = row_refs[which % BUFFERS], picked_refs[which % BUFFERS]
        taps_ref, group_ref = taps_refs[which % BUFFERS], group_refs[which % BUFFERS]
        weighted = []
        for u in range(UNROLL):
            slot, sample, _ = read(turn * UNROLL + u)
            columns = slice(128 * u, 128 * u + 128)
            taps, group = taps_ref[:, columns], group_ref[:, columns]
            residuals, pieces = [], []
            for part in range(2):
                model = jnp.sum(picked_ref[part, :, columns], axis=0, keepdims=True)
                residual = sample(part) - model
                residuals.append(residual)
                value = (residual * taps).astype(jnp.bfloat16)
                pieces += [jnp.where(group == k, value, zero) for k in range(groups)]
            residual_ref[slot] = jnp.concatenate(residuals, axis=0).astype(jnp.bfloat16)
            weighted.append(jnp.concatenate(pieces, axis=0))
        grid_ref[chunk_tile(turn)] += lax.dot_general(
            jnp.concatenate(weighted, axis=1),
            row_ref[...],
            (((1,), (1,)), ((), ())),
            preferred_element_type=jnp.float32,
        )

    def step(turn, carry):
        for which in range(CHUNKS):
            front(turn * CHUNKS + which + AHEAD, which + AHEAD)
            back(turn * CHUNKS + which, which)
        return carry

    for which in range(AHEAD):
        front(which, which)
    lax.fori_loop(0, scalar_div(chunks + CHUNKS - 1, CHUNKS), step, 0)
    half = tiles // 2
    member = member_ref[0]
    for t in range(half):
        own_ref[t] = grid_ref[member * half + t]
        other_ref[t] = grid_ref[(1 - member) * half + t].astype(jnp.bfloat16)


def body(visibilities, uv_cell, sub_pixel, w_plane, block_tile, model_grid, kernel_table, coupling):
    owners = lax.axis_size("tile")
    pairs = owners // 2
    _, blocks, _, rows = visibilities.shape
    capacity = 2 * (3 * blocks // owners)
    _, tiles_here, side, wide = model_grid.shape
    planes, oversample, support = kernel_table.shape
    slots = pairs * (capacity + 1)
    member = lax.axis_index("tile") // pairs
    swap = [(t, (t + pairs) % owners) for t in range(owners)]
    halves = [list(range(pairs)), list(range(pairs, owners))]

    model = lax.all_gather(
        model_grid[0],
        "tile",
        axis=0,
        tiled=True,
        axis_index_groups=[[t, t + pairs] for t in range(pairs)],
    )
    sent, slot = pl.pallas_call(
        lambda *refs: pack_kernel(pairs, capacity, tiles_here, planes, *refs),
        out_shape=(
            jax.ShapeDtypeStruct((pairs * rows_per_source(capacity), rows), jnp.int32),
            jax.ShapeDtypeStruct((blocks,), jnp.int32),
        ),
        in_specs=[HBM] * 5,
        out_specs=(VMEM, SMEM),
        scratch_shapes=[
            pltpu.SMEM((blocks,), jnp.int32),
            pltpu.SMEM((blocks,), jnp.int32),
            pltpu.VMEM((blocks, 2, rows), jnp.float32),
            pltpu.VMEM((blocks, 2, rows), jnp.int32),
            pltpu.VMEM((blocks, 2, rows), jnp.int32),
            pltpu.SMEM((pairs, 2, rows), jnp.int32),
            pltpu.VMEM((pairs, 2, rows), jnp.int32),
            pltpu.SMEM((pairs * 2 * tiles_here,), jnp.int32),
            pltpu.SemaphoreType.DMA((5,)),
            pltpu.SemaphoreType.DMA,
        ],
        compiler_params=WHOLE_PARAMS,
        name="pack_blocks",
    )(w_plane[0], block_tile[0], visibilities[0], uv_cell[0], sub_pixel[0])
    got = lax.all_to_all(
        sent, "tile", split_axis=0, concat_axis=0, tiled=True, axis_index_groups=halves
    )
    own_row = lax.dynamic_index_in_dim(coupling, lax.axis_index("freq"), 0, keepdims=False)
    slot, own_row, got = lax.optimization_barrier(
        (slot + lax.div(lax.axis_index("tile"), owners), own_row, got)
    )
    table = jnp.pad(
        kernel_table.astype(jnp.float32), ((0, 8), (0, 0), (0, 16 - support))
    ).reshape(planes + 8, 16 * oversample)
    residual, own, other = pl.pallas_call(
        lambda *refs: grid_kernel(pairs, capacity, *refs),
        out_shape=(
            jax.ShapeDtypeStruct((slots, 2, rows), jnp.bfloat16),
            jax.ShapeDtypeStruct((tiles_here, wide, side), jnp.float32),
            jax.ShapeDtypeStruct((tiles_here, wide, side), jnp.bfloat16),
        ),
        in_specs=[SMEM, VMEM, VMEM, VMEM],
        out_specs=(VMEM, VMEM, VMEM),
        scratch_shapes=[
            pltpu.VMEM((2 * tiles_here, wide, side), jnp.bfloat16),
            pltpu.VMEM((2 * tiles_here, wide, side), jnp.float32),
            pltpu.VMEM((pairs, 2, rows), jnp.int32),
            pltpu.SMEM((pairs, 2, rows), jnp.int32),
            pltpu.SMEM(
                (slots + capacity + (2 * tiles_here + CHUNKS + AHEAD) * UNROLL,), jnp.int32
            ),
            pltpu.SemaphoreType.DMA,
            *[pltpu.VMEM((side, UNROLL * rows), jnp.bfloat16)] * BUFFERS,
            *[pltpu.VMEM((2, 16, UNROLL * rows), jnp.float32)] * BUFFERS,
            *[pltpu.VMEM((16, UNROLL * rows), jnp.float32)] * BUFFERS,
            *[pltpu.VMEM((16, UNROLL * rows), jnp.bfloat16)] * BUFFERS,
        ],
        compiler_params=PARAMS,
        name="grid_blocks",
    )(member[None], got, table, model)

    returned = lax.all_to_all(
        residual, "tile", split_axis=0, concat_axis=0, tiled=True, axis_index_groups=halves
    )
    grid_sum = own + lax.ppermute(other, "tile", swap).astype(jnp.float32)
    grids = lax.all_gather(grid_sum.astype(jnp.bfloat16)[None], "freq", axis=0, tiled=True)
    residuals, coupled_grid = pl.pallas_call(
        finish_kernel,
        out_shape=(
            jax.ShapeDtypeStruct((blocks, 2, rows), jnp.float32),
            jax.ShapeDtypeStruct((tiles_here, side, wide), jnp.float32),
        ),
        in_specs=[SMEM, SMEM, VMEM, VMEM],
        out_specs=(VMEM, VMEM),
        compiler_params=PARAMS,
        name="finish",
    )(own_row, slot, returned, grids)
    return (residuals[None], coupled_grid[None])


def solution(mesh):
    return jax.shard_map(
        body,
        mesh=mesh,
        in_specs=(
            P("freq", "tile", None, None),
            P("freq", "tile", None, None),
            P("freq", "tile", None, None),
            P("freq", "tile"),
            P("freq", "tile"),
            P("freq", "tile", None, None),
            P(),
            P(),
        ),
        out_specs=(P("freq", "tile", None, None), P("freq", "tile", None, None)),
        check_vma=False,
    )
```

```python
import jax
import jax.numpy as jnp
from jax import lax
from jax.experimental import pallas as pl
from jax.experimental.pallas import tpu as pltpu
from jax.sharding import PartitionSpec as P

UNROLL = 4
CHUNKS = 18
AHEAD = 1
BUFFERS = 6
VMEM = pl.BlockSpec(memory_space=pltpu.VMEM)
SMEM = pl.BlockSpec(memory_space=pltpu.SMEM)
HBM = pl.BlockSpec(memory_space=pltpu.HBM)
PARAMS = pltpu.CompilerParams(vmem_limit_bytes=32 * 1024 * 1024)
WHOLE_PARAMS = pltpu.CompilerParams(vmem_limit_bytes=62 * 1024 * 1024)
TILE_SHIFT = 12
PLANE_SHIFT = 16
SOURCE_SHIFT = 21
FULL = 32767
SCALE = 2.0**20


def scalar_div(value, count):
    shift = count.bit_length() - 1
    return value >> shift if count == 1 << shift else lax.div(value, count)


def first_slot(local, rank, capacity):
    half = capacity // 2
    return (local >> 1) * half + jnp.where((local & 1) == 0, rank, half - 1 - rank)


def rows_per_source(capacity):
    return (3 * (capacity + 1) + 7) // 8 * 8


def two_halves(high, low):
    return (high << 16) | (low & 0xFFFF)


def pack_kernel(pairs, capacity, tiles_here, planes, plane_hbm, tile_hbm, vis_hbm, cell_hbm, sub_hbm,
                sent_ref, slot_ref, plane_ref, tile_ref, vis_ref, cell_ref, sub_ref, about_ref, turned_ref,
                count_ref, load_sem, about_sem):
    blocks = tile_ref.shape[0]
    stride = rows_per_source(capacity)
    loads = [
        pltpu.make_async_copy(source, target, load_sem.at[i])
        for i, (source, target) in enumerate(
            [
                (tile_hbm, tile_ref),
                (plane_hbm, plane_ref),
                (vis_hbm, vis_ref),
                (cell_hbm, cell_ref),
                (sub_hbm, sub_ref),
            ]
        )
    ]
    for copy in loads:
        copy.start()
    for d in range(pairs):
        for t in range(2 * tiles_here):
            count_ref[d * 2 * tiles_here + t] = 0
    for copy in loads[:2]:
        copy.wait()

    def assign(b):
        tile = tile_ref[b]
        owner = scalar_div(tile, tiles_here)
        high = (owner >= pairs).astype(jnp.int32)
        pair = owner - high * pairs
        local = tile - (owner - high) * tiles_here
        key = pair * (2 * tiles_here) + local
        rank = count_ref[key]
        count_ref[key] = rank + 1
        place = first_slot(local, rank, capacity)
        slot_ref[b] = pair * (capacity + 1) + place
        about_ref[pair, 0, place] = plane_ref[b] << PLANE_SHIFT

    def each(work):
        def step(turn, carry):
            for which in range(8):
                work(turn * 8 + which)
            return carry

        lax.fori_loop(0, blocks // 8, step, 0)

    each(assign)
    for d in range(pairs):
        for t in range(2 * tiles_here):
            about_ref[d, 1, t] = count_ref[d * 2 * tiles_here + t]
    turn_about = pltpu.make_async_copy(about_ref, turned_ref, about_sem)
    turn_about.start()
    for copy in loads[2:]:
        copy.wait()
    largest = jnp.max(jnp.max(jnp.abs(vis_ref[...]), axis=0), keepdims=True)
    largest = jnp.maximum(jnp.ceil(largest * SCALE), 1.0)
    inverse = (FULL * SCALE) / largest

    def move(b):
        slot = slot_ref[b]
        row = 3 * slot + scalar_div(slot, capacity + 1) * (stride - 3 * (capacity + 1))
        value = jnp.clip(jnp.round(vis_ref[b] * inverse), -FULL, FULL).astype(jnp.int32)
        for i, pair in enumerate([value, cell_ref[b], sub_ref[b]]):
            sent_ref[pl.ds(row + i, 1), :] = two_halves(pair[0:1], pair[1:2])

    each(move)
    turn_about.wait()
    lane = lax.broadcasted_iota(jnp.int32, (1, 128), 1)
    for d in range(pairs):
        row = d * stride + 3 * capacity
        sent_ref[row : row + 1, :] = turned_ref[d, 0:1, :]
        sent_ref[row + 1 : row + 2, :] = jnp.zeros((1, 128), jnp.int32)
        sent_ref[row + 2 : row + 3, :] = jnp.where(
            lane < 2 * tiles_here, turned_ref[d, 1:2, :], largest.astype(jnp.int32)
        )


def finish_kernel(row_ref, slot_ref, returned_ref, grid_ref, residual_ref, coupled_ref):
    planes, tiles_here = grid_ref.shape[:2]
    for t in range(tiles_here):
        coupled_ref[t] = sum(
            row_ref[g] * grid_ref[g, t].astype(jnp.float32) for g in range(planes)
        ).T

    def step(turn, carry):
        for which in range(8):
            b = turn * 8 + which
            residual_ref[b] = returned_ref[slot_ref[b]].astype(jnp.float32)
        return carry

    lax.fori_loop(0, residual_ref.shape[0] // 8, step, 0)


def spread_parts(start, offset, table):
    sublane = lax.broadcasted_iota(jnp.int32, (8, 128), 0)
    taps, group = [], []
    for low in (0, 8):
        delta = sublane + low - start
        taps.append(
            jnp.take_along_axis(table, (delta & 15) + offset, axis=1, mode="promise_in_bounds")
        )
        group.append((15 - delta) >> 4)
    return jnp.concatenate(taps, axis=0), jnp.concatenate(group, axis=0)


def grid_kernel(pairs, capacity, member_ref, got_ref, table_ref, model_ref, residual_ref, own_ref,
                other_ref, turned_ref, grid_ref, code_ref, about_ref, list_ref, sem, *buffers):
    row_refs, picked_refs = buffers[:BUFFERS], buffers[BUFFERS:]
    tiles, side, wide = model_ref.shape
    groups = side // 16
    zero_row = table_ref.shape[0] - 8
    stride = rows_per_source(capacity)
    lane = lax.broadcasted_iota(jnp.int32, (1, 128), 1)
    for s in range(pairs):
        row = s * stride + 3 * capacity
        code_ref[s, 0:1, :] = got_ref[row : row + 1, :] + (
            lane + s * (capacity + 1) + (s << SOURCE_SHIFT)
        )
        code_ref[s, 1:2, :] = got_ref[row + 2 : row + 3, :]
    fill = pltpu.make_async_copy(code_ref, about_ref, sem)
    fill.start()
    for t in range(tiles):
        turned_ref[t] = model_ref[t].T
    grid_ref[...] = jnp.zeros_like(grid_ref)
    fill.wait()

    start = jnp.int32(0)
    for t in range(tiles):
        count = jnp.int32(0)
        for s in range(pairs):
            count = count + about_ref[s, 1, t]
        spare = -count & (UNROLL - 1)
        for u in range(UNROLL):
            list_ref[start + u] = (zero_row << PLANE_SHIFT) + (t << TILE_SHIFT) + capacity

        def enlist(s, filled, t=t):
            first = t // 2 * (capacity // 2)
            found = about_ref[s, 1, t]

            def some(turn, carry):
                for which in range(16):
                    k = turn * 16 + which
                    place = k if t % 2 == 0 else capacity // 2 - 1 - k
                    code = about_ref[s, 0, jnp.maximum(first + place, 0)]
                    list_ref[filled + k] = code + (t << TILE_SHIFT)
                return carry

            lax.fori_loop(0, (found + 15) >> 4, some, 0)
            return filled + found

        lax.fori_loop(0, pairs, enlist, start + spare)
        start = start + count + spare
    for u in range((CHUNKS + AHEAD) * UNROLL):
        list_ref[start + u] = (zero_row << PLANE_SHIFT) + capacity
    chunks = start >> UNROLL.bit_length() - 1
    zero = jnp.zeros((16, 128), jnp.bfloat16)

    def read(which):
        entry = list_ref[which]
        slot = entry & ((1 << TILE_SHIFT) - 1)
        plane = (entry >> PLANE_SHIFT) & ((1 << (SOURCE_SHIFT - PLANE_SHIFT)) - 1)
        source = entry >> SOURCE_SHIFT
        row = 3 * slot + source * (stride - 3 * (capacity + 1))
        table = jnp.broadcast_to(table_ref[pl.ds(plane, 1), :], (8, 128))

        def words(i):
            return got_ref[pl.ds(row + i, 1), :]

        def parts(shift):
            start = (words(1) >> shift) & 0xFFFF
            offset = ((words(2) >> shift) & 7) << 4
            return spread_parts(
                jnp.broadcast_to(start, (8, 128)), jnp.broadcast_to(offset, (8, 128)), table
            )

        def sample(part):
            step = about_ref[source, 1, tiles].astype(jnp.float32) * (1.0 / (FULL * SCALE))
            return ((words(0) << (16 * part)) >> 16).astype(jnp.float32) * step

        return slot, sample, parts

    def chunk_tile(turn):
        return (list_ref[turn * UNROLL] >> TILE_SHIFT) & 15

    def front(turn, which):
        row_ref, picked_ref = row_refs[which % len(row_refs)], picked_refs[which % len(picked_refs)]
        blocks = [read(turn * UNROLL + u) for u in range(UNROLL)]
        for u, (_, _, parts) in enumerate(blocks):
            taps, group = parts(16)
            taps = taps.astype(jnp.bfloat16)
            group = group.astype(jnp.float32).astype(jnp.bfloat16)
            for k in range(groups):
                row_ref[16 * k : 16 * k + 16, 128 * u : 128 * u + 128] = jnp.where(
                    group == k, taps, zero
                )
        partial = jnp.dot(
            turned_ref[chunk_tile(turn)], row_ref[...], preferred_element_type=jnp.float32
        )
        for u, (_, _, parts) in enumerate(blocks):
            columns = slice(128 * u, 128 * u + 128)
            taps, group = parts(0)
            for part in range(2):
                picked = jnp.zeros((16, 128), jnp.float32)
                for k in range(groups):
                    low = part * side + 16 * k
                    picked = jnp.where(group == k, partial[low : low + 16, columns], picked)
                picked_ref[part, :, columns] = picked * taps

    def back(turn, which):
        row_ref, picked_ref = row_refs[which % len(row_refs)], picked_refs[which % len(picked_refs)]
        weighted = []
        for u in range(UNROLL):
            slot, sample, parts = read(turn * UNROLL + u)
            columns = slice(128 * u, 128 * u + 128)
            taps, group = parts(0)
            group = group.astype(jnp.float32).astype(jnp.bfloat16)
            residuals, pieces = [], []
            for part in range(2):
                model = jnp.sum(picked_ref[part, :, columns], axis=0, keepdims=True)
                residual = sample(part) - model
                residuals.append(residual)
                value = (residual * taps).astype(jnp.bfloat16)
                pieces += [jnp.where(group == k, value, zero) for k in range(groups)]
            residual_ref[slot] = jnp.concatenate(residuals, axis=0).astype(jnp.bfloat16)
            weighted.append(jnp.concatenate(pieces, axis=0))
        grid_ref[chunk_tile(turn)] += lax.dot_general(
            jnp.concatenate(weighted, axis=1),
            row_ref[...],
            (((1,), (1,)), ((), ())),
            preferred_element_type=jnp.float32,
        )

    def step(turn, carry):
        for which in range(CHUNKS):
            front(turn * CHUNKS + which + AHEAD, which + AHEAD)
            back(turn * CHUNKS + which, which)
        return carry

    for which in range(AHEAD):
        front(which, which)
    lax.fori_loop(0, scalar_div(chunks + CHUNKS - 1, CHUNKS), step, 0)
    half = tiles // 2
    member = member_ref[0]
    for t in range(half):
        own_ref[t] = grid_ref[member * half + t]
        other_ref[t] = grid_ref[(1 - member) * half + t].astype(jnp.bfloat16)


def body(visibilities, uv_cell, sub_pixel, w_plane, block_tile, model_grid, kernel_table, coupling):
    owners = lax.axis_size("tile")
    pairs = owners // 2
    _, blocks, _, rows = visibilities.shape
    capacity = 2 * (3 * blocks // owners)
    _, tiles_here, side, wide = model_grid.shape
    planes, oversample, support = kernel_table.shape
    slots = pairs * (capacity + 1)
    member = lax.axis_index("tile") // pairs
    swap = [(t, (t + pairs) % owners) for t in range(owners)]
    halves = [list(range(pairs)), list(range(pairs, owners))]

    model = lax.all_gather(
        model_grid[0],
        "tile",
        axis=0,
        tiled=True,
        axis_index_groups=[[t, t + pairs] for t in range(pairs)],
    )
    sent, slot = pl.pallas_call(
        lambda *refs: pack_kernel(pairs, capacity, tiles_here, planes, *refs),
        out_shape=(
            jax.ShapeDtypeStruct((pairs * rows_per_source(capacity), rows), jnp.int32),
            jax.ShapeDtypeStruct((blocks,), jnp.int32),
        ),
        in_specs=[HBM] * 5,
        out_specs=(VMEM, SMEM),
        scratch_shapes=[
            pltpu.SMEM((blocks,), jnp.int32),
            pltpu.SMEM((blocks,), jnp.int32),
            pltpu.VMEM((blocks, 2, rows), jnp.float32),
            pltpu.VMEM((blocks, 2, rows), jnp.int32),
            pltpu.VMEM((blocks, 2, rows), jnp.int32),
            pltpu.SMEM((pairs, 2, rows), jnp.int32),
            pltpu.VMEM((pairs, 2, rows), jnp.int32),
            pltpu.SMEM((pairs * 2 * tiles_here,), jnp.int32),
            pltpu.SemaphoreType.DMA((5,)),
            pltpu.SemaphoreType.DMA,
        ],
        compiler_params=WHOLE_PARAMS,
        name="pack_blocks",
    )(w_plane[0], block_tile[0], visibilities[0], uv_cell[0], sub_pixel[0])
    got = lax.all_to_all(
        sent, "tile", split_axis=0, concat_axis=0, tiled=True, axis_index_groups=halves
    )
    own_row = lax.dynamic_index_in_dim(coupling, lax.axis_index("freq"), 0, keepdims=False)
    slot, own_row, got = lax.optimization_barrier(
        (slot + lax.div(lax.axis_index("tile"), owners), own_row, got)
    )
    table = jnp.pad(
        kernel_table.astype(jnp.float32), ((0, 8), (0, 0), (0, 16 - support))
    ).reshape(planes + 8, 16 * oversample)
    residual, own, other = pl.pallas_call(
        lambda *refs: grid_kernel(pairs, capacity, *refs),
        out_shape=(
            jax.ShapeDtypeStruct((slots, 2, rows), jnp.bfloat16),
            jax.ShapeDtypeStruct((tiles_here, wide, side), jnp.float32),
            jax.ShapeDtypeStruct((tiles_here, wide, side), jnp.bfloat16),
        ),
        in_specs=[SMEM, VMEM, VMEM, VMEM],
        out_specs=(VMEM, VMEM, VMEM),
        scratch_shapes=[
            pltpu.VMEM((2 * tiles_here, wide, side), jnp.bfloat16),
            pltpu.VMEM((2 * tiles_here, wide, side), jnp.float32),
            pltpu.VMEM((pairs, 2, rows), jnp.int32),
            pltpu.SMEM((pairs, 2, rows), jnp.int32),
            pltpu.SMEM(
                (slots + capacity + (2 * tiles_here + CHUNKS + AHEAD) * UNROLL,), jnp.int32
            ),
            pltpu.SemaphoreType.DMA,
            *[pltpu.VMEM((side, UNROLL * rows), jnp.bfloat16)] * BUFFERS,
            *[pltpu.VMEM((2, 16, UNROLL * rows), jnp.float32)] * BUFFERS,
        ],
        compiler_params=PARAMS,
        name="grid_blocks",
    )(member[None], got, table, model)

    returned = lax.all_to_all(
        residual, "tile", split_axis=0, concat_axis=0, tiled=True, axis_index_groups=halves
    )
    grid_sum = own + lax.ppermute(other, "tile", swap).astype(jnp.float32)
    grids = lax.all_gather(grid_sum.astype(jnp.bfloat16)[None], "freq", axis=0, tiled=True)
    residuals, coupled_grid = pl.pallas_call(
        finish_kernel,
        out_shape=(
            jax.ShapeDtypeStruct((blocks, 2, rows), jnp.float32),
            jax.ShapeDtypeStruct((tiles_here, side, wide), jnp.float32),
        ),
        in_specs=[SMEM, SMEM, VMEM, VMEM],
        out_specs=(VMEM, VMEM),
        compiler_params=PARAMS,
        name="finish",
    )(own_row, slot, returned, grids)
    return (residuals[None], coupled_grid[None])


def solution(mesh):
    return jax.shard_map(
        body,
        mesh=mesh,
        in_specs=(
            P("freq", "tile", None, None),
            P("freq", "tile", None, None),
            P("freq", "tile", None, None),
            P("freq", "tile"),
            P("freq", "tile"),
            P("freq", "tile", None, None),
            P(),
            P(),
        ),
        out_specs=(P("freq", "tile", None, None), P("freq", "tile", None, None)),
        check_vma=False,
    )
```

```python
import jax
import jax.numpy as jnp
from jax import lax
from jax.experimental import pallas as pl
from jax.experimental.pallas import tpu as pltpu
from jax.sharding import PartitionSpec as P

UNROLL = 2
CHUNKS = 35
AHEAD = 1
BUFFERS = 5
VMEM = pl.BlockSpec(memory_space=pltpu.VMEM)
SMEM = pl.BlockSpec(memory_space=pltpu.SMEM)
HBM = pl.BlockSpec(memory_space=pltpu.HBM)
PARAMS = pltpu.CompilerParams(vmem_limit_bytes=32 * 1024 * 1024)
WHOLE_PARAMS = pltpu.CompilerParams(vmem_limit_bytes=62 * 1024 * 1024)
TILE_SHIFT = 12
PLANE_SHIFT = 16
SOURCE_SHIFT = 21
FULL = 32767
SCALE = 2.0**20


def scalar_div(value, count):
    shift = count.bit_length() - 1
    return value >> shift if count == 1 << shift else lax.div(value, count)


def first_slot(local, rank, capacity):
    half = capacity // 2
    return (local >> 1) * half + jnp.where((local & 1) == 0, rank, half - 1 - rank)


def rows_per_source(capacity):
    return (3 * (capacity + 1) + 7) // 8 * 8


def two_halves(high, low):
    return (high << 16) | (low & 0xFFFF)


def pack_kernel(pairs, capacity, tiles_here, planes, plane_hbm, tile_hbm, vis_hbm, cell_hbm, sub_hbm,
                sent_ref, slot_ref, row_ref, plane_ref, tile_ref, vis_ref, cell_ref, sub_ref, about_ref, turned_ref,
                count_ref, load_sem, about_sem):
    blocks = tile_ref.shape[0]
    stride = rows_per_source(capacity)
    loads = [
        pltpu.make_async_copy(source, target, load_sem.at[i])
        for i, (source, target) in enumerate(
            [
                (tile_hbm, tile_ref),
                (plane_hbm, plane_ref),
                (vis_hbm, vis_ref),
                (cell_hbm, cell_ref),
                (sub_hbm, sub_ref),
            ]
        )
    ]
    for copy in loads:
        copy.start()
    for d in range(pairs):
        for t in range(2 * tiles_here):
            count_ref[d * 2 * tiles_here + t] = 0
    for copy in loads[:2]:
        copy.wait()

    def assign(b):
        tile = tile_ref[b]
        owner = scalar_div(tile, tiles_here)
        high = (owner >= pairs).astype(jnp.int32)
        pair = owner - high * pairs
        local = tile - (owner - high) * tiles_here
        key = pair * (2 * tiles_here) + local
        rank = count_ref[key]
        count_ref[key] = rank + 1
        place = first_slot(local, rank, capacity)
        slot_ref[b] = pair * (capacity + 1) + place
        row_ref[b] = pair * stride + 3 * place
        about_ref[pair, 0, place] = plane_ref[b] << PLANE_SHIFT

    def each(work):
        def step(turn, carry):
            for which in range(8):
                work(turn * 8 + which)
            return carry

        lax.fori_loop(0, blocks // 8, step, 0)

    each(assign)
    for d in range(pairs):
        for t in range(2 * tiles_here):
            about_ref[d, 1, t] = count_ref[d * 2 * tiles_here + t]
    turn_about = pltpu.make_async_copy(about_ref, turned_ref, about_sem)
    turn_about.start()
    for copy in loads[2:]:
        copy.wait()
    largest = jnp.max(jnp.max(jnp.abs(vis_ref[...]), axis=0), keepdims=True)
    largest = jnp.maximum(jnp.ceil(largest * SCALE), 1.0)
    inverse = (FULL * SCALE) / largest

    def move(b):
        row = row_ref[b]
        value = jnp.clip(jnp.round(vis_ref[b] * inverse), -FULL, FULL).astype(jnp.int32)
        for i, pair in enumerate([value, cell_ref[b], sub_ref[b]]):
            sent_ref[pl.ds(row + i, 1), :] = two_halves(pair[0:1], pair[1:2])

    each(move)
    turn_about.wait()
    lane = lax.broadcasted_iota(jnp.int32, (1, 128), 1)
    for d in range(pairs):
        row = d * stride + 3 * capacity
        sent_ref[row : row + 1, :] = turned_ref[d, 0:1, :]
        sent_ref[row + 1 : row + 2, :] = jnp.zeros((1, 128), jnp.int32)
        sent_ref[row + 2 : row + 3, :] = jnp.where(
            lane < 2 * tiles_here, turned_ref[d, 1:2, :], largest.astype(jnp.int32)
        )


def finish_kernel(row_ref, slot_ref, returned_ref, grid_ref, residual_ref, coupled_ref):
    planes, tiles_here = grid_ref.shape[:2]
    for t in range(tiles_here):
        coupled_ref[t] = sum(
            row_ref[g] * grid_ref[g, t].astype(jnp.float32) for g in range(planes)
        ).T

    def step(turn, carry):
        for which in range(8):
            b = turn * 8 + which
            residual_ref[b] = returned_ref[slot_ref[b]].astype(jnp.float32)
        return carry

    lax.fori_loop(0, residual_ref.shape[0] // 8, step, 0)


def spread_parts(start, offset, table):
    sublane = lax.broadcasted_iota(jnp.int32, (8, 128), 0)
    taps, group = [], []
    for low in (0, 8):
        delta = sublane + low - start
        taps.append(
            jnp.take_along_axis(table, (delta & 15) + offset, axis=1, mode="promise_in_bounds")
        )
        group.append((15 - delta) >> 4)
    return jnp.concatenate(taps, axis=0), jnp.concatenate(group, axis=0)


def grid_kernel(pairs, capacity, member_ref, got_ref, table_ref, model_ref, residual_ref, own_ref,
                other_ref, turned_ref, grid_ref, code_ref, about_ref, list_ref, sem, *buffers):
    row_refs, picked_refs = buffers[:BUFFERS], buffers[BUFFERS:]
    tiles, side, wide = model_ref.shape
    groups = side // 16
    zero_row = table_ref.shape[0] - 8
    stride = rows_per_source(capacity)
    lane = lax.broadcasted_iota(jnp.int32, (1, 128), 1)
    for s in range(pairs):
        row = s * stride + 3 * capacity
        code_ref[s, 0:1, :] = got_ref[row : row + 1, :] + (
            lane + s * (capacity + 1) + (s << SOURCE_SHIFT)
        )
        code_ref[s, 1:2, :] = got_ref[row + 2 : row + 3, :]
    fill = pltpu.make_async_copy(code_ref, about_ref, sem)
    fill.start()
    for t in range(tiles):
        turned_ref[t] = model_ref[t].T
    grid_ref[...] = jnp.zeros_like(grid_ref)
    fill.wait()

    start = jnp.int32(0)
    for t in range(tiles):
        count = jnp.int32(0)
        for s in range(pairs):
            count = count + about_ref[s, 1, t]
        spare = -count & (UNROLL - 1)
        for u in range(UNROLL):
            list_ref[start + u] = (zero_row << PLANE_SHIFT) + (t << TILE_SHIFT) + capacity

        def enlist(s, filled, t=t):
            first = t // 2 * (capacity // 2)
            found = about_ref[s, 1, t]

            def some(turn, carry):
                for which in range(16):
                    k = turn * 16 + which
                    place = k if t % 2 == 0 else capacity // 2 - 1 - k
                    code = about_ref[s, 0, jnp.maximum(first + place, 0)]
                    list_ref[filled + k] = code + (t << TILE_SHIFT)
                return carry

            lax.fori_loop(0, (found + 15) >> 4, some, 0)
            return filled + found

        lax.fori_loop(0, pairs, enlist, start + spare)
        start = start + count + spare
    for u in range((CHUNKS + AHEAD) * UNROLL):
        list_ref[start + u] = (zero_row << PLANE_SHIFT) + capacity
    chunks = start >> UNROLL.bit_length() - 1
    zero = jnp.zeros((16, 128), jnp.bfloat16)

    def read(which):
        entry = list_ref[which]
        slot = entry & ((1 << TILE_SHIFT) - 1)
        plane = (entry >> PLANE_SHIFT) & ((1 << (SOURCE_SHIFT - PLANE_SHIFT)) - 1)
        source = entry >> SOURCE_SHIFT
        row = 3 * slot + source * (stride - 3 * (capacity + 1))
        table = jnp.broadcast_to(table_ref[pl.ds(plane, 1), :], (8, 128))

        def words(i):
            return got_ref[pl.ds(row + i, 1), :]

        def parts(shift):
            start = (words(1) >> shift) & 0xFFFF
            offset = ((words(2) >> shift) & 7) << 4
            return spread_parts(
                jnp.broadcast_to(start, (8, 128)), jnp.broadcast_to(offset, (8, 128)), table
            )

        def sample(part):
            step = about_ref[source, 1, tiles].astype(jnp.float32) * (1.0 / (FULL * SCALE))
            return ((words(0) << (16 * part)) >> 16).astype(jnp.float32) * step

        return slot, sample, parts

    def chunk_tile(turn):
        return (list_ref[turn * UNROLL] >> TILE_SHIFT) & 15

    def front(turn, which):
        row_ref, picked_ref = row_refs[which % len(row_refs)], picked_refs[which % len(picked_refs)]
        blocks = [read(turn * UNROLL + u) for u in range(UNROLL)]
        for u, (_, _, parts) in enumerate(blocks):
            taps, group = parts(16)
            taps = taps.astype(jnp.bfloat16)
            group = group.astype(jnp.float32).astype(jnp.bfloat16)
            for k in range(groups):
                row_ref[16 * k : 16 * k + 16, 128 * u : 128 * u + 128] = jnp.where(
                    group == k, taps, zero
                )
        partial = jnp.dot(
            turned_ref[chunk_tile(turn)], row_ref[...], preferred_element_type=jnp.float32
        )
        for u, (_, _, parts) in enumerate(blocks):
            columns = slice(128 * u, 128 * u + 128)
            taps, group = parts(0)
            for part in range(2):
                picked = jnp.zeros((16, 128), jnp.float32)
                for k in range(groups):
                    low = part * side + 16 * k
                    picked = jnp.where(group == k, partial[low : low + 16, columns], picked)
                picked_ref[part, :, columns] = picked * taps

    def back(turn, which):
        row_ref, picked_ref = row_refs[which % len(row_refs)], picked_refs[which % len(picked_refs)]
        weighted = []
        for u in range(UNROLL):
            slot, sample, parts = read(turn * UNROLL + u)
            columns = slice(128 * u, 128 * u + 128)
            taps, group = parts(0)
            group = group.astype(jnp.float32).astype(jnp.bfloat16)
            residuals, pieces = [], []
            for part in range(2):
                model = jnp.sum(picked_ref[part, :, columns], axis=0, keepdims=True)
                residual = sample(part) - model
                residuals.append(residual)
                value = (residual * taps).astype(jnp.bfloat16)
                pieces += [jnp.where(group == k, value, zero) for k in range(groups)]
            residual_ref[slot] = jnp.concatenate(residuals, axis=0).astype(jnp.bfloat16)
            weighted.append(jnp.concatenate(pieces, axis=0))
        grid_ref[chunk_tile(turn)] += lax.dot_general(
            jnp.concatenate(weighted, axis=1),
            row_ref[...],
            (((1,), (1,)), ((), ())),
            preferred_element_type=jnp.float32,
        )

    def step(turn, carry):
        for which in range(CHUNKS):
            front(turn * CHUNKS + which + AHEAD, which + AHEAD)
            back(turn * CHUNKS + which, which)
        return carry

    for which in range(AHEAD):
        front(which, which)
    lax.fori_loop(0, scalar_div(chunks + CHUNKS - 1, CHUNKS), step, 0)
    half = tiles // 2
    member = member_ref[0]
    for t in range(half):
        own_ref[t] = grid_ref[member * half + t]
        other_ref[t] = grid_ref[(1 - member) * half + t].astype(jnp.bfloat16)


def body(visibilities, uv_cell, sub_pixel, w_plane, block_tile, model_grid, kernel_table, coupling):
    owners = lax.axis_size("tile")
    pairs = owners // 2
    _, blocks, _, rows = visibilities.shape
    capacity = 2 * (3 * blocks // owners)
    _, tiles_here, side, wide = model_grid.shape
    planes, oversample, support = kernel_table.shape
    slots = pairs * (capacity + 1)
    member = lax.axis_index("tile") // pairs
    swap = [(t, (t + pairs) % owners) for t in range(owners)]
    halves = [list(range(pairs)), list(range(pairs, owners))]

    model = lax.all_gather(
        model_grid[0],
        "tile",
        axis=0,
        tiled=True,
        axis_index_groups=[[t, t + pairs] for t in range(pairs)],
    )
    sent, slot = pl.pallas_call(
        lambda *refs: pack_kernel(pairs, capacity, tiles_here, planes, *refs),
        out_shape=(
            jax.ShapeDtypeStruct((pairs * rows_per_source(capacity), rows), jnp.int32),
            jax.ShapeDtypeStruct((blocks,), jnp.int32),
        ),
        in_specs=[HBM] * 5,
        out_specs=(VMEM, SMEM),
        scratch_shapes=[
            pltpu.SMEM((blocks,), jnp.int32),
            pltpu.SMEM((blocks,), jnp.int32),
            pltpu.SMEM((blocks,), jnp.int32),
            pltpu.VMEM((blocks, 2, rows), jnp.float32),
            pltpu.VMEM((blocks, 2, rows), jnp.int32),
            pltpu.VMEM((blocks, 2, rows), jnp.int32),
            pltpu.SMEM((pairs, 2, rows), jnp.int32),
            pltpu.VMEM((pairs, 2, rows), jnp.int32),
            pltpu.SMEM((pairs * 2 * tiles_here,), jnp.int32),
            pltpu.SemaphoreType.DMA((5,)),
            pltpu.SemaphoreType.DMA,
        ],
        compiler_params=WHOLE_PARAMS,
        name="pack_blocks",
    )(w_plane[0], block_tile[0], visibilities[0], uv_cell[0], sub_pixel[0])
    got = lax.all_to_all(
        sent, "tile", split_axis=0, concat_axis=0, tiled=True, axis_index_groups=halves
    )
    own_row = lax.dynamic_index_in_dim(coupling, lax.axis_index("freq"), 0, keepdims=False)
    slot, own_row, got = lax.optimization_barrier(
        (slot + lax.div(lax.axis_index("tile"), owners), own_row, got)
    )
    table = jnp.pad(
        kernel_table.astype(jnp.float32), ((0, 8), (0, 0), (0, 16 - support))
    ).reshape(planes + 8, 16 * oversample)
    residual, own, other = pl.pallas_call(
        lambda *refs: grid_kernel(pairs, capacity, *refs),
        out_shape=(
            jax.ShapeDtypeStruct((slots, 2, rows), jnp.bfloat16),
            jax.ShapeDtypeStruct((tiles_here, wide, side), jnp.float32),
            jax.ShapeDtypeStruct((tiles_here, wide, side), jnp.bfloat16),
        ),
        in_specs=[SMEM, VMEM, VMEM, VMEM],
        out_specs=(VMEM, VMEM, VMEM),
        scratch_shapes=[
            pltpu.VMEM((2 * tiles_here, wide, side), jnp.bfloat16),
            pltpu.VMEM((2 * tiles_here, wide, side), jnp.float32),
            pltpu.VMEM((pairs, 2, rows), jnp.int32),
            pltpu.SMEM((pairs, 2, rows), jnp.int32),
            pltpu.SMEM(
                (slots + capacity + (2 * tiles_here + CHUNKS + AHEAD) * UNROLL,), jnp.int32
            ),
            pltpu.SemaphoreType.DMA,
            *[pltpu.VMEM((side, UNROLL * rows), jnp.bfloat16)] * BUFFERS,
            *[pltpu.VMEM((2, 16, UNROLL * rows), jnp.float32)] * BUFFERS,
        ],
        compiler_params=PARAMS,
        name="grid_blocks",
    )(member[None], got, table, model)

    returned = lax.all_to_all(
        residual, "tile", split_axis=0, concat_axis=0, tiled=True, axis_index_groups=halves
    )
    grid_sum = own + lax.ppermute(other, "tile", swap).astype(jnp.float32)
    grids = lax.all_gather(grid_sum.astype(jnp.bfloat16)[None], "freq", axis=0, tiled=True)
    residuals, coupled_grid = pl.pallas_call(
        finish_kernel,
        out_shape=(
            jax.ShapeDtypeStruct((blocks, 2, rows), jnp.float32),
            jax.ShapeDtypeStruct((tiles_here, side, wide), jnp.float32),
        ),
        in_specs=[SMEM, SMEM, VMEM, VMEM],
        out_specs=(VMEM, VMEM),
        compiler_params=PARAMS,
        name="finish",
    )(own_row, slot, returned, grids)
    return (residuals[None], coupled_grid[None])


def solution(mesh):
    return jax.shard_map(
        body,
        mesh=mesh,
        in_specs=(
            P("freq", "tile", None, None),
            P("freq", "tile", None, None),
            P("freq", "tile", None, None),
            P("freq", "tile"),
            P("freq", "tile"),
            P("freq", "tile", None, None),
            P(),
            P(),
        ),
        out_specs=(P("freq", "tile", None, None), P("freq", "tile", None, None)),
        check_vma=False,
    )
```

```python
import jax
import jax.numpy as jnp
from jax import lax
from jax.experimental import pallas as pl
from jax.experimental.pallas import tpu as pltpu
from jax.sharding import PartitionSpec as P

UNROLL = 2
CHUNKS = 35
AHEAD = 2
BUFFERS = 5
VMEM = pl.BlockSpec(memory_space=pltpu.VMEM)
SMEM = pl.BlockSpec(memory_space=pltpu.SMEM)
HBM = pl.BlockSpec(memory_space=pltpu.HBM)
PARAMS = pltpu.CompilerParams(vmem_limit_bytes=32 * 1024 * 1024)
WHOLE_PARAMS = pltpu.CompilerParams(vmem_limit_bytes=62 * 1024 * 1024)
TILE_SHIFT = 12
PLANE_SHIFT = 16
SOURCE_SHIFT = 21
FULL = 32767
SCALE = 2.0**20


def scalar_div(value, count):
    shift = count.bit_length() - 1
    return value >> shift if count == 1 << shift else lax.div(value, count)


def first_slot(local, rank, capacity):
    half = capacity // 2
    return (local >> 1) * half + jnp.where((local & 1) == 0, rank, half - 1 - rank)


def rows_per_source(capacity):
    return (3 * (capacity + 1) + 7) // 8 * 8


def two_halves(high, low):
    return (high << 16) | (low & 0xFFFF)


def pack_kernel(pairs, capacity, tiles_here, plane_hbm, tile_hbm, vis_hbm, cell_hbm, sub_hbm,
                sent_ref, slot_ref, row_ref, plane_ref, tile_ref, vis_ref, cell_ref, sub_ref, code_ref,
                count_ref, load_sem):
    blocks = tile_ref.shape[0]
    stride = rows_per_source(capacity)
    tiles = 2 * tiles_here
    lane = lax.broadcasted_iota(jnp.int32, (1, 128), 1)
    loads = [
        pltpu.make_async_copy(source, target, load_sem.at[i])
        for i, (source, target) in enumerate(
            [
                (tile_hbm, tile_ref),
                (plane_hbm, plane_ref),
                (vis_hbm, vis_ref),
                (cell_hbm, cell_ref),
                (sub_hbm, sub_ref),
            ]
        )
    ]
    for copy in loads:
        copy.start()
    for key in range(pairs * tiles):
        count_ref[key] = 0
    for copy in loads:
        copy.wait()

    def assign(b):
        tile = tile_ref[b]
        owner = scalar_div(tile, tiles_here)
        high = (owner >= pairs).astype(jnp.int32)
        pair = owner - high * pairs
        local = tile - (owner - high) * tiles_here
        key = pair * tiles + local
        rank = count_ref[key]
        count_ref[key] = rank + 1
        place = first_slot(local, rank, capacity)
        slot_ref[b] = pair * (capacity + 1) + place
        row_ref[b] = pair * stride + 3 * place
        codes = code_ref[pl.ds(pair, 1), :]
        code_ref[pl.ds(pair, 1), :] = jnp.where(lane == place, plane_ref[b] << PLANE_SHIFT, codes)

    largest = jnp.max(jnp.max(jnp.abs(vis_ref[...]), axis=0, keepdims=True), axis=1, keepdims=True)
    largest = jnp.maximum(jnp.ceil(largest * SCALE), 1.0)
    inverse = (FULL * SCALE) / largest

    def move(four):
        rows = pl.ds(pl.multiple_of(8 * four, 8), 8)
        value = jnp.clip(jnp.round(vis_ref[rows, :] * inverse), -FULL, FULL).astype(jnp.int32)
        words = [
            two_halves(parts, pltpu.roll(parts, 7, 0))
            for parts in [value, cell_ref[rows, :], sub_ref[rows, :]]
        ]
        for u in range(4):
            row = row_ref[4 * four + u]
            for i, word in enumerate(words):
                sent_ref[pl.ds(row + i, 1), :] = word[2 * u : 2 * u + 1]

    def step(turn, carry):
        for which in range(8):
            assign(8 * turn + 8 + which)
        move(2 * turn)
        move(2 * turn + 1)
        return carry

    for which in range(8):
        assign(which)
    lax.fori_loop(0, blocks // 8 - 1, step, 0)
    move(blocks // 4 - 2)
    move(blocks // 4 - 1)
    for d in range(pairs):
        counts = jnp.broadcast_to(largest.astype(jnp.int32), (1, 128))
        for t in range(tiles):
            counts = jnp.where(lane == t, count_ref[d * tiles + t], counts)
        row = d * stride + 3 * capacity
        sent_ref[row : row + 1, :] = code_ref[d : d + 1, :]
        sent_ref[row + 1 : row + 2, :] = jnp.zeros((1, 128), jnp.int32)
        sent_ref[row + 2 : row + 3, :] = counts


def finish_kernel(row_ref, slot_ref, returned_ref, grid_ref, residual_ref, coupled_ref):
    planes, tiles_here = grid_ref.shape[:2]
    for t in range(tiles_here):
        coupled_ref[t] = sum(
            row_ref[g] * grid_ref[g, t].astype(jnp.float32) for g in range(planes)
        ).T

    def step(turn, carry):
        for which in range(8):
            b = turn * 8 + which
            residual_ref[b] = returned_ref[slot_ref[b]].astype(jnp.float32)
        return carry

    lax.fori_loop(0, residual_ref.shape[0] // 8, step, 0)


def spread_parts(start, offset, table):
    sublane = lax.broadcasted_iota(jnp.int32, (8, 128), 0)
    taps, group = [], []
    for low in (0, 8):
        delta = sublane + low - start
        taps.append(
            jnp.take_along_axis(table, (delta & 15) + offset, axis=1, mode="promise_in_bounds")
        )
        group.append((15 - delta) >> 4)
    return jnp.concatenate(taps, axis=0), jnp.concatenate(group, axis=0)


def grid_kernel(pairs, capacity, member_ref, got_ref, table_ref, model_ref, residual_ref, own_ref,
                other_ref, turned_ref, grid_ref, code_ref, about_ref, list_ref, sem, *buffers):
    row_refs, picked_refs = buffers[:BUFFERS], buffers[BUFFERS:]
    tiles, side, wide = model_ref.shape
    groups = side // 16
    zero_row = table_ref.shape[0] - 8
    stride = rows_per_source(capacity)
    lane = lax.broadcasted_iota(jnp.int32, (1, 128), 1)
    for s in range(pairs):
        row = s * stride + 3 * capacity
        code_ref[s, 0:1, :] = got_ref[row : row + 1, :] + (
            lane + s * (capacity + 1) + (s << SOURCE_SHIFT)
        )
        code_ref[s, 1:2, :] = got_ref[row + 2 : row + 3, :]
    fill = pltpu.make_async_copy(code_ref, about_ref, sem)
    fill.start()
    for t in range(tiles):
        turned_ref[t] = model_ref[t].T
    grid_ref[...] = jnp.zeros_like(grid_ref)
    fill.wait()

    start = jnp.int32(0)
    for t in range(tiles):
        count = jnp.int32(0)
        for s in range(pairs):
            count = count + about_ref[s, 1, t]
        spare = -count & (UNROLL - 1)
        for u in range(UNROLL):
            list_ref[start + u] = (zero_row << PLANE_SHIFT) + (t << TILE_SHIFT) + capacity

        def enlist(s, filled, t=t):
            first = t // 2 * (capacity // 2)
            found = about_ref[s, 1, t]

            def some(turn, carry):
                for which in range(16):
                    k = turn * 16 + which
                    place = k if t % 2 == 0 else capacity // 2 - 1 - k
                    code = about_ref[s, 0, jnp.maximum(first + place, 0)]
                    list_ref[filled + k] = code + (t << TILE_SHIFT)
                return carry

            lax.fori_loop(0, (found + 15) >> 4, some, 0)
            return filled + found

        lax.fori_loop(0, pairs, enlist, start + spare)
        start = start + count + spare
    for u in range((CHUNKS + AHEAD) * UNROLL):
        list_ref[start + u] = (zero_row << PLANE_SHIFT) + capacity
    chunks = start >> UNROLL.bit_length() - 1
    zero = jnp.zeros((16, 128), jnp.bfloat16)

    def read(which):
        entry = list_ref[which]
        slot = entry & ((1 << TILE_SHIFT) - 1)
        plane = (entry >> PLANE_SHIFT) & ((1 << (SOURCE_SHIFT - PLANE_SHIFT)) - 1)
        source = entry >> SOURCE_SHIFT
        row = 3 * slot + source * (stride - 3 * (capacity + 1))
        table = jnp.broadcast_to(table_ref[pl.ds(plane, 1), :], (8, 128))

        def words(i):
            return got_ref[pl.ds(row + i, 1), :]

        def parts(shift):
            start = (words(1) >> shift) & 0xFFFF
            offset = ((words(2) >> shift) & 7) << 4
            return spread_parts(
                jnp.broadcast_to(start, (8, 128)), jnp.broadcast_to(offset, (8, 128)), table
            )

        def sample(part):
            step = about_ref[source, 1, tiles].astype(jnp.float32) * (1.0 / (FULL * SCALE))
            return ((words(0) << (16 * part)) >> 16).astype(jnp.float32) * step

        return slot, sample, parts

    def chunk_tile(turn):
        return (list_ref[turn * UNROLL] >> TILE_SHIFT) & 15

    def front(turn, which):
        row_ref, picked_ref = row_refs[which % len(row_refs)], picked_refs[which % len(picked_refs)]
        blocks = [read(turn * UNROLL + u) for u in range(UNROLL)]
        for u, (_, _, parts) in enumerate(blocks):
            taps, group = parts(16)
            taps = taps.astype(jnp.bfloat16)
            group = group.astype(jnp.float32).astype(jnp.bfloat16)
            for k in range(groups):
                row_ref[16 * k : 16 * k + 16, 128 * u : 128 * u + 128] = jnp.where(
                    group == k, taps, zero
                )
        partial = jnp.dot(
            turned_ref[chunk_tile(turn)], row_ref[...], preferred_element_type=jnp.float32
        )
        for u, (_, _, parts) in enumerate(blocks):
            columns = slice(128 * u, 128 * u + 128)
            taps, group = parts(0)
            for part in range(2):
                picked = jnp.zeros((16, 128), jnp.float32)
                for k in range(groups):
                    low = part * side + 16 * k
                    picked = jnp.where(group == k, partial[low : low + 16, columns], picked)
                picked_ref[part, :, columns] = picked * taps

    def back(turn, which):
        row_ref, picked_ref = row_refs[which % len(row_refs)], picked_refs[which % len(picked_refs)]
        weighted = []
        for u in range(UNROLL):
            slot, sample, parts = read(turn * UNROLL + u)
            columns = slice(128 * u, 128 * u + 128)
            taps, group = parts(0)
            group = group.astype(jnp.float32).astype(jnp.bfloat16)
            residuals, pieces = [], []
            for part in range(2):
                model = jnp.sum(picked_ref[part, :, columns], axis=0, keepdims=True)
                residual = sample(part) - model
                residuals.append(residual)
                value = (residual * taps).astype(jnp.bfloat16)
                pieces += [jnp.where(group == k, value, zero) for k in range(groups)]
            residual_ref[slot] = jnp.concatenate(residuals, axis=0).astype(jnp.bfloat16)
            weighted.append(jnp.concatenate(pieces, axis=0))
        grid_ref[chunk_tile(turn)] += lax.dot_general(
            jnp.concatenate(weighted, axis=1),
            row_ref[...],
            (((1,), (1,)), ((), ())),
            preferred_element_type=jnp.float32,
        )

    def step(turn, carry):
        for which in range(CHUNKS):
            front(turn * CHUNKS + which + AHEAD, which + AHEAD)
            back(turn * CHUNKS + which, which)
        return carry

    for which in range(AHEAD):
        front(which, which)
    lax.fori_loop(0, scalar_div(chunks + CHUNKS - 1, CHUNKS), step, 0)
    half = tiles // 2
    member = member_ref[0]
    for t in range(half):
        own_ref[t] = grid_ref[member * half + t]
        other_ref[t] = grid_ref[(1 - member) * half + t].astype(jnp.bfloat16)


def body(visibilities, uv_cell, sub_pixel, w_plane, block_tile, model_grid, kernel_table, coupling):
    owners = lax.axis_size("tile")
    pairs = owners // 2
    _, blocks, _, rows = visibilities.shape
    capacity = 2 * (3 * blocks // owners)
    _, tiles_here, side, wide = model_grid.shape
    planes, oversample, support = kernel_table.shape
    slots = pairs * (capacity + 1)
    member = lax.axis_index("tile") // pairs
    swap = [(t, (t + pairs) % owners) for t in range(owners)]
    halves = [list(range(pairs)), list(range(pairs, owners))]

    model = lax.all_gather(
        model_grid[0],
        "tile",
        axis=0,
        tiled=True,
        axis_index_groups=[[t, t + pairs] for t in range(pairs)],
    )
    sent, slot = pl.pallas_call(
        lambda *refs: pack_kernel(pairs, capacity, tiles_here, *refs),
        out_shape=(
            jax.ShapeDtypeStruct((pairs * rows_per_source(capacity), rows), jnp.int32),
            jax.ShapeDtypeStruct((blocks,), jnp.int32),
        ),
        in_specs=[HBM] * 5,
        out_specs=(VMEM, SMEM),
        scratch_shapes=[
            pltpu.SMEM((blocks,), jnp.int32),
            pltpu.SMEM((blocks,), jnp.int32),
            pltpu.SMEM((blocks,), jnp.int32),
            pltpu.VMEM((2 * blocks, rows), jnp.float32),
            pltpu.VMEM((2 * blocks, rows), jnp.int32),
            pltpu.VMEM((2 * blocks, rows), jnp.int32),
            pltpu.VMEM((pairs, rows), jnp.int32),
            pltpu.SMEM((pairs * 2 * tiles_here,), jnp.int32),
            pltpu.SemaphoreType.DMA((5,)),
        ],
        compiler_params=WHOLE_PARAMS,
        name="pack_blocks",
    )(
        w_plane[0],
        block_tile[0],
        *[array.reshape(2 * blocks, rows) for array in (visibilities, uv_cell, sub_pixel)],
    )
    got = lax.all_to_all(
        sent, "tile", split_axis=0, concat_axis=0, tiled=True, axis_index_groups=halves
    )
    own_row = lax.dynamic_index_in_dim(coupling, lax.axis_index("freq"), 0, keepdims=False)
    slot, own_row, got = lax.optimization_barrier(
        (slot + lax.div(lax.axis_index("tile"), owners), own_row, got)
    )
    table = jnp.pad(
        kernel_table.astype(jnp.float32), ((0, 8), (0, 0), (0, 16 - support))
    ).reshape(planes + 8, 16 * oversample)
    residual, own, other = pl.pallas_call(
        lambda *refs: grid_kernel(pairs, capacity, *refs),
        out_shape=(
            jax.ShapeDtypeStruct((slots, 2, rows), jnp.bfloat16),
            jax.ShapeDtypeStruct((tiles_here, wide, side), jnp.float32),
            jax.ShapeDtypeStruct((tiles_here, wide, side), jnp.bfloat16),
        ),
        in_specs=[SMEM, VMEM, VMEM, VMEM],
        out_specs=(VMEM, VMEM, VMEM),
        scratch_shapes=[
            pltpu.VMEM((2 * tiles_here, wide, side), jnp.bfloat16),
            pltpu.VMEM((2 * tiles_here, wide, side), jnp.float32),
            pltpu.VMEM((pairs, 2, rows), jnp.int32),
            pltpu.SMEM((pairs, 2, rows), jnp.int32),
            pltpu.SMEM(
                (slots + capacity + (2 * tiles_here + CHUNKS + AHEAD) * UNROLL,), jnp.int32
            ),
            pltpu.SemaphoreType.DMA,
            *[pltpu.VMEM((side, UNROLL * rows), jnp.bfloat16)] * BUFFERS,
            *[pltpu.VMEM((2, 16, UNROLL * rows), jnp.float32)] * BUFFERS,
        ],
        compiler_params=PARAMS,
        name="grid_blocks",
    )(member[None], got, table, model)

    returned = lax.all_to_all(
        residual, "tile", split_axis=0, concat_axis=0, tiled=True, axis_index_groups=halves
    )
    grid_sum = own + lax.ppermute(other, "tile", swap).astype(jnp.float32)
    grids = lax.all_gather(grid_sum.astype(jnp.bfloat16)[None], "freq", axis=0, tiled=True)
    residuals, coupled_grid = pl.pallas_call(
        finish_kernel,
        out_shape=(
            jax.ShapeDtypeStruct((blocks, 2, rows), jnp.float32),
            jax.ShapeDtypeStruct((tiles_here, side, wide), jnp.float32),
        ),
        in_specs=[SMEM, SMEM, VMEM, VMEM],
        out_specs=(VMEM, VMEM),
        compiler_params=PARAMS,
        name="finish",
    )(own_row, slot, returned, grids)
    return (residuals[None], coupled_grid[None])


def solution(mesh):
    return jax.shard_map(
        body,
        mesh=mesh,
        in_specs=(
            P("freq", "tile", None, None),
            P("freq", "tile", None, None),
            P("freq", "tile", None, None),
            P("freq", "tile"),
            P("freq", "tile"),
            P("freq", "tile", None, None),
            P(),
            P(),
        ),
        out_specs=(P("freq", "tile", None, None), P("freq", "tile", None, None)),
        check_vma=False,
    )
```

```python
import jax
import jax.numpy as jnp
from jax import lax
from jax.experimental import pallas as pl
from jax.experimental.pallas import tpu as pltpu
from jax.sharding import PartitionSpec as P

UNROLL = 2
CHUNKS = 35
AHEAD = 2
BUFFERS = 5
VMEM = pl.BlockSpec(memory_space=pltpu.VMEM)
SMEM = pl.BlockSpec(memory_space=pltpu.SMEM)
HBM = pl.BlockSpec(memory_space=pltpu.HBM)
PARAMS = pltpu.CompilerParams(vmem_limit_bytes=32 * 1024 * 1024)
WHOLE_PARAMS = pltpu.CompilerParams(vmem_limit_bytes=62 * 1024 * 1024)
TILE_SHIFT = 12
PLANE_SHIFT = 16
SOURCE_SHIFT = 21
FULL = 32767
SCALE = 2.0**20


def scalar_div(value, count):
    shift = count.bit_length() - 1
    return value >> shift if count == 1 << shift else lax.div(value, count)


def first_slot(local, rank, capacity):
    half = capacity // 2
    return (local >> 1) * half + jnp.where((local & 1) == 0, rank, half - 1 - rank)


def rows_per_source(capacity):
    return (3 * (capacity + 1) + 7) // 8 * 8


def two_halves(high, low):
    return (high << 16) | (low & 0xFFFF)


def pack_kernel(pairs, capacity, tiles_here, plane_hbm, tile_hbm, vis_hbm, cell_hbm, sub_hbm,
                sent_ref, slot_ref, row_ref, plane_ref, tile_ref, vis_ref, cell_ref, sub_ref, code_ref,
                count_ref, load_sem):
    blocks = tile_ref.shape[0]
    stride = rows_per_source(capacity)
    tiles = 2 * tiles_here
    lane = lax.broadcasted_iota(jnp.int32, (1, 128), 1)
    loads = [
        pltpu.make_async_copy(source, target, load_sem.at[i])
        for i, (source, target) in enumerate(
            [
                (tile_hbm, tile_ref),
                (plane_hbm, plane_ref),
                (vis_hbm, vis_ref),
                (cell_hbm, cell_ref),
                (sub_hbm, sub_ref),
            ]
        )
    ]
    for copy in loads:
        copy.start()
    for key in range(pairs * tiles):
        count_ref[key] = 0
    for copy in loads:
        copy.wait()

    def assign(b):
        tile = tile_ref[b]
        owner = scalar_div(tile, tiles_here)
        high = (owner >= pairs).astype(jnp.int32)
        pair = owner - high * pairs
        local = tile - (owner - high) * tiles_here
        key = pair * tiles + local
        rank = count_ref[key]
        count_ref[key] = rank + 1
        place = first_slot(local, rank, capacity)
        slot_ref[b] = pair * (capacity + 1) + place
        row_ref[b] = pair * stride + 3 * place
        codes = code_ref[pl.ds(pair, 1), :]
        code_ref[pl.ds(pair, 1), :] = jnp.where(lane == place, plane_ref[b] << PLANE_SHIFT, codes)

    largest = jnp.max(jnp.max(jnp.abs(vis_ref[...]), axis=0, keepdims=True), axis=1, keepdims=True)
    largest = jnp.maximum(jnp.ceil(largest * SCALE), 1.0)
    inverse = (FULL * SCALE) / largest

    def move(four):
        rows = pl.ds(pl.multiple_of(8 * four, 8), 8)
        value = jnp.clip(jnp.round(vis_ref[rows, :] * inverse), -FULL, FULL).astype(jnp.int32)
        words = [
            two_halves(parts, pltpu.roll(parts, 7, 0))
            for parts in [value, cell_ref[rows, :], sub_ref[rows, :]]
        ]
        for u in range(4):
            row = row_ref[4 * four + u]
            for i, word in enumerate(words):
                sent_ref[pl.ds(row + i, 1), :] = word[2 * u : 2 * u + 1]

    def step(turn, carry):
        for which in range(8):
            assign(8 * turn + 8 + which)
        move(2 * turn)
        move(2 * turn + 1)
        return carry

    for which in range(8):
        assign(which)
    lax.fori_loop(0, blocks // 8 - 1, step, 0)
    move(blocks // 4 - 2)
    move(blocks // 4 - 1)
    for d in range(pairs):
        counts = jnp.broadcast_to(largest.astype(jnp.int32), (1, 128))
        for t in range(tiles):
            counts = jnp.where(lane == t, count_ref[d * tiles + t], counts)
        row = d * stride + 3 * capacity
        sent_ref[row : row + 1, :] = code_ref[d : d + 1, :]
        sent_ref[row + 1 : row + 2, :] = jnp.zeros((1, 128), jnp.int32)
        sent_ref[row + 2 : row + 3, :] = counts


def finish_kernel(row_ref, slot_ref, returned_ref, grid_ref, residual_ref, coupled_ref):
    planes, tiles_here = grid_ref.shape[:2]
    for t in range(tiles_here):
        coupled_ref[t] = sum(
            row_ref[g] * grid_ref[g, t].astype(jnp.float32) for g in range(planes)
        ).T

    def step(turn, carry):
        for which in range(8):
            b = turn * 8 + which
            residual_ref[b] = returned_ref[slot_ref[b]].astype(jnp.float32)
        return carry

    lax.fori_loop(0, residual_ref.shape[0] // 8, step, 0)


def spread_parts(start, offset, table):
    sublane = lax.broadcasted_iota(jnp.int32, (8, 128), 0)
    taps, group = [], []
    for low in (0, 8):
        delta = sublane + low - start
        taps.append(
            jnp.take_along_axis(table, (delta & 15) + offset, axis=1, mode="promise_in_bounds")
        )
        group.append((15 - delta) >> 4)
    return jnp.concatenate(taps, axis=0), jnp.concatenate(group, axis=0)


def grid_kernel(pairs, capacity, member_ref, got_ref, raw_ref, model_ref, residual_ref, own_ref,
                other_ref, table_ref, spread_ref, turned_ref, grid_ref, code_ref, about_ref, list_ref, sem, *buffers):
    row_refs, picked_refs = buffers[:BUFFERS], buffers[BUFFERS:]
    tiles, side, wide = model_ref.shape
    groups = side // 16
    zero_row = raw_ref.shape[1]
    stride = rows_per_source(capacity)
    lane = lax.broadcasted_iota(jnp.int32, (1, 128), 1)
    for s in range(pairs):
        row = s * stride + 3 * capacity
        code_ref[s, 0:1, :] = got_ref[row : row + 1, :] + (
            lane + s * (capacity + 1) + (s << SOURCE_SHIFT)
        )
        code_ref[s, 1:2, :] = got_ref[row + 2 : row + 3, :]
    fill = pltpu.make_async_copy(code_ref, about_ref, sem)
    fill.start()
    spread_ref[...] = jnp.zeros_like(spread_ref)
    raw = raw_ref[...].astype(jnp.float32)
    for o in range(raw.shape[0] // 8):
        spread_ref[16 * o : 16 * o + 8, :zero_row] = raw[8 * o : 8 * o + 8]
    table_ref[...] = spread_ref[...].T
    for t in range(tiles):
        turned_ref[t] = model_ref[t].T
    grid_ref[...] = jnp.zeros_like(grid_ref)
    fill.wait()

    start = jnp.int32(0)
    for t in range(tiles):
        count = jnp.int32(0)
        for s in range(pairs):
            count = count + about_ref[s, 1, t]
        spare = -count & (UNROLL - 1)
        for u in range(UNROLL):
            list_ref[start + u] = (zero_row << PLANE_SHIFT) + (t << TILE_SHIFT) + capacity

        def enlist(s, filled, t=t):
            found = about_ref[s, 1, t]

            def some(low, high):
                for k in range(low, high):
                    place = k if t % 2 == 0 else capacity // 2 - 1 - k
                    code = about_ref[s, 0, t // 2 * (capacity // 2) + place]
                    list_ref[filled + k] = code + (t << TILE_SHIFT)

            few = capacity // 3

            @pl.when(found > 0)
            def _():
                some(0, few)

                @pl.when(found > few)
                def _():
                    some(few, capacity // 2)

            return filled + found

        lax.fori_loop(0, pairs, enlist, start + spare)
        start = start + count + spare
    for u in range((CHUNKS + AHEAD) * UNROLL):
        list_ref[start + u] = (zero_row << PLANE_SHIFT) + capacity
    chunks = start >> UNROLL.bit_length() - 1
    zero = jnp.zeros((16, 128), jnp.bfloat16)

    def read(which):
        entry = list_ref[which]
        slot = entry & ((1 << TILE_SHIFT) - 1)
        plane = (entry >> PLANE_SHIFT) & ((1 << (SOURCE_SHIFT - PLANE_SHIFT)) - 1)
        source = entry >> SOURCE_SHIFT
        row = 3 * slot + source * (stride - 3 * (capacity + 1))
        table = jnp.broadcast_to(table_ref[pl.ds(plane, 1), :], (8, 128))

        def words(i):
            return got_ref[pl.ds(row + i, 1), :]

        def parts(shift):
            start = (words(1) >> shift) & 0xFFFF
            offset = ((words(2) >> shift) & 7) << 4
            return spread_parts(
                jnp.broadcast_to(start, (8, 128)), jnp.broadcast_to(offset, (8, 128)), table
            )

        def sample(part):
            step = about_ref[source, 1, tiles].astype(jnp.float32) * (1.0 / (FULL * SCALE))
            return ((words(0) << (16 * part)) >> 16).astype(jnp.float32) * step

        return slot, sample, parts

    def chunk_tile(turn):
        return (list_ref[turn * UNROLL] >> TILE_SHIFT) & 15

    def front(turn, which):
        row_ref, picked_ref = row_refs[which % len(row_refs)], picked_refs[which % len(picked_refs)]
        blocks = [read(turn * UNROLL + u) for u in range(UNROLL)]
        for u, (_, _, parts) in enumerate(blocks):
            taps, group = parts(16)
            taps = taps.astype(jnp.bfloat16)
            group = group.astype(jnp.float32).astype(jnp.bfloat16)
            for k in range(groups):
                row_ref[16 * k : 16 * k + 16, 128 * u : 128 * u + 128] = jnp.where(
                    group == k, taps, zero
                )
        partial = jnp.dot(
            turned_ref[chunk_tile(turn)], row_ref[...], preferred_element_type=jnp.float32
        )
        for u, (_, _, parts) in enumerate(blocks):
            columns = slice(128 * u, 128 * u + 128)
            taps, group = parts(0)
            for part in range(2):
                picked = jnp.zeros((16, 128), jnp.float32)
                for k in range(groups):
                    low = part * side + 16 * k
                    picked = jnp.where(group == k, partial[low : low + 16, columns], picked)
                picked_ref[part, :, columns] = picked * taps

    def back(turn, which):
        row_ref, picked_ref = row_refs[which % len(row_refs)], picked_refs[which % len(picked_refs)]
        weighted = []
        for u in range(UNROLL):
            slot, sample, parts = read(turn * UNROLL + u)
            columns = slice(128 * u, 128 * u + 128)
            taps, group = parts(0)
            group = group.astype(jnp.float32).astype(jnp.bfloat16)
            residuals, pieces = [], []
            for part in range(2):
                model = jnp.sum(picked_ref[part, :, columns], axis=0, keepdims=True)
                residual = sample(part) - model
                residuals.append(residual)
                value = (residual * taps).astype(jnp.bfloat16)
                pieces += [jnp.where(group == k, value, zero) for k in range(groups)]
            residual_ref[slot] = jnp.concatenate(residuals, axis=0).astype(jnp.bfloat16)
            weighted.append(jnp.concatenate(pieces, axis=0))
        grid_ref[chunk_tile(turn)] += lax.dot_general(
            jnp.concatenate(weighted, axis=1),
            row_ref[...],
            (((1,), (1,)), ((), ())),
            preferred_element_type=jnp.float32,
        )

    def step(turn, carry):
        for which in range(CHUNKS):
            front(turn * CHUNKS + which + AHEAD, which + AHEAD)
            back(turn * CHUNKS + which, which)
        return carry

    for which in range(AHEAD):
        front(which, which)
    lax.fori_loop(0, scalar_div(chunks + CHUNKS - 1, CHUNKS), step, 0)
    half = tiles // 2
    member = member_ref[0]
    for t in range(half):
        own_ref[t] = grid_ref[member * half + t]
        other_ref[t] = grid_ref[(1 - member) * half + t].astype(jnp.bfloat16)


def body(visibilities, uv_cell, sub_pixel, w_plane, block_tile, model_grid, kernel_table, coupling):
    owners = lax.axis_size("tile")
    pairs = owners // 2
    _, blocks, _, rows = visibilities.shape
    capacity = 2 * (3 * blocks // owners)
    _, tiles_here, side, wide = model_grid.shape
    planes, oversample, support = kernel_table.shape
    slots = pairs * (capacity + 1)
    member = lax.axis_index("tile") // pairs
    swap = [(t, (t + pairs) % owners) for t in range(owners)]
    halves = [list(range(pairs)), list(range(pairs, owners))]

    model = lax.all_gather(
        model_grid[0],
        "tile",
        axis=0,
        tiled=True,
        axis_index_groups=[[t, t + pairs] for t in range(pairs)],
    )
    sent, slot = pl.pallas_call(
        lambda *refs: pack_kernel(pairs, capacity, tiles_here, *refs),
        out_shape=(
            jax.ShapeDtypeStruct((pairs * rows_per_source(capacity), rows), jnp.int32),
            jax.ShapeDtypeStruct((blocks,), jnp.int32),
        ),
        in_specs=[HBM] * 5,
        out_specs=(VMEM, SMEM),
        scratch_shapes=[
            pltpu.SMEM((blocks,), jnp.int32),
            pltpu.SMEM((blocks,), jnp.int32),
            pltpu.SMEM((blocks,), jnp.int32),
            pltpu.VMEM((2 * blocks, rows), jnp.float32),
            pltpu.VMEM((2 * blocks, rows), jnp.int32),
            pltpu.VMEM((2 * blocks, rows), jnp.int32),
            pltpu.VMEM((pairs, rows), jnp.int32),
            pltpu.SMEM((pairs * 2 * tiles_here,), jnp.int32),
            pltpu.SemaphoreType.DMA((5,)),
        ],
        compiler_params=WHOLE_PARAMS,
        name="pack_blocks",
    )(
        w_plane[0],
        block_tile[0],
        *[array.reshape(2 * blocks, rows) for array in (visibilities, uv_cell, sub_pixel)],
    )
    got = lax.all_to_all(
        sent, "tile", split_axis=0, concat_axis=0, tiled=True, axis_index_groups=halves
    )
    own_row = lax.dynamic_index_in_dim(coupling, lax.axis_index("freq"), 0, keepdims=False)
    slot, own_row, got = lax.optimization_barrier(
        (slot + lax.div(lax.axis_index("tile"), owners), own_row, got)
    )
    table = jnp.transpose(kernel_table, (1, 2, 0)).reshape(oversample * support, planes)
    residual, own, other = pl.pallas_call(
        lambda *refs: grid_kernel(pairs, capacity, *refs),
        out_shape=(
            jax.ShapeDtypeStruct((slots, 2, rows), jnp.bfloat16),
            jax.ShapeDtypeStruct((tiles_here, wide, side), jnp.float32),
            jax.ShapeDtypeStruct((tiles_here, wide, side), jnp.bfloat16),
        ),
        in_specs=[SMEM, VMEM, VMEM, VMEM],
        out_specs=(VMEM, VMEM, VMEM),
        scratch_shapes=[
            pltpu.VMEM((16 * oversample, 128), jnp.float32),
            pltpu.VMEM((16 * oversample, 128), jnp.float32),
            pltpu.VMEM((2 * tiles_here, wide, side), jnp.bfloat16),
            pltpu.VMEM((2 * tiles_here, wide, side), jnp.float32),
            pltpu.VMEM((pairs, 2, rows), jnp.int32),
            pltpu.SMEM((pairs, 2, rows), jnp.int32),
            pltpu.SMEM(
                (slots + capacity + (2 * tiles_here + CHUNKS + AHEAD) * UNROLL,), jnp.int32
            ),
            pltpu.SemaphoreType.DMA,
            *[pltpu.VMEM((side, UNROLL * rows), jnp.bfloat16)] * BUFFERS,
            *[pltpu.VMEM((2, 16, UNROLL * rows), jnp.float32)] * BUFFERS,
        ],
        compiler_params=PARAMS,
        name="grid_blocks",
    )(member[None], got, table, model)

    returned = lax.all_to_all(
        residual, "tile", split_axis=0, concat_axis=0, tiled=True, axis_index_groups=halves
    )
    grid_sum = own + lax.ppermute(other, "tile", swap).astype(jnp.float32)
    grids = lax.all_gather(grid_sum.astype(jnp.bfloat16)[None], "freq", axis=0, tiled=True)
    residuals, coupled_grid = pl.pallas_call(
        finish_kernel,
        out_shape=(
            jax.ShapeDtypeStruct((blocks, 2, rows), jnp.float32),
            jax.ShapeDtypeStruct((tiles_here, side, wide), jnp.float32),
        ),
        in_specs=[SMEM, SMEM, VMEM, VMEM],
        out_specs=(VMEM, VMEM),
        compiler_params=PARAMS,
        name="finish",
    )(own_row, slot, returned, grids)
    return (residuals[None], coupled_grid[None])


def solution(mesh):
    return jax.shard_map(
        body,
        mesh=mesh,
        in_specs=(
            P("freq", "tile", None, None),
            P("freq", "tile", None, None),
            P("freq", "tile", None, None),
            P("freq", "tile"),
            P("freq", "tile"),
            P("freq", "tile", None, None),
            P(),
            P(),
        ),
        out_specs=(P("freq", "tile", None, None), P("freq", "tile", None, None)),
        check_vma=False,
    )
```

```python
import jax
import jax.numpy as jnp
from jax import lax
from jax.experimental import pallas as pl
from jax.experimental.pallas import tpu as pltpu
from jax.sharding import PartitionSpec as P

UNROLL = 2
CHUNKS = 35
AHEAD = 2
BUFFERS = 5
VMEM = pl.BlockSpec(memory_space=pltpu.VMEM)
SMEM = pl.BlockSpec(memory_space=pltpu.SMEM)
HBM = pl.BlockSpec(memory_space=pltpu.HBM)
PARAMS = pltpu.CompilerParams(vmem_limit_bytes=32 * 1024 * 1024)
WHOLE_PARAMS = pltpu.CompilerParams(vmem_limit_bytes=62 * 1024 * 1024)
TILE_SHIFT = 12
PLANE_SHIFT = 16
SOURCE_SHIFT = 21
FULL = 32767
SCALE = 2.0**20


def scalar_div(value, count):
    shift = count.bit_length() - 1
    return value >> shift if count == 1 << shift else lax.div(value, count)


def first_slot(local, rank, capacity):
    half = capacity // 2
    return (local >> 1) * half + jnp.where((local & 1) == 0, rank, half - 1 - rank)


def rows_per_source(capacity):
    return (3 * (capacity + 1) + 7) // 8 * 8


def two_halves(high, low):
    return (high << 16) | (low & 0xFFFF)


def pack_kernel(pairs, capacity, tiles_here, plane_hbm, tile_hbm, vis_hbm, cell_hbm, sub_hbm,
                sent_ref, slot_ref, row_ref, plane_ref, tile_ref, vis_ref, cell_ref, sub_ref, code_ref,
                count_ref, load_sem):
    blocks = tile_ref.shape[0]
    stride = rows_per_source(capacity)
    tiles = 2 * tiles_here
    lane = lax.broadcasted_iota(jnp.int32, (1, 128), 1)
    loads = [
        pltpu.make_async_copy(source, target, load_sem.at[i])
        for i, (source, target) in enumerate(
            [
                (tile_hbm, tile_ref),
                (plane_hbm, plane_ref),
                (vis_hbm, vis_ref),
                (cell_hbm, cell_ref),
                (sub_hbm, sub_ref),
            ]
        )
    ]
    for copy in loads:
        copy.start()
    for key in range(pairs * tiles):
        count_ref[key] = 0
    for copy in loads:
        copy.wait()

    def assign(b):
        tile = tile_ref[b]
        owner = scalar_div(tile, tiles_here)
        high = (owner >= pairs).astype(jnp.int32)
        pair = owner - high * pairs
        local = tile - (owner - high) * tiles_here
        key = pair * tiles + local
        rank = count_ref[key]
        count_ref[key] = rank + 1
        place = first_slot(local, rank, capacity)
        slot_ref[b] = pair * (capacity + 1) + place
        row_ref[b] = pair * stride + 3 * place
        codes = code_ref[pl.ds(pair, 1), :]
        code_ref[pl.ds(pair, 1), :] = jnp.where(lane == place, plane_ref[b] << PLANE_SHIFT, codes)

    largest = jnp.max(jnp.max(jnp.abs(vis_ref[...]), axis=0, keepdims=True), axis=1, keepdims=True)
    largest = jnp.maximum(jnp.ceil(largest * SCALE), 1.0)
    inverse = (FULL * SCALE) / largest

    def move(four):
        rows = pl.ds(pl.multiple_of(8 * four, 8), 8)
        value = jnp.clip(jnp.round(vis_ref[rows, :] * inverse), -FULL, FULL).astype(jnp.int32)
        words = [
            two_halves(parts, pltpu.roll(parts, 7, 0))
            for parts in [value, cell_ref[rows, :], sub_ref[rows, :]]
        ]
        for u in range(4):
            row = row_ref[4 * four + u]
            for i, word in enumerate(words):
                sent_ref[pl.ds(row + i, 1), :] = word[2 * u : 2 * u + 1]

    def step(turn, carry):
        for which in range(8):
            assign(8 * turn + 8 + which)
        move(2 * turn)
        move(2 * turn + 1)
        return carry

    for which in range(8):
        assign(which)
    lax.fori_loop(0, blocks // 8 - 1, step, 0)
    move(blocks // 4 - 2)
    move(blocks // 4 - 1)
    for d in range(pairs):
        counts = jnp.broadcast_to(largest.astype(jnp.int32), (1, 128))
        for t in range(tiles):
            counts = jnp.where(lane == t, count_ref[d * tiles + t], counts)
        row = d * stride + 3 * capacity
        sent_ref[row : row + 1, :] = code_ref[d : d + 1, :]
        sent_ref[row + 1 : row + 2, :] = jnp.zeros((1, 128), jnp.int32)
        sent_ref[row + 2 : row + 3, :] = counts


def finish_kernel(row_ref, slot_ref, returned_ref, grid_ref, residual_ref, coupled_ref):
    planes, tiles_here = grid_ref.shape[:2]
    for t in range(tiles_here):
        coupled_ref[t] = sum(
            row_ref[g] * grid_ref[g, t].astype(jnp.float32) for g in range(planes)
        ).T

    def step(turn, carry):
        for which in range(8):
            b = turn * 8 + which
            residual_ref[b] = returned_ref[slot_ref[b]].astype(jnp.float32)
        return carry

    lax.fori_loop(0, residual_ref.shape[0] // 8, step, 0)


def spread_parts(start, offset, table):
    sublane = lax.broadcasted_iota(jnp.int32, (8, 128), 0)
    taps, group = [], []
    for low in (0, 8):
        delta = sublane + low - start
        taps.append(
            jnp.take_along_axis(table, (delta & 15) + offset, axis=1, mode="promise_in_bounds")
        )
        group.append((15 - delta) >> 4)
    return jnp.concatenate(taps, axis=0), jnp.concatenate(group, axis=0)


def grid_kernel(pairs, capacity, member_ref, got_ref, table_ref, model_ref, residual_ref, own_ref,
                other_ref, turned_ref, grid_ref, code_ref, about_ref, list_ref, sem, *buffers):
    row_refs, picked_refs = buffers[:BUFFERS], buffers[BUFFERS:]
    tiles, side, wide = model_ref.shape
    groups = side // 16
    zero_row = table_ref.shape[0] - 8
    stride = rows_per_source(capacity)
    lane = lax.broadcasted_iota(jnp.int32, (1, 128), 1)
    for s in range(pairs):
        row = s * stride + 3 * capacity
        code_ref[s, 0:1, :] = got_ref[row : row + 1, :] + (
            lane + s * (capacity + 1) + (s << SOURCE_SHIFT)
        )
        code_ref[s, 1:2, :] = got_ref[row + 2 : row + 3, :]
    fill = pltpu.make_async_copy(code_ref, about_ref, sem)
    fill.start()
    for t in range(tiles):
        turned_ref[t] = model_ref[t].T
    grid_ref[...] = jnp.zeros_like(grid_ref)
    fill.wait()

    start = jnp.int32(0)
    for t in range(tiles):
        count = jnp.int32(0)
        for s in range(pairs):
            count = count + about_ref[s, 1, t]
        spare = -count & (UNROLL - 1)
        for u in range(UNROLL):
            list_ref[start + u] = (zero_row << PLANE_SHIFT) + (t << TILE_SHIFT) + capacity

        def enlist(s, filled, t=t):
            found = about_ref[s, 1, t]

            def some(low, high):
                for k in range(low, high):
                    place = k if t % 2 == 0 else capacity // 2 - 1 - k
                    code = about_ref[s, 0, t // 2 * (capacity // 2) + place]
                    list_ref[filled + k] = code + (t << TILE_SHIFT)

            few = capacity // 3

            @pl.when(found > 0)
            def _():
                some(0, few)

                @pl.when(found > few)
                def _():
                    some(few, capacity // 2)

            return filled + found

        lax.fori_loop(0, pairs, enlist, start + spare)
        start = start + count + spare
    for u in range((CHUNKS + AHEAD) * UNROLL):
        list_ref[start + u] = (zero_row << PLANE_SHIFT) + capacity
    chunks = start >> UNROLL.bit_length() - 1
    zero = jnp.zeros((16, 128), jnp.bfloat16)

    def read(which):
        entry = list_ref[which]
        slot = entry & ((1 << TILE_SHIFT) - 1)
        plane = (entry >> PLANE_SHIFT) & ((1 << (SOURCE_SHIFT - PLANE_SHIFT)) - 1)
        source = entry >> SOURCE_SHIFT
        row = 3 * slot + source * (stride - 3 * (capacity + 1))
        table = jnp.broadcast_to(table_ref[pl.ds(plane, 1), :], (8, 128))

        def words(i):
            return got_ref[pl.ds(row + i, 1), :]

        def parts(shift):
            start = (words(1) >> shift) & 0xFFFF
            offset = ((words(2) >> shift) & 7) << 4
            return spread_parts(
                jnp.broadcast_to(start, (8, 128)), jnp.broadcast_to(offset, (8, 128)), table
            )

        def sample(part):
            step = about_ref[source, 1, tiles].astype(jnp.float32) * (1.0 / (FULL * SCALE))
            return ((words(0) << (16 * part)) >> 16).astype(jnp.float32) * step

        return slot, sample, parts

    def chunk_tile(turn):
        return (list_ref[turn * UNROLL] >> TILE_SHIFT) & 15

    def front(turn, which):
        row_ref, picked_ref = row_refs[which % len(row_refs)], picked_refs[which % len(picked_refs)]
        blocks = [read(turn * UNROLL + u) for u in range(UNROLL)]
        matrices = []
        for _, _, parts in blocks:
            taps, group = parts(16)
            taps = taps.astype(jnp.bfloat16)
            group = group.astype(jnp.float32).astype(jnp.bfloat16)
            matrices.append(
                jnp.concatenate([jnp.where(group == k, taps, zero) for k in range(groups)], axis=0)
            )
        row_matrix = jnp.concatenate(matrices, axis=1)
        row_ref[...] = row_matrix
        partial = jnp.dot(
            turned_ref[chunk_tile(turn)], row_matrix, preferred_element_type=jnp.float32
        )
        for u, (_, _, parts) in enumerate(blocks):
            columns = slice(128 * u, 128 * u + 128)
            taps, group = parts(0)
            for part in range(2):
                picked = jnp.zeros((16, 128), jnp.float32)
                for k in range(groups):
                    low = part * side + 16 * k
                    picked = jnp.where(group == k, partial[low : low + 16, columns], picked)
                picked_ref[part, :, columns] = picked * taps

    def back(turn, which):
        row_ref, picked_ref = row_refs[which % len(row_refs)], picked_refs[which % len(picked_refs)]
        weighted = []
        for u in range(UNROLL):
            slot, sample, parts = read(turn * UNROLL + u)
            columns = slice(128 * u, 128 * u + 128)
            taps, group = parts(0)
            group = group.astype(jnp.float32).astype(jnp.bfloat16)
            residuals, pieces = [], []
            for part in range(2):
                model = jnp.sum(picked_ref[part, :, columns], axis=0, keepdims=True)
                residual = sample(part) - model
                residuals.append(residual)
                value = (residual * taps).astype(jnp.bfloat16)
                pieces += [jnp.where(group == k, value, zero) for k in range(groups)]
            residual_ref[slot] = jnp.concatenate(residuals, axis=0).astype(jnp.bfloat16)
            weighted.append(jnp.concatenate(pieces, axis=0))
        grid_ref[chunk_tile(turn)] += lax.dot_general(
            jnp.concatenate(weighted, axis=1),
            row_ref[...],
            (((1,), (1,)), ((), ())),
            preferred_element_type=jnp.float32,
        )

    def step(turn, carry):
        for which in range(CHUNKS):
            front(turn * CHUNKS + which + AHEAD, which + AHEAD)
            back(turn * CHUNKS + which, which)
        return carry

    for which in range(AHEAD):
        front(which, which)
    lax.fori_loop(0, scalar_div(chunks + CHUNKS - 1, CHUNKS), step, 0)
    half = tiles // 2
    member = member_ref[0]
    for t in range(half):
        own_ref[t] = grid_ref[member * half + t]
        other_ref[t] = grid_ref[(1 - member) * half + t].astype(jnp.bfloat16)


def body(visibilities, uv_cell, sub_pixel, w_plane, block_tile, model_grid, kernel_table, coupling):
    owners = lax.axis_size("tile")
    pairs = owners // 2
    _, blocks, _, rows = visibilities.shape
    capacity = 2 * (3 * blocks // owners)
    _, tiles_here, side, wide = model_grid.shape
    planes, oversample, support = kernel_table.shape
    slots = pairs * (capacity + 1)
    member = lax.axis_index("tile") // pairs
    swap = [(t, (t + pairs) % owners) for t in range(owners)]
    halves = [list(range(pairs)), list(range(pairs, owners))]

    model = lax.all_gather(
        model_grid[0],
        "tile",
        axis=0,
        tiled=True,
        axis_index_groups=[[t, t + pairs] for t in range(pairs)],
    )
    sent, slot = pl.pallas_call(
        lambda *refs: pack_kernel(pairs, capacity, tiles_here, *refs),
        out_shape=(
            jax.ShapeDtypeStruct((pairs * rows_per_source(capacity), rows), jnp.int32),
            jax.ShapeDtypeStruct((blocks,), jnp.int32),
        ),
        in_specs=[HBM] * 5,
        out_specs=(VMEM, SMEM),
        scratch_shapes=[
            pltpu.SMEM((blocks,), jnp.int32),
            pltpu.SMEM((blocks,), jnp.int32),
            pltpu.SMEM((blocks,), jnp.int32),
            pltpu.VMEM((2 * blocks, rows), jnp.float32),
            pltpu.VMEM((2 * blocks, rows), jnp.int32),
            pltpu.VMEM((2 * blocks, rows), jnp.int32),
            pltpu.VMEM((pairs, rows), jnp.int32),
            pltpu.SMEM((pairs * 2 * tiles_here,), jnp.int32),
            pltpu.SemaphoreType.DMA((5,)),
        ],
        compiler_params=WHOLE_PARAMS,
        name="pack_blocks",
    )(
        w_plane[0],
        block_tile[0],
        *[array.reshape(2 * blocks, rows) for array in (visibilities, uv_cell, sub_pixel)],
    )
    got = lax.all_to_all(
        sent, "tile", split_axis=0, concat_axis=0, tiled=True, axis_index_groups=halves
    )
    own_row = lax.dynamic_index_in_dim(coupling, lax.axis_index("freq"), 0, keepdims=False)
    slot, own_row, got = lax.optimization_barrier(
        (slot + lax.div(lax.axis_index("tile"), owners), own_row, got)
    )
    table = jnp.pad(
        kernel_table.astype(jnp.float32), ((0, 8), (0, 0), (0, 16 - support))
    ).reshape(planes + 8, 16 * oversample)
    residual, own, other = pl.pallas_call(
        lambda *refs: grid_kernel(pairs, capacity, *refs),
        out_shape=(
            jax.ShapeDtypeStruct((slots, 2, rows), jnp.bfloat16),
            jax.ShapeDtypeStruct((tiles_here, wide, side), jnp.float32),
            jax.ShapeDtypeStruct((tiles_here, wide, side), jnp.bfloat16),
        ),
        in_specs=[SMEM, VMEM, VMEM, VMEM],
        out_specs=(VMEM, VMEM, VMEM),
        scratch_shapes=[
            pltpu.VMEM((2 * tiles_here, wide, side), jnp.bfloat16),
            pltpu.VMEM((2 * tiles_here, wide, side), jnp.float32),
            pltpu.VMEM((pairs, 2, rows), jnp.int32),
            pltpu.SMEM((pairs, 2, rows), jnp.int32),
            pltpu.SMEM(
                (slots + capacity + (2 * tiles_here + CHUNKS + AHEAD) * UNROLL,), jnp.int32
            ),
            pltpu.SemaphoreType.DMA,
            *[pltpu.VMEM((side, UNROLL * rows), jnp.bfloat16)] * BUFFERS,
            *[pltpu.VMEM((2, 16, UNROLL * rows), jnp.float32)] * BUFFERS,
        ],
        compiler_params=PARAMS,
        name="grid_blocks",
    )(member[None], got, table, model)

    returned = lax.all_to_all(
        residual, "tile", split_axis=0, concat_axis=0, tiled=True, axis_index_groups=halves
    )
    grid_sum = own + lax.ppermute(other, "tile", swap).astype(jnp.float32)
    grids = lax.all_gather(grid_sum.astype(jnp.bfloat16)[None], "freq", axis=0, tiled=True)
    residuals, coupled_grid = pl.pallas_call(
        finish_kernel,
        out_shape=(
            jax.ShapeDtypeStruct((blocks, 2, rows), jnp.float32),
            jax.ShapeDtypeStruct((tiles_here, side, wide), jnp.float32),
        ),
        in_specs=[SMEM, SMEM, VMEM, VMEM],
        out_specs=(VMEM, VMEM),
        compiler_params=PARAMS,
        name="finish",
    )(own_row, slot, returned, grids)
    return (residuals[None], coupled_grid[None])


def solution(mesh):
    return jax.shard_map(
        body,
        mesh=mesh,
        in_specs=(
            P("freq", "tile", None, None),
            P("freq", "tile", None, None),
            P("freq", "tile", None, None),
            P("freq", "tile"),
            P("freq", "tile"),
            P("freq", "tile", None, None),
            P(),
            P(),
        ),
        out_specs=(P("freq", "tile", None, None), P("freq", "tile", None, None)),
        check_vma=False,
    )
```

```python
import jax
import jax.numpy as jnp
from jax import lax
from jax.experimental import pallas as pl
from jax.experimental.pallas import tpu as pltpu
from jax.sharding import PartitionSpec as P

UNROLL = 2
CHUNKS = 35
AHEAD = 3
BUFFERS = 5
VMEM = pl.BlockSpec(memory_space=pltpu.VMEM)
SMEM = pl.BlockSpec(memory_space=pltpu.SMEM)
HBM = pl.BlockSpec(memory_space=pltpu.HBM)
PARAMS = pltpu.CompilerParams(vmem_limit_bytes=32 * 1024 * 1024)
WHOLE_PARAMS = pltpu.CompilerParams(vmem_limit_bytes=62 * 1024 * 1024)
TILE_SHIFT = 12
PLANE_SHIFT = 16
SOURCE_SHIFT = 21
FULL = 32767
SCALE = 2.0**20


def scalar_div(value, count):
    shift = count.bit_length() - 1
    return value >> shift if count == 1 << shift else lax.div(value, count)


def first_slot(local, rank, capacity):
    half = capacity // 2
    return (local >> 1) * half + jnp.where((local & 1) == 0, rank, half - 1 - rank)


def rows_per_source(capacity):
    return (3 * (capacity + 1) + 7) // 8 * 8


def two_halves(high, low):
    return (high << 16) | (low & 0xFFFF)


def pack_kernel(pairs, capacity, tiles_here, plane_hbm, tile_hbm, vis_hbm, cell_hbm, sub_hbm,
                sent_ref, slot_ref, row_ref, plane_ref, tile_ref, vis_ref, cell_ref, sub_ref, code_ref,
                count_ref, load_sem):
    blocks = tile_ref.shape[0]
    stride = rows_per_source(capacity)
    tiles = 2 * tiles_here
    lane = lax.broadcasted_iota(jnp.int32, (1, 128), 1)
    loads = [
        pltpu.make_async_copy(source, target, load_sem.at[i])
        for i, (source, target) in enumerate(
            [
                (tile_hbm, tile_ref),
                (plane_hbm, plane_ref),
                (vis_hbm, vis_ref),
                (cell_hbm, cell_ref),
                (sub_hbm, sub_ref),
            ]
        )
    ]
    for copy in loads:
        copy.start()
    for key in range(pairs * tiles):
        count_ref[key] = 0
    for copy in loads:
        copy.wait()

    def assign(b):
        tile = tile_ref[b]
        owner = scalar_div(tile, tiles_here)
        high = (owner >= pairs).astype(jnp.int32)
        pair = owner - high * pairs
        local = tile - (owner - high) * tiles_here
        key = pair * tiles + local
        rank = count_ref[key]
        count_ref[key] = rank + 1
        place = first_slot(local, rank, capacity)
        slot_ref[b] = pair * (capacity + 1) + place
        row_ref[b] = pair * stride + 3 * place
        codes = code_ref[pl.ds(pair, 1), :]
        code_ref[pl.ds(pair, 1), :] = jnp.where(lane == place, plane_ref[b] << PLANE_SHIFT, codes)

    largest = jnp.max(jnp.max(jnp.abs(vis_ref[...]), axis=0, keepdims=True), axis=1, keepdims=True)
    largest = jnp.maximum(jnp.ceil(largest * SCALE), 1.0)
    inverse = (FULL * SCALE) / largest

    def move(four):
        rows = pl.ds(pl.multiple_of(8 * four, 8), 8)
        value = jnp.clip(jnp.round(vis_ref[rows, :] * inverse), -FULL, FULL).astype(jnp.int32)
        words = [
            two_halves(parts, pltpu.roll(parts, 7, 0))
            for parts in [value, cell_ref[rows, :], sub_ref[rows, :]]
        ]
        for u in range(4):
            row = row_ref[4 * four + u]
            for i, word in enumerate(words):
                sent_ref[pl.ds(row + i, 1), :] = word[2 * u : 2 * u + 1]

    def step(turn, carry):
        for which in range(8):
            assign(8 * turn + 8 + which)
        move(2 * turn)
        move(2 * turn + 1)
        return carry

    for which in range(8):
        assign(which)
    lax.fori_loop(0, blocks // 8 - 1, step, 0)
    move(blocks // 4 - 2)
    move(blocks // 4 - 1)
    for d in range(pairs):
        counts = jnp.broadcast_to(largest.astype(jnp.int32), (1, 128))
        for t in range(tiles):
            counts = jnp.where(lane == t, count_ref[d * tiles + t], counts)
        row = d * stride + 3 * capacity
        sent_ref[row : row + 1, :] = code_ref[d : d + 1, :]
        sent_ref[row + 1 : row + 2, :] = jnp.zeros((1, 128), jnp.int32)
        sent_ref[row + 2 : row + 3, :] = counts


def finish_kernel(row_ref, slot_ref, returned_ref, grid_ref, residual_ref, coupled_hbm, coupled_ref, sem):
    planes, tiles_here = grid_ref.shape[:2]
    for t in range(tiles_here):
        coupled_ref[t] = sum(
            row_ref[g] * grid_ref[g, t].astype(jnp.float32) for g in range(planes)
        ).T
    leave = pltpu.make_async_copy(coupled_ref, coupled_hbm, sem)
    leave.start()

    def step(turn, carry):
        for which in range(8):
            b = turn * 8 + which
            residual_ref[b] = returned_ref[slot_ref[b]].astype(jnp.float32)
        return carry

    lax.fori_loop(0, residual_ref.shape[0] // 8, step, 0)
    leave.wait()


def spread_parts(start, offset, table):
    sublane = lax.broadcasted_iota(jnp.int32, (8, 128), 0)
    taps, group = [], []
    for low in (0, 8):
        delta = sublane + low - start
        taps.append(
            jnp.take_along_axis(table, (delta & 15) + offset, axis=1, mode="promise_in_bounds")
        )
        group.append((15 - delta) >> 4)
    return jnp.concatenate(taps, axis=0), jnp.concatenate(group, axis=0)


def grid_kernel(pairs, capacity, member_ref, got_ref, table_ref, model_ref, residual_ref, own_ref,
                other_ref, turned_ref, grid_ref, code_ref, about_ref, list_ref, sem, *buffers):
    row_refs, picked_refs = buffers[:BUFFERS], buffers[BUFFERS:]
    tiles, side, wide = model_ref.shape
    groups = side // 16
    zero_row = table_ref.shape[0] - 8
    stride = rows_per_source(capacity)
    lane = lax.broadcasted_iota(jnp.int32, (1, 128), 1)
    for s in range(pairs):
        row = s * stride + 3 * capacity
        code_ref[s, 0:1, :] = got_ref[row : row + 1, :] + (
            lane + s * (capacity + 1) + (s << SOURCE_SHIFT)
        )
        code_ref[s, 1:2, :] = got_ref[row + 2 : row + 3, :]
    fill = pltpu.make_async_copy(code_ref, about_ref, sem)
    fill.start()
    for t in range(tiles):
        turned_ref[t] = model_ref[t].T
    grid_ref[...] = jnp.zeros_like(grid_ref)
    fill.wait()

    start = jnp.int32(0)
    for t in range(tiles):
        count = jnp.int32(0)
        for s in range(pairs):
            count = count + about_ref[s, 1, t]
        spare = -count & (UNROLL - 1)
        for u in range(UNROLL):
            list_ref[start + u] = (zero_row << PLANE_SHIFT) + (t << TILE_SHIFT) + capacity

        def enlist(s, filled, t=t):
            found = about_ref[s, 1, t]

            def some(low, high):
                for k in range(low, high):
                    place = k if t % 2 == 0 else capacity // 2 - 1 - k
                    code = about_ref[s, 0, t // 2 * (capacity // 2) + place]
                    list_ref[filled + k] = code + (t << TILE_SHIFT)

            few = capacity // 3

            @pl.when(found > 0)
            def _():
                some(0, few)

                @pl.when(found > few)
                def _():
                    some(few, capacity // 2)

            return filled + found

        lax.fori_loop(0, pairs, enlist, start + spare)
        start = start + count + spare
    for u in range((CHUNKS + AHEAD) * UNROLL):
        list_ref[start + u] = (zero_row << PLANE_SHIFT) + capacity
    chunks = start >> UNROLL.bit_length() - 1
    zero = jnp.zeros((16, 128), jnp.bfloat16)

    def read(which):
        entry = list_ref[which]
        slot = entry & ((1 << TILE_SHIFT) - 1)
        plane = (entry >> PLANE_SHIFT) & ((1 << (SOURCE_SHIFT - PLANE_SHIFT)) - 1)
        source = entry >> SOURCE_SHIFT
        row = 3 * slot + source * (stride - 3 * (capacity + 1))
        table = jnp.broadcast_to(table_ref[pl.ds(plane, 1), :], (8, 128))

        def words(i):
            return got_ref[pl.ds(row + i, 1), :]

        def parts(shift):
            start = (words(1) >> shift) & 0xFFFF
            offset = ((words(2) >> shift) & 7) << 4
            return spread_parts(
                jnp.broadcast_to(start, (8, 128)), jnp.broadcast_to(offset, (8, 128)), table
            )

        def sample(part):
            step = about_ref[source, 1, tiles].astype(jnp.float32) * (1.0 / (FULL * SCALE))
            return ((words(0) << (16 * part)) >> 16).astype(jnp.float32) * step

        return slot, sample, parts

    def chunk_tile(turn):
        return (list_ref[turn * UNROLL] >> TILE_SHIFT) & 15

    def front(turn, which):
        row_ref, picked_ref = row_refs[which % len(row_refs)], picked_refs[which % len(picked_refs)]
        blocks = [read(turn * UNROLL + u) for u in range(UNROLL)]
        matrices = []
        for _, _, parts in blocks:
            taps, group = parts(16)
            taps = taps.astype(jnp.bfloat16)
            group = group.astype(jnp.float32).astype(jnp.bfloat16)
            matrices.append(
                jnp.concatenate([jnp.where(group == k, taps, zero) for k in range(groups)], axis=0)
            )
        row_matrix = jnp.concatenate(matrices, axis=1)
        row_ref[...] = row_matrix
        partial = jnp.dot(
            turned_ref[chunk_tile(turn)], row_matrix, preferred_element_type=jnp.float32
        )
        for u, (_, _, parts) in enumerate(blocks):
            columns = slice(128 * u, 128 * u + 128)
            taps, group = parts(0)
            for part in range(2):
                picked = jnp.zeros((16, 128), jnp.float32)
                for k in range(groups):
                    low = part * side + 16 * k
                    picked = jnp.where(group == k, partial[low : low + 16, columns], picked)
                picked_ref[part, :, columns] = picked * taps

    def back(turn, which):
        row_ref, picked_ref = row_refs[which % len(row_refs)], picked_refs[which % len(picked_refs)]
        weighted = []
        for u in range(UNROLL):
            slot, sample, parts = read(turn * UNROLL + u)
            columns = slice(128 * u, 128 * u + 128)
            taps, group = parts(0)
            group = group.astype(jnp.float32).astype(jnp.bfloat16)
            residuals, pieces = [], []
            for part in range(2):
                model = jnp.sum(picked_ref[part, :, columns], axis=0, keepdims=True)
                residual = sample(part) - model
                residuals.append(residual)
                value = (residual * taps).astype(jnp.bfloat16)
                pieces += [jnp.where(group == k, value, zero) for k in range(groups)]
            residual_ref[slot] = jnp.concatenate(residuals, axis=0).astype(jnp.bfloat16)
            weighted.append(jnp.concatenate(pieces, axis=0))
        grid_ref[chunk_tile(turn)] += lax.dot_general(
            jnp.concatenate(weighted, axis=1),
            row_ref[...],
            (((1,), (1,)), ((), ())),
            preferred_element_type=jnp.float32,
        )

    def step(turn, carry):
        for which in range(CHUNKS):
            front(turn * CHUNKS + which + AHEAD, which + AHEAD)
            back(turn * CHUNKS + which, which)
        return carry

    for which in range(AHEAD):
        front(which, which)
    lax.fori_loop(0, scalar_div(chunks + CHUNKS - 1, CHUNKS), step, 0)
    half = tiles // 2
    member = member_ref[0]
    for t in range(half):
        own_ref[t] = grid_ref[member * half + t]
        other_ref[t] = grid_ref[(1 - member) * half + t].astype(jnp.bfloat16)


def body(visibilities, uv_cell, sub_pixel, w_plane, block_tile, model_grid, kernel_table, coupling):
    owners = lax.axis_size("tile")
    pairs = owners // 2
    _, blocks, _, rows = visibilities.shape
    capacity = 2 * (3 * blocks // owners)
    _, tiles_here, side, wide = model_grid.shape
    planes, oversample, support = kernel_table.shape
    slots = pairs * (capacity + 1)
    member = lax.axis_index("tile") // pairs
    swap = [(t, (t + pairs) % owners) for t in range(owners)]
    halves = [list(range(pairs)), list(range(pairs, owners))]

    model = lax.all_gather(
        model_grid[0],
        "tile",
        axis=0,
        tiled=True,
        axis_index_groups=[[t, t + pairs] for t in range(pairs)],
    )
    sent, slot = pl.pallas_call(
        lambda *refs: pack_kernel(pairs, capacity, tiles_here, *refs),
        out_shape=(
            jax.ShapeDtypeStruct((pairs * rows_per_source(capacity), rows), jnp.int32),
            jax.ShapeDtypeStruct((blocks,), jnp.int32),
        ),
        in_specs=[HBM] * 5,
        out_specs=(VMEM, SMEM),
        scratch_shapes=[
            pltpu.SMEM((blocks,), jnp.int32),
            pltpu.SMEM((blocks,), jnp.int32),
            pltpu.SMEM((blocks,), jnp.int32),
            pltpu.VMEM((2 * blocks, rows), jnp.float32),
            pltpu.VMEM((2 * blocks, rows), jnp.int32),
            pltpu.VMEM((2 * blocks, rows), jnp.int32),
            pltpu.VMEM((pairs, rows), jnp.int32),
            pltpu.SMEM((pairs * 2 * tiles_here,), jnp.int32),
            pltpu.SemaphoreType.DMA((5,)),
        ],
        compiler_params=WHOLE_PARAMS,
        name="pack_blocks",
    )(
        w_plane[0],
        block_tile[0],
        *[array.reshape(2 * blocks, rows) for array in (visibilities, uv_cell, sub_pixel)],
    )
    got = lax.all_to_all(
        sent, "tile", split_axis=0, concat_axis=0, tiled=True, axis_index_groups=halves
    )
    own_row = lax.dynamic_index_in_dim(coupling, lax.axis_index("freq"), 0, keepdims=False)
    slot, own_row, got = lax.optimization_barrier(
        (slot + lax.div(lax.axis_index("tile"), owners), own_row, got)
    )
    table = jnp.pad(
        kernel_table.astype(jnp.float32), ((0, 8), (0, 0), (0, 16 - support))
    ).reshape(planes + 8, 16 * oversample)
    residual, own, other = pl.pallas_call(
        lambda *refs: grid_kernel(pairs, capacity, *refs),
        out_shape=(
            jax.ShapeDtypeStruct((slots, 2, rows), jnp.bfloat16),
            jax.ShapeDtypeStruct((tiles_here, wide, side), jnp.float32),
            jax.ShapeDtypeStruct((tiles_here, wide, side), jnp.bfloat16),
        ),
        in_specs=[SMEM, VMEM, VMEM, VMEM],
        out_specs=(VMEM, VMEM, VMEM),
        scratch_shapes=[
            pltpu.VMEM((2 * tiles_here, wide, side), jnp.bfloat16),
            pltpu.VMEM((2 * tiles_here, wide, side), jnp.float32),
            pltpu.VMEM((pairs, 2, rows), jnp.int32),
            pltpu.SMEM((pairs, 2, rows), jnp.int32),
            pltpu.SMEM(
                (slots + capacity + (2 * tiles_here + CHUNKS + AHEAD) * UNROLL,), jnp.int32
            ),
            pltpu.SemaphoreType.DMA,
            *[pltpu.VMEM((side, UNROLL * rows), jnp.bfloat16)] * BUFFERS,
            *[pltpu.VMEM((2, 16, UNROLL * rows), jnp.float32)] * BUFFERS,
        ],
        compiler_params=PARAMS,
        name="grid_blocks",
    )(member[None], got, table, model)

    returned = lax.all_to_all(
        residual, "tile", split_axis=0, concat_axis=0, tiled=True, axis_index_groups=halves
    )
    grid_sum = own + lax.ppermute(other, "tile", swap).astype(jnp.float32)
    grids = lax.all_gather(grid_sum.astype(jnp.bfloat16)[None], "freq", axis=0, tiled=True)
    residuals, coupled_grid = pl.pallas_call(
        finish_kernel,
        out_shape=(
            jax.ShapeDtypeStruct((blocks, 2, rows), jnp.float32),
            jax.ShapeDtypeStruct((tiles_here, side, wide), jnp.float32),
        ),
        in_specs=[SMEM, SMEM, VMEM, VMEM],
        out_specs=(VMEM, HBM),
        scratch_shapes=[
            pltpu.VMEM((tiles_here, side, wide), jnp.float32),
            pltpu.SemaphoreType.DMA,
        ],
        compiler_params=PARAMS,
        name="finish",
    )(own_row, slot, returned, grids)
    return (residuals[None], coupled_grid[None])


def solution(mesh):
    return jax.shard_map(
        body,
        mesh=mesh,
        in_specs=(
            P("freq", "tile", None, None),
            P("freq", "tile", None, None),
            P("freq", "tile", None, None),
            P("freq", "tile"),
            P("freq", "tile"),
            P("freq", "tile", None, None),
            P(),
            P(),
        ),
        out_specs=(P("freq", "tile", None, None), P("freq", "tile", None, None)),
        check_vma=False,
    )
```

```python
import jax
import jax.numpy as jnp
from jax import lax
from jax.experimental import pallas as pl
from jax.experimental.pallas import tpu as pltpu
from jax.sharding import PartitionSpec as P

UNROLL = 2
CHUNKS = 35
AHEAD = 2
BUFFERS = 5
VMEM = pl.BlockSpec(memory_space=pltpu.VMEM)
SMEM = pl.BlockSpec(memory_space=pltpu.SMEM)
HBM = pl.BlockSpec(memory_space=pltpu.HBM)
PARAMS = pltpu.CompilerParams(vmem_limit_bytes=32 * 1024 * 1024)
WHOLE_PARAMS = pltpu.CompilerParams(vmem_limit_bytes=62 * 1024 * 1024)
TILE_SHIFT = 12
PLANE_SHIFT = 16
SOURCE_SHIFT = 21
FULL = 32767
SCALE = 2.0**20


def scalar_div(value, count):
    shift = count.bit_length() - 1
    return value >> shift if count == 1 << shift else lax.div(value, count)


def first_slot(local, rank, capacity):
    half = capacity // 2
    return (local >> 1) * half + jnp.where((local & 1) == 0, rank, half - 1 - rank)


def rows_per_source(capacity):
    return (3 * (capacity + 1) + 7) // 8 * 8


def two_halves(high, low):
    return (high << 16) | (low & 0xFFFF)


def pack_kernel(pairs, capacity, tiles_here, plane_hbm, tile_hbm, vis_hbm, cell_hbm, sub_hbm,
                sent_ref, slot_ref, row_ref, plane_ref, tile_ref, vis_ref, cell_ref, sub_ref, code_ref,
                count_ref, load_sem):
    blocks = tile_ref.shape[0]
    stride = rows_per_source(capacity)
    tiles = 2 * tiles_here
    lane = lax.broadcasted_iota(jnp.int32, (1, 128), 1)
    loads = [
        pltpu.make_async_copy(source, target, load_sem.at[i])
        for i, (source, target) in enumerate(
            [
                (tile_hbm, tile_ref),
                (plane_hbm, plane_ref),
                (vis_hbm, vis_ref),
                (cell_hbm, cell_ref),
                (sub_hbm, sub_ref),
            ]
        )
    ]
    for copy in loads:
        copy.start()
    for key in range(pairs * tiles):
        count_ref[key] = 0
    for copy in loads:
        copy.wait()

    def assign(b):
        tile = tile_ref[b]
        owner = scalar_div(tile, tiles_here)
        high = (owner >= pairs).astype(jnp.int32)
        pair = owner - high * pairs
        local = tile - (owner - high) * tiles_here
        key = pair * tiles + local
        rank = count_ref[key]
        count_ref[key] = rank + 1
        place = first_slot(local, rank, capacity)
        slot_ref[b] = pair * (capacity + 1) + place
        row_ref[b] = pair * stride + 3 * place
        codes = code_ref[pl.ds(pair, 1), :]
        code_ref[pl.ds(pair, 1), :] = jnp.where(lane == place, plane_ref[b] << PLANE_SHIFT, codes)

    largest = jnp.max(jnp.max(jnp.abs(vis_ref[...]), axis=0, keepdims=True), axis=1, keepdims=True)
    largest = jnp.maximum(jnp.ceil(largest * SCALE), 1.0)
    inverse = (FULL * SCALE) / largest

    def move(four):
        rows = pl.ds(pl.multiple_of(8 * four, 8), 8)
        value = jnp.clip(jnp.round(vis_ref[rows, :] * inverse), -FULL, FULL).astype(jnp.int32)
        words = [
            two_halves(parts, pltpu.roll(parts, 7, 0))
            for parts in [value, cell_ref[rows, :], sub_ref[rows, :]]
        ]
        for u in range(4):
            row = row_ref[4 * four + u]
            for i, word in enumerate(words):
                sent_ref[pl.ds(row + i, 1), :] = word[2 * u : 2 * u + 1]

    def step(turn, carry):
        for which in range(8):
            assign(8 * turn + 8 + which)
        move(2 * turn)
        move(2 * turn + 1)
        return carry

    for which in range(8):
        assign(which)
    lax.fori_loop(0, blocks // 8 - 1, step, 0)
    move(blocks // 4 - 2)
    move(blocks // 4 - 1)
    for d in range(pairs):
        counts = jnp.broadcast_to(largest.astype(jnp.int32), (1, 128))
        for t in range(tiles):
            counts = jnp.where(lane == t, count_ref[d * tiles + t], counts)
        row = d * stride + 3 * capacity
        sent_ref[row : row + 1, :] = code_ref[d : d + 1, :]
        sent_ref[row + 1 : row + 2, :] = jnp.zeros((1, 128), jnp.int32)
        sent_ref[row + 2 : row + 3, :] = counts


def finish_kernel(row_ref, slot_ref, returned_ref, grid_ref, residual_ref, coupled_ref):
    planes, tiles_here = grid_ref.shape[:2]
    for t in range(tiles_here):
        coupled_ref[t] = sum(
            row_ref[g] * grid_ref[g, t].astype(jnp.float32) for g in range(planes)
        ).T

    def step(turn, carry):
        for which in range(8):
            b = turn * 8 + which
            residual_ref[b] = returned_ref[slot_ref[b]].astype(jnp.float32)
        return carry

    lax.fori_loop(0, residual_ref.shape[0] // 8, step, 0)


def spread_parts(start, offset, table):
    sublane = lax.broadcasted_iota(jnp.int32, (8, 128), 0)
    taps, group = [], []
    for low in (0, 8):
        delta = sublane + low - start
        taps.append(
            jnp.take_along_axis(table, (delta & 15) + offset, axis=1, mode="promise_in_bounds")
        )
        group.append((15 - delta) >> 4)
    return jnp.concatenate(taps, axis=0), jnp.concatenate(group, axis=0)


def grid_kernel(pairs, capacity, member_ref, got_ref, table_ref, model_ref, residual_ref, own_ref,
                other_ref, turned_ref, grid_ref, code_ref, about_ref, list_ref, sem, *buffers):
    row_refs, kept_refs = buffers[:BUFFERS], buffers[BUFFERS:]
    tiles, side, wide = model_ref.shape
    groups = side // 16
    zero_row = table_ref.shape[0] - 8
    stride = rows_per_source(capacity)
    lane = lax.broadcasted_iota(jnp.int32, (1, 128), 1)
    for s in range(pairs):
        row = s * stride + 3 * capacity
        code_ref[s, 0:1, :] = got_ref[row : row + 1, :] + (
            lane + s * (capacity + 1) + (s << SOURCE_SHIFT)
        )
        code_ref[s, 1:2, :] = got_ref[row + 2 : row + 3, :]
    fill = pltpu.make_async_copy(code_ref, about_ref, sem)
    fill.start()
    for t in range(tiles):
        turned_ref[t] = model_ref[t].T
    grid_ref[...] = jnp.zeros_like(grid_ref)
    fill.wait()

    start = jnp.int32(0)
    for t in range(tiles):
        count = jnp.int32(0)
        for s in range(pairs):
            count = count + about_ref[s, 1, t]
        spare = -count & (UNROLL - 1)
        for u in range(UNROLL):
            list_ref[start + u] = (zero_row << PLANE_SHIFT) + (t << TILE_SHIFT) + capacity

        def enlist(s, filled, t=t):
            found = about_ref[s, 1, t]

            def some(low, high):
                for k in range(low, high):
                    place = k if t % 2 == 0 else capacity // 2 - 1 - k
                    code = about_ref[s, 0, t // 2 * (capacity // 2) + place]
                    list_ref[filled + k] = code + (t << TILE_SHIFT)

            few = capacity // 3

            @pl.when(found > 0)
            def _():
                some(0, few)

                @pl.when(found > few)
                def _():
                    some(few, capacity // 2)

            return filled + found

        lax.fori_loop(0, pairs, enlist, start + spare)
        start = start + count + spare
    for u in range((CHUNKS + AHEAD) * UNROLL):
        list_ref[start + u] = (zero_row << PLANE_SHIFT) + capacity
    chunks = start >> UNROLL.bit_length() - 1
    zero = jnp.zeros((16, 128), jnp.bfloat16)

    def read(which):
        entry = list_ref[which]
        slot = entry & ((1 << TILE_SHIFT) - 1)
        plane = (entry >> PLANE_SHIFT) & ((1 << (SOURCE_SHIFT - PLANE_SHIFT)) - 1)
        source = entry >> SOURCE_SHIFT
        row = 3 * slot + source * (stride - 3 * (capacity + 1))
        table = jnp.broadcast_to(table_ref[pl.ds(plane, 1), :], (8, 128))

        def words(i):
            return got_ref[pl.ds(row + i, 1), :]

        def parts(shift):
            start = (words(1) >> shift) & 0xFFFF
            offset = ((words(2) >> shift) & 7) << 4
            return spread_parts(
                jnp.broadcast_to(start, (8, 128)), jnp.broadcast_to(offset, (8, 128)), table
            )

        def sample(part):
            step = about_ref[source, 1, tiles].astype(jnp.float32) * (1.0 / (FULL * SCALE))
            return ((words(0) << (16 * part)) >> 16).astype(jnp.float32) * step

        return slot, sample, parts

    def chunk_tile(turn):
        return (list_ref[turn * UNROLL] >> TILE_SHIFT) & 15

    def front(turn, which):
        row_ref, kept_ref = row_refs[which % len(row_refs)], kept_refs[which % len(kept_refs)]
        blocks = [read(turn * UNROLL + u) for u in range(UNROLL)]
        matrices = []
        for _, _, parts in blocks:
            taps, group = parts(16)
            taps = taps.astype(jnp.bfloat16)
            group = group.astype(jnp.float32).astype(jnp.bfloat16)
            matrices.append(
                jnp.concatenate([jnp.where(group == k, taps, zero) for k in range(groups)], axis=0)
            )
        row_matrix = jnp.concatenate(matrices, axis=1)
        row_ref[...] = row_matrix
        partial = jnp.dot(
            turned_ref[chunk_tile(turn)], row_matrix, preferred_element_type=jnp.float32
        )
        for u, (slot, sample, parts) in enumerate(blocks):
            columns = slice(128 * u, 128 * u + 128)
            taps, group = parts(0)
            residuals = []
            for part in range(2):
                picked = jnp.zeros((16, 128), jnp.float32)
                for k in range(groups):
                    low = part * side + 16 * k
                    picked = jnp.where(group == k, partial[low : low + 16, columns], picked)
                model = jnp.sum(picked * taps, axis=0, keepdims=True)
                residuals.append(sample(part) - model)
                kept_ref[part : part + 1, columns] = residuals[part]
            residual_ref[slot] = jnp.concatenate(residuals, axis=0).astype(jnp.bfloat16)

    def back(turn, which):
        row_ref, kept_ref = row_refs[which % len(row_refs)], kept_refs[which % len(kept_refs)]
        weighted = []
        for u in range(UNROLL):
            _, _, parts = read(turn * UNROLL + u)
            columns = slice(128 * u, 128 * u + 128)
            taps, group = parts(0)
            group = group.astype(jnp.float32).astype(jnp.bfloat16)
            pieces = []
            for part in range(2):
                value = (kept_ref[part : part + 1, columns] * taps).astype(jnp.bfloat16)
                pieces += [jnp.where(group == k, value, zero) for k in range(groups)]
            weighted.append(jnp.concatenate(pieces, axis=0))
        grid_ref[chunk_tile(turn)] += lax.dot_general(
            jnp.concatenate(weighted, axis=1),
            row_ref[...],
            (((1,), (1,)), ((), ())),
            preferred_element_type=jnp.float32,
        )

    def step(turn, carry):
        for which in range(CHUNKS):
            front(turn * CHUNKS + which + AHEAD, which + AHEAD)
            back(turn * CHUNKS + which, which)
        return carry

    for which in range(AHEAD):
        front(which, which)
    lax.fori_loop(0, scalar_div(chunks + CHUNKS - 1, CHUNKS), step, 0)
    half = tiles // 2
    member = member_ref[0]
    for t in range(half):
        own_ref[t] = grid_ref[member * half + t]
        other_ref[t] = grid_ref[(1 - member) * half + t].astype(jnp.bfloat16)


def body(visibilities, uv_cell, sub_pixel, w_plane, block_tile, model_grid, kernel_table, coupling):
    owners = lax.axis_size("tile")
    pairs = owners // 2
    _, blocks, _, rows = visibilities.shape
    capacity = 2 * (3 * blocks // owners)
    _, tiles_here, side, wide = model_grid.shape
    planes, oversample, support = kernel_table.shape
    slots = pairs * (capacity + 1)
    member = lax.axis_index("tile") // pairs
    swap = [(t, (t + pairs) % owners) for t in range(owners)]
    halves = [list(range(pairs)), list(range(pairs, owners))]

    model = lax.all_gather(
        model_grid[0],
        "tile",
        axis=0,
        tiled=True,
        axis_index_groups=[[t, t + pairs] for t in range(pairs)],
    )
    sent, slot = pl.pallas_call(
        lambda *refs: pack_kernel(pairs, capacity, tiles_here, *refs),
        out_shape=(
            jax.ShapeDtypeStruct((pairs * rows_per_source(capacity), rows), jnp.int32),
            jax.ShapeDtypeStruct((blocks,), jnp.int32),
        ),
        in_specs=[HBM] * 5,
        out_specs=(VMEM, SMEM),
        scratch_shapes=[
            pltpu.SMEM((blocks,), jnp.int32),
            pltpu.SMEM((blocks,), jnp.int32),
            pltpu.SMEM((blocks,), jnp.int32),
            pltpu.VMEM((2 * blocks, rows), jnp.float32),
            pltpu.VMEM((2 * blocks, rows), jnp.int32),
            pltpu.VMEM((2 * blocks, rows), jnp.int32),
            pltpu.VMEM((pairs, rows), jnp.int32),
            pltpu.SMEM((pairs * 2 * tiles_here,), jnp.int32),
            pltpu.SemaphoreType.DMA((5,)),
        ],
        compiler_params=WHOLE_PARAMS,
        name="pack_blocks",
    )(
        w_plane[0],
        block_tile[0],
        *[array.reshape(2 * blocks, rows) for array in (visibilities, uv_cell, sub_pixel)],
    )
    got = lax.all_to_all(
        sent, "tile", split_axis=0, concat_axis=0, tiled=True, axis_index_groups=halves
    )
    own_row = lax.dynamic_index_in_dim(coupling, lax.axis_index("freq"), 0, keepdims=False)
    slot, own_row, got = lax.optimization_barrier(
        (slot + lax.div(lax.axis_index("tile"), owners), own_row, got)
    )
    table = jnp.pad(
        kernel_table.astype(jnp.float32), ((0, 8), (0, 0), (0, 16 - support))
    ).reshape(planes + 8, 16 * oversample)
    residual, own, other = pl.pallas_call(
        lambda *refs: grid_kernel(pairs, capacity, *refs),
        out_shape=(
            jax.ShapeDtypeStruct((slots, 2, rows), jnp.bfloat16),
            jax.ShapeDtypeStruct((tiles_here, wide, side), jnp.float32),
            jax.ShapeDtypeStruct((tiles_here, wide, side), jnp.bfloat16),
        ),
        in_specs=[SMEM, VMEM, VMEM, VMEM],
        out_specs=(VMEM, VMEM, VMEM),
        scratch_shapes=[
            pltpu.VMEM((2 * tiles_here, wide, side), jnp.bfloat16),
            pltpu.VMEM((2 * tiles_here, wide, side), jnp.float32),
            pltpu.VMEM((pairs, 2, rows), jnp.int32),
            pltpu.SMEM((pairs, 2, rows), jnp.int32),
            pltpu.SMEM(
                (slots + capacity + (2 * tiles_here + CHUNKS + AHEAD) * UNROLL,), jnp.int32
            ),
            pltpu.SemaphoreType.DMA,
            *[pltpu.VMEM((side, UNROLL * rows), jnp.bfloat16)] * BUFFERS,
            *[pltpu.VMEM((8, UNROLL * rows), jnp.float32)] * BUFFERS,
        ],
        compiler_params=PARAMS,
        name="grid_blocks",
    )(member[None], got, table, model)

    returned = lax.all_to_all(
        residual, "tile", split_axis=0, concat_axis=0, tiled=True, axis_index_groups=halves
    )
    grid_sum = own + lax.ppermute(other, "tile", swap).astype(jnp.float32)
    grids = lax.all_gather(grid_sum.astype(jnp.bfloat16)[None], "freq", axis=0, tiled=True)
    residuals, coupled_grid = pl.pallas_call(
        finish_kernel,
        out_shape=(
            jax.ShapeDtypeStruct((blocks, 2, rows), jnp.float32),
            jax.ShapeDtypeStruct((tiles_here, side, wide), jnp.float32),
        ),
        in_specs=[SMEM, SMEM, VMEM, VMEM],
        out_specs=(VMEM, VMEM),
        compiler_params=PARAMS,
        name="finish",
    )(own_row, slot, returned, grids)
    return (residuals[None], coupled_grid[None])


def solution(mesh):
    return jax.shard_map(
        body,
        mesh=mesh,
        in_specs=(
            P("freq", "tile", None, None),
            P("freq", "tile", None, None),
            P("freq", "tile", None, None),
            P("freq", "tile"),
            P("freq", "tile"),
            P("freq", "tile", None, None),
            P(),
            P(),
        ),
        out_specs=(P("freq", "tile", None, None), P("freq", "tile", None, None)),
        check_vma=False,
    )
```

```python
import jax
import jax.numpy as jnp
from jax import lax
from jax.experimental import pallas as pl
from jax.experimental.pallas import tpu as pltpu
from jax.sharding import PartitionSpec as P

UNROLL = 2
CHUNKS = 35
AHEAD = 2
BUFFERS = 5
VMEM = pl.BlockSpec(memory_space=pltpu.VMEM)
SMEM = pl.BlockSpec(memory_space=pltpu.SMEM)
HBM = pl.BlockSpec(memory_space=pltpu.HBM)
PARAMS = pltpu.CompilerParams(vmem_limit_bytes=32 * 1024 * 1024)
WHOLE_PARAMS = pltpu.CompilerParams(vmem_limit_bytes=62 * 1024 * 1024)
TILE_SHIFT = 12
PLANE_SHIFT = 16
SOURCE_SHIFT = 21
FULL = 32767
SCALE = 2.0**20


def scalar_div(value, count):
    shift = count.bit_length() - 1
    return value >> shift if count == 1 << shift else lax.div(value, count)


def first_slot(local, rank, capacity):
    half = capacity // 2
    return (local >> 1) * half + jnp.where((local & 1) == 0, rank, half - 1 - rank)


def rows_per_source(capacity):
    return (3 * (capacity + 1) + 7) // 8 * 8


def two_halves(high, low):
    return (high << 16) | (low & 0xFFFF)


def pack_kernel(pairs, capacity, tiles_here, plane_hbm, tile_hbm, vis_hbm, cell_hbm, sub_hbm,
                sent_ref, slot_ref, row_ref, plane_ref, tile_ref, vis_ref, cell_ref, sub_ref, code_ref,
                count_ref, load_sem):
    blocks = tile_ref.shape[0]
    stride = rows_per_source(capacity)
    tiles = 2 * tiles_here
    lane = lax.broadcasted_iota(jnp.int32, (1, 128), 1)
    loads = [
        pltpu.make_async_copy(source, target, load_sem.at[i])
        for i, (source, target) in enumerate(
            [
                (tile_hbm, tile_ref),
                (plane_hbm, plane_ref),
                (vis_hbm, vis_ref),
                (cell_hbm, cell_ref),
                (sub_hbm, sub_ref),
            ]
        )
    ]
    for copy in loads:
        copy.start()
    for key in range(pairs * tiles):
        count_ref[key] = 0
    for copy in loads:
        copy.wait()

    def assign(b):
        tile = tile_ref[b]
        owner = scalar_div(tile, tiles_here)
        high = (owner >= pairs).astype(jnp.int32)
        pair = owner - high * pairs
        local = tile - (owner - high) * tiles_here
        key = pair * tiles + local
        rank = count_ref[key]
        count_ref[key] = rank + 1
        place = first_slot(local, rank, capacity)
        slot_ref[b] = pair * (capacity + 1) + place
        row_ref[b] = pair * stride + 3 * place
        codes = code_ref[pl.ds(pair, 1), :]
        code_ref[pl.ds(pair, 1), :] = jnp.where(lane == place, plane_ref[b] << PLANE_SHIFT, codes)

    largest = jnp.max(jnp.max(jnp.abs(vis_ref[...]), axis=0, keepdims=True), axis=1, keepdims=True)
    largest = jnp.maximum(jnp.ceil(largest * SCALE), 1.0)
    inverse = (FULL * SCALE) / largest

    def move(four):
        rows = pl.ds(pl.multiple_of(8 * four, 8), 8)
        value = jnp.clip(jnp.round(vis_ref[rows, :] * inverse), -FULL, FULL).astype(jnp.int32)
        words = [
            two_halves(parts, pltpu.roll(parts, 7, 0))
            for parts in [value, cell_ref[rows, :], sub_ref[rows, :]]
        ]
        for u in range(4):
            row = row_ref[4 * four + u]
            for i, word in enumerate(words):
                sent_ref[pl.ds(row + i, 1), :] = word[2 * u : 2 * u + 1]

    def step(turn, carry):
        for which in range(8):
            assign(8 * turn + 8 + which)
        move(2 * turn)
        move(2 * turn + 1)
        return carry

    for which in range(8):
        assign(which)
    lax.fori_loop(0, blocks // 8 - 1, step, 0)
    move(blocks // 4 - 2)
    move(blocks // 4 - 1)
    for d in range(pairs):
        counts = jnp.broadcast_to(largest.astype(jnp.int32), (1, 128))
        for t in range(tiles):
            counts = jnp.where(lane == t, count_ref[d * tiles + t], counts)
        row = d * stride + 3 * capacity
        sent_ref[row : row + 1, :] = code_ref[d : d + 1, :]
        sent_ref[row + 1 : row + 2, :] = jnp.zeros((1, 128), jnp.int32)
        sent_ref[row + 2 : row + 3, :] = counts


def finish_kernel(row_ref, slot_ref, returned_ref, grid_ref, residual_ref, coupled_ref):
    planes, tiles_here = grid_ref.shape[:2]
    for t in range(tiles_here):
        coupled_ref[t] = sum(
            row_ref[g] * grid_ref[g, t].astype(jnp.float32) for g in range(planes)
        ).T

    def step(turn, carry):
        for which in range(32):
            b = turn * 32 + which
            residual_ref[b] = returned_ref[slot_ref[b]].astype(jnp.float32)
        return carry

    lax.fori_loop(0, residual_ref.shape[0] // 32, step, 0)


def spread_parts(start, offset, table):
    sublane = lax.broadcasted_iota(jnp.int32, (8, 128), 0)
    taps, group = [], []
    for low in (0, 8):
        delta = sublane + low - start
        taps.append(
            jnp.take_along_axis(table, (delta & 15) + offset, axis=1, mode="promise_in_bounds")
        )
        group.append((15 - delta) >> 4)
    return jnp.concatenate(taps, axis=0), jnp.concatenate(group, axis=0)


def grid_kernel(pairs, capacity, member_ref, got_ref, table_ref, model_ref, residual_ref, own_ref,
                other_ref, turned_ref, grid_ref, code_ref, about_ref, list_ref, sem, *buffers):
    row_refs, picked_refs = buffers[:BUFFERS], buffers[BUFFERS:]
    tiles, side, wide = model_ref.shape
    groups = side // 16
    zero_row = table_ref.shape[0] - 8
    stride = rows_per_source(capacity)
    lane = lax.broadcasted_iota(jnp.int32, (1, 128), 1)
    for s in range(pairs):
        row = s * stride + 3 * capacity
        code_ref[s, 0:1, :] = got_ref[row : row + 1, :] + (
            lane + s * (capacity + 1) + (s << SOURCE_SHIFT)
        )
        code_ref[s, 1:2, :] = got_ref[row + 2 : row + 3, :]
    fill = pltpu.make_async_copy(code_ref, about_ref, sem)
    fill.start()
    for t in range(tiles):
        turned_ref[t] = model_ref[t].T
    grid_ref[...] = jnp.zeros_like(grid_ref)
    fill.wait()

    start = jnp.int32(0)
    for t in range(tiles):
        count = jnp.int32(0)
        for s in range(pairs):
            count = count + about_ref[s, 1, t]
        spare = -count & (UNROLL - 1)
        for u in range(UNROLL):
            list_ref[start + u] = (zero_row << PLANE_SHIFT) + (t << TILE_SHIFT) + capacity

        def enlist(s, filled, t=t):
            found = about_ref[s, 1, t]

            def some(low, high):
                for k in range(low, high):
                    place = k if t % 2 == 0 else capacity // 2 - 1 - k
                    code = about_ref[s, 0, t // 2 * (capacity // 2) + place]
                    list_ref[filled + k] = code + (t << TILE_SHIFT)

            few = capacity // 3

            @pl.when(found > 0)
            def _():
                some(0, few)

                @pl.when(found > few)
                def _():
                    some(few, capacity // 2)

            return filled + found

        lax.fori_loop(0, pairs, enlist, start + spare)
        start = start + count + spare
    for u in range((CHUNKS + AHEAD) * UNROLL):
        list_ref[start + u] = (zero_row << PLANE_SHIFT) + capacity
    chunks = start >> UNROLL.bit_length() - 1
    zero = jnp.zeros((16, 128), jnp.bfloat16)

    def read(which):
        entry = list_ref[which]
        slot = entry & ((1 << TILE_SHIFT) - 1)
        plane = (entry >> PLANE_SHIFT) & ((1 << (SOURCE_SHIFT - PLANE_SHIFT)) - 1)
        source = entry >> SOURCE_SHIFT
        row = 3 * slot + source * (stride - 3 * (capacity + 1))
        table = jnp.broadcast_to(table_ref[pl.ds(plane, 1), :], (8, 128))

        def words(i):
            return got_ref[pl.ds(row + i, 1), :]

        def parts(shift):
            start = (words(1) >> shift) & 0xFFFF
            offset = ((words(2) >> shift) & 7) << 4
            return spread_parts(
                jnp.broadcast_to(start, (8, 128)), jnp.broadcast_to(offset, (8, 128)), table
            )

        def sample(part):
            step = about_ref[source, 1, tiles].astype(jnp.float32) * (1.0 / (FULL * SCALE))
            return ((words(0) << (16 * part)) >> 16).astype(jnp.float32) * step

        return slot, sample, parts

    def chunk_tile(turn):
        return (list_ref[turn * UNROLL] >> TILE_SHIFT) & 15

    def front(turn, which):
        row_ref, picked_ref = row_refs[which % len(row_refs)], picked_refs[which % len(picked_refs)]
        blocks = [read(turn * UNROLL + u) for u in range(UNROLL)]
        matrices = []
        for _, _, parts in blocks:
            taps, group = parts(16)
            taps = taps.astype(jnp.bfloat16)
            group = group.astype(jnp.float32).astype(jnp.bfloat16)
            matrices.append(
                jnp.concatenate([jnp.where(group == k, taps, zero) for k in range(groups)], axis=0)
            )
        row_matrix = jnp.concatenate(matrices, axis=1)
        row_ref[...] = row_matrix
        partial = jnp.dot(
            turned_ref[chunk_tile(turn)], row_matrix, preferred_element_type=jnp.float32
        )
        for u, (_, _, parts) in enumerate(blocks):
            columns = slice(128 * u, 128 * u + 128)
            taps, group = parts(0)
            for part in range(2):
                picked = jnp.zeros((16, 128), jnp.float32)
                for k in range(groups):
                    low = part * side + 16 * k
                    picked = jnp.where(group == k, partial[low : low + 16, columns], picked)
                picked_ref[part, :, columns] = picked * taps

    def back(turn, which):
        row_ref, picked_ref = row_refs[which % len(row_refs)], picked_refs[which % len(picked_refs)]
        weighted = []
        for u in range(UNROLL):
            slot, sample, parts = read(turn * UNROLL + u)
            columns = slice(128 * u, 128 * u + 128)
            taps, group = parts(0)
            group = group.astype(jnp.float32).astype(jnp.bfloat16)
            residuals, pieces = [], []
            for part in range(2):
                model = jnp.sum(picked_ref[part, :, columns], axis=0, keepdims=True)
                residual = sample(part) - model
                residuals.append(residual)
                value = (residual * taps).astype(jnp.bfloat16)
                pieces += [jnp.where(group == k, value, zero) for k in range(groups)]
            residual_ref[slot] = jnp.concatenate(residuals, axis=0).astype(jnp.bfloat16)
            weighted.append(jnp.concatenate(pieces, axis=0))
        grid_ref[chunk_tile(turn)] += lax.dot_general(
            jnp.concatenate(weighted, axis=1),
            row_ref[...],
            (((1,), (1,)), ((), ())),
            preferred_element_type=jnp.float32,
        )

    def step(turn, carry):
        for which in range(CHUNKS):
            front(turn * CHUNKS + which + AHEAD, which + AHEAD)
            back(turn * CHUNKS + which, which)
        return carry

    for which in range(AHEAD):
        front(which, which)
    lax.fori_loop(0, scalar_div(chunks + CHUNKS - 1, CHUNKS), step, 0)
    half = tiles // 2
    member = member_ref[0]
    for t in range(half):
        own_ref[t] = grid_ref[member * half + t]
        other_ref[t] = grid_ref[(1 - member) * half + t].astype(jnp.bfloat16)


def body(visibilities, uv_cell, sub_pixel, w_plane, block_tile, model_grid, kernel_table, coupling):
    owners = lax.axis_size("tile")
    pairs = owners // 2
    _, blocks, _, rows = visibilities.shape
    capacity = 2 * (3 * blocks // owners)
    _, tiles_here, side, wide = model_grid.shape
    planes, oversample, support = kernel_table.shape
    slots = pairs * (capacity + 1)
    member = lax.axis_index("tile") // pairs
    swap = [(t, (t + pairs) % owners) for t in range(owners)]
    halves = [list(range(pairs)), list(range(pairs, owners))]

    model = lax.all_gather(
        model_grid[0],
        "tile",
        axis=0,
        tiled=True,
        axis_index_groups=[[t, t + pairs] for t in range(pairs)],
    )
    sent, slot = pl.pallas_call(
        lambda *refs: pack_kernel(pairs, capacity, tiles_here, *refs),
        out_shape=(
            jax.ShapeDtypeStruct((pairs * rows_per_source(capacity), rows), jnp.int32),
            jax.ShapeDtypeStruct((blocks,), jnp.int32),
        ),
        in_specs=[HBM] * 5,
        out_specs=(VMEM, SMEM),
        scratch_shapes=[
            pltpu.SMEM((blocks,), jnp.int32),
            pltpu.SMEM((blocks,), jnp.int32),
            pltpu.SMEM((blocks,), jnp.int32),
            pltpu.VMEM((2 * blocks, rows), jnp.float32),
            pltpu.VMEM((2 * blocks, rows), jnp.int32),
            pltpu.VMEM((2 * blocks, rows), jnp.int32),
            pltpu.VMEM((pairs, rows), jnp.int32),
            pltpu.SMEM((pairs * 2 * tiles_here,), jnp.int32),
            pltpu.SemaphoreType.DMA((5,)),
        ],
        compiler_params=WHOLE_PARAMS,
        name="pack_blocks",
    )(
        w_plane[0],
        block_tile[0],
        *[array.reshape(2 * blocks, rows) for array in (visibilities, uv_cell, sub_pixel)],
    )
    got = lax.all_to_all(
        sent, "tile", split_axis=0, concat_axis=0, tiled=True, axis_index_groups=halves
    )
    own_row = lax.dynamic_index_in_dim(coupling, lax.axis_index("freq"), 0, keepdims=False)
    slot, own_row, got = lax.optimization_barrier(
        (slot + lax.div(lax.axis_index("tile"), owners), own_row, got)
    )
    table = jnp.pad(
        kernel_table.astype(jnp.float32), ((0, 8), (0, 0), (0, 16 - support))
    ).reshape(planes + 8, 16 * oversample)
    residual, own, other = pl.pallas_call(
        lambda *refs: grid_kernel(pairs, capacity, *refs),
        out_shape=(
            jax.ShapeDtypeStruct((slots, 2, rows), jnp.bfloat16),
            jax.ShapeDtypeStruct((tiles_here, wide, side), jnp.float32),
            jax.ShapeDtypeStruct((tiles_here, wide, side), jnp.bfloat16),
        ),
        in_specs=[SMEM, VMEM, VMEM, VMEM],
        out_specs=(VMEM, VMEM, VMEM),
        scratch_shapes=[
            pltpu.VMEM((2 * tiles_here, wide, side), jnp.bfloat16),
            pltpu.VMEM((2 * tiles_here, wide, side), jnp.float32),
            pltpu.VMEM((pairs, 2, rows), jnp.int32),
            pltpu.SMEM((pairs, 2, rows), jnp.int32),
            pltpu.SMEM(
                (slots + capacity + (2 * tiles_here + CHUNKS + AHEAD) * UNROLL,), jnp.int32
            ),
            pltpu.SemaphoreType.DMA,
            *[pltpu.VMEM((side, UNROLL * rows), jnp.bfloat16)] * BUFFERS,
            *[pltpu.VMEM((2, 16, UNROLL * rows), jnp.float32)] * BUFFERS,
        ],
        compiler_params=PARAMS,
        name="grid_blocks",
    )(member[None], got, table, model)

    returned = lax.all_to_all(
        residual, "tile", split_axis=0, concat_axis=0, tiled=True, axis_index_groups=halves
    )
    grid_sum = own + lax.ppermute(other, "tile", swap).astype(jnp.float32)
    grids = lax.all_gather(grid_sum.astype(jnp.bfloat16)[None], "freq", axis=0, tiled=True)
    residuals, coupled_grid = pl.pallas_call(
        finish_kernel,
        out_shape=(
            jax.ShapeDtypeStruct((blocks, 2, rows), jnp.float32),
            jax.ShapeDtypeStruct((tiles_here, side, wide), jnp.float32),
        ),
        in_specs=[SMEM, SMEM, VMEM, VMEM],
        out_specs=(VMEM, VMEM),
        compiler_params=PARAMS,
        name="finish",
    )(own_row, slot, returned, grids)
    return (residuals[None], coupled_grid[None])


def solution(mesh):
    return jax.shard_map(
        body,
        mesh=mesh,
        in_specs=(
            P("freq", "tile", None, None),
            P("freq", "tile", None, None),
            P("freq", "tile", None, None),
            P("freq", "tile"),
            P("freq", "tile"),
            P("freq", "tile", None, None),
            P(),
            P(),
        ),
        out_specs=(P("freq", "tile", None, None), P("freq", "tile", None, None)),
        check_vma=False,
    )
```
